32 devices in a mesh: grp: 2 (over y), mon: 4 (over z), pair: 2 (over x), sub: 2 (over core).
Axes of the slice: x: 2, y: 2, z: 4, core: 2. Of those that a mesh axis runs over, the one named last changes fastest.
Arguments:
- dfactors: bfloat16 [8192, 1024], P('mon', 'sub'), may hold values from -0.5 to 0.5
- block_mask: int32 [64, 1024], P('mon', 'sub'), may hold values 0 or 1
- base_flow: float32 [8192], P('mon'), may hold values from -5 to 5
- branch_row: int32 [1024], replicated, may hold values from 0 to 8191, as said below
- pair_slots: int32 [3072, 2], P(('grp', 'pair')), parts along dimension 0, may hold values from 0 to 1023, as said below
- pair_counts: int32 [4], P(('grp', 'pair')), parts along dimension 0, may hold values from 1 to 768, 1024 in all
Outputs:
- post_flows: bfloat16 [8192, 3072], P(('mon', 'sub'), ('grp', 'pair')), parts along dimension 1
The draws below stay inside these ranges and needn't reach their ends.
There are 2 independent parts, one for each index of `grp`. The reference program is written for one: setup_inputs(seed, part) draws one part's arguments, and reference() takes and returns one part's arrays. A program takes and returns all parts, laid end to end along the dimension named above; an argument that names none is the same for every part. Nothing has to cross between parts.
Inputs may be any that keep to these rules, and one draw needn't show every extreme that they name: `branch_row`: all entries distinct. `pair_slots`: the two candidates of a slot differ; empty slots hold valid pairs too. `pair_counts`: the counts sum to 1024; an owner's live slots are its first ones.
All inputs are finite; a program needn't handle non-finite values. No bound on the sum of `block_mask` or of `pair_counts` on one device may be relied on, other than what follows from the above.
Results may differ from the reference program's by a relative error of at most 0.004.
Values may be sent and summed in bfloat16 or wider, within the bound.
No kernel may reach another device: no remote copies, remote signals or barrier semaphores. Data moves between devices by JAX's collectives and lax.ppermute only.
A program may use at most 64 MiB of HBM per device.

```python
import math
import jax
import jax.numpy as jnp
import numpy as np
from jax import lax

BLOCK = 128
C = 1024
MB_DEV = 16
M = 8192
PAIRS = 1024
PCAP = 768
SLOTS = 1536
N_MON = 4
N_PAIR = 2
N_SUB = 2


def draw_branch_row(key, part):
    return jax.random.permutation(jax.random.fold_in(key, 11), M)[:C].astype(jnp.int32)


def draw_pair_slots(key, part):
    first_out = jax.random.randint(jax.random.fold_in(key, 21), (SLOTS,), 0, C)
    offset_draw = jax.random.randint(jax.random.fold_in(key, 22), (SLOTS,), 1, C)
    second_out = (first_out + offset_draw) % C
    first_out = first_out.at[0].set(C - 1)
    second_out = second_out.at[0].set(0)
    return jnp.stack([first_out, second_out], axis=1).astype(jnp.int32)


def place_ends(drawn, stream_key, least, high):
    spot = [jax.random.randint(jax.random.fold_in(stream_key, axis), (), 0, length) for axis, length in enumerate(drawn.shape)]
    widest = drawn.shape.index(max(drawn.shape))
    next_to = spot[:widest] + [(spot[widest] + 1) % drawn.shape[widest]] + spot[widest + 1:]
    return drawn.at[tuple(spot)].set(least).at[tuple(next_to)].set(high)


def shard_levels(own_key, extent, shards, smallest, top_value):
    def one(dim, blocks):
        heights = jax.random.uniform(jax.random.fold_in(jax.random.fold_in(own_key, 6), dim), (blocks,), jnp.float32, smallest / len(shards), top_value / len(shards))
        return jnp.repeat(jnp.exp(heights), extent[dim] // blocks).reshape((-1,) + (1,) * (len(extent) - dim - 1))

    gain = one(*shards[0])
    for cut in shards[1:]:
        gain = gain * one(*cut)
    return gain


def length_profile(amount, total, most, skew):
    weights = [(1 << 20) // math.isqrt(grade ** skew) + 1 for grade in range(2, amount + 1)]
    spare, given = total - most - (amount - 1), [1] * (amount - 1)
    while spare > 0:
        free = [i for i in range(amount - 1) if given[i] < most]
        whole, left = sum([weights[i] for i in free]), spare
        for i in free:
            more = min(most - given[i], max(1, left * weights[i] // whole), spare)
            given[i] = given[i] + more
            spare = spare - more
    return np.array([most] + given)


def ragged_sizes(key, amount, total, reach, slope):
    if amount == 2:
        one = jax.random.randint(key, (), max(1, total - reach), min(reach, total - 1) + 1)
        return jnp.stack([one, total - one])
    sizes = jnp.asarray(length_profile(amount, total, reach, slope), jnp.int32)
    twos = (amount - 1) // 2
    donor, sink = sizes[1:1 + 2 * twos:2], sizes[2:2 + 2 * twos:2]
    slack = jnp.minimum(donor - 1, reach - sink)
    shifted = jax.random.randint(jax.random.fold_in(key, 1), (twos,), 0, 1 << 20) % (slack + 1)
    sizes = sizes.at[1:1 + 2 * twos:2].set(donor - shifted).at[2:2 + 2 * twos:2].set(sink + shifted)
    return sizes[jax.random.permutation(jax.random.fold_in(key, 2), amount)]


def scatter_about(stream_key, extent, deviation, most, split=(), kind=jnp.bfloat16):
    drawn = jax.random.normal(stream_key, extent, jnp.float32) * deviation
    if len(split) > 0:
        drawn = shard_levels(stream_key, extent, split, -0.22, 0.18) * drawn
    return jnp.clip(drawn, min=-most, max=most).astype(kind)


def setup_inputs(seed: int = 0, part: int = 0) -> dict:
    keys = jax.random.split(jax.random.key(seed), 7)
    own_keys = jax.random.split(jax.random.fold_in(keys[6], part), 7)
    dfactors = jnp.clip(jax.random.uniform(keys[0], (M, C), jnp.float32, -0.5, 0.5) * shard_levels(keys[0], (M, C), ((0, 4), (1, 2)), -0.4, 0.0), -0.5, 0.5).astype(jnp.bfloat16)
    block_mask = place_ends((jax.random.randint(keys[1], (M // BLOCK, C), 0, 4) < 3).astype(jnp.int32), jax.random.fold_in(keys[1], 1), 0, 1)
    base_flow = scatter_about(keys[2], (M,), 1.0, 5.0, ((0, 4),), jnp.float32)
    branch_row = draw_branch_row(jax.random.fold_in(keys[6], 71), part)
    pair_slots = draw_pair_slots(jax.random.fold_in(jax.random.fold_in(keys[6], part), 71), part)
    pair_counts = ragged_sizes(own_keys[5], N_PAIR, PAIRS, PCAP, 2).astype(jnp.int32)
    return {"dfactors": dfactors, "block_mask": block_mask, "base_flow": base_flow, "branch_row": branch_row, "pair_slots": pair_slots, "pair_counts": pair_counts}


def reference(dfactors, block_mask, base_flow, branch_row, pair_slots, pair_counts):
    col_width = C // N_SUB
    block_keep = jnp.repeat(block_mask.astype(jnp.bfloat16), BLOCK, axis=0)
    masked = dfactors * block_keep
    first_out = pair_slots[:, 0]
    second_out = pair_slots[:, 1]
    first_row = branch_row[first_out]
    second_row = branch_row[second_out]
    cross_first = masked[first_row, second_out].astype(jnp.float32)
    cross_second = masked[second_row, first_out].astype(jnp.float32)
    flow_first = base_flow[first_row]
    flow_second = base_flow[second_row]
    determinant = 1.0 - cross_first * cross_second
    shift_first = (flow_first + cross_first * flow_second) / determinant
    shift_second = (flow_second + cross_second * flow_first) / determinant
    columns = jnp.arange(C, dtype=jnp.int32)[:, None]
    shift = (jnp.where(columns == first_out[None, :], shift_first[None, :], jnp.float32(0.0))
             + jnp.where(columns == second_out[None, :], shift_second[None, :], jnp.float32(0.0))).astype(jnp.bfloat16)
    slot_ids = jnp.arange(SLOTS, dtype=jnp.int32)
    live_slot = ((slot_ids % PCAP) < pair_counts[slot_ids // PCAP]).astype(jnp.float32)
    row_blocks = masked.reshape(N_MON, MB_DEV * BLOCK, C)
    flow_blocks = base_flow.reshape(N_MON, MB_DEV * BLOCK)

    def one_block(inputs):
        rows_here, flows_here = inputs
        total = jnp.zeros((rows_here.shape[0], SLOTS), jnp.float32)
        for which in range(N_SUB):
            partial_value = jnp.dot(rows_here[:, which * col_width:(which + 1) * col_width],
                              shift[which * col_width:(which + 1) * col_width],
                              preferred_element_type=jnp.float32).astype(jnp.bfloat16)
            total = total + lax.optimization_barrier(partial_value).astype(jnp.float32)
        return ((flows_here[:, None] + total) * live_slot[None, :]).astype(jnp.bfloat16)

    result = lax.map(one_block, (row_blocks, flow_blocks))
    return result.reshape(M, SLOTS)
```

```python
import functools

import jax
import jax.numpy as jnp
from jax import lax
from jax.experimental import pallas as pl
from jax.experimental.pallas import tpu as pltpu
from jax.sharding import PartitionSpec as P

BLOCK = 128
VMEM_LIMIT = 48 * 1024 * 1024


def chunk_of(total, want):
    size = min(total, want)
    while total % size:
        size -= BLOCK
    return size


def gather_kernel(d_hbm, mask_ref, base_ref, rows_ref, slots_ref, out_ref, d_ref, hot_ref, sems):
    chunks, chunk, cols = d_ref.shape
    rows_dev = chunks * chunk
    candidates = rows_ref.shape[1]
    cap = slots_ref.shape[1]
    sub_index = lax.axis_index("sub")
    row_start = lax.axis_index("mon") * rows_dev
    col_start = pl.multiple_of(sub_index * cols, cols)
    copies = [
        pltpu.make_async_copy(d_hbm.at[pl.ds(i * chunk, chunk)], d_ref.at[i], sems.at[i])
        for i in range(chunks)
    ]
    for copy in copies:
        copy.start()

    for half in range(2):
        slot = slots_ref[half : half + 1, :]
        for c in range(0, candidates, 128):
            ids = lax.broadcasted_iota(jnp.int32, (128, cap), 0) + c
            hot_ref[c : c + 128, half * cap : (half + 1) * cap] = jnp.where(
                ids == slot, 1.0, 0.0
            ).astype(jnp.bfloat16)

    branch = rows_ref[...]
    which = lax.broadcasted_iota(jnp.int32, (8, candidates), 0)
    digits = jnp.where(
        which == 0,
        branch & 255,
        jnp.where(which == 1, (branch >> 8) & 255, jnp.where(which == 2, branch >> 16, 0)),
    )
    found = jnp.dot(
        digits.astype(jnp.float32).astype(jnp.bfloat16),
        hot_ref[...],
        preferred_element_type=jnp.float32,
    ).astype(jnp.int32)
    row = found[0:1] + (found[1:2] << 8) + (found[2:3] << 16) - row_start

    base = base_ref[...]
    blocks = base.shape[0]
    top = base.astype(jnp.bfloat16)
    rest = base - top.astype(jnp.float32)
    mid = rest.astype(jnp.bfloat16)
    low = (rest - mid.astype(jnp.float32)).astype(jnp.bfloat16)
    block_hot = jnp.where(
        lax.broadcasted_iota(jnp.int32, (blocks, 2 * cap), 0) == (row >> 7), 1.0, 0.0
    ).astype(jnp.bfloat16)
    lines = jnp.zeros((BLOCK, 2 * cap), jnp.float32)
    for part in (top, mid, low):
        lines += lax.dot_general(
            part, block_hot, (((0,), (0,)), ((), ())), preferred_element_type=jnp.float32
        )
    lane = lax.broadcasted_iota(jnp.int32, (BLOCK, 2 * cap), 0)
    flow = jnp.sum(jnp.where(lane == (row & 127), lines, 0.0), axis=0, keepdims=True)
    flow = jnp.where(sub_index == 0, flow, 0.0)

    totals = [jnp.zeros((8, cap), jnp.float32) for _ in range(2)]
    for i in range(chunks):
        copies[i].wait()
        pieces = []
        for b in range(chunk // BLOCK):
            keep = mask_ref[i * (chunk // BLOCK) + b : i * (chunk // BLOCK) + b + 1, :]
            pieces.append(
                d_ref[i, b * BLOCK : (b + 1) * BLOCK, :]
                * keep.astype(jnp.float32).astype(jnp.bfloat16)
            )
        masked = jnp.concatenate(pieces, axis=0)
        for half in range(2):
            values = jnp.dot(
                masked,
                hot_ref[pl.ds(col_start, cols), half * cap : (half + 1) * cap],
                preferred_element_type=jnp.float32,
            )
            want = row[:, (1 - half) * cap : (2 - half) * cap]
            ids = lax.broadcasted_iota(jnp.int32, (chunk, cap), 0) + i * chunk
            picked = jnp.where(ids == want, values, 0.0)
            totals[half] += jnp.sum(picked.reshape(chunk // 8, 8, cap), axis=0)
    out_ref[0:1, :] = jnp.sum(totals[1], axis=0, keepdims=True)
    out_ref[1:2, :] = jnp.sum(totals[0], axis=0, keepdims=True)
    out_ref[2:3, :] = flow[:, :cap]
    out_ref[3:4, :] = flow[:, cap:]


def columns_kernel(n_sub, *refs):
    d_hbm = refs[:n_sub]
    mask_refs = refs[n_sub : 2 * n_sub]
    slots_ref, first_ref, second_ref, d_ref, hot_ref, sems = refs[2 * n_sub :]
    chunks, _, chunk, cols = d_ref.shape
    my_rows = chunks * chunk
    cap = slots_ref.shape[1]
    sub_index = lax.axis_index("sub")
    my_start = pl.multiple_of(sub_index * my_rows, my_rows)
    copies = []
    for i in range(chunks):
        for s in range(n_sub):
            copies.append(
                pltpu.make_async_copy(
                    d_hbm[s].at[pl.ds(my_start + i * chunk, chunk)],
                    d_ref.at[i, s],
                    sems.at[i, s],
                )
            )
            copies[-1].start()
    for s in range(n_sub):
        col_start = lax.rem(sub_index + n_sub - s, n_sub) * cols
        for half in range(2):
            slot = slots_ref[half : half + 1, :] - col_start
            for c in range(0, cols, 128):
                ids = lax.broadcasted_iota(jnp.int32, (128, cap), 0) + c
                hot_ref[s * cols + c : s * cols + c + 128, half * cap : (half + 1) * cap] = (
                    jnp.where(ids == slot, 1.0, 0.0).astype(jnp.bfloat16)
                )
    per = chunk // BLOCK
    for i in range(chunks):
        parts = []
        for s in range(n_sub):
            copies[i * n_sub + s].wait()
            keep = mask_refs[s][pl.ds(sub_index * (my_rows // BLOCK), my_rows // BLOCK), :]
            keep = keep.astype(jnp.float32).astype(jnp.bfloat16)
            parts.append(
                jnp.concatenate(
                    [
                        d_ref[i, s, b * BLOCK : (b + 1) * BLOCK, :] * keep[i * per + b : i * per + b + 1]
                        for b in range(per)
                    ],
                    axis=0,
                )
            )
        masked = jnp.concatenate(parts, axis=1)
        for half, ref in enumerate((first_ref, second_ref)):
            ref[i * chunk : (i + 1) * chunk, :] = jnp.dot(
                masked,
                hot_ref[:, half * cap : (half + 1) * cap],
                preferred_element_type=jnp.float32,
            ).astype(jnp.bfloat16)


def flows_kernel(n_parts, *refs):
    part_refs = refs[:n_parts]
    count_ref, base_ref, first_ref, second_ref, out_ref, line_ref = refs[n_parts:]
    cap = out_ref.shape[1]
    chunk = out_ref.shape[0]
    per = chunk // BLOCK
    step = pl.program_id(0)
    steps = pl.num_programs(0)

    @pl.when(step == 0)
    def _():
        total = part_refs[0][...]
        for ref in part_refs[1:]:
            total = total + ref[...]
        cross_first, cross_second = total[0:1], total[1:2]
        flow_first, flow_second = total[2:3], total[3:4]
        determinant = 1.0 - cross_first * cross_second
        line_ref[0:1] = (flow_first + cross_first * flow_second) / determinant
        line_ref[1:2] = (flow_second + cross_second * flow_first) / determinant

    shift_first = line_ref[0:1].astype(jnp.bfloat16).astype(jnp.float32)
    shift_second = line_ref[1:2].astype(jnp.bfloat16).astype(jnp.float32)
    live = lax.broadcasted_iota(jnp.int32, (1, cap), 1) < count_ref[0]
    block0 = (lax.axis_index("sub") * steps + step) * per
    for b in range(per):
        column = jnp.swapaxes(
            jnp.broadcast_to(base_ref[pl.ds(block0 + b, 1), :], (8, BLOCK)), 0, 1
        )[:, 0:1]
        rows = slice(b * BLOCK, (b + 1) * BLOCK)
        value = (
            column
            + shift_first * first_ref[rows, :].astype(jnp.float32)
            + shift_second * second_ref[rows, :].astype(jnp.float32)
        )
        out_ref[rows, :] = jnp.where(live, value, 0.0).astype(jnp.bfloat16)


def on_device(dfactors, block_mask, base_flow, branch_row, pair_slots, pair_counts):
    rows_dev, cols = dfactors.shape
    candidates = branch_row.shape[0]
    cap = pair_slots.shape[0]
    n_sub = lax.axis_size("sub")
    n_mon = lax.axis_size("mon")
    my_rows = rows_dev // n_sub
    slots = pair_slots.T
    base = base_flow.reshape(rows_dev // BLOCK, BLOCK)
    any_space = pl.BlockSpec(memory_space=pl.ANY)
    vmem = pl.BlockSpec(memory_space=pltpu.VMEM)

    factors = [dfactors]
    masks = [block_mask]
    for s in range(1, n_sub):
        perm = [(i, (i + s) % n_sub) for i in range(n_sub)]
        factors.append(lax.ppermute(dfactors, "sub", perm))
        masks.append(lax.ppermute(block_mask, "sub", perm))

    chunk = chunk_of(rows_dev, 256)
    chunks = rows_dev // chunk
    share = pl.pallas_call(
        gather_kernel,
        out_shape=jax.ShapeDtypeStruct((4, cap), jnp.float32),
        in_specs=[any_space, vmem, vmem, vmem, vmem],
        out_specs=vmem,
        scratch_shapes=[
            pltpu.VMEM((chunks, chunk, cols), jnp.bfloat16),
            pltpu.VMEM((candidates, 2 * cap), jnp.bfloat16),
            pltpu.SemaphoreType.DMA((chunks,)),
        ],
        compiler_params=pltpu.CompilerParams(vmem_limit_bytes=VMEM_LIMIT),
        cost_estimate=pl.CostEstimate(
            flops=4 * rows_dev * cols * cap, bytes_accessed=rows_dev * cols * 2, transcendentals=0
        ),
        name="pair_values",
    )(dfactors, block_mask, base, branch_row.reshape(1, candidates), slots)

    shares = [share]
    for dm in range(n_mon):
        for ds in range(n_sub):
            if dm or ds:
                perm = [
                    (m * n_sub + s, ((m + dm) % n_mon) * n_sub + (s + ds) % n_sub)
                    for m in range(n_mon)
                    for s in range(n_sub)
                ]
                shares.append(lax.ppermute(share, ("mon", "sub"), perm))

    my_chunk = chunk_of(my_rows, 256)
    my_chunks = my_rows // my_chunk
    first, second = pl.pallas_call(
        functools.partial(columns_kernel, n_sub),
        out_shape=[jax.ShapeDtypeStruct((my_rows, cap), jnp.bfloat16)] * 2,
        in_specs=[any_space] * n_sub + [vmem] * n_sub + [vmem],
        out_specs=[vmem, vmem],
        scratch_shapes=[
            pltpu.VMEM((my_chunks, n_sub, my_chunk, cols), jnp.bfloat16),
            pltpu.VMEM((n_sub * cols, 2 * cap), jnp.bfloat16),
            pltpu.SemaphoreType.DMA((my_chunks, n_sub)),
        ],
        compiler_params=pltpu.CompilerParams(vmem_limit_bytes=VMEM_LIMIT),
        cost_estimate=pl.CostEstimate(
            flops=4 * my_rows * cols * n_sub * cap,
            bytes_accessed=my_rows * (cols * n_sub + 2 * cap) * 2,
            transcendentals=0,
        ),
        name="pair_columns",
    )(*factors, *masks, slots)

    smem = pl.BlockSpec(memory_space=pltpu.SMEM)
    block = pl.BlockSpec((my_chunk, cap), lambda i: (i, 0))
    return pl.pallas_call(
        functools.partial(flows_kernel, len(shares)),
        out_shape=jax.ShapeDtypeStruct((my_rows, cap), jnp.bfloat16),
        grid=(my_chunks,),
        in_specs=[vmem] * len(shares) + [smem, vmem, block, block],
        out_specs=block,
        scratch_shapes=[pltpu.VMEM((8, cap), jnp.float32)],
        compiler_params=pltpu.CompilerParams(vmem_limit_bytes=VMEM_LIMIT),
        name="post_flows",
    )(*shares, pair_counts, base, first, second)


def solution(mesh):
    return jax.shard_map(
        on_device,
        mesh=mesh,
        in_specs=(
            P("mon", "sub"),
            P("mon", "sub"),
            P("mon"),
            P(),
            P(("grp", "pair"), None),
            P(("grp", "pair")),
        ),
        out_specs=P(("mon", "sub"), ("grp", "pair")),
        check_vma=False,
    )
```

```python
import functools

import jax
import jax.numpy as jnp
from jax import lax
from jax.experimental import pallas as pl
from jax.experimental.pallas import tpu as pltpu
from jax.sharding import PartitionSpec as P

BLOCK = 128
LANES = 128
VMEM_LIMIT = 56 * 1024 * 1024
F32 = jnp.float32
BF16 = jnp.bfloat16


def chunk_of(total, want):
    size = min(total, want)
    while total % size:
        size -= BLOCK
    return size


def one_hot(hit):
    return jnp.where(hit, 1.0, 0.0).astype(BF16)


def rows_iota(shape):
    return lax.broadcasted_iota(jnp.int32, shape, 0)


def look_up(parts, index):
    blocks = parts[0].shape[0]
    table = jnp.concatenate([part.astype(F32) for part in parts], axis=0).astype(BF16)
    block = lax.rem(rows_iota((len(parts) * blocks, index.shape[1])), blocks)
    lines = lax.dot_general(
        table,
        one_hot(block == (index >> 7)),
        (((0,), (0,)), ((), ())),
        preferred_element_type=F32,
    )
    lane = rows_iota(lines.shape)
    return jnp.sum(jnp.where(lane == (index & 127), lines, 0.0), axis=0, keepdims=True)


def split_int(table):
    return [
        (table & mask).astype(F32).astype(BF16) for mask in (0xFF, 0xFF00, 0xFF0000)
    ]


def split_float(table):
    top = table.astype(BF16)
    rest = table - top.astype(F32)
    mid = rest.astype(BF16)
    return [top, mid, (rest - mid.astype(F32)).astype(BF16)]


def keep_blocks(values, mask, first_block):
    return jnp.concatenate(
        [
            values[b * BLOCK : (b + 1) * BLOCK]
            * mask[first_block + b : first_block + b + 1].astype(F32).astype(BF16)
            for b in range(values.shape[0] // BLOCK)
        ],
        axis=0,
    )


def values_kernel(
    d_hbm, mask_hbm, base_hbm, rows_hbm, slots_hbm, out_ref,
    d_ref, mask_ref, base_ref, rows_ref, slots_ref, hot_ref, sems, d_sems,
):
    chunks, chunk, cols = d_ref.shape
    rows_dev = chunks * chunk
    cap = slots_ref.shape[1]
    sub_index = lax.axis_index("sub")
    small = [
        pltpu.make_async_copy(src, dst, sems.at[i])
        for i, (src, dst) in enumerate(
            [(slots_hbm, slots_ref), (rows_hbm, rows_ref), (base_hbm, base_ref), (mask_hbm, mask_ref)]
        )
    ]
    large = [
        pltpu.make_async_copy(d_hbm.at[pl.ds(i * chunk, chunk)], d_ref.at[i], d_sems.at[i])
        for i in range(chunks)
    ]
    for copy in small + large:
        copy.start()
    small[0].wait()
    first, second = slots_ref[0:1, :], slots_ref[1:2, :]
    column = jnp.concatenate([second, first], axis=1) - sub_index * cols
    for c in range(0, cols, LANES):
        hot_ref[c : c + LANES, :] = one_hot(rows_iota((LANES, 2 * cap)) + c == column)
    small[1].wait()
    row = look_up(split_int(rows_ref[...]), jnp.concatenate([first, second], axis=1))
    row = row.astype(jnp.int32) - lax.axis_index("mon") * rows_dev
    small[2].wait()
    flow = jnp.where(sub_index == 0, look_up(split_float(base_ref[...]), row), 0.0)
    small[3].wait()
    total = jnp.zeros((8, 2 * cap), F32)
    for i in range(chunks):
        large[i].wait()
        masked = keep_blocks(d_ref[i], mask_ref, i * (chunk // BLOCK))
        values = jnp.dot(masked, hot_ref[...], preferred_element_type=F32)
        picked = jnp.where(rows_iota((chunk, 2 * cap)) + i * chunk == row, values, 0.0)
        total += jnp.sum(picked.reshape(chunk // 8, 8, 2 * cap), axis=0)
    cross = jnp.sum(total, axis=0, keepdims=True)
    for copy in range(out_ref.shape[0]):
        out_ref[copy, 0:1, :] = cross[:, :cap]
        out_ref[copy, 1:2, :] = cross[:, cap:]
        out_ref[copy, 2:3, :] = flow[:, :cap]
        out_ref[copy, 3:4, :] = flow[:, cap:]


def flows_kernel(n_sub, *refs):
    d_hbm = refs[:n_sub]
    mask_hbm = refs[n_sub : 2 * n_sub]
    (
        shares_hbm, slots_hbm, base_hbm, count_hbm, out_hbm,
        d_ref, mask_ref, shares_ref, slots_ref, base_ref, count_ref,
        shift_ref, post_ref, sems, d_sems, mask_sems, out_sems,
    ) = refs[2 * n_sub :]
    chunks, _, chunk, cols = d_ref.shape
    my_rows = chunks * chunk
    my_blocks = my_rows // BLOCK
    cap = slots_ref.shape[1]
    parts, _, width = post_ref.shape
    sub_index = lax.axis_index("sub")
    my_start = pl.multiple_of(sub_index * my_rows, my_rows)
    my_block = pl.multiple_of(sub_index * my_blocks, my_blocks)
    small = [
        pltpu.make_async_copy(src, dst, sems.at[i])
        for i, (src, dst) in enumerate(
            [
                (shares_hbm, shares_ref),
                (slots_hbm, slots_ref),
                (base_hbm.at[pl.ds(my_block, my_blocks)], base_ref),
                (count_hbm, count_ref),
            ]
        )
    ]
    masks = [
        pltpu.make_async_copy(
            mask_hbm[s].at[pl.ds(my_block, my_blocks)], mask_ref.at[s], mask_sems.at[s]
        )
        for s in range(n_sub)
    ]
    large = [
        [
            pltpu.make_async_copy(
                d_hbm[s].at[pl.ds(my_start + i * chunk, chunk)], d_ref.at[i, s], d_sems.at[i, s]
            )
            for s in range(n_sub)
        ]
        for i in range(chunks)
    ]
    for copy in small + masks + [copy for copies in large for copy in copies]:
        copy.start()
    for copy in small:
        copy.wait()
    total = jnp.sum(shares_ref[...], axis=0)
    cross_first, cross_second = total[0:1], total[1:2]
    flow_first, flow_second = total[2:3], total[3:4]
    determinant = 1.0 - cross_first * cross_second
    shift_first = (flow_first + cross_first * flow_second) / determinant
    shift_second = (flow_second + cross_second * flow_first) / determinant
    first, second = slots_ref[0:1, :], slots_ref[1:2, :]
    live = lax.broadcasted_iota(jnp.int32, (1, cap), 1) < count_ref[0]
    base = jnp.swapaxes(base_ref[...], 0, 1)
    out_copies = []
    for part in range(parts):
        lanes = slice(part * width, (part + 1) * width)
        for s in range(n_sub):
            col_start = lax.rem(sub_index + n_sub - s, n_sub) * cols
            for c in range(0, cols, LANES):
                ids = rows_iota((LANES, width)) + c
                shift_ref[s * cols + c : s * cols + c + LANES, :] = jnp.where(
                    ids == first[:, lanes] - col_start,
                    shift_first[:, lanes],
                    jnp.where(ids == second[:, lanes] - col_start, shift_second[:, lanes], 0.0),
                ).astype(BF16)
        for i in range(chunks):
            if part == 0:
                for s in range(n_sub):
                    if i == 0:
                        masks[s].wait()
                    large[i][s].wait()
                    d_ref[i, s] = keep_blocks(d_ref[i, s], mask_ref[s], i * (chunk // BLOCK))
            change = jnp.zeros((chunk, width), F32)
            for s in range(n_sub):
                change += jnp.dot(
                    d_ref[i, s],
                    shift_ref[s * cols : (s + 1) * cols, :],
                    preferred_element_type=F32,
                )
            for b in range(chunk // BLOCK):
                block = i * (chunk // BLOCK) + b
                value = base[:, block : block + 1] + change[b * BLOCK : (b + 1) * BLOCK]
                post_ref[part, block * BLOCK : (block + 1) * BLOCK, :] = jnp.where(
                    live[:, lanes], value, 0.0
                ).astype(BF16)
        out_copies.append(
            pltpu.make_async_copy(post_ref.at[part], out_hbm.at[:, lanes], out_sems.at[part])
        )
        out_copies[-1].start()
    for copy in out_copies:
        copy.wait()


def on_device(dfactors, block_mask, base_flow, branch_row, pair_slots, pair_counts):
    rows_dev, cols = dfactors.shape
    blocks = rows_dev // BLOCK
    candidates = branch_row.shape[0]
    cap = pair_slots.shape[0]
    n_sub = lax.axis_size("sub")
    group = lax.axis_size("mon") * n_sub
    my_rows = rows_dev // n_sub
    slots = pair_slots.T
    base = base_flow.reshape(blocks, BLOCK)
    table = branch_row.reshape(candidates // LANES, LANES)
    hbm = pl.BlockSpec(memory_space=pltpu.HBM)
    received = pl.BlockSpec(memory_space=pl.ANY)

    factors = [dfactors]
    masks = [block_mask]
    for s in range(1, n_sub):
        perm = [(i, (i + s) % n_sub) for i in range(n_sub)]
        factors.append(lax.ppermute(dfactors, "sub", perm))
        masks.append(lax.ppermute(block_mask, "sub", perm))

    chunk = chunk_of(rows_dev, 256)
    chunks = rows_dev // chunk
    shares = pl.pallas_call(
        values_kernel,
        out_shape=jax.ShapeDtypeStruct((group, 4, cap), F32),
        in_specs=[hbm] * 5,
        out_specs=pl.BlockSpec(memory_space=pltpu.VMEM),
        scratch_shapes=[
            pltpu.VMEM((chunks, chunk, cols), BF16),
            pltpu.VMEM((blocks, cols), jnp.int32),
            pltpu.VMEM((blocks, BLOCK), F32),
            pltpu.VMEM((candidates // LANES, LANES), jnp.int32),
            pltpu.VMEM((2, cap), jnp.int32),
            pltpu.VMEM((cols, 2 * cap), BF16),
            pltpu.SemaphoreType.DMA((4,)),
            pltpu.SemaphoreType.DMA((chunks,)),
        ],
        compiler_params=pltpu.CompilerParams(vmem_limit_bytes=VMEM_LIMIT),
        cost_estimate=pl.CostEstimate(
            flops=4 * rows_dev * cols * cap, bytes_accessed=rows_dev * cols * 2, transcendentals=0
        ),
        name="pair_values",
    )(dfactors, block_mask, base, table, slots)

    shares = lax.all_to_all(shares, ("mon", "sub"), 0, 0, tiled=True)

    my_chunk = chunk_of(my_rows, 256)
    my_chunks = my_rows // my_chunk
    width = chunk_of(cap, 256)
    return pl.pallas_call(
        functools.partial(flows_kernel, n_sub),
        out_shape=jax.ShapeDtypeStruct((my_rows, cap), BF16),
        in_specs=([hbm] + [received] * (n_sub - 1)) * 2 + [received] + [hbm] * 3,
        out_specs=hbm,
        scratch_shapes=[
            pltpu.VMEM((my_chunks, n_sub, my_chunk, cols), BF16),
            pltpu.VMEM((n_sub, my_rows // BLOCK, cols), jnp.int32),
            pltpu.VMEM((group, 4, cap), F32),
            pltpu.VMEM((2, cap), jnp.int32),
            pltpu.VMEM((my_rows // BLOCK, BLOCK), F32),
            pltpu.SMEM((1,), jnp.int32),
            pltpu.VMEM((n_sub * cols, width), BF16),
            pltpu.VMEM((cap // width, my_rows, width), BF16),
            pltpu.SemaphoreType.DMA((4,)),
            pltpu.SemaphoreType.DMA((my_chunks, n_sub)),
            pltpu.SemaphoreType.DMA((n_sub,)),
            pltpu.SemaphoreType.DMA((cap // width,)),
        ],
        compiler_params=pltpu.CompilerParams(vmem_limit_bytes=VMEM_LIMIT),
        cost_estimate=pl.CostEstimate(
            flops=2 * my_rows * cols * n_sub * cap,
            bytes_accessed=my_rows * (cols * n_sub + cap) * 2,
            transcendentals=0,
        ),
        name="post_flows",
    )(*factors, *masks, shares, slots, base, pair_counts)


def solution(mesh):
    return jax.shard_map(
        on_device,
        mesh=mesh,
        in_specs=(
            P("mon", "sub"),
            P("mon", "sub"),
            P("mon"),
            P(),
            P(("grp", "pair"), None),
            P(("grp", "pair")),
        ),
        out_specs=P(("mon", "sub"), ("grp", "pair")),
        check_vma=False,
    )
```

```python
import functools

import jax
import jax.numpy as jnp
from jax import lax
from jax.experimental import pallas as pl
from jax.experimental.pallas import tpu as pltpu
from jax.sharding import PartitionSpec as P

BLOCK = 128
LANES = 128
SUBLANES = 8
ENDS = 256
VMEM_LIMIT = 16 * 1024 * 1024
F32 = jnp.float32
BF16 = jnp.bfloat16
I32 = jnp.int32


def chunk_of(total, want):
    size = min(total, want)
    while total % size:
        size -= BLOCK
    return size


def dense_rows(cap):
    return -(-cap // (LANES * SUBLANES)) * SUBLANES


def one_hot(hit):
    return jnp.where(hit, 1.0, 0.0).astype(BF16)


def iota(shape, axis):
    return lax.broadcasted_iota(I32, shape, axis)


def dense(line):
    cap = line.shape[1]
    rows = dense_rows(cap)
    pieces = [line[:, c : c + LANES] for c in range(0, cap, LANES)]
    if len(pieces) < rows:
        pieces.append(jnp.zeros((rows - len(pieces), LANES), line.dtype))
    return jnp.concatenate(pieces, axis=0)


def look_up(table, index):
    high, low = index >> 7, index & 127
    found = jnp.zeros(index.shape, table.dtype)
    for b in range(table.shape[0]):
        line = jnp.broadcast_to(table[b : b + 1], index.shape)
        value = jnp.take_along_axis(line, low, axis=1, mode="promise_in_bounds")
        found = jnp.where(high == b, value, found)
    return found


def values_kernel(
    n_sub, d_hbm, mask_hbm, base_hbm, rows_hbm, slots_hbm, *refs
):
    share_ref, *note_refs = refs[:n_sub]
    (
        d_ref, mask_ref, base_ref, rows_ref, slots_ref, perm_ref, hot_ref, cross_ref, sems, d_sems
    ) = refs[n_sub:]
    chunks, chunk, cols = d_ref.shape
    rows_dev = chunks * chunk
    cap = slots_ref.shape[1]
    lines = cap // LANES
    rows = dense_rows(cap)
    sub_index = lax.axis_index("sub")
    small = [
        pltpu.make_async_copy(src, dst, sems.at[i])
        for i, (src, dst) in enumerate(
            [(slots_hbm, slots_ref), (rows_hbm, rows_ref), (base_hbm, base_ref), (mask_hbm, mask_ref)]
        )
    ]
    large = [
        pltpu.make_async_copy(d_hbm.at[pl.ds(i * chunk, chunk)], d_ref.at[i], d_sems.at[i])
        for i in range(chunks)
    ]
    for copy in small + large:
        copy.start()

    small[0].wait()
    small[1].wait()
    first, second = dense(slots_ref[0:1, :]), dense(slots_ref[1:2, :])
    table = rows_ref[...]
    row = jnp.concatenate([look_up(table, first), look_up(table, second)], axis=0)
    row = row - lax.axis_index("mon") * rows_dev
    col = jnp.concatenate([second, first], axis=0) - sub_index * cols
    used = lax.rem(iota(row.shape, 0), rows) < lines
    here = used & (row >= 0) & (row < rows_dev) & (col >= 0) & (col < cols)

    flags = one_hot(here)
    height = flags.shape[0]
    above = jnp.dot(
        one_hot(iota((height, height), 1) < iota((height, height), 0)),
        flags,
        preferred_element_type=F32,
    ).astype(BF16)
    place = jnp.dot(
        jnp.concatenate([flags, above], axis=1),
        jnp.concatenate(
            [
                one_hot(iota((LANES, LANES), 0) <= iota((LANES, LANES), 1)),
                jnp.ones((LANES, LANES), BF16),
            ],
            axis=0,
        ),
        preferred_element_type=F32,
    ).astype(I32)
    place = jnp.where(here, place - 1, -1)
    digits = [(x >> shift) & 255 for x in (col, row) for shift in (0, 8)]
    order = [half * rows + b for half in range(2) for b in range(lines)]
    ends = jnp.concatenate(
        [jnp.concatenate([x[r : r + 1] for x in digits], axis=0) for r in order], axis=1
    )
    ends = ends.astype(F32).astype(BF16)

    def pick(start):
        for at, r in enumerate(order):
            perm_ref[:, at * LANES : (at + 1) * LANES] = one_hot(
                iota((ENDS, LANES), 0) + start == place[r : r + 1]
            )
        packed = lax.dot_general(
            ends, perm_ref[...], (((1,), (1,)), ((), ())), preferred_element_type=F32
        ).astype(I32)
        end_col = packed[0:1] + (packed[1:2] << 8)
        end_row = packed[2:3] + (packed[3:4] << 8)
        hot_ref[...] = one_hot(iota((cols, ENDS), 0) == end_col)
        keep = jnp.dot(
            mask_ref[...].astype(F32).astype(BF16), hot_ref[...], preferred_element_type=F32
        )
        keep = jnp.sum(
            jnp.where(iota(keep.shape, 0) == (end_row >> 7), keep, 0.0), axis=0, keepdims=True
        )
        total = jnp.zeros((SUBLANES, ENDS), F32)
        for i in range(chunks):
            values = jnp.dot(d_ref[i], hot_ref[...], preferred_element_type=F32)
            picked = jnp.where(iota((chunk, ENDS), 0) + i * chunk == end_row, values, 0.0)
            total += jnp.sum(picked.reshape(chunk // SUBLANES, SUBLANES, ENDS), axis=0)
        value = jnp.sum(total, axis=0, keepdims=True) * keep
        return jnp.dot(
            jnp.broadcast_to(value, (SUBLANES, ENDS)).astype(BF16),
            perm_ref[...],
            preferred_element_type=F32,
        )

    small[2].wait()
    small[3].wait()
    flow = jnp.where(sub_index == 0, look_up(base_ref[...], row), 0.0)
    for copy in large:
        copy.wait()
    cross_ref[...] = pick(0)
    count = jnp.max(place) + 1

    @pl.when(count > ENDS)
    def _():
        def more(i, _):
            cross_ref[...] += pick(i * ENDS)
            return 0

        lax.fori_loop(1, pl.cdiv(count, ENDS), more, 0)

    for ref in (share_ref, *note_refs):
        for half in range(2):
            for b in range(rows):
                at = (half * lines + b) * LANES
                ref[half * rows + b : half * rows + b + 1, :] = (
                    cross_ref[0:1, at : at + LANES] if b < lines else jnp.zeros((1, LANES), F32)
                )
        ref[2 * rows : 4 * rows, :] = flow
    my_blocks = mask_ref.shape[0] // n_sub
    for s, ref in enumerate(note_refs, 1):
        block = pl.multiple_of(lax.rem(sub_index + s, n_sub) * my_blocks, my_blocks)
        for c in range(cols // LANES):
            at = 4 * rows + c * my_blocks
            ref[at : at + my_blocks, :] = mask_ref[
                pl.ds(block, my_blocks), c * LANES : (c + 1) * LANES
            ].astype(F32)


def flows_kernel(n_sub, n_shares, *refs):
    d_any, refs = refs[:n_sub], refs[n_sub:]
    note_refs, refs = refs[: n_sub - 1], refs[n_sub - 1 :]
    share_refs, refs = refs[:n_shares], refs[n_shares:]
    (
        mask_hbm, slots_hbm, base_hbm, count_ref, out_hbm,
        d_ref, mask_ref, slots_ref, base_ref, shift_ref, post_ref,
        sems, d_sems, out_sems,
    ) = refs
    my_rows, all_cols = d_ref.shape
    cols = all_cols // n_sub
    my_blocks = my_rows // BLOCK
    cap = slots_ref.shape[1]
    rows = dense_rows(cap)
    parts, _, width = post_ref.shape
    sub_index = lax.axis_index("sub")
    my_start = pl.multiple_of(sub_index * my_rows, my_rows)
    my_block = pl.multiple_of(sub_index * my_blocks, my_blocks)
    small = [
        pltpu.make_async_copy(src, dst, sems.at[i])
        for i, (src, dst) in enumerate(
            [
                (slots_hbm, slots_ref),
                (base_hbm.at[pl.ds(my_block, my_blocks)], base_ref),
                (mask_hbm.at[pl.ds(my_block, my_blocks)], mask_ref),
            ]
        )
    ]
    large = [
        pltpu.make_async_copy(
            d_any[s].at[pl.ds(my_start, my_rows)],
            d_ref.at[:, s * cols : (s + 1) * cols],
            d_sems.at[s],
        )
        for s in range(n_sub)
    ]
    for copy in small + large:
        copy.start()
    total = share_refs[0][...]
    for ref in share_refs[1:]:
        total = total + ref[...]
    cross_first, cross_second, flow_first, flow_second = (
        total[i * rows : (i + 1) * rows] for i in range(4)
    )
    determinant = 1.0 - cross_first * cross_second
    shift_first = (flow_first + cross_first * flow_second) / determinant
    shift_second = (flow_second + cross_second * flow_first) / determinant
    for copy in small:
        copy.wait()
    first, second = slots_ref[0:1, :], slots_ref[1:2, :]
    live = iota((1, cap), 1) < count_ref[0]
    base = jnp.swapaxes(base_ref[...], 0, 1)

    def build(part):
        for b in range(width // LANES):
            line = part * (width // LANES) + b
            lanes = slice(line * LANES, (line + 1) * LANES)
            for s in range(n_sub):
                start = lax.rem(sub_index + n_sub - s, n_sub) * cols
                ids = iota((cols, LANES), 0)
                shift_ref[part, s * cols : (s + 1) * cols, b * LANES : (b + 1) * LANES] = jnp.where(
                    ids == first[:, lanes] - start,
                    shift_first[line : line + 1],
                    jnp.where(
                        ids == second[:, lanes] - start, shift_second[line : line + 1], 0.0
                    ),
                ).astype(BF16)

    build(0)
    for s in range(n_sub):
        large[s].wait()
        if s == 0:
            keep = mask_ref[...].astype(F32).astype(BF16)
        else:
            keep = jnp.concatenate(
                [
                    note_refs[s - 1][4 * rows + c * my_blocks : 4 * rows + (c + 1) * my_blocks, :]
                    for c in range(cols // LANES)
                ],
                axis=1,
            ).astype(BF16)
        for b in range(my_blocks):
            place = (slice(b * BLOCK, (b + 1) * BLOCK), slice(s * cols, (s + 1) * cols))
            d_ref[place] = d_ref[place] * keep[b : b + 1]
    out_copies = []
    for part in range(parts):
        lanes = slice(part * width, (part + 1) * width)
        change = jnp.dot(d_ref[...], shift_ref[part], preferred_element_type=F32)
        if part + 1 < parts:
            build(part + 1)
        for b in range(my_blocks):
            block = slice(b * BLOCK, (b + 1) * BLOCK)
            post_ref[part, block, :] = jnp.where(
                live[:, lanes], base[:, b : b + 1] + change[block], 0.0
            ).astype(BF16)
        out_copies.append(
            pltpu.make_async_copy(post_ref.at[part], out_hbm.at[:, lanes], out_sems.at[part])
        )
        out_copies[-1].start()
    for copy in out_copies:
        copy.wait()


def sum_over_mon(share, n_mon):
    if n_mon & (n_mon - 1):
        return [share] + [
            lax.ppermute(share, "mon", [(i, (i + s) % n_mon) for i in range(n_mon)])
            for s in range(1, n_mon)
        ]
    parts = [share]
    step = 1
    while step < n_mon:
        share = functools.reduce(jnp.add, parts)
        parts = [share, lax.ppermute(share, "mon", [(i, i ^ step) for i in range(n_mon)])]
        step *= 2
    return parts


def on_device(dfactors, block_mask, base_flow, branch_row, pair_slots, pair_counts):
    rows_dev, cols = dfactors.shape
    blocks = rows_dev // BLOCK
    candidates = branch_row.shape[0]
    cap = pair_slots.shape[0]
    rows = dense_rows(cap)
    n_sub = lax.axis_size("sub")
    my_rows = rows_dev // n_sub
    slots = pair_slots.T
    base = base_flow.reshape(blocks, BLOCK)
    table = branch_row.reshape(candidates // LANES, LANES)
    hbm = pl.BlockSpec(memory_space=pltpu.HBM)
    in_hbm = functools.partial(pltpu.with_memory_space_constraint, memory_space=pltpu.HBM)
    vmem = pl.BlockSpec(memory_space=pltpu.VMEM)
    params = pltpu.CompilerParams(vmem_limit_bytes=VMEM_LIMIT)
    rings = [[(i, (i + s) % n_sub) for i in range(n_sub)] for s in range(n_sub)]

    factors = [dfactors] + [lax.ppermute(dfactors, "sub", ring) for ring in rings[1:]]

    chunk = chunk_of(rows_dev, 512)
    chunks = rows_dev // chunk
    note_rows = 4 * rows + (cols // LANES) * (my_rows // BLOCK)
    share, *notes = pl.pallas_call(
        functools.partial(values_kernel, n_sub),
        out_shape=[jax.ShapeDtypeStruct((4 * rows, LANES), F32)]
        + [jax.ShapeDtypeStruct((note_rows, LANES), F32)] * (n_sub - 1),
        in_specs=[hbm] * 5,
        out_specs=[vmem] * n_sub,
        scratch_shapes=[
            pltpu.VMEM((chunks, chunk, cols), BF16),
            pltpu.VMEM((blocks, cols), I32),
            pltpu.VMEM((blocks, BLOCK), F32),
            pltpu.VMEM((candidates // LANES, LANES), I32),
            pltpu.VMEM((2, cap), I32),
            pltpu.VMEM((ENDS, 2 * cap), BF16),
            pltpu.VMEM((cols, ENDS), BF16),
            pltpu.VMEM((SUBLANES, 2 * cap), F32),
            pltpu.SemaphoreType.DMA((4,)),
            pltpu.SemaphoreType.DMA((chunks,)),
        ],
        compiler_params=params,
        cost_estimate=pl.CostEstimate(
            flops=2 * rows_dev * cols * ENDS, bytes_accessed=rows_dev * cols * 2, transcendentals=0
        ),
        name="pair_values",
    )(*map(in_hbm, (dfactors, block_mask, base, table, slots)))

    notes = [lax.ppermute(note, "sub", ring) for note, ring in zip(notes, rings[1:])]
    share = functools.reduce(jnp.add, [share] + [note[: 4 * rows] for note in notes])
    shares = sum_over_mon(share, lax.axis_size("mon"))

    width = chunk_of(cap, 256)
    return pl.pallas_call(
        functools.partial(flows_kernel, n_sub, len(shares)),
        out_shape=jax.ShapeDtypeStruct((my_rows, cap), BF16),
        in_specs=[hbm]
        + [pl.BlockSpec(memory_space=pl.ANY)] * (n_sub - 1)
        + [vmem] * (n_sub - 1 + len(shares))
        + [hbm] * 3
        + [pl.BlockSpec(memory_space=pltpu.SMEM)],
        out_specs=hbm,
        scratch_shapes=[
            pltpu.VMEM((my_rows, n_sub * cols), BF16),
            pltpu.VMEM((my_rows // BLOCK, cols), I32),
            pltpu.VMEM((2, cap), I32),
            pltpu.VMEM((my_rows // BLOCK, BLOCK), F32),
            pltpu.VMEM((cap // width, n_sub * cols, width), BF16),
            pltpu.VMEM((cap // width, my_rows, width), BF16),
            pltpu.SemaphoreType.DMA((3,)),
            pltpu.SemaphoreType.DMA((n_sub,)),
            pltpu.SemaphoreType.DMA((cap // width,)),
        ],
        compiler_params=params,
        cost_estimate=pl.CostEstimate(
            flops=2 * my_rows * cols * n_sub * cap,
            bytes_accessed=my_rows * (cols * n_sub + cap) * 2,
            transcendentals=0,
        ),
        name="post_flows",
    )(
        in_hbm(dfactors),
        *factors[1:],
        *notes,
        *shares,
        *map(in_hbm, (block_mask, slots, base)),
        pair_counts,
    )


def solution(mesh):
    return jax.shard_map(
        on_device,
        mesh=mesh,
        in_specs=(
            P("mon", "sub"),
            P("mon", "sub"),
            P("mon"),
            P(),
            P(("grp", "pair"), None),
            P(("grp", "pair")),
        ),
        out_specs=P(("mon", "sub"), ("grp", "pair")),
        check_vma=False,
    )
```

```python
import functools

import jax
import jax.numpy as jnp
from jax import lax
from jax.experimental import pallas as pl
from jax.experimental.pallas import tpu as pltpu
from jax.sharding import PartitionSpec as P

BLOCK = 128
LANES = 128
SUBLANES = 8
ENDS = 256
VMEM_LIMIT = 16 * 1024 * 1024
F32 = jnp.float32
BF16 = jnp.bfloat16
I32 = jnp.int32


def chunk_of(total, want):
    size = min(total, want)
    while total % size:
        size -= BLOCK
    return size


def dense_rows(cap):
    return -(-cap // (LANES * SUBLANES)) * SUBLANES


def one_hot(hit):
    return jnp.where(hit, 1.0, 0.0).astype(BF16)


def iota(shape, axis):
    return lax.broadcasted_iota(I32, shape, axis)


def dense(line):
    cap = line.shape[1]
    rows = dense_rows(cap)
    pieces = [line[:, c : c + LANES] for c in range(0, cap, LANES)]
    if len(pieces) < rows:
        pieces.append(jnp.zeros((rows - len(pieces), LANES), line.dtype))
    return jnp.concatenate(pieces, axis=0)


def look_up(table, index):
    high, low = index >> 7, index & 127
    found = jnp.zeros(index.shape, table.dtype)
    for b in range(table.shape[0]):
        line = jnp.broadcast_to(table[b : b + 1], index.shape)
        value = jnp.take_along_axis(line, low, axis=1, mode="promise_in_bounds")
        found = jnp.where(high == b, value, found)
    return found


def values_kernel(
    n_sub, d_hbm, mask_hbm, base_hbm, rows_hbm, slots_hbm, *refs
):
    share_ref, *note_refs = refs[:n_sub]
    (
        d_ref, mask_ref, base_ref, slots_ref, rows_ref, perm_ref, hot_ref, cross_ref, sems, d_sems
    ) = refs[n_sub:]
    rows_dev, cols = d_ref.shape
    chunks = d_sems.shape[0]
    chunk = rows_dev // chunks
    cap = slots_ref.shape[1]
    lines = cap // LANES
    rows = dense_rows(cap)
    sub_index = lax.axis_index("sub")
    small = [
        pltpu.make_async_copy(src, dst, sems.at[i])
        for i, (src, dst) in enumerate(
            [(slots_hbm, slots_ref), (rows_hbm, rows_ref), (base_hbm, base_ref), (mask_hbm, mask_ref)]
        )
    ]
    large = [
        pltpu.make_async_copy(
            d_hbm.at[pl.ds(i * chunk, chunk)], d_ref.at[pl.ds(i * chunk, chunk)], d_sems.at[i]
        )
        for i in range(chunks)
    ]
    for copy in small + large:
        copy.start()

    small[0].wait()
    small[1].wait()
    first, second = dense(slots_ref[0:1, :]), dense(slots_ref[1:2, :])
    table = rows_ref[...]
    row = jnp.concatenate([look_up(table, first), look_up(table, second)], axis=0)
    row = row - lax.axis_index("mon") * rows_dev
    col = jnp.concatenate([second, first], axis=0) - sub_index * cols
    used = lax.rem(iota(row.shape, 0), rows) < lines
    here = used & (row >= 0) & (row < rows_dev) & (col >= 0) & (col < cols)

    flags = one_hot(here)
    height = flags.shape[0]
    above = jnp.dot(
        one_hot(iota((height, height), 1) < iota((height, height), 0)),
        flags,
        preferred_element_type=F32,
    ).astype(BF16)
    place = jnp.dot(
        jnp.concatenate([flags, above], axis=1),
        jnp.concatenate(
            [
                one_hot(iota((LANES, LANES), 0) <= iota((LANES, LANES), 1)),
                jnp.ones((LANES, LANES), BF16),
            ],
            axis=0,
        ),
        preferred_element_type=F32,
    ).astype(I32)
    place = jnp.where(here, place - 1, -1)
    digits = [(x >> shift) & 255 for x in (col, row) for shift in (0, 8)]
    order = [half * rows + b for half in range(2) for b in range(lines)]
    ends = jnp.concatenate(
        [jnp.concatenate([x[r : r + 1] for x in digits], axis=0) for r in order], axis=1
    )
    ends = ends.astype(F32).astype(BF16)

    def pick(start):
        for at, r in enumerate(order):
            perm_ref[:, at * LANES : (at + 1) * LANES] = one_hot(
                iota((ENDS, LANES), 0) + start == place[r : r + 1]
            )
        packed = lax.dot_general(
            ends, perm_ref[...], (((1,), (1,)), ((), ())), preferred_element_type=F32
        ).astype(I32)
        end_col = packed[0:1] + (packed[1:2] << 8)
        end_row = packed[2:3] + (packed[3:4] << 8)
        hot_ref[...] = one_hot(iota((cols, ENDS), 0) == end_col)
        keep = jnp.dot(
            mask_ref[...].astype(F32).astype(BF16), hot_ref[...], preferred_element_type=F32
        )
        keep = jnp.sum(
            jnp.where(iota(keep.shape, 0) == (end_row >> 7), keep, 0.0), axis=0, keepdims=True
        )
        total = jnp.zeros((SUBLANES, ENDS), F32)
        for i in range(chunks):
            values = jnp.dot(
                d_ref[i * chunk : (i + 1) * chunk, :], hot_ref[...], preferred_element_type=F32
            )
            picked = jnp.where(iota((chunk, ENDS), 0) + i * chunk == end_row, values, 0.0)
            total += jnp.sum(picked.reshape(chunk // SUBLANES, SUBLANES, ENDS), axis=0)
        value = jnp.sum(total, axis=0, keepdims=True) * keep
        return jnp.dot(
            jnp.broadcast_to(value, (SUBLANES, ENDS)).astype(BF16),
            perm_ref[...],
            preferred_element_type=F32,
        )

    small[2].wait()
    small[3].wait()
    flow = jnp.where(sub_index == 0, look_up(base_ref[...], row), 0.0)
    for copy in large:
        copy.wait()
    cross_ref[...] = pick(0)
    count = jnp.max(place) + 1

    @pl.when(count > ENDS)
    def _():
        def more(i, _):
            cross_ref[...] += pick(i * ENDS)
            return 0

        lax.fori_loop(1, pl.cdiv(count, ENDS), more, 0)

    for ref in (share_ref, *note_refs):
        for half in range(2):
            for b in range(rows):
                at = (half * lines + b) * LANES
                ref[half * rows + b : half * rows + b + 1, :] = (
                    cross_ref[0:1, at : at + LANES] if b < lines else jnp.zeros((1, LANES), F32)
                )
        ref[2 * rows : 4 * rows, :] = flow
    my_blocks = mask_ref.shape[0] // n_sub
    for s, ref in enumerate(note_refs, 1):
        block = pl.multiple_of(lax.rem(sub_index + s, n_sub) * my_blocks, my_blocks)
        for c in range(cols // LANES):
            at = 4 * rows + c * my_blocks
            ref[at : at + my_blocks, :] = mask_ref[
                pl.ds(block, my_blocks), c * LANES : (c + 1) * LANES
            ].astype(F32)


def pick_columns(slot, starts, cols, masked_ref, hot_ref, out_ref):
    parts, _, width = hot_ref.shape
    for part in range(parts):
        lanes = slice(part * width, (part + 1) * width)
        for s, start in enumerate(starts):
            hot_ref[part, s * cols : (s + 1) * cols, :] = one_hot(
                iota((cols, width), 0) == slot[:, lanes] - start
            )
        out_ref[:, lanes] = jnp.dot(
            masked_ref[...], hot_ref[part], preferred_element_type=F32
        ).astype(BF16)


def column_starts(n_sub, cols):
    return [lax.rem(lax.axis_index("sub") + n_sub - s, n_sub) * cols for s in range(n_sub)]


def first_kernel(n_sub, *refs):
    d_refs, refs = refs[:n_sub], refs[n_sub:]
    note_refs, refs = refs[: n_sub - 1], refs[n_sub - 1 :]
    mask_ref, slots_ref, share_ref, masked_ref, first_ref, shared_ref, hot_ref = refs
    shared_ref[...] = share_ref[...]
    my_rows, all_cols = masked_ref.shape
    cols = all_cols // n_sub
    my_blocks = my_rows // BLOCK
    share_rows = note_refs[0].shape[0] - (cols // LANES) * my_blocks if note_refs else 0
    sub_index = lax.axis_index("sub")
    my_start = pl.multiple_of(sub_index * my_rows, my_rows)
    my_block = pl.multiple_of(sub_index * my_blocks, my_blocks)
    for s in range(n_sub):
        if s == 0:
            keep = mask_ref[pl.ds(my_block, my_blocks), :].astype(F32)
        else:
            keep = jnp.concatenate(
                [
                    note_refs[s - 1][share_rows + c * my_blocks : share_rows + (c + 1) * my_blocks, :]
                    for c in range(cols // LANES)
                ],
                axis=1,
            )
        keep = keep.astype(BF16)
        for b in range(my_blocks):
            masked_ref[b * BLOCK : (b + 1) * BLOCK, s * cols : (s + 1) * cols] = (
                d_refs[s][pl.ds(my_start + b * BLOCK, BLOCK), :] * keep[b : b + 1]
            )
    pick_columns(
        slots_ref[0:1, :], column_starts(n_sub, cols), cols, masked_ref, hot_ref, first_ref
    )


def second_kernel(n_sub, masked_ref, slots_ref, second_ref, hot_ref):
    cols = masked_ref.shape[1] // n_sub
    pick_columns(
        slots_ref[1:2, :], column_starts(n_sub, cols), cols, masked_ref, hot_ref, second_ref
    )


def flows_kernel(n_shares, *refs):
    share_refs, refs = refs[:n_shares], refs[n_shares:]
    base_ref, first_ref, second_ref, count_ref, out_hbm, post_ref, out_sems = refs
    my_rows, cap = post_ref.shape
    my_blocks = my_rows // BLOCK
    rows = dense_rows(cap)
    total = share_refs[0][...]
    for ref in share_refs[1:]:
        total = total + ref[...]
    cross_first, cross_second, flow_first, flow_second = (
        total[i * rows : (i + 1) * rows] for i in range(4)
    )
    determinant = 1.0 - cross_first * cross_second
    shift_first = (flow_first + cross_first * flow_second) / determinant
    shift_second = (flow_second + cross_second * flow_first) / determinant
    shift_first = shift_first.astype(BF16).astype(F32)
    shift_second = shift_second.astype(BF16).astype(F32)
    my_block = pl.multiple_of(lax.axis_index("sub") * my_blocks, my_blocks)
    base = jnp.swapaxes(base_ref[pl.ds(my_block, my_blocks), :], 0, 1)
    out_copies = []
    for b in range(my_blocks):
        block = slice(b * BLOCK, (b + 1) * BLOCK)
        start = jnp.broadcast_to(base[:, b : b + 1], (BLOCK, LANES))
        for line in range(cap // LANES):
            lanes = slice(line * LANES, (line + 1) * LANES)
            value = (
                start
                + shift_first[line : line + 1] * first_ref[block, lanes].astype(F32)
                + shift_second[line : line + 1] * second_ref[block, lanes].astype(F32)
            )
            live = iota((1, LANES), 1) + line * LANES < count_ref[0]
            post_ref[block, lanes] = jnp.where(live, value, 0.0).astype(BF16)
        out_copies.append(
            pltpu.make_async_copy(post_ref.at[block], out_hbm.at[block], out_sems.at[b])
        )
        out_copies[-1].start()
    for copy in out_copies:
        copy.wait()


def sum_over_mon(share, handed_on, n_mon):
    if n_mon & (n_mon - 1):
        return [handed_on] + [
            lax.ppermute(share, "mon", [(i, (i + s) % n_mon) for i in range(n_mon)])
            for s in range(1, n_mon)
        ]
    parts = [handed_on]
    step = 1
    while step < n_mon:
        sent = share if step == 1 else functools.reduce(jnp.add, parts)
        got = lax.ppermute(sent, "mon", [(i, i ^ step) for i in range(n_mon)])
        parts = [handed_on if step == 1 else sent, got]
        step *= 2
    return parts


def on_device(dfactors, block_mask, base_flow, branch_row, pair_slots, pair_counts):
    rows_dev, cols = dfactors.shape
    blocks = rows_dev // BLOCK
    candidates = branch_row.shape[0]
    cap = pair_slots.shape[0]
    rows = dense_rows(cap)
    n_sub = lax.axis_size("sub")
    my_rows = rows_dev // n_sub
    slots = pair_slots.T
    base = base_flow.reshape(blocks, BLOCK)
    table = branch_row.reshape(candidates // LANES, LANES)
    hbm = pl.BlockSpec(memory_space=pltpu.HBM)
    in_hbm = functools.partial(pltpu.with_memory_space_constraint, memory_space=pltpu.HBM)
    in_vmem = functools.partial(pltpu.with_memory_space_constraint, memory_space=pltpu.VMEM)
    vmem = pl.BlockSpec(memory_space=pltpu.VMEM)
    params = pltpu.CompilerParams(vmem_limit_bytes=VMEM_LIMIT)
    rings = [[(i, (i + s) % n_sub) for i in range(n_sub)] for s in range(n_sub)]

    factors = [dfactors] + [lax.ppermute(dfactors, "sub", ring) for ring in rings[1:]]

    chunks = rows_dev // chunk_of(rows_dev, 512)
    note_rows = 4 * rows + (cols // LANES) * (my_rows // BLOCK)
    outs = pl.pallas_call(
        functools.partial(values_kernel, n_sub),
        out_shape=[pltpu.VMEM((4 * rows, LANES), F32)]
        + [pltpu.VMEM((note_rows, LANES), F32)] * (n_sub - 1)
        + [
            pltpu.VMEM((rows_dev, cols), BF16),
            pltpu.VMEM((blocks, cols), I32),
            pltpu.VMEM((blocks, BLOCK), F32),
            pltpu.VMEM((2, cap), I32),
        ],
        in_specs=[hbm] * 5,
        out_specs=[vmem] * (n_sub + 4),
        scratch_shapes=[
            pltpu.VMEM((candidates // LANES, LANES), I32),
            pltpu.VMEM((ENDS, 2 * cap), BF16),
            pltpu.VMEM((cols, ENDS), BF16),
            pltpu.VMEM((SUBLANES, 2 * cap), F32),
            pltpu.SemaphoreType.DMA((4,)),
            pltpu.SemaphoreType.DMA((chunks,)),
        ],
        compiler_params=params,
        cost_estimate=pl.CostEstimate(
            flops=2 * rows_dev * cols * ENDS, bytes_accessed=rows_dev * cols * 2, transcendentals=0
        ),
        name="pair_values",
    )(*map(in_hbm, (dfactors, block_mask, base, table, slots)))
    share, notes = outs[0], outs[1:n_sub]
    factors[0], block_mask, base, slots = outs[n_sub:]

    notes = [lax.ppermute(note, "sub", ring) for note, ring in zip(notes, rings[1:])]
    share = functools.reduce(jnp.add, [share] + [note[: 4 * rows] for note in notes])

    width = chunk_of(cap, 256)
    hot = pltpu.VMEM((cap // width, n_sub * cols, width), BF16)
    columns = pltpu.VMEM((my_rows, cap), BF16)
    columns_cost = pl.CostEstimate(
        flops=2 * my_rows * cols * n_sub * cap,
        bytes_accessed=my_rows * (cols * n_sub + cap) * 2,
        transcendentals=0,
    )
    masked, first, handed_on = pl.pallas_call(
        functools.partial(first_kernel, n_sub),
        out_shape=[
            pltpu.VMEM((my_rows, n_sub * cols), BF16),
            columns,
            pltpu.VMEM(share.shape, F32),
        ],
        in_specs=[vmem] * (2 * n_sub + 2),
        out_specs=[vmem] * 3,
        scratch_shapes=[hot],
        compiler_params=params,
        cost_estimate=columns_cost,
        name="first_columns",
    )(*map(in_vmem, (*factors, *notes, block_mask, slots, share)))
    shares = sum_over_mon(share, handed_on, lax.axis_size("mon"))
    second = pl.pallas_call(
        functools.partial(second_kernel, n_sub),
        out_shape=columns,
        in_specs=[vmem] * 2,
        out_specs=vmem,
        scratch_shapes=[hot],
        compiler_params=params,
        cost_estimate=columns_cost,
        name="second_columns",
    )(*map(in_vmem, (masked, slots)))
    return pl.pallas_call(
        functools.partial(flows_kernel, len(shares)),
        out_shape=jax.ShapeDtypeStruct((my_rows, cap), BF16),
        in_specs=[vmem] * (len(shares) + 3) + [pl.BlockSpec(memory_space=pltpu.SMEM)],
        out_specs=hbm,
        scratch_shapes=[
            pltpu.VMEM((my_rows, cap), BF16),
            pltpu.SemaphoreType.DMA((my_rows // BLOCK,)),
        ],
        compiler_params=params,
        cost_estimate=pl.CostEstimate(
            flops=6 * my_rows * cap, bytes_accessed=my_rows * cap * 2, transcendentals=0
        ),
        name="post_flows",
    )(*map(in_vmem, (*shares, base, first, second)), pair_counts)


def solution(mesh):
    return jax.shard_map(
        on_device,
        mesh=mesh,
        in_specs=(
            P("mon", "sub"),
            P("mon", "sub"),
            P("mon"),
            P(),
            P(("grp", "pair"), None),
            P(("grp", "pair")),
        ),
        out_specs=P(("mon", "sub"), ("grp", "pair")),
        check_vma=False,
    )
```

```python
import functools

import jax
import jax.numpy as jnp
from jax import lax
from jax.experimental import pallas as pl
from jax.experimental.pallas import tpu as pltpu
from jax.sharding import PartitionSpec as P

BLOCK = 128
LANES = 128
SUBLANES = 8
ENDS = 256
VMEM_LIMIT = 16 * 1024 * 1024
F32 = jnp.float32
BF16 = jnp.bfloat16
I32 = jnp.int32


def chunk_of(total, want):
    size = min(total, want)
    while total % size:
        size -= BLOCK
    return size


def dense_rows(cap):
    return -(-cap // (LANES * SUBLANES)) * SUBLANES


def one_hot(hit):
    return jnp.where(hit, 1.0, 0.0).astype(BF16)


def iota(shape, axis):
    return lax.broadcasted_iota(I32, shape, axis)


def dense(line):
    cap = line.shape[1]
    rows = dense_rows(cap)
    pieces = [line[:, c : c + LANES] for c in range(0, cap, LANES)]
    if len(pieces) < rows:
        pieces.append(jnp.zeros((rows - len(pieces), LANES), line.dtype))
    return jnp.concatenate(pieces, axis=0)


def look_up(table, index):
    high, low = index >> 7, index & 127
    found = jnp.zeros(index.shape, table.dtype)
    for b in range(table.shape[0]):
        line = jnp.broadcast_to(table[b : b + 1], index.shape)
        value = jnp.take_along_axis(line, low, axis=1, mode="promise_in_bounds")
        found = jnp.where(high == b, value, found)
    return found


def values_kernel(
    n_sub, d_hbm, mask_hbm, base_hbm, rows_hbm, slots_hbm, *refs
):
    share_ref, *note_refs = refs[:n_sub]
    (
        d_ref, mask_ref, base_ref, slots_ref, rows_ref, perm_ref, hot_ref, cross_ref, sems, d_sems
    ) = refs[n_sub:]
    rows_dev, cols = d_ref.shape
    chunks = d_sems.shape[0]
    chunk = rows_dev // chunks
    cap = slots_ref.shape[1]
    lines = cap // LANES
    rows = dense_rows(cap)
    sub_index = lax.axis_index("sub")
    small = [
        pltpu.make_async_copy(src, dst, sems.at[i])
        for i, (src, dst) in enumerate(
            [(slots_hbm, slots_ref), (rows_hbm, rows_ref), (base_hbm, base_ref), (mask_hbm, mask_ref)]
        )
    ]
    large = [
        pltpu.make_async_copy(
            d_hbm.at[pl.ds(i * chunk, chunk)], d_ref.at[pl.ds(i * chunk, chunk)], d_sems.at[i]
        )
        for i in range(chunks)
    ]
    for copy in small + large:
        copy.start()

    small[0].wait()
    small[1].wait()
    first, second = dense(slots_ref[0:1, :]), dense(slots_ref[1:2, :])
    table = rows_ref[...]
    row = jnp.concatenate([look_up(table, first), look_up(table, second)], axis=0)
    row = row - lax.axis_index("mon") * rows_dev
    col = jnp.concatenate([second, first], axis=0) - sub_index * cols
    used = lax.rem(iota(row.shape, 0), rows) < lines
    here = used & (row >= 0) & (row < rows_dev) & (col >= 0) & (col < cols)

    flags = one_hot(here)
    height = flags.shape[0]
    above = jnp.dot(
        one_hot(iota((height, height), 1) < iota((height, height), 0)),
        flags,
        preferred_element_type=F32,
    ).astype(BF16)
    place = jnp.dot(
        jnp.concatenate([flags, above], axis=1),
        jnp.concatenate(
            [
                one_hot(iota((LANES, LANES), 0) <= iota((LANES, LANES), 1)),
                jnp.ones((LANES, LANES), BF16),
            ],
            axis=0,
        ),
        preferred_element_type=F32,
    ).astype(I32)
    place = jnp.where(here, place - 1, -1)
    digits = [(x >> shift) & 255 for x in (col, row) for shift in (0, 8)]
    order = [half * rows + b for half in range(2) for b in range(lines)]
    ends = jnp.concatenate(
        [jnp.concatenate([x[r : r + 1] for x in digits], axis=0) for r in order], axis=1
    )
    ends = ends.astype(F32).astype(BF16)

    def pick(start):
        for at, r in enumerate(order):
            perm_ref[:, at * LANES : (at + 1) * LANES] = one_hot(
                iota((ENDS, LANES), 0) + start == place[r : r + 1]
            )
        packed = lax.dot_general(
            ends, perm_ref[...], (((1,), (1,)), ((), ())), preferred_element_type=F32
        ).astype(I32)
        end_col = packed[0:1] + (packed[1:2] << 8)
        end_row = packed[2:3] + (packed[3:4] << 8)
        hot_ref[...] = one_hot(iota((cols, ENDS), 0) == end_col)
        keep = jnp.dot(
            mask_ref[...].astype(F32).astype(BF16), hot_ref[...], preferred_element_type=F32
        )
        keep = jnp.sum(
            jnp.where(iota(keep.shape, 0) == (end_row >> 7), keep, 0.0), axis=0, keepdims=True
        )
        total = jnp.zeros((SUBLANES, ENDS), F32)
        for i in range(chunks):
            values = jnp.dot(
                d_ref[i * chunk : (i + 1) * chunk, :], hot_ref[...], preferred_element_type=F32
            )
            picked = jnp.where(iota((chunk, ENDS), 0) + i * chunk == end_row, values, 0.0)
            total += jnp.sum(picked.reshape(chunk // SUBLANES, SUBLANES, ENDS), axis=0)
        value = jnp.sum(total, axis=0, keepdims=True) * keep
        return jnp.dot(
            jnp.broadcast_to(value, (SUBLANES, ENDS)).astype(BF16),
            perm_ref[...],
            preferred_element_type=F32,
        )

    small[2].wait()
    small[3].wait()
    flow = jnp.where(sub_index == 0, look_up(base_ref[...], row), 0.0)
    for copy in large:
        copy.wait()
    cross_ref[...] = pick(0)
    count = jnp.max(place) + 1

    @pl.when(count > ENDS)
    def _():
        def more(i, _):
            cross_ref[...] += pick(i * ENDS)
            return 0

        lax.fori_loop(1, pl.cdiv(count, ENDS), more, 0)

    for ref in (share_ref, *note_refs):
        for half in range(2):
            for b in range(rows):
                at = (half * lines + b) * LANES
                ref[half * rows + b : half * rows + b + 1, :] = (
                    cross_ref[0:1, at : at + LANES] if b < lines else jnp.zeros((1, LANES), F32)
                )
        ref[2 * rows : 4 * rows, :] = flow
    my_blocks = mask_ref.shape[0] // n_sub
    for s, ref in enumerate(note_refs, 1):
        block = pl.multiple_of(lax.rem(sub_index + s, n_sub) * my_blocks, my_blocks)
        for c in range(cols // LANES):
            at = 4 * rows + c * my_blocks
            ref[at : at + my_blocks, :] = mask_ref[
                pl.ds(block, my_blocks), c * LANES : (c + 1) * LANES
            ].astype(F32)


def pick_columns(slot, starts, cols, masked_ref, hot_ref, out_ref):
    parts, _, width = hot_ref.shape
    for part in range(parts):
        lanes = slice(part * width, (part + 1) * width)
        for s, start in enumerate(starts):
            hot_ref[part, s * cols : (s + 1) * cols, :] = one_hot(
                iota((cols, width), 0) == slot[:, lanes] - start
            )
        out_ref[:, lanes] = jnp.dot(
            masked_ref[...], hot_ref[part], preferred_element_type=F32
        ).astype(BF16)


def column_starts(n_sub, cols):
    return [lax.rem(lax.axis_index("sub") + n_sub - s, n_sub) * cols for s in range(n_sub)]


def first_kernel(n_sub, *refs):
    d_refs, refs = refs[:n_sub], refs[n_sub:]
    note_refs, refs = refs[: n_sub - 1], refs[n_sub - 1 :]
    mask_ref, slots_ref, share_ref, masked_ref, first_ref, shared_ref, hot_ref = refs
    shared_ref[...] = share_ref[...]
    my_rows, all_cols = masked_ref.shape
    cols = all_cols // n_sub
    my_blocks = my_rows // BLOCK
    share_rows = note_refs[0].shape[0] - (cols // LANES) * my_blocks if note_refs else 0
    sub_index = lax.axis_index("sub")
    my_start = pl.multiple_of(sub_index * my_rows, my_rows)
    my_block = pl.multiple_of(sub_index * my_blocks, my_blocks)
    for s in range(n_sub):
        if s == 0:
            keep = mask_ref[pl.ds(my_block, my_blocks), :].astype(F32)
        else:
            keep = jnp.concatenate(
                [
                    note_refs[s - 1][share_rows + c * my_blocks : share_rows + (c + 1) * my_blocks, :]
                    for c in range(cols // LANES)
                ],
                axis=1,
            )
        keep = keep.astype(BF16)
        for b in range(my_blocks):
            masked_ref[b * BLOCK : (b + 1) * BLOCK, s * cols : (s + 1) * cols] = (
                d_refs[s][pl.ds(my_start + b * BLOCK, BLOCK), :] * keep[b : b + 1]
            )
    pick_columns(
        slots_ref[0:1, :], column_starts(n_sub, cols), cols, masked_ref, hot_ref, first_ref
    )


def second_kernel(n_sub, lower, masked_ref, slots_ref, *refs):
    second_ref, hot_ref = refs[-2:]
    cols = masked_ref.shape[1] // n_sub

    @pl.when((lax.axis_index("mon") < lax.axis_size("mon") // 2) == lower)
    def _():
        pick_columns(
            slots_ref[1:2, :], column_starts(n_sub, cols), cols, masked_ref, hot_ref, second_ref
        )


def sums_kernel(n_prefix, *refs):
    *share_refs, prefix_ref, rest_ref = refs
    shares = [ref[...] for ref in share_refs]
    prefix_ref[...] = functools.reduce(jnp.add, shares[:n_prefix])
    rest_ref[...] = functools.reduce(jnp.add, shares[n_prefix:], jnp.zeros(rest_ref.shape, F32))


def flows_kernel(n_shares, *refs):
    share_refs, refs = refs[:n_shares], refs[n_shares:]
    base_ref, first_ref, second_ref, count_ref, out_hbm, post_ref, out_sems = refs
    my_rows, cap = post_ref.shape
    my_blocks = my_rows // BLOCK
    rows = dense_rows(cap)
    total = share_refs[0][...]
    for ref in share_refs[1:]:
        total = total + ref[...]
    cross_first, cross_second, flow_first, flow_second = (
        total[i * rows : (i + 1) * rows] for i in range(4)
    )
    determinant = 1.0 - cross_first * cross_second
    shift_first = (flow_first + cross_first * flow_second) / determinant
    shift_second = (flow_second + cross_second * flow_first) / determinant
    shift_first = shift_first.astype(BF16).astype(F32)
    shift_second = shift_second.astype(BF16).astype(F32)
    my_block = pl.multiple_of(lax.axis_index("sub") * my_blocks, my_blocks)
    base = jnp.swapaxes(base_ref[pl.ds(my_block, my_blocks), :], 0, 1)
    out_copies = []
    for b in range(my_blocks):
        block = slice(b * BLOCK, (b + 1) * BLOCK)
        start = jnp.broadcast_to(base[:, b : b + 1], (BLOCK, LANES))
        for line in range(cap // LANES):
            lanes = slice(line * LANES, (line + 1) * LANES)
            value = (
                start
                + shift_first[line : line + 1] * first_ref[block, lanes].astype(F32)
                + shift_second[line : line + 1] * second_ref[block, lanes].astype(F32)
            )
            live = iota((1, LANES), 1) + line * LANES < count_ref[0]
            post_ref[block, lanes] = jnp.where(live, value, 0.0).astype(BF16)
        out_copies.append(
            pltpu.make_async_copy(post_ref.at[block], out_hbm.at[block], out_sems.at[b])
        )
        out_copies[-1].start()
    for copy in out_copies:
        copy.wait()


def early_pairs(n_mon):
    half = n_mon // 2
    if n_mon & (n_mon - 1):
        return [[(i, (i + k) % n_mon) for i in range(n_mon)] for k in range(1, n_mon)]
    return [
        [(i, i ^ k) for i in range(n_mon) if (i ^ k) < i or (i >= half and (i ^ k) >= half)]
        for k in range(n_mon - 1, 0, -1)
    ]


def lower_pairs(n_mon):
    half = n_mon // 2
    if n_mon & (n_mon - 1):
        return []
    return [[(i, i ^ k) for i in range(half) if (i ^ k) > i] for k in range(1, half)]


def crossing_pairs(n_mon):
    half = n_mon // 2
    if n_mon & (n_mon - 1):
        return []
    return [[(half - 1, half + k)] for k in range(half)]


def send(share, pairs):
    return [lax.ppermute(share, "mon", some) for some in pairs]


def on_device(dfactors, block_mask, base_flow, branch_row, pair_slots, pair_counts):
    rows_dev, cols = dfactors.shape
    blocks = rows_dev // BLOCK
    candidates = branch_row.shape[0]
    cap = pair_slots.shape[0]
    rows = dense_rows(cap)
    n_sub = lax.axis_size("sub")
    my_rows = rows_dev // n_sub
    slots = pair_slots.T
    base = base_flow.reshape(blocks, BLOCK)
    table = branch_row.reshape(candidates // LANES, LANES)
    hbm = pl.BlockSpec(memory_space=pltpu.HBM)
    in_hbm = functools.partial(pltpu.with_memory_space_constraint, memory_space=pltpu.HBM)
    in_vmem = functools.partial(pltpu.with_memory_space_constraint, memory_space=pltpu.VMEM)
    vmem = pl.BlockSpec(memory_space=pltpu.VMEM)
    params = pltpu.CompilerParams(vmem_limit_bytes=VMEM_LIMIT)
    rings = [[(i, (i + s) % n_sub) for i in range(n_sub)] for s in range(n_sub)]

    factors = [dfactors] + [lax.ppermute(dfactors, "sub", ring) for ring in rings[1:]]

    chunks = rows_dev // chunk_of(rows_dev, 512)
    note_rows = 4 * rows + (cols // LANES) * (my_rows // BLOCK)
    outs = pl.pallas_call(
        functools.partial(values_kernel, n_sub),
        out_shape=[pltpu.VMEM((4 * rows, LANES), F32)]
        + [pltpu.VMEM((note_rows, LANES), F32)] * (n_sub - 1)
        + [
            pltpu.VMEM((rows_dev, cols), BF16),
            pltpu.VMEM((blocks, cols), I32),
            pltpu.VMEM((blocks, BLOCK), F32),
            pltpu.VMEM((2, cap), I32),
        ],
        in_specs=[hbm] * 5,
        out_specs=[vmem] * (n_sub + 4),
        scratch_shapes=[
            pltpu.VMEM((candidates // LANES, LANES), I32),
            pltpu.VMEM((ENDS, 2 * cap), BF16),
            pltpu.VMEM((cols, ENDS), BF16),
            pltpu.VMEM((SUBLANES, 2 * cap), F32),
            pltpu.SemaphoreType.DMA((4,)),
            pltpu.SemaphoreType.DMA((chunks,)),
        ],
        compiler_params=params,
        cost_estimate=pl.CostEstimate(
            flops=2 * rows_dev * cols * ENDS, bytes_accessed=rows_dev * cols * 2, transcendentals=0
        ),
        name="pair_values",
    )(*map(in_hbm, (dfactors, block_mask, base, table, slots)))
    share, notes = outs[0], outs[1:n_sub]
    factors[0], block_mask, base, slots = outs[n_sub:]

    notes = [lax.ppermute(note, "sub", ring) for note, ring in zip(notes, rings[1:])]
    share = functools.reduce(jnp.add, [share] + [note[: 4 * rows] for note in notes])
    n_mon = lax.axis_size("mon")
    shares = send(share, early_pairs(n_mon))

    width = chunk_of(cap, 256)
    hot = pltpu.VMEM((cap // width, n_sub * cols, width), BF16)
    columns = pltpu.VMEM((my_rows, cap), BF16)
    columns_cost = pl.CostEstimate(
        flops=2 * my_rows * cols * n_sub * cap,
        bytes_accessed=my_rows * (cols * n_sub + cap) * 2,
        transcendentals=0,
    )
    masked, first, handed_on = pl.pallas_call(
        functools.partial(first_kernel, n_sub),
        out_shape=[
            pltpu.VMEM((my_rows, n_sub * cols), BF16),
            columns,
            pltpu.VMEM(share.shape, F32),
        ],
        in_specs=[vmem] * (2 * n_sub + 2),
        out_specs=[vmem] * 3,
        scratch_shapes=[hot],
        compiler_params=params,
        cost_estimate=columns_cost,
        name="first_columns",
    )(*map(in_vmem, (*factors, *notes, block_mask, slots, share)))
    prefix = [handed_on, *send(handed_on, lower_pairs(n_mon))]

    def second_columns(lower, *earlier):
        return pl.pallas_call(
            functools.partial(second_kernel, n_sub, lower),
            out_shape=columns,
            in_specs=[vmem] * (2 + len(earlier)),
            out_specs=vmem,
            input_output_aliases={2: 0} if earlier else {},
            scratch_shapes=[hot],
            compiler_params=params,
            cost_estimate=pl.CostEstimate(
                flops=columns_cost.flops // 2,
                bytes_accessed=columns_cost.bytes_accessed // 2,
                transcendentals=0,
            ),
            name="second_columns_lower" if lower else "second_columns_upper",
        )(*map(in_vmem, (masked, slots, *earlier)))

    second = second_columns(True)
    prefix, rest = pl.pallas_call(
        functools.partial(sums_kernel, len(prefix)),
        out_shape=[pltpu.VMEM(share.shape, F32)] * 2,
        in_specs=[vmem] * (len(prefix) + len(shares)),
        out_specs=[vmem] * 2,
        compiler_params=params,
        name="sums",
    )(*map(in_vmem, (*prefix, *shares)))
    shares = [prefix, rest, *send(prefix, crossing_pairs(n_mon))]
    second = second_columns(False, second)
    return pl.pallas_call(
        functools.partial(flows_kernel, len(shares)),
        out_shape=jax.ShapeDtypeStruct((my_rows, cap), BF16),
        in_specs=[vmem] * (len(shares) + 3) + [pl.BlockSpec(memory_space=pltpu.SMEM)],
        out_specs=hbm,
        scratch_shapes=[
            pltpu.VMEM((my_rows, cap), BF16),
            pltpu.SemaphoreType.DMA((my_rows // BLOCK,)),
        ],
        compiler_params=params,
        cost_estimate=pl.CostEstimate(
            flops=6 * my_rows * cap, bytes_accessed=my_rows * cap * 2, transcendentals=0
        ),
        name="post_flows",
    )(*map(in_vmem, (*shares, base, first, second)), pair_counts)


def solution(mesh):
    return jax.shard_map(
        on_device,
        mesh=mesh,
        in_specs=(
            P("mon", "sub"),
            P("mon", "sub"),
            P("mon"),
            P(),
            P(("grp", "pair"), None),
            P(("grp", "pair")),
        ),
        out_specs=P(("mon", "sub"), ("grp", "pair")),
        check_vma=False,
    )
```

```python
import functools

import jax
import jax.numpy as jnp
from jax import lax
from jax.experimental import pallas as pl
from jax.experimental.pallas import tpu as pltpu
from jax.sharding import PartitionSpec as P

BLOCK = 128
LANES = 128
SUBLANES = 8
ENDS = 256
VMEM_LIMIT = 16 * 1024 * 1024
F32 = jnp.float32
BF16 = jnp.bfloat16
I32 = jnp.int32


def chunk_of(total, want):
    size = min(total, want)
    while total % size:
        size -= BLOCK
    return size


def dense_rows(cap):
    return -(-cap // (LANES * SUBLANES)) * SUBLANES


def one_hot(hit):
    return jnp.where(hit, 1.0, 0.0).astype(BF16)


def iota(shape, axis):
    return lax.broadcasted_iota(I32, shape, axis)


def dense(line):
    cap = line.shape[1]
    rows = dense_rows(cap)
    pieces = [line[:, c : c + LANES] for c in range(0, cap, LANES)]
    if len(pieces) < rows:
        pieces.append(jnp.zeros((rows - len(pieces), LANES), line.dtype))
    return jnp.concatenate(pieces, axis=0)


def look_up(table, index):
    high, low = index >> 7, index & 127
    found = jnp.zeros(index.shape, table.dtype)
    for b in range(table.shape[0]):
        line = jnp.broadcast_to(table[b : b + 1], index.shape)
        value = jnp.take_along_axis(line, low, axis=1, mode="promise_in_bounds")
        found = jnp.where(high == b, value, found)
    return found


def values_kernel(
    n_sub, d_hbm, mask_hbm, base_hbm, rows_hbm, slots_hbm, *refs
):
    share_ref, *note_refs = refs[:n_sub]
    (
        d_ref, mask_ref, base_ref, slots_ref, rows_ref, perm_ref, hot_ref, cross_ref, sems, d_sems
    ) = refs[n_sub:]
    rows_dev, cols = d_ref.shape
    chunks = d_sems.shape[0]
    chunk = rows_dev // chunks
    cap = slots_ref.shape[1]
    lines = cap // LANES
    rows = dense_rows(cap)
    sub_index = lax.axis_index("sub")
    small = [
        pltpu.make_async_copy(src, dst, sems.at[i])
        for i, (src, dst) in enumerate(
            [(slots_hbm, slots_ref), (rows_hbm, rows_ref), (base_hbm, base_ref), (mask_hbm, mask_ref)]
        )
    ]
    large = [
        pltpu.make_async_copy(
            d_hbm.at[pl.ds(i * chunk, chunk)], d_ref.at[pl.ds(i * chunk, chunk)], d_sems.at[i]
        )
        for i in range(chunks)
    ]
    for copy in small + large:
        copy.start()

    small[0].wait()
    small[1].wait()
    first, second = dense(slots_ref[0:1, :]), dense(slots_ref[1:2, :])
    table = rows_ref[...]
    row = jnp.concatenate([look_up(table, first), look_up(table, second)], axis=0)
    row = row - lax.axis_index("mon") * rows_dev
    col = jnp.concatenate([second, first], axis=0) - sub_index * cols
    used = lax.rem(iota(row.shape, 0), rows) < lines
    here = used & (row >= 0) & (row < rows_dev) & (col >= 0) & (col < cols)

    flags = one_hot(here)
    height = flags.shape[0]
    above = jnp.dot(
        one_hot(iota((height, height), 1) < iota((height, height), 0)),
        flags,
        preferred_element_type=F32,
    ).astype(BF16)
    place = jnp.dot(
        jnp.concatenate([flags, above], axis=1),
        jnp.concatenate(
            [
                one_hot(iota((LANES, LANES), 0) <= iota((LANES, LANES), 1)),
                jnp.ones((LANES, LANES), BF16),
            ],
            axis=0,
        ),
        preferred_element_type=F32,
    ).astype(I32)
    place = jnp.where(here, place - 1, -1)
    digits = [(x >> shift) & 255 for x in (col, row) for shift in (0, 8)]
    order = [half * rows + b for half in range(2) for b in range(lines)]
    ends = jnp.concatenate(
        [jnp.concatenate([x[r : r + 1] for x in digits], axis=0) for r in order], axis=1
    )
    ends = ends.astype(F32).astype(BF16)

    def pick(start):
        for at, r in enumerate(order):
            perm_ref[:, at * LANES : (at + 1) * LANES] = one_hot(
                iota((ENDS, LANES), 0) + start == place[r : r + 1]
            )
        packed = lax.dot_general(
            ends, perm_ref[...], (((1,), (1,)), ((), ())), preferred_element_type=F32
        ).astype(I32)
        end_col = packed[0:1] + (packed[1:2] << 8)
        end_row = packed[2:3] + (packed[3:4] << 8)
        hot_ref[...] = one_hot(iota((cols, ENDS), 0) == end_col)
        keep = jnp.dot(
            mask_ref[...].astype(F32).astype(BF16), hot_ref[...], preferred_element_type=F32
        )
        keep = jnp.sum(
            jnp.where(iota(keep.shape, 0) == (end_row >> 7), keep, 0.0), axis=0, keepdims=True
        )
        total = jnp.zeros((SUBLANES, ENDS), F32)
        for i in range(chunks):
            values = jnp.dot(
                d_ref[i * chunk : (i + 1) * chunk, :], hot_ref[...], preferred_element_type=F32
            )
            picked = jnp.where(iota((chunk, ENDS), 0) + i * chunk == end_row, values, 0.0)
            total += jnp.sum(picked.reshape(chunk // SUBLANES, SUBLANES, ENDS), axis=0)
        value = jnp.sum(total, axis=0, keepdims=True) * keep
        return jnp.dot(
            jnp.broadcast_to(value, (SUBLANES, ENDS)).astype(BF16),
            perm_ref[...],
            preferred_element_type=F32,
        )

    small[2].wait()
    small[3].wait()
    flow = jnp.where(sub_index == 0, look_up(base_ref[...], row), 0.0)
    for copy in large:
        copy.wait()
    cross_ref[...] = pick(0)
    count = jnp.max(place) + 1

    @pl.when(count > ENDS)
    def _():
        def more(i, _):
            cross_ref[...] += pick(i * ENDS)
            return 0

        lax.fori_loop(1, pl.cdiv(count, ENDS), more, 0)

    for ref in (share_ref, *note_refs):
        for half in range(2):
            for b in range(rows):
                at = (half * lines + b) * LANES
                ref[half * rows + b : half * rows + b + 1, :] = (
                    cross_ref[0:1, at : at + LANES] if b < lines else jnp.zeros((1, LANES), F32)
                )
        ref[2 * rows : 4 * rows, :] = flow
    my_blocks = mask_ref.shape[0] // n_sub
    for s, ref in enumerate(note_refs, 1):
        block = pl.multiple_of(lax.rem(sub_index + s, n_sub) * my_blocks, my_blocks)
        for c in range(cols // LANES):
            at = 4 * rows + c * my_blocks
            ref[at : at + my_blocks, :] = mask_ref[
                pl.ds(block, my_blocks), c * LANES : (c + 1) * LANES
            ].astype(F32)


def pick_columns(slot, starts, cols, masked_ref, hot_ref, out_ref):
    parts, _, width = hot_ref.shape
    for part in range(parts):
        lanes = slice(part * width, (part + 1) * width)
        for s, start in enumerate(starts):
            hot_ref[part, s * cols : (s + 1) * cols, :] = one_hot(
                iota((cols, width), 0) == slot[:, lanes] - start
            )
        out_ref[:, lanes] = jnp.dot(
            masked_ref[...], hot_ref[part], preferred_element_type=F32
        ).astype(BF16)


def column_starts(n_sub, cols):
    return [lax.rem(lax.axis_index("sub") + n_sub - s, n_sub) * cols for s in range(n_sub)]


def first_kernel(n_sub, *refs):
    d_refs, refs = refs[:n_sub], refs[n_sub:]
    note_refs, refs = refs[: n_sub - 1], refs[n_sub - 1 :]
    mask_ref, slots_ref, masked_ref, first_ref, hot_ref = refs
    my_rows, all_cols = masked_ref.shape
    cols = all_cols // n_sub
    my_blocks = my_rows // BLOCK
    share_rows = note_refs[0].shape[0] - (cols // LANES) * my_blocks if note_refs else 0
    sub_index = lax.axis_index("sub")
    my_start = pl.multiple_of(sub_index * my_rows, my_rows)
    my_block = pl.multiple_of(sub_index * my_blocks, my_blocks)
    for s in range(n_sub):
        if s == 0:
            keep = mask_ref[pl.ds(my_block, my_blocks), :].astype(F32)
        else:
            keep = jnp.concatenate(
                [
                    note_refs[s - 1][share_rows + c * my_blocks : share_rows + (c + 1) * my_blocks, :]
                    for c in range(cols // LANES)
                ],
                axis=1,
            )
        keep = keep.astype(BF16)
        for b in range(my_blocks):
            masked_ref[b * BLOCK : (b + 1) * BLOCK, s * cols : (s + 1) * cols] = (
                d_refs[s][pl.ds(my_start + b * BLOCK, BLOCK), :] * keep[b : b + 1]
            )
    pick_columns(
        slots_ref[0:1, :], column_starts(n_sub, cols), cols, masked_ref, hot_ref, first_ref
    )


def second_kernel(n_sub, masked_ref, slots_ref, second_ref, hot_ref):
    cols = masked_ref.shape[1] // n_sub
    pick_columns(
        slots_ref[1:2, :], column_starts(n_sub, cols), cols, masked_ref, hot_ref, second_ref
    )


def flows_kernel(shares_ref, *refs):
    base_ref, first_ref, second_ref, count_ref, out_hbm, post_ref, out_sems = refs
    my_rows, cap = post_ref.shape
    my_blocks = my_rows // BLOCK
    rows = dense_rows(cap)
    total = jnp.sum(shares_ref[...], axis=0)
    cross_first, cross_second, flow_first, flow_second = (
        total[i * rows : (i + 1) * rows] for i in range(4)
    )
    determinant = 1.0 - cross_first * cross_second
    shift_first = (flow_first + cross_first * flow_second) / determinant
    shift_second = (flow_second + cross_second * flow_first) / determinant
    shift_first = shift_first.astype(BF16).astype(F32)
    shift_second = shift_second.astype(BF16).astype(F32)
    my_block = pl.multiple_of(lax.axis_index("sub") * my_blocks, my_blocks)
    base = jnp.swapaxes(base_ref[pl.ds(my_block, my_blocks), :], 0, 1)
    out_copies = []
    for b in range(my_blocks):
        block = slice(b * BLOCK, (b + 1) * BLOCK)
        start = jnp.broadcast_to(base[:, b : b + 1], (BLOCK, LANES))
        for line in range(cap // LANES):
            lanes = slice(line * LANES, (line + 1) * LANES)
            value = (
                start
                + shift_first[line : line + 1] * first_ref[block, lanes].astype(F32)
                + shift_second[line : line + 1] * second_ref[block, lanes].astype(F32)
            )
            live = iota((1, LANES), 1) + line * LANES < count_ref[0]
            post_ref[block, lanes] = jnp.where(live, value, 0.0).astype(BF16)
        out_copies.append(
            pltpu.make_async_copy(post_ref.at[block], out_hbm.at[block], out_sems.at[b])
        )
        out_copies[-1].start()
    for copy in out_copies:
        copy.wait()


def on_device(dfactors, block_mask, base_flow, branch_row, pair_slots, pair_counts):
    rows_dev, cols = dfactors.shape
    blocks = rows_dev // BLOCK
    candidates = branch_row.shape[0]
    cap = pair_slots.shape[0]
    rows = dense_rows(cap)
    n_sub = lax.axis_size("sub")
    my_rows = rows_dev // n_sub
    slots = pair_slots.T
    base = base_flow.reshape(blocks, BLOCK)
    table = branch_row.reshape(candidates // LANES, LANES)
    hbm = pl.BlockSpec(memory_space=pltpu.HBM)
    in_hbm = functools.partial(pltpu.with_memory_space_constraint, memory_space=pltpu.HBM)
    in_vmem = functools.partial(pltpu.with_memory_space_constraint, memory_space=pltpu.VMEM)
    vmem = pl.BlockSpec(memory_space=pltpu.VMEM)
    params = pltpu.CompilerParams(vmem_limit_bytes=VMEM_LIMIT)
    rings = [[(i, (i + s) % n_sub) for i in range(n_sub)] for s in range(n_sub)]

    factors = [dfactors] + [lax.ppermute(dfactors, "sub", ring) for ring in rings[1:]]

    chunks = rows_dev // chunk_of(rows_dev, 512)
    note_rows = 4 * rows + (cols // LANES) * (my_rows // BLOCK)
    outs = pl.pallas_call(
        functools.partial(values_kernel, n_sub),
        out_shape=[pltpu.VMEM((4 * rows, LANES), F32)]
        + [pltpu.VMEM((note_rows, LANES), F32)] * (n_sub - 1)
        + [
            pltpu.VMEM((rows_dev, cols), BF16),
            pltpu.VMEM((blocks, cols), I32),
            pltpu.VMEM((blocks, BLOCK), F32),
            pltpu.VMEM((2, cap), I32),
        ],
        in_specs=[hbm] * 5,
        out_specs=[vmem] * (n_sub + 4),
        scratch_shapes=[
            pltpu.VMEM((candidates // LANES, LANES), I32),
            pltpu.VMEM((ENDS, 2 * cap), BF16),
            pltpu.VMEM((cols, ENDS), BF16),
            pltpu.VMEM((SUBLANES, 2 * cap), F32),
            pltpu.SemaphoreType.DMA((4,)),
            pltpu.SemaphoreType.DMA((chunks,)),
        ],
        compiler_params=params,
        cost_estimate=pl.CostEstimate(
            flops=2 * rows_dev * cols * ENDS, bytes_accessed=rows_dev * cols * 2, transcendentals=0
        ),
        name="pair_values",
    )(*map(in_hbm, (dfactors, block_mask, base, table, slots)))
    share, notes = outs[0], outs[1:n_sub]
    factors[0], block_mask, base, slots = outs[n_sub:]

    notes = [lax.ppermute(note, "sub", ring) for note, ring in zip(notes, rings[1:])]
    share = functools.reduce(jnp.add, [share] + [note[: 4 * rows] for note in notes])
    n_mon = lax.axis_size("mon")
    shares = lax.all_to_all(
        jnp.broadcast_to(share, (n_mon, *share.shape)), "mon", 0, 0, tiled=True
    )

    width = chunk_of(cap, 256)
    hot = pltpu.VMEM((cap // width, n_sub * cols, width), BF16)
    columns = pltpu.VMEM((my_rows, cap), BF16)
    columns_cost = pl.CostEstimate(
        flops=2 * my_rows * cols * n_sub * cap,
        bytes_accessed=my_rows * (cols * n_sub + cap) * 2,
        transcendentals=0,
    )
    masked, first = pl.pallas_call(
        functools.partial(first_kernel, n_sub),
        out_shape=[pltpu.VMEM((my_rows, n_sub * cols), BF16), columns],
        in_specs=[vmem] * (2 * n_sub + 1),
        out_specs=[vmem] * 2,
        scratch_shapes=[hot],
        compiler_params=params,
        cost_estimate=columns_cost,
        name="first_columns",
    )(*map(in_vmem, (*factors, *notes, block_mask, slots)))
    second = pl.pallas_call(
        functools.partial(second_kernel, n_sub),
        out_shape=columns,
        in_specs=[vmem] * 2,
        out_specs=vmem,
        scratch_shapes=[hot],
        compiler_params=params,
        cost_estimate=columns_cost,
        name="second_columns",
    )(*map(in_vmem, (masked, slots)))
    return pl.pallas_call(
        flows_kernel,
        out_shape=jax.ShapeDtypeStruct((my_rows, cap), BF16),
        in_specs=[vmem] * 4 + [pl.BlockSpec(memory_space=pltpu.SMEM)],
        out_specs=hbm,
        scratch_shapes=[
            pltpu.VMEM((my_rows, cap), BF16),
            pltpu.SemaphoreType.DMA((my_rows // BLOCK,)),
        ],
        compiler_params=params,
        cost_estimate=pl.CostEstimate(
            flops=6 * my_rows * cap, bytes_accessed=my_rows * cap * 2, transcendentals=0
        ),
        name="post_flows",
    )(*map(in_vmem, (shares, base, first, second)), pair_counts)


def solution(mesh):
    return jax.shard_map(
        on_device,
        mesh=mesh,
        in_specs=(
            P("mon", "sub"),
            P("mon", "sub"),
            P("mon"),
            P(),
            P(("grp", "pair"), None),
            P(("grp", "pair")),
        ),
        out_specs=P(("mon", "sub"), ("grp", "pair")),
        check_vma=False,
    )
```

```python
import functools

import jax
import jax.numpy as jnp
from jax import lax
from jax.experimental import pallas as pl
from jax.experimental.pallas import tpu as pltpu
from jax.sharding import PartitionSpec as P

BLOCK = 128
LANES = 128
SUBLANES = 8
ENDS = 256
VMEM_LIMIT = 16 * 1024 * 1024
F32 = jnp.float32
BF16 = jnp.bfloat16
I32 = jnp.int32


def chunk_of(total, want):
    size = min(total, want)
    while total % size:
        size -= BLOCK
    return size


def dense_rows(cap):
    return -(-cap // (LANES * SUBLANES)) * SUBLANES


def one_hot(hit):
    return jnp.where(hit, 1.0, 0.0).astype(BF16)


def iota(shape, axis):
    return lax.broadcasted_iota(I32, shape, axis)


def dense(line):
    cap = line.shape[1]
    rows = dense_rows(cap)
    pieces = [line[:, c : c + LANES] for c in range(0, cap, LANES)]
    if len(pieces) < rows:
        pieces.append(jnp.zeros((rows - len(pieces), LANES), line.dtype))
    return jnp.concatenate(pieces, axis=0)


def look_up(table, index):
    high, low = index >> 7, index & 127
    found = jnp.zeros(index.shape, table.dtype)
    for b in range(table.shape[0]):
        line = jnp.broadcast_to(table[b : b + 1], index.shape)
        value = jnp.take_along_axis(line, low, axis=1, mode="promise_in_bounds")
        found = jnp.where(high == b, value, found)
    return found


def values_kernel(
    n_sub, d_hbm, mask_hbm, base_hbm, rows_hbm, slots_hbm, *refs
):
    share_ref, *note_refs = refs[:n_sub]
    (
        d_ref, mask_ref, base_ref, slots_ref, rows_ref, perm_ref, hot_ref, cross_ref, sems, d_sems
    ) = refs[n_sub:]
    rows_dev, cols = d_ref.shape
    chunks = d_sems.shape[0]
    chunk = rows_dev // chunks
    cap = slots_ref.shape[1]
    lines = cap // LANES
    rows = dense_rows(cap)
    sub_index = lax.axis_index("sub")
    small = [
        pltpu.make_async_copy(src, dst, sems.at[i])
        for i, (src, dst) in enumerate(
            [(slots_hbm, slots_ref), (rows_hbm, rows_ref), (base_hbm, base_ref), (mask_hbm, mask_ref)]
        )
    ]
    large = [
        pltpu.make_async_copy(
            d_hbm.at[pl.ds(i * chunk, chunk)], d_ref.at[pl.ds(i * chunk, chunk)], d_sems.at[i]
        )
        for i in range(chunks)
    ]
    for copy in small + large:
        copy.start()

    for copy in small:
        copy.wait()
    first, second = dense(slots_ref[0:1, :]), dense(slots_ref[1:2, :])
    table = rows_ref[...]
    row = jnp.concatenate([look_up(table, first), look_up(table, second)], axis=0)
    row = row - lax.axis_index("mon") * rows_dev
    col = jnp.concatenate([second, first], axis=0) - sub_index * cols
    used = lax.rem(iota(row.shape, 0), rows) < lines
    here = used & (row >= 0) & (row < rows_dev) & (col >= 0) & (col < cols)

    counts = jnp.dot(
        one_hot(here),
        one_hot(iota((LANES, 2 * LANES), 0) <= iota((LANES, 2 * LANES), 1)),
        preferred_element_type=F32,
    )
    inner, totals = counts[:, :LANES], counts[:, LANES:]
    height = totals.shape[0]
    above, step = totals, 1
    while step < height:
        moved = pltpu.roll(above, step, 0)
        above = above + jnp.where(iota(above.shape, 0) >= step, moved, 0.0)
        step *= 2
    place = jnp.where(here, (inner + above - totals).astype(I32) - 1, -1)
    count = jnp.max(place) + 1
    digits = [(x >> shift) & 255 for x in (col, row) for shift in (0, 8)]
    order = [half * rows + b for half in range(2) for b in range(lines)]
    ends = jnp.concatenate(
        [jnp.concatenate([x[r : r + 1] for x in digits], axis=0) for r in order], axis=1
    )
    ends = ends.astype(F32).astype(BF16)

    def pick(start):
        for at, r in enumerate(order):
            perm_ref[:, at * LANES : (at + 1) * LANES] = one_hot(
                iota((ENDS, LANES), 0) + start == place[r : r + 1]
            )
        packed = lax.dot_general(
            ends, perm_ref[...], (((1,), (1,)), ((), ())), preferred_element_type=F32
        ).astype(I32)
        end_col = packed[0:1] + (packed[1:2] << 8)
        end_row = packed[2:3] + (packed[3:4] << 8)
        hot_ref[...] = one_hot(iota((cols, ENDS), 0) == end_col)
        keep = jnp.dot(
            mask_ref[...].astype(F32).astype(BF16), hot_ref[...], preferred_element_type=F32
        )
        keep = jnp.sum(
            jnp.where(iota(keep.shape, 0) == (end_row >> 7), keep, 0.0), axis=0, keepdims=True
        )
        total = jnp.zeros((SUBLANES, ENDS), F32)
        for i in range(chunks):
            if isinstance(start, int):
                large[i].wait()
            values = jnp.dot(
                d_ref[i * chunk : (i + 1) * chunk, :], hot_ref[...], preferred_element_type=F32
            )
            picked = jnp.where(iota((chunk, ENDS), 0) + i * chunk == end_row, values, 0.0)
            total += jnp.sum(picked.reshape(chunk // SUBLANES, SUBLANES, ENDS), axis=0)
        value = jnp.sum(total, axis=0, keepdims=True) * keep
        return jnp.dot(
            jnp.broadcast_to(value, (SUBLANES, ENDS)).astype(BF16),
            perm_ref[...],
            preferred_element_type=F32,
        )

    flow = jnp.where(sub_index == 0, look_up(base_ref[...], row), 0.0)
    cross_ref[...] = pick(0)
    @pl.when(count > ENDS)
    def _():
        def more(i, _):
            cross_ref[...] += pick(i * ENDS)
            return 0

        lax.fori_loop(1, pl.cdiv(count, ENDS), more, 0)

    cross = [
        dense(cross_ref[0:1, half * cap : (half + 1) * cap]) for half in range(2)
    ]
    share = jnp.concatenate([*cross, flow], axis=0).astype(BF16)
    share_ref[...] = share
    my_blocks = mask_ref.shape[0] // n_sub
    for s, ref in enumerate(note_refs, 1):
        block = pl.multiple_of(lax.rem(sub_index + s, n_sub) * my_blocks, my_blocks)
        keep = mask_ref[pl.ds(block, my_blocks), :].astype(F32)
        keep = [keep[:, c : c + LANES] for c in range(0, cols, LANES)]
        ref[...] = jnp.concatenate([share, jnp.concatenate(keep, axis=0).astype(BF16)], axis=0)


def pick_columns(slot, starts, cols, masked_ref, hot_ref, out_ref):
    parts, _, width = hot_ref.shape
    for part in range(parts):
        lanes = slice(part * width, (part + 1) * width)
        for s, start in enumerate(starts):
            hot_ref[part, s * cols : (s + 1) * cols, :] = one_hot(
                iota((cols, width), 0) == slot[:, lanes] - start
            )
        out_ref[:, lanes] = jnp.dot(
            masked_ref[...], hot_ref[part], preferred_element_type=F32
        ).astype(BF16)


def column_starts(n_sub, cols):
    return [lax.rem(lax.axis_index("sub") + n_sub - s, n_sub) * cols for s in range(n_sub)]


def first_kernel(n_sub, *refs):
    d_refs, refs = refs[:n_sub], refs[n_sub:]
    note_refs, refs = refs[: n_sub - 1], refs[n_sub - 1 :]
    mask_ref, slots_ref, share_ref, masked_ref, first_ref, shared_ref, hot_ref = refs
    shared_ref[...] = share_ref[...]
    my_rows, all_cols = masked_ref.shape
    cols = all_cols // n_sub
    my_blocks = my_rows // BLOCK
    share_rows = note_refs[0].shape[0] - (cols // LANES) * my_blocks if note_refs else 0
    sub_index = lax.axis_index("sub")
    my_start = pl.multiple_of(sub_index * my_rows, my_rows)
    my_block = pl.multiple_of(sub_index * my_blocks, my_blocks)
    for s in range(n_sub):
        if s == 0:
            keep = mask_ref[pl.ds(my_block, my_blocks), :].astype(F32)
        else:
            note = note_refs[s - 1][share_rows:, :].astype(F32)
            keep = jnp.concatenate(
                [note[c : c + my_blocks] for c in range(0, note.shape[0], my_blocks)], axis=1
            )
        keep = keep.astype(BF16)
        for b in range(my_blocks):
            masked_ref[b * BLOCK : (b + 1) * BLOCK, s * cols : (s + 1) * cols] = (
                d_refs[s][pl.ds(my_start + b * BLOCK, BLOCK), :] * keep[b : b + 1]
            )
    pick_columns(
        slots_ref[0:1, :], column_starts(n_sub, cols), cols, masked_ref, hot_ref, first_ref
    )


def second_kernel(n_sub, masked_ref, slots_ref, second_ref, hot_ref):
    cols = masked_ref.shape[1] // n_sub
    pick_columns(
        slots_ref[1:2, :], column_starts(n_sub, cols), cols, masked_ref, hot_ref, second_ref
    )


def flows_kernel(n_shares, *refs):
    share_refs, refs = refs[:n_shares], refs[n_shares:]
    base_ref, first_ref, second_ref, count_ref, out_hbm, post_ref, out_sems = refs
    my_rows, cap = post_ref.shape
    my_blocks = my_rows // BLOCK
    rows = dense_rows(cap)
    total = share_refs[0][...].astype(F32)
    for ref in share_refs[1:]:
        total = total + ref[...].astype(F32)
    cross_first, cross_second, flow_first, flow_second = (
        total[i * rows : (i + 1) * rows] for i in range(4)
    )
    determinant = 1.0 - cross_first * cross_second
    shift_first = (flow_first + cross_first * flow_second) / determinant
    shift_second = (flow_second + cross_second * flow_first) / determinant
    shift_first = shift_first.astype(BF16).astype(F32)
    shift_second = shift_second.astype(BF16).astype(F32)
    my_block = pl.multiple_of(lax.axis_index("sub") * my_blocks, my_blocks)
    base = jnp.swapaxes(base_ref[pl.ds(my_block, my_blocks), :], 0, 1)
    out_copies = []
    for b in range(my_blocks):
        block = slice(b * BLOCK, (b + 1) * BLOCK)
        start = jnp.broadcast_to(base[:, b : b + 1], (BLOCK, LANES))
        for line in range(cap // LANES):
            lanes = slice(line * LANES, (line + 1) * LANES)
            value = (
                start
                + shift_first[line : line + 1] * first_ref[block, lanes].astype(F32)
                + shift_second[line : line + 1] * second_ref[block, lanes].astype(F32)
            )
            live = iota((1, LANES), 1) + line * LANES < count_ref[0]
            post_ref[block, lanes] = jnp.where(live, value, 0.0).astype(BF16)
        out_copies.append(
            pltpu.make_async_copy(post_ref.at[block], out_hbm.at[block], out_sems.at[b])
        )
        out_copies[-1].start()
    for copy in out_copies:
        copy.wait()


def sum_over_mon(share, handed_on, n_mon):
    if n_mon & (n_mon - 1):
        return [handed_on] + [
            lax.ppermute(share, "mon", [(i, (i + s) % n_mon) for i in range(n_mon)])
            for s in range(1, n_mon)
        ]
    parts = [handed_on]
    step = 1
    while step < n_mon:
        sent = share if step == 1 else functools.reduce(jnp.add, parts)
        got = lax.ppermute(sent, "mon", [(i, i ^ step) for i in range(n_mon)])
        parts = [handed_on if step == 1 else sent, got]
        step *= 2
    return parts


def on_device(dfactors, block_mask, base_flow, branch_row, pair_slots, pair_counts):
    rows_dev, cols = dfactors.shape
    blocks = rows_dev // BLOCK
    candidates = branch_row.shape[0]
    cap = pair_slots.shape[0]
    rows = dense_rows(cap)
    n_sub = lax.axis_size("sub")
    my_rows = rows_dev // n_sub
    slots = pair_slots.T
    base = base_flow.reshape(blocks, BLOCK)
    table = branch_row.reshape(candidates // LANES, LANES)
    hbm = pl.BlockSpec(memory_space=pltpu.HBM)
    in_hbm = functools.partial(pltpu.with_memory_space_constraint, memory_space=pltpu.HBM)
    in_vmem = functools.partial(pltpu.with_memory_space_constraint, memory_space=pltpu.VMEM)
    vmem = pl.BlockSpec(memory_space=pltpu.VMEM)
    params = pltpu.CompilerParams(vmem_limit_bytes=VMEM_LIMIT)
    rings = [[(i, (i + s) % n_sub) for i in range(n_sub)] for s in range(n_sub)]

    factors = [dfactors] + [lax.ppermute(dfactors, "sub", ring) for ring in rings[1:]]

    chunks = rows_dev // chunk_of(rows_dev, 512)
    note_rows = 4 * rows + (cols // LANES) * (my_rows // BLOCK)
    outs = pl.pallas_call(
        functools.partial(values_kernel, n_sub),
        out_shape=[pltpu.VMEM((4 * rows, LANES), BF16)]
        + [pltpu.VMEM((note_rows, LANES), BF16)] * (n_sub - 1)
        + [
            pltpu.VMEM((rows_dev, cols), BF16),
            pltpu.VMEM((blocks, cols), I32),
            pltpu.VMEM((blocks, BLOCK), F32),
            pltpu.VMEM((2, cap), I32),
        ],
        in_specs=[hbm] * 5,
        out_specs=[vmem] * (n_sub + 4),
        scratch_shapes=[
            pltpu.VMEM((candidates // LANES, LANES), I32),
            pltpu.VMEM((ENDS, 2 * cap), BF16),
            pltpu.VMEM((cols, ENDS), BF16),
            pltpu.VMEM((SUBLANES, 2 * cap), F32),
            pltpu.SemaphoreType.DMA((4,)),
            pltpu.SemaphoreType.DMA((chunks,)),
        ],
        compiler_params=params,
        cost_estimate=pl.CostEstimate(
            flops=2 * rows_dev * cols * ENDS, bytes_accessed=rows_dev * cols * 2, transcendentals=0
        ),
        name="pair_values",
    )(*map(in_hbm, (dfactors, block_mask, base, table, slots)))
    share, notes = outs[0], outs[1:n_sub]
    factors[0], block_mask, base, slots = outs[n_sub:]

    notes = [lax.ppermute(note, "sub", ring) for note, ring in zip(notes, rings[1:])]
    share = functools.reduce(jnp.add, [share] + [note[: 4 * rows] for note in notes])

    width = chunk_of(cap, 256)
    hot = pltpu.VMEM((cap // width, n_sub * cols, width), BF16)
    columns = pltpu.VMEM((my_rows, cap), BF16)
    columns_cost = pl.CostEstimate(
        flops=2 * my_rows * cols * n_sub * cap,
        bytes_accessed=my_rows * (cols * n_sub + cap) * 2,
        transcendentals=0,
    )
    masked, first, handed_on = pl.pallas_call(
        functools.partial(first_kernel, n_sub),
        out_shape=[
            pltpu.VMEM((my_rows, n_sub * cols), BF16),
            columns,
            pltpu.VMEM(share.shape, share.dtype),
        ],
        in_specs=[vmem] * (2 * n_sub + 2),
        out_specs=[vmem] * 3,
        scratch_shapes=[hot],
        compiler_params=params,
        cost_estimate=columns_cost,
        name="first_columns",
    )(*map(in_vmem, (*factors, *notes, block_mask, slots, share)))
    shares = sum_over_mon(share, handed_on, lax.axis_size("mon"))
    second = pl.pallas_call(
        functools.partial(second_kernel, n_sub),
        out_shape=columns,
        in_specs=[vmem] * 2,
        out_specs=vmem,
        scratch_shapes=[hot],
        compiler_params=params,
        cost_estimate=columns_cost,
        name="second_columns",
    )(*map(in_vmem, (masked, slots)))
    return pl.pallas_call(
        functools.partial(flows_kernel, len(shares)),
        out_shape=jax.ShapeDtypeStruct((my_rows, cap), BF16),
        in_specs=[vmem] * (len(shares) + 3) + [pl.BlockSpec(memory_space=pltpu.SMEM)],
        out_specs=hbm,
        scratch_shapes=[
            pltpu.VMEM((my_rows, cap), BF16),
            pltpu.SemaphoreType.DMA((my_rows // BLOCK,)),
        ],
        compiler_params=params,
        cost_estimate=pl.CostEstimate(
            flops=6 * my_rows * cap, bytes_accessed=my_rows * cap * 2, transcendentals=0
        ),
        name="post_flows",
    )(*map(in_vmem, (*shares, base, first, second)), pair_counts)


def solution(mesh):
    return jax.shard_map(
        on_device,
        mesh=mesh,
        in_specs=(
            P("mon", "sub"),
            P("mon", "sub"),
            P("mon"),
            P(),
            P(("grp", "pair"), None),
            P(("grp", "pair")),
        ),
        out_specs=P(("mon", "sub"), ("grp", "pair")),
        check_vma=False,
    )
```

```python
import functools

import jax
import jax.numpy as jnp
from jax import lax
from jax.experimental import pallas as pl
from jax.experimental.pallas import tpu as pltpu
from jax.sharding import PartitionSpec as P

BLOCK = 128
LANES = 128
SUBLANES = 8
ENDS = 256
VMEM_LIMIT = 16 * 1024 * 1024
F32 = jnp.float32
BF16 = jnp.bfloat16
I32 = jnp.int32


def chunk_of(total, want):
    size = min(total, want)
    while total % size:
        size -= BLOCK
    return size


def dense_rows(cap):
    return -(-cap // (LANES * SUBLANES)) * SUBLANES


def one_hot(hit):
    return jnp.where(hit, 1.0, 0.0).astype(BF16)


def iota(shape, axis):
    return lax.broadcasted_iota(I32, shape, axis)


def dense(line):
    cap = line.shape[1]
    rows = dense_rows(cap)
    pieces = [line[:, c : c + LANES] for c in range(0, cap, LANES)]
    if len(pieces) < rows:
        pieces.append(jnp.zeros((rows - len(pieces), LANES), line.dtype))
    return jnp.concatenate(pieces, axis=0)


def look_up(table, index):
    high, low = index >> 7, index & 127
    found = jnp.zeros(index.shape, table.dtype)
    for b in range(table.shape[0]):
        line = jnp.broadcast_to(table[b : b + 1], index.shape)
        value = jnp.take_along_axis(line, low, axis=1, mode="promise_in_bounds")
        found = jnp.where(high == b, value, found)
    return found


def values_kernel(
    n_sub, d_hbm, mask_hbm, base_hbm, rows_hbm, slots_hbm, *refs
):
    share_ref, *note_refs = refs[:n_sub]
    (
        d_ref, mask_ref, base_ref, slots_ref, rows_ref, perm_ref, hot_ref, cross_ref, sems, d_sems
    ) = refs[n_sub:]
    rows_dev, cols = d_ref.shape
    chunks = d_sems.shape[0]
    chunk = rows_dev // chunks
    cap = slots_ref.shape[1]
    lines = cap // LANES
    rows = dense_rows(cap)
    sub_index = lax.axis_index("sub")
    small = [
        pltpu.make_async_copy(src, dst, sems.at[i])
        for i, (src, dst) in enumerate(
            [(slots_hbm, slots_ref), (rows_hbm, rows_ref), (base_hbm, base_ref), (mask_hbm, mask_ref)]
        )
    ]
    large = [
        pltpu.make_async_copy(
            d_hbm.at[pl.ds(i * chunk, chunk)], d_ref.at[pl.ds(i * chunk, chunk)], d_sems.at[i]
        )
        for i in range(chunks)
    ]
    for copy in small + large:
        copy.start()

    for copy in small:
        copy.wait()
    first, second = dense(slots_ref[0:1, :]), dense(slots_ref[1:2, :])
    table = rows_ref[...]
    row = jnp.concatenate([look_up(table, first), look_up(table, second)], axis=0)
    row = row - lax.axis_index("mon") * rows_dev
    col = jnp.concatenate([second, first], axis=0) - sub_index * cols
    used = lax.rem(iota(row.shape, 0), rows) < lines
    here = used & (row >= 0) & (row < rows_dev) & (col >= 0) & (col < cols)

    flags = one_hot(here)
    height = flags.shape[0]
    above = jnp.dot(
        one_hot(iota((height, height), 1) < iota((height, height), 0)),
        flags,
        preferred_element_type=F32,
    ).astype(BF16)
    place = jnp.dot(
        jnp.concatenate([flags, above], axis=1),
        jnp.concatenate(
            [
                one_hot(iota((LANES, LANES), 0) <= iota((LANES, LANES), 1)),
                jnp.ones((LANES, LANES), BF16),
            ],
            axis=0,
        ),
        preferred_element_type=F32,
    ).astype(I32)
    place = jnp.where(here, place - 1, -1)
    digits = [(x >> shift) & 255 for x in (col, row) for shift in (0, 8)]
    order = [half * rows + b for half in range(2) for b in range(lines)]
    ends = jnp.concatenate(
        [jnp.concatenate([x[r : r + 1] for x in digits], axis=0) for r in order], axis=1
    )
    ends = ends.astype(F32).astype(BF16)

    def pick(start, copies=()):
        for at, r in enumerate(order):
            perm_ref[:, at * LANES : (at + 1) * LANES] = one_hot(
                iota((ENDS, LANES), 0) + start == place[r : r + 1]
            )
        packed = lax.dot_general(
            ends, perm_ref[...], (((1,), (1,)), ((), ())), preferred_element_type=F32
        ).astype(I32)
        end_col = packed[0:1] + (packed[1:2] << 8)
        end_row = packed[2:3] + (packed[3:4] << 8)
        hot_ref[...] = one_hot(iota((cols, ENDS), 0) == end_col)
        keep = jnp.dot(
            mask_ref[...].astype(F32).astype(BF16), hot_ref[...], preferred_element_type=F32
        )
        keep = jnp.sum(
            jnp.where(iota(keep.shape, 0) == (end_row >> 7), keep, 0.0), axis=0, keepdims=True
        )
        for copy in copies:
            copy.wait()
        total = jnp.zeros((SUBLANES, ENDS), F32)
        for i in range(chunks):
            values = jnp.dot(
                d_ref[i * chunk : (i + 1) * chunk, :], hot_ref[...], preferred_element_type=F32
            )
            picked = jnp.where(iota((chunk, ENDS), 0) + i * chunk == end_row, values, 0.0)
            total += jnp.sum(picked.reshape(chunk // SUBLANES, SUBLANES, ENDS), axis=0)
        value = jnp.sum(total, axis=0, keepdims=True) * keep
        return jnp.dot(
            jnp.broadcast_to(value, (SUBLANES, ENDS)).astype(BF16),
            perm_ref[...],
            preferred_element_type=F32,
        )

    flow = jnp.where(sub_index == 0, look_up(base_ref[...], row), 0.0)
    cross_ref[...] = pick(0, large)
    count = jnp.max(place) + 1

    @pl.when(count > ENDS)
    def _():
        def more(i, _):
            cross_ref[...] += pick(i * ENDS)
            return 0

        lax.fori_loop(1, pl.cdiv(count, ENDS), more, 0)

    for ref in (share_ref, *note_refs):
        for half in range(2):
            for b in range(rows):
                at = (half * lines + b) * LANES
                ref[half * rows + b : half * rows + b + 1, :] = (
                    cross_ref[0:1, at : at + LANES] if b < lines else jnp.zeros((1, LANES), F32)
                )
        ref[2 * rows : 4 * rows, :] = flow
    my_blocks = mask_ref.shape[0] // n_sub
    for s, ref in enumerate(note_refs, 1):
        block = pl.multiple_of(lax.rem(sub_index + s, n_sub) * my_blocks, my_blocks)
        for c in range(cols // LANES):
            at = 4 * rows + c * my_blocks
            ref[at : at + my_blocks, :] = mask_ref[
                pl.ds(block, my_blocks), c * LANES : (c + 1) * LANES
            ].astype(F32)


def pick_columns(slot, starts, cols, masked_ref, hot_ref, out_ref):
    parts, _, width = hot_ref.shape
    for part in range(parts):
        lanes = slice(part * width, (part + 1) * width)
        for s, start in enumerate(starts):
            hot_ref[part, s * cols : (s + 1) * cols, :] = one_hot(
                iota((cols, width), 0) == slot[:, lanes] - start
            )
        out_ref[:, lanes] = jnp.dot(
            masked_ref[...], hot_ref[part], preferred_element_type=F32
        ).astype(BF16)


def column_starts(n_sub, cols):
    return [lax.rem(lax.axis_index("sub") + n_sub - s, n_sub) * cols for s in range(n_sub)]


def first_kernel(n_sub, *refs):
    d_refs, refs = refs[:n_sub], refs[n_sub:]
    note_refs, refs = refs[: n_sub - 1], refs[n_sub - 1 :]
    mask_ref, slots_ref, share_ref, masked_ref, first_ref, shared_ref, hot_ref = refs
    shared_ref[...] = share_ref[...]
    my_rows, all_cols = masked_ref.shape
    cols = all_cols // n_sub
    my_blocks = my_rows // BLOCK
    share_rows = note_refs[0].shape[0] - (cols // LANES) * my_blocks if note_refs else 0
    sub_index = lax.axis_index("sub")
    my_start = pl.multiple_of(sub_index * my_rows, my_rows)
    my_block = pl.multiple_of(sub_index * my_blocks, my_blocks)
    for s in range(n_sub):
        if s == 0:
            keep = mask_ref[pl.ds(my_block, my_blocks), :].astype(F32)
        else:
            keep = jnp.concatenate(
                [
                    note_refs[s - 1][share_rows + c * my_blocks : share_rows + (c + 1) * my_blocks, :]
                    for c in range(cols // LANES)
                ],
                axis=1,
            )
        keep = keep.astype(BF16)
        for b in range(my_blocks):
            masked_ref[b * BLOCK : (b + 1) * BLOCK, s * cols : (s + 1) * cols] = (
                d_refs[s][pl.ds(my_start + b * BLOCK, BLOCK), :] * keep[b : b + 1]
            )
    pick_columns(
        slots_ref[0:1, :], column_starts(n_sub, cols), cols, masked_ref, hot_ref, first_ref
    )


def second_kernel(n_sub, masked_ref, slots_ref, second_ref, hot_ref):
    cols = masked_ref.shape[1] // n_sub
    pick_columns(
        slots_ref[1:2, :], column_starts(n_sub, cols), cols, masked_ref, hot_ref, second_ref
    )


def flows_kernel(n_shares, *refs):
    share_refs, refs = refs[:n_shares], refs[n_shares:]
    base_ref, first_ref, second_ref, count_ref, out_hbm, post_ref, out_sems = refs
    my_rows, cap = post_ref.shape
    my_blocks = my_rows // BLOCK
    rows = dense_rows(cap)
    total = share_refs[0][...]
    for ref in share_refs[1:]:
        total = total + ref[...]
    cross_first, cross_second, flow_first, flow_second = (
        total[i * rows : (i + 1) * rows] for i in range(4)
    )
    determinant = 1.0 - cross_first * cross_second
    shift_first = (flow_first + cross_first * flow_second) / determinant
    shift_second = (flow_second + cross_second * flow_first) / determinant
    lines = range(cap // LANES)
    weights = [
        [
            jnp.broadcast_to(shift[line : line + 1], (BLOCK, LANES)).astype(BF16)
            for line in lines
        ]
        for shift in (shift_first, shift_second)
    ]
    live = [iota((1, LANES), 1) + line * LANES < count_ref[0] for line in lines]
    my_block = pl.multiple_of(lax.axis_index("sub") * my_blocks, my_blocks)
    base = jnp.swapaxes(base_ref[pl.ds(my_block, my_blocks), :], 0, 1)
    out_copies = []
    for b in range(my_blocks):
        block = slice(b * BLOCK, (b + 1) * BLOCK)
        start = jnp.broadcast_to(base[:, b : b + 1], (BLOCK, LANES))
        for line in lines:
            lanes = slice(line * LANES, (line + 1) * LANES)
            change = (
                weights[0][line] * first_ref[block, lanes]
                + weights[1][line] * second_ref[block, lanes]
            )
            post_ref[block, lanes] = jnp.where(
                live[line], start + change.astype(F32), 0.0
            ).astype(BF16)
        out_copies.append(
            pltpu.make_async_copy(post_ref.at[block], out_hbm.at[block], out_sems.at[b])
        )
        out_copies[-1].start()
    for copy in out_copies:
        copy.wait()


def sum_over_mon(share, handed_on, n_mon):
    if n_mon & (n_mon - 1):
        return [handed_on] + [
            lax.ppermute(share, "mon", [(i, (i + s) % n_mon) for i in range(n_mon)])
            for s in range(1, n_mon)
        ]
    parts = [handed_on]
    step = 1
    while step < n_mon:
        sent = share if step == 1 else functools.reduce(jnp.add, parts)
        got = lax.ppermute(sent, "mon", [(i, i ^ step) for i in range(n_mon)])
        parts = [handed_on if step == 1 else sent, got]
        step *= 2
    return parts


def on_device(dfactors, block_mask, base_flow, branch_row, pair_slots, pair_counts):
    rows_dev, cols = dfactors.shape
    blocks = rows_dev // BLOCK
    candidates = branch_row.shape[0]
    cap = pair_slots.shape[0]
    rows = dense_rows(cap)
    n_sub = lax.axis_size("sub")
    my_rows = rows_dev // n_sub
    slots = pair_slots.T
    base = base_flow.reshape(blocks, BLOCK)
    table = branch_row.reshape(candidates // LANES, LANES)
    hbm = pl.BlockSpec(memory_space=pltpu.HBM)
    in_hbm = functools.partial(pltpu.with_memory_space_constraint, memory_space=pltpu.HBM)
    in_vmem = functools.partial(pltpu.with_memory_space_constraint, memory_space=pltpu.VMEM)
    vmem = pl.BlockSpec(memory_space=pltpu.VMEM)
    params = pltpu.CompilerParams(vmem_limit_bytes=VMEM_LIMIT)
    rings = [[(i, (i + s) % n_sub) for i in range(n_sub)] for s in range(n_sub)]

    factors = [dfactors] + [lax.ppermute(dfactors, "sub", ring) for ring in rings[1:]]

    chunks = rows_dev // chunk_of(rows_dev, 512)
    note_rows = 4 * rows + (cols // LANES) * (my_rows // BLOCK)
    outs = pl.pallas_call(
        functools.partial(values_kernel, n_sub),
        out_shape=[pltpu.VMEM((4 * rows, LANES), F32)]
        + [pltpu.VMEM((note_rows, LANES), F32)] * (n_sub - 1)
        + [
            pltpu.VMEM((rows_dev, cols), BF16),
            pltpu.VMEM((blocks, cols), I32),
            pltpu.VMEM((blocks, BLOCK), F32),
            pltpu.VMEM((2, cap), I32),
        ],
        in_specs=[hbm] * 5,
        out_specs=[vmem] * (n_sub + 4),
        scratch_shapes=[
            pltpu.VMEM((candidates // LANES, LANES), I32),
            pltpu.VMEM((ENDS, 2 * cap), BF16),
            pltpu.VMEM((cols, ENDS), BF16),
            pltpu.VMEM((SUBLANES, 2 * cap), F32),
            pltpu.SemaphoreType.DMA((4,)),
            pltpu.SemaphoreType.DMA((chunks,)),
        ],
        compiler_params=params,
        cost_estimate=pl.CostEstimate(
            flops=2 * rows_dev * cols * ENDS, bytes_accessed=rows_dev * cols * 2, transcendentals=0
        ),
        name="pair_values",
    )(*map(in_hbm, (dfactors, block_mask, base, table, slots)))
    share, notes = outs[0], outs[1:n_sub]
    factors[0], block_mask, base, slots = outs[n_sub:]

    notes = [lax.ppermute(note, "sub", ring) for note, ring in zip(notes, rings[1:])]
    share = functools.reduce(jnp.add, [share] + [note[: 4 * rows] for note in notes])

    width = chunk_of(cap, 256)
    hot = pltpu.VMEM((cap // width, n_sub * cols, width), BF16)
    columns = pltpu.VMEM((my_rows, cap), BF16)
    columns_cost = pl.CostEstimate(
        flops=2 * my_rows * cols * n_sub * cap,
        bytes_accessed=my_rows * (cols * n_sub + cap) * 2,
        transcendentals=0,
    )
    masked, first, handed_on = pl.pallas_call(
        functools.partial(first_kernel, n_sub),
        out_shape=[
            pltpu.VMEM((my_rows, n_sub * cols), BF16),
            columns,
            pltpu.VMEM(share.shape, F32),
        ],
        in_specs=[vmem] * (2 * n_sub + 2),
        out_specs=[vmem] * 3,
        scratch_shapes=[hot],
        compiler_params=params,
        cost_estimate=columns_cost,
        name="first_columns",
    )(*map(in_vmem, (*factors, *notes, block_mask, slots, share)))
    shares = sum_over_mon(share, handed_on, lax.axis_size("mon"))
    second = pl.pallas_call(
        functools.partial(second_kernel, n_sub),
        out_shape=columns,
        in_specs=[vmem] * 2,
        out_specs=vmem,
        scratch_shapes=[hot],
        compiler_params=params,
        cost_estimate=columns_cost,
        name="second_columns",
    )(*map(in_vmem, (masked, slots)))
    return pl.pallas_call(
        functools.partial(flows_kernel, len(shares)),
        out_shape=jax.ShapeDtypeStruct((my_rows, cap), BF16),
        in_specs=[vmem] * (len(shares) + 3) + [pl.BlockSpec(memory_space=pltpu.SMEM)],
        out_specs=hbm,
        scratch_shapes=[
            pltpu.VMEM((my_rows, cap), BF16),
            pltpu.SemaphoreType.DMA((my_rows // BLOCK,)),
        ],
        compiler_params=params,
        cost_estimate=pl.CostEstimate(
            flops=6 * my_rows * cap, bytes_accessed=my_rows * cap * 2, transcendentals=0
        ),
        name="post_flows",
    )(*map(in_vmem, (*shares, base, first, second)), pair_counts)


def solution(mesh):
    return jax.shard_map(
        on_device,
        mesh=mesh,
        in_specs=(
            P("mon", "sub"),
            P("mon", "sub"),
            P("mon"),
            P(),
            P(("grp", "pair"), None),
            P(("grp", "pair")),
        ),
        out_specs=P(("mon", "sub"), ("grp", "pair")),
        check_vma=False,
    )
```

```python
import functools

import jax
import jax.numpy as jnp
from jax import lax
from jax.experimental import pallas as pl
from jax.experimental.pallas import tpu as pltpu
from jax.sharding import PartitionSpec as P

BLOCK = 128
LANES = 128
SUBLANES = 8
ENDS = 256
VMEM_LIMIT = 16 * 1024 * 1024
F32 = jnp.float32
BF16 = jnp.bfloat16
I32 = jnp.int32


def chunk_of(total, want):
    size = min(total, want)
    while total % size:
        size -= BLOCK
    return size


def dense_rows(cap):
    return -(-cap // (LANES * SUBLANES)) * SUBLANES


def one_hot(hit):
    return jnp.where(hit, 1.0, 0.0).astype(BF16)


def iota(shape, axis):
    return lax.broadcasted_iota(I32, shape, axis)


def dense(line):
    cap = line.shape[1]
    rows = dense_rows(cap)
    pieces = [line[:, c : c + LANES] for c in range(0, cap, LANES)]
    if len(pieces) < rows:
        pieces.append(jnp.zeros((rows - len(pieces), LANES), line.dtype))
    return jnp.concatenate(pieces, axis=0)


def look_up(table, index):
    high, low = index >> 7, index & 127
    found = jnp.zeros(index.shape, table.dtype)
    for b in range(table.shape[0]):
        line = jnp.broadcast_to(table[b : b + 1], index.shape)
        value = jnp.take_along_axis(line, low, axis=1, mode="promise_in_bounds")
        found = jnp.where(high == b, value, found)
    return found


def values_kernel(
    n_sub, d_hbm, mask_hbm, base_hbm, rows_hbm, slots_hbm, *refs
):
    share_ref, *note_refs = refs[:n_sub]
    (
        d_ref, mask_ref, base_ref, slots_ref, rows_ref, perm_ref, hot_ref, cross_ref, sems, d_sems
    ) = refs[n_sub:]
    rows_dev, cols = d_ref.shape
    chunks = d_sems.shape[0]
    chunk = rows_dev // chunks
    cap = slots_ref.shape[1]
    lines = cap // LANES
    rows = dense_rows(cap)
    sub_index = lax.axis_index("sub")
    small = [
        pltpu.make_async_copy(src, dst, sems.at[i])
        for i, (src, dst) in enumerate(
            [(slots_hbm, slots_ref), (rows_hbm, rows_ref), (base_hbm, base_ref), (mask_hbm, mask_ref)]
        )
    ]
    large = [
        pltpu.make_async_copy(
            d_hbm.at[pl.ds(i * chunk, chunk)], d_ref.at[pl.ds(i * chunk, chunk)], d_sems.at[i]
        )
        for i in range(chunks)
    ]
    for copy in small + large:
        copy.start()

    small[0].wait()
    small[1].wait()
    first, second = dense(slots_ref[0:1, :]), dense(slots_ref[1:2, :])
    table = rows_ref[...]
    row = jnp.concatenate([look_up(table, first), look_up(table, second)], axis=0)
    row = row - lax.axis_index("mon") * rows_dev
    col = jnp.concatenate([second, first], axis=0) - sub_index * cols
    used = lax.rem(iota(row.shape, 0), rows) < lines
    here = used & (row >= 0) & (row < rows_dev) & (col >= 0) & (col < cols)

    flags = one_hot(here)
    height = flags.shape[0]
    above = jnp.dot(
        one_hot(iota((height, height), 1) < iota((height, height), 0)),
        flags,
        preferred_element_type=F32,
    ).astype(BF16)
    place = jnp.dot(
        jnp.concatenate([flags, above], axis=1),
        jnp.concatenate(
            [
                one_hot(iota((LANES, LANES), 0) <= iota((LANES, LANES), 1)),
                jnp.ones((LANES, LANES), BF16),
            ],
            axis=0,
        ),
        preferred_element_type=F32,
    ).astype(I32)
    place = jnp.where(here, place - 1, -1)
    digits = [(x >> shift) & 255 for x in (col, row) for shift in (0, 8)]
    order = [half * rows + b for half in range(2) for b in range(lines)]
    ends = jnp.concatenate(
        [jnp.concatenate([x[r : r + 1] for x in digits], axis=0) for r in order], axis=1
    )
    ends = ends.astype(F32).astype(BF16)

    def pick(start):
        for at, r in enumerate(order):
            perm_ref[:, at * LANES : (at + 1) * LANES] = one_hot(
                iota((ENDS, LANES), 0) + start == place[r : r + 1]
            )
        packed = lax.dot_general(
            ends, perm_ref[...], (((1,), (1,)), ((), ())), preferred_element_type=F32
        ).astype(I32)
        end_col = packed[0:1] + (packed[1:2] << 8)
        end_row = packed[2:3] + (packed[3:4] << 8)
        hot_ref[...] = one_hot(iota((cols, ENDS), 0) == end_col)
        keep = jnp.dot(
            mask_ref[...].astype(F32).astype(BF16), hot_ref[...], preferred_element_type=F32
        )
        keep = jnp.sum(
            jnp.where(iota(keep.shape, 0) == (end_row >> 7), keep, 0.0), axis=0, keepdims=True
        )
        total = jnp.zeros((SUBLANES, ENDS), F32)
        for i in range(chunks):
            values = jnp.dot(
                d_ref[i * chunk : (i + 1) * chunk, :], hot_ref[...], preferred_element_type=F32
            )
            picked = jnp.where(iota((chunk, ENDS), 0) + i * chunk == end_row, values, 0.0)
            total += jnp.sum(picked.reshape(chunk // SUBLANES, SUBLANES, ENDS), axis=0)
        value = jnp.sum(total, axis=0, keepdims=True) * keep
        return jnp.dot(
            jnp.broadcast_to(value, (SUBLANES, ENDS)).astype(BF16),
            perm_ref[...],
            preferred_element_type=F32,
        )

    for copy in small[2:] + large:
        copy.wait()
    cross_ref[...] = pick(0)
    flow = jnp.where(sub_index == 0, look_up(base_ref[...], row), 0.0)
    count = jnp.max(place) + 1

    @pl.when(count > ENDS)
    def _():
        def more(i, _):
            cross_ref[...] += pick(i * ENDS)
            return 0

        lax.fori_loop(1, pl.cdiv(count, ENDS), more, 0)

    for ref in (share_ref, *note_refs):
        for half in range(2):
            for b in range(rows):
                at = (half * lines + b) * LANES
                ref[half * rows + b : half * rows + b + 1, :] = (
                    cross_ref[0:1, at : at + LANES] if b < lines else jnp.zeros((1, LANES), F32)
                )
        ref[2 * rows : 4 * rows, :] = flow
    my_blocks = mask_ref.shape[0] // n_sub
    for s, ref in enumerate(note_refs, 1):
        block = pl.multiple_of(lax.rem(sub_index + s, n_sub) * my_blocks, my_blocks)
        for c in range(cols // LANES):
            at = 4 * rows + c * my_blocks
            ref[at : at + my_blocks, :] = mask_ref[
                pl.ds(block, my_blocks), c * LANES : (c + 1) * LANES
            ].astype(F32)


def pick_columns(count, slot, starts, cols, masked_ref, hot_ref, out_ref):
    parts, _, width = hot_ref.shape
    live_parts = jnp.minimum((count + width - 1) // width, parts)

    def pick(n_parts):
        for part in range(n_parts):
            lanes = slice(part * width, (part + 1) * width)
            for s, start in enumerate(starts):
                hot_ref[part, s * cols : (s + 1) * cols, :] = one_hot(
                    iota((cols, width), 0) == slot[:, lanes] - start
                )
            out_ref[:, lanes] = jnp.dot(
                masked_ref[...], hot_ref[part], preferred_element_type=F32
            ).astype(BF16)

    for n_parts in range(1, parts + 1):
        pl.when(live_parts == n_parts)(functools.partial(pick, n_parts))


def column_starts(n_sub, cols):
    return [lax.rem(lax.axis_index("sub") + n_sub - s, n_sub) * cols for s in range(n_sub)]


def first_kernel(n_sub, *refs):
    d_refs, refs = refs[:n_sub], refs[n_sub:]
    note_refs, refs = refs[: n_sub - 1], refs[n_sub - 1 :]
    mask_ref, slots_ref, share_ref, count_ref, masked_ref, first_ref, shared_ref, hot_ref = refs
    shared_ref[...] = share_ref[...]
    my_rows, all_cols = masked_ref.shape
    cols = all_cols // n_sub
    my_blocks = my_rows // BLOCK
    share_rows = note_refs[0].shape[0] - (cols // LANES) * my_blocks if note_refs else 0
    sub_index = lax.axis_index("sub")
    my_start = pl.multiple_of(sub_index * my_rows, my_rows)
    my_block = pl.multiple_of(sub_index * my_blocks, my_blocks)
    for s in range(n_sub):
        if s == 0:
            keep = mask_ref[pl.ds(my_block, my_blocks), :].astype(F32)
        else:
            keep = jnp.concatenate(
                [
                    note_refs[s - 1][share_rows + c * my_blocks : share_rows + (c + 1) * my_blocks, :]
                    for c in range(cols // LANES)
                ],
                axis=1,
            )
        keep = keep.astype(BF16)
        for b in range(my_blocks):
            masked_ref[b * BLOCK : (b + 1) * BLOCK, s * cols : (s + 1) * cols] = (
                d_refs[s][pl.ds(my_start + b * BLOCK, BLOCK), :] * keep[b : b + 1]
            )
    starts = column_starts(n_sub, cols)
    pick_columns(count_ref[0], slots_ref[0:1, :], starts, cols, masked_ref, hot_ref, first_ref)


def second_kernel(n_sub, masked_ref, slots_ref, count_ref, second_ref, hot_ref):
    cols = masked_ref.shape[1] // n_sub
    starts = column_starts(n_sub, cols)
    pick_columns(count_ref[0], slots_ref[1:2, :], starts, cols, masked_ref, hot_ref, second_ref)


def flows_kernel(n_shares, *refs):
    share_refs, refs = refs[:n_shares], refs[n_shares:]
    base_ref, first_ref, second_ref, count_ref, out_hbm, post_ref, out_sems = refs
    my_rows, cap = post_ref.shape
    my_blocks = my_rows // BLOCK
    rows = dense_rows(cap)
    total = share_refs[0][...]
    for ref in share_refs[1:]:
        total = total + ref[...]
    cross_first, cross_second, flow_first, flow_second = (
        total[i * rows : (i + 1) * rows] for i in range(4)
    )
    determinant = 1.0 - cross_first * cross_second
    shift_first = (flow_first + cross_first * flow_second) / determinant
    shift_second = (flow_second + cross_second * flow_first) / determinant
    lines = range(cap // LANES)
    weights = [
        [
            jnp.broadcast_to(shift[line : line + 1], (BLOCK, LANES)).astype(BF16)
            for line in lines
        ]
        for shift in (shift_first, shift_second)
    ]
    live = [iota((1, LANES), 1) + line * LANES < count_ref[0] for line in lines]
    my_block = pl.multiple_of(lax.axis_index("sub") * my_blocks, my_blocks)
    base = jnp.swapaxes(base_ref[pl.ds(my_block, my_blocks), :], 0, 1)
    out_copies = []
    for b in range(my_blocks):
        block = slice(b * BLOCK, (b + 1) * BLOCK)
        start = jnp.broadcast_to(base[:, b : b + 1], (BLOCK, LANES))
        for line in lines:
            lanes = slice(line * LANES, (line + 1) * LANES)
            change = (
                weights[0][line] * first_ref[block, lanes]
                + weights[1][line] * second_ref[block, lanes]
            )
            post_ref[block, lanes] = jnp.where(
                live[line], start + change.astype(F32), 0.0
            ).astype(BF16)
        out_copies.append(
            pltpu.make_async_copy(post_ref.at[block], out_hbm.at[block], out_sems.at[b])
        )
        out_copies[-1].start()
    for copy in out_copies:
        copy.wait()


def sum_over_mon(share, handed_on, n_mon):
    if n_mon & (n_mon - 1):
        return [handed_on] + [
            lax.ppermute(share, "mon", [(i, (i + s) % n_mon) for i in range(n_mon)])
            for s in range(1, n_mon)
        ]
    parts = [handed_on]
    step = 1
    while step < n_mon:
        sent = share if step == 1 else functools.reduce(jnp.add, parts)
        got = lax.ppermute(sent, "mon", [(i, i ^ step) for i in range(n_mon)])
        parts = [handed_on if step == 1 else sent, got]
        step *= 2
    return parts


def on_device(dfactors, block_mask, base_flow, branch_row, pair_slots, pair_counts):
    rows_dev, cols = dfactors.shape
    blocks = rows_dev // BLOCK
    candidates = branch_row.shape[0]
    cap = pair_slots.shape[0]
    rows = dense_rows(cap)
    n_sub = lax.axis_size("sub")
    my_rows = rows_dev // n_sub
    slots = pair_slots.T
    base = base_flow.reshape(blocks, BLOCK)
    table = branch_row.reshape(candidates // LANES, LANES)
    hbm = pl.BlockSpec(memory_space=pltpu.HBM)
    in_hbm = functools.partial(pltpu.with_memory_space_constraint, memory_space=pltpu.HBM)
    in_vmem = functools.partial(pltpu.with_memory_space_constraint, memory_space=pltpu.VMEM)
    vmem = pl.BlockSpec(memory_space=pltpu.VMEM)
    smem = pl.BlockSpec(memory_space=pltpu.SMEM)
    params = pltpu.CompilerParams(vmem_limit_bytes=VMEM_LIMIT)
    rings = [[(i, (i + s) % n_sub) for i in range(n_sub)] for s in range(n_sub)]

    factors = [dfactors] + [lax.ppermute(dfactors, "sub", ring) for ring in rings[1:]]

    chunks = rows_dev // chunk_of(rows_dev, 512)
    note_rows = 4 * rows + (cols // LANES) * (my_rows // BLOCK)
    outs = pl.pallas_call(
        functools.partial(values_kernel, n_sub),
        out_shape=[pltpu.VMEM((4 * rows, LANES), F32)]
        + [pltpu.VMEM((note_rows, LANES), F32)] * (n_sub - 1)
        + [
            pltpu.VMEM((rows_dev, cols), BF16),
            pltpu.VMEM((blocks, cols), I32),
            pltpu.VMEM((blocks, BLOCK), F32),
            pltpu.VMEM((2, cap), I32),
        ],
        in_specs=[hbm] * 5,
        out_specs=[vmem] * (n_sub + 4),
        scratch_shapes=[
            pltpu.VMEM((candidates // LANES, LANES), I32),
            pltpu.VMEM((ENDS, 2 * cap), BF16),
            pltpu.VMEM((cols, ENDS), BF16),
            pltpu.VMEM((SUBLANES, 2 * cap), F32),
            pltpu.SemaphoreType.DMA((4,)),
            pltpu.SemaphoreType.DMA((chunks,)),
        ],
        compiler_params=params,
        cost_estimate=pl.CostEstimate(
            flops=2 * rows_dev * cols * ENDS, bytes_accessed=rows_dev * cols * 2, transcendentals=0
        ),
        name="pair_values",
    )(*map(in_hbm, (dfactors, block_mask, base, table, slots)))
    share, notes = outs[0], outs[1:n_sub]
    factors[0], block_mask, base, slots = outs[n_sub:]

    notes = [lax.ppermute(note, "sub", ring) for note, ring in zip(notes, rings[1:])]
    share = functools.reduce(jnp.add, [share] + [note[: 4 * rows] for note in notes])

    width = chunk_of(cap, 256)
    hot = pltpu.VMEM((cap // width, n_sub * cols, width), BF16)
    columns = pltpu.VMEM((my_rows, cap), BF16)
    columns_cost = pl.CostEstimate(
        flops=2 * my_rows * cols * n_sub * cap,
        bytes_accessed=my_rows * (cols * n_sub + cap) * 2,
        transcendentals=0,
    )
    masked, first, handed_on = pl.pallas_call(
        functools.partial(first_kernel, n_sub),
        out_shape=[
            pltpu.VMEM((my_rows, n_sub * cols), BF16),
            columns,
            pltpu.VMEM(share.shape, F32),
        ],
        in_specs=[vmem] * (2 * n_sub + 2) + [smem],
        out_specs=[vmem] * 3,
        scratch_shapes=[hot],
        compiler_params=params,
        cost_estimate=columns_cost,
        name="first_columns",
    )(*map(in_vmem, (*factors, *notes, block_mask, slots, share)), pair_counts)
    shares = sum_over_mon(share, handed_on, lax.axis_size("mon"))
    second = pl.pallas_call(
        functools.partial(second_kernel, n_sub),
        out_shape=columns,
        in_specs=[vmem] * 2 + [smem],
        out_specs=vmem,
        scratch_shapes=[hot],
        compiler_params=params,
        cost_estimate=columns_cost,
        name="second_columns",
    )(*map(in_vmem, (masked, slots)), pair_counts)
    return pl.pallas_call(
        functools.partial(flows_kernel, len(shares)),
        out_shape=jax.ShapeDtypeStruct((my_rows, cap), BF16),
        in_specs=[vmem] * (len(shares) + 3) + [smem],
        out_specs=hbm,
        scratch_shapes=[
            pltpu.VMEM((my_rows, cap), BF16),
            pltpu.SemaphoreType.DMA((my_rows // BLOCK,)),
        ],
        compiler_params=params,
        cost_estimate=pl.CostEstimate(
            flops=6 * my_rows * cap, bytes_accessed=my_rows * cap * 2, transcendentals=0
        ),
        name="post_flows",
    )(*map(in_vmem, (*shares, base, first, second)), pair_counts)


def solution(mesh):
    return jax.shard_map(
        on_device,
        mesh=mesh,
        in_specs=(
            P("mon", "sub"),
            P("mon", "sub"),
            P("mon"),
            P(),
            P(("grp", "pair"), None),
            P(("grp", "pair")),
        ),
        out_specs=P(("mon", "sub"), ("grp", "pair")),
        check_vma=False,
    )
```

```python
import functools

import jax
import jax.numpy as jnp
from jax import lax
from jax.experimental import pallas as pl
from jax.experimental.pallas import tpu as pltpu
from jax.sharding import PartitionSpec as P

BLOCK = 128
LANES = 128
SUBLANES = 8
ENDS = 256
VMEM_LIMIT = 16 * 1024 * 1024
F32 = jnp.float32
BF16 = jnp.bfloat16
I32 = jnp.int32


def chunk_of(total, want):
    size = min(total, want)
    while total % size:
        size -= BLOCK
    return size


def dense_rows(cap):
    return -(-cap // (LANES * SUBLANES)) * SUBLANES


def one_hot(hit):
    return jnp.where(hit, 1.0, 0.0).astype(BF16)


def iota(shape, axis):
    return lax.broadcasted_iota(I32, shape, axis)


def dense(line):
    cap = line.shape[1]
    rows = dense_rows(cap)
    pieces = [line[:, c : c + LANES] for c in range(0, cap, LANES)]
    if len(pieces) < rows:
        pieces.append(jnp.zeros((rows - len(pieces), LANES), line.dtype))
    return jnp.concatenate(pieces, axis=0)


def look_up(table, index):
    high, low = index >> 7, index & 127
    found = jnp.zeros(index.shape, table.dtype)
    for b in range(table.shape[0]):
        line = jnp.broadcast_to(table[b : b + 1], index.shape)
        value = jnp.take_along_axis(line, low, axis=1, mode="promise_in_bounds")
        found = jnp.where(high == b, value, found)
    return found


def values_kernel(
    n_sub, d_hbm, mask_hbm, base_hbm, rows_hbm, slots_hbm, *refs
):
    share_ref, *note_refs = refs[:n_sub]
    (
        d_ref, mask_ref, base_ref, slots_ref, rows_ref, perm_ref, hot_ref, cross_ref, sems, d_sems
    ) = refs[n_sub:]
    rows_dev, cols = d_ref.shape
    chunks = d_sems.shape[0]
    chunk = rows_dev // chunks
    cap = slots_ref.shape[1]
    lines = cap // LANES
    rows = dense_rows(cap)
    sub_index = lax.axis_index("sub")
    small = [
        pltpu.make_async_copy(src, dst, sems.at[i])
        for i, (src, dst) in enumerate(
            [(slots_hbm, slots_ref), (rows_hbm, rows_ref), (base_hbm, base_ref), (mask_hbm, mask_ref)]
        )
    ]
    large = [
        pltpu.make_async_copy(
            d_hbm.at[pl.ds(i * chunk, chunk)], d_ref.at[pl.ds(i * chunk, chunk)], d_sems.at[i]
        )
        for i in range(chunks)
    ]
    for copy in small + large:
        copy.start()

    small[0].wait()
    small[1].wait()
    first, second = dense(slots_ref[0:1, :]), dense(slots_ref[1:2, :])
    table = rows_ref[...]
    row = jnp.concatenate([look_up(table, first), look_up(table, second)], axis=0)
    row = row - lax.axis_index("mon") * rows_dev
    col = jnp.concatenate([second, first], axis=0) - sub_index * cols
    used = lax.rem(iota(row.shape, 0), rows) < lines
    here = used & (row >= 0) & (row < rows_dev) & (col >= 0) & (col < cols)

    flags = one_hot(here)
    height = flags.shape[0]
    above = jnp.dot(
        one_hot(iota((height, height), 1) < iota((height, height), 0)),
        flags,
        preferred_element_type=F32,
    ).astype(BF16)
    place = jnp.dot(
        jnp.concatenate([flags, above], axis=1),
        jnp.concatenate(
            [
                one_hot(iota((LANES, LANES), 0) <= iota((LANES, LANES), 1)),
                jnp.ones((LANES, LANES), BF16),
            ],
            axis=0,
        ),
        preferred_element_type=F32,
    ).astype(I32)
    place = jnp.where(here, place - 1, -1)
    digits = [(x >> shift) & 255 for x in (col, row) for shift in (0, 8)]
    order = [half * rows + b for half in range(2) for b in range(lines)]
    ends = jnp.concatenate(
        [jnp.concatenate([x[r : r + 1] for x in digits], axis=0) for r in order], axis=1
    )
    ends = ends.astype(F32).astype(BF16)

    def pick(start):
        for at, r in enumerate(order):
            perm_ref[:, at * LANES : (at + 1) * LANES] = one_hot(
                iota((ENDS, LANES), 0) + start == place[r : r + 1]
            )
        packed = lax.dot_general(
            ends, perm_ref[...], (((1,), (1,)), ((), ())), preferred_element_type=F32
        ).astype(I32)
        end_col = packed[0:1] + (packed[1:2] << 8)
        end_row = packed[2:3] + (packed[3:4] << 8)
        hot_ref[...] = one_hot(iota((cols, ENDS), 0) == end_col)
        keep = jnp.dot(
            mask_ref[...].astype(F32).astype(BF16), hot_ref[...], preferred_element_type=F32
        )
        keep = jnp.sum(
            jnp.where(iota(keep.shape, 0) == (end_row >> 7), keep, 0.0), axis=0, keepdims=True
        )
        total = jnp.zeros((SUBLANES, ENDS), F32)
        for i in range(chunks):
            values = jnp.dot(
                d_ref[i * chunk : (i + 1) * chunk, :], hot_ref[...], preferred_element_type=F32
            )
            picked = jnp.where(iota((chunk, ENDS), 0) + i * chunk == end_row, values, 0.0)
            total += jnp.sum(picked.reshape(chunk // SUBLANES, SUBLANES, ENDS), axis=0)
        value = jnp.sum(total, axis=0, keepdims=True) * keep
        return jnp.dot(
            jnp.broadcast_to(value, (SUBLANES, ENDS)).astype(BF16),
            perm_ref[...],
            preferred_element_type=F32,
        )

    for copy in small[2:] + large:
        copy.wait()
    cross_ref[...] = pick(0)
    flow = jnp.where(sub_index == 0, look_up(base_ref[...], row), 0.0)
    count = jnp.max(place) + 1

    @pl.when(count > ENDS)
    def _():
        def more(i, _):
            cross_ref[...] += pick(i * ENDS)
            return 0

        lax.fori_loop(1, pl.cdiv(count, ENDS), more, 0)

    for ref in (share_ref, *note_refs):
        for half in range(2):
            for b in range(rows):
                at = (half * lines + b) * LANES
                ref[half * rows + b : half * rows + b + 1, :] = (
                    cross_ref[0:1, at : at + LANES] if b < lines else jnp.zeros((1, LANES), F32)
                )
        ref[2 * rows : 4 * rows, :] = flow
    my_blocks = mask_ref.shape[0] // n_sub
    for s, ref in enumerate(note_refs, 1):
        block = pl.multiple_of(lax.rem(sub_index + s, n_sub) * my_blocks, my_blocks)
        for c in range(cols // LANES):
            at = 4 * rows + c * my_blocks
            ref[at : at + my_blocks, :] = mask_ref[
                pl.ds(block, my_blocks), c * LANES : (c + 1) * LANES
            ].astype(F32)


def pick_columns(count, slot, starts, cols, masked_ref, hot_ref, out_ref, prepare=lambda: None):
    parts, _, width = hot_ref.shape
    live_parts = jnp.minimum((count + width - 1) // width, parts)

    def pick(n_parts):
        prepare()
        for part in range(n_parts):
            lanes = slice(part * width, (part + 1) * width)
            for s, start in enumerate(starts):
                hot_ref[part, s * cols : (s + 1) * cols, :] = one_hot(
                    iota((cols, width), 0) == slot[:, lanes] - start
                )
            out_ref[:, lanes] = jnp.dot(
                masked_ref[...], hot_ref[part], preferred_element_type=F32
            ).astype(BF16)

    for n_parts in range(1, parts + 1):
        pl.when(live_parts == n_parts)(functools.partial(pick, n_parts))


def column_starts(n_sub, cols):
    return [lax.rem(lax.axis_index("sub") + n_sub - s, n_sub) * cols for s in range(n_sub)]


def first_kernel(n_sub, *refs):
    d_refs, refs = refs[:n_sub], refs[n_sub:]
    note_refs, refs = refs[: n_sub - 1], refs[n_sub - 1 :]
    mask_ref, slots_ref, share_ref, count_ref, masked_ref, first_ref, shared_ref, hot_ref = refs
    shared_ref[...] = share_ref[...]
    my_rows, all_cols = masked_ref.shape
    cols = all_cols // n_sub
    my_blocks = my_rows // BLOCK
    share_rows = note_refs[0].shape[0] - (cols // LANES) * my_blocks if note_refs else 0
    sub_index = lax.axis_index("sub")
    my_start = pl.multiple_of(sub_index * my_rows, my_rows)
    my_block = pl.multiple_of(sub_index * my_blocks, my_blocks)
    def prepare():
        for s in range(n_sub):
            if s == 0:
                keep = mask_ref[pl.ds(my_block, my_blocks), :].astype(F32)
            else:
                keep = jnp.concatenate(
                    [
                        note_refs[s - 1][share_rows + c * my_blocks : share_rows + (c + 1) * my_blocks, :]
                        for c in range(cols // LANES)
                    ],
                    axis=1,
                )
            keep = keep.astype(BF16)
            for b in range(my_blocks):
                masked_ref[b * BLOCK : (b + 1) * BLOCK, s * cols : (s + 1) * cols] = (
                    d_refs[s][pl.ds(my_start + b * BLOCK, BLOCK), :] * keep[b : b + 1]
                )

    starts = column_starts(n_sub, cols)
    pick_columns(
        count_ref[0], slots_ref[0:1, :], starts, cols, masked_ref, hot_ref, first_ref, prepare
    )


def second_kernel(n_sub, masked_ref, slots_ref, count_ref, second_ref, hot_ref):
    cols = masked_ref.shape[1] // n_sub
    starts = column_starts(n_sub, cols)
    pick_columns(count_ref[0], slots_ref[1:2, :], starts, cols, masked_ref, hot_ref, second_ref)


def flows_kernel(n_shares, *refs):
    share_refs, refs = refs[:n_shares], refs[n_shares:]
    base_ref, first_ref, second_ref, count_ref, out_hbm, post_ref, out_sems = refs
    my_rows, cap = post_ref.shape
    my_blocks = my_rows // BLOCK
    rows = dense_rows(cap)
    total = share_refs[0][...]
    for ref in share_refs[1:]:
        total = total + ref[...]
    cross_first, cross_second, flow_first, flow_second = (
        total[i * rows : (i + 1) * rows] for i in range(4)
    )
    determinant = 1.0 - cross_first * cross_second
    shift_first = (flow_first + cross_first * flow_second) / determinant
    shift_second = (flow_second + cross_second * flow_first) / determinant
    lines = range(cap // LANES)
    weights = [
        [
            jnp.broadcast_to(shift[line : line + 1], (BLOCK, LANES)).astype(BF16)
            for line in lines
        ]
        for shift in (shift_first, shift_second)
    ]
    live = [iota((1, LANES), 1) + line * LANES < count_ref[0] for line in lines]
    my_block = pl.multiple_of(lax.axis_index("sub") * my_blocks, my_blocks)
    base = jnp.swapaxes(base_ref[pl.ds(my_block, my_blocks), :], 0, 1)
    out_copies = []
    for b in range(my_blocks):
        block = slice(b * BLOCK, (b + 1) * BLOCK)
        start = jnp.broadcast_to(base[:, b : b + 1], (BLOCK, LANES))
        for line in lines:
            lanes = slice(line * LANES, (line + 1) * LANES)
            change = (
                weights[0][line] * first_ref[block, lanes]
                + weights[1][line] * second_ref[block, lanes]
            )
            post_ref[block, lanes] = jnp.where(
                live[line], start + change.astype(F32), 0.0
            ).astype(BF16)
        out_copies.append(
            pltpu.make_async_copy(post_ref.at[block], out_hbm.at[block], out_sems.at[b])
        )
        out_copies[-1].start()
    for copy in out_copies:
        copy.wait()


def sum_over_mon(share, handed_on, n_mon, n_sub):
    def swap(sent, partner):
        perm = [
            (m * n_sub + s, partner(m) * n_sub + n_sub - 1 - s)
            for m in range(n_mon)
            for s in range(n_sub)
        ]
        return lax.ppermute(sent, ("mon", "sub"), perm)

    if n_mon & (n_mon - 1):
        return [handed_on] + [
            swap(share, lambda m, k=k: (m + k) % n_mon) for k in range(1, n_mon)
        ]
    parts = [handed_on]
    step = 1
    while step < n_mon:
        sent = share if step == 1 else functools.reduce(jnp.add, parts)
        got = swap(sent, lambda m, k=step: m ^ k)
        parts = [handed_on if step == 1 else sent, got]
        step *= 2
    return parts


def on_device(dfactors, block_mask, base_flow, branch_row, pair_slots, pair_counts):
    rows_dev, cols = dfactors.shape
    blocks = rows_dev // BLOCK
    candidates = branch_row.shape[0]
    cap = pair_slots.shape[0]
    rows = dense_rows(cap)
    n_sub = lax.axis_size("sub")
    my_rows = rows_dev // n_sub
    slots = pair_slots.T
    base = base_flow.reshape(blocks, BLOCK)
    table = branch_row.reshape(candidates // LANES, LANES)
    hbm = pl.BlockSpec(memory_space=pltpu.HBM)
    in_hbm = functools.partial(pltpu.with_memory_space_constraint, memory_space=pltpu.HBM)
    in_vmem = functools.partial(pltpu.with_memory_space_constraint, memory_space=pltpu.VMEM)
    vmem = pl.BlockSpec(memory_space=pltpu.VMEM)
    smem = pl.BlockSpec(memory_space=pltpu.SMEM)
    params = pltpu.CompilerParams(vmem_limit_bytes=VMEM_LIMIT)
    rings = [[(i, (i + s) % n_sub) for i in range(n_sub)] for s in range(n_sub)]

    factors = [dfactors] + [lax.ppermute(dfactors, "sub", ring) for ring in rings[1:]]

    chunks = rows_dev // chunk_of(rows_dev, 512)
    note_rows = 4 * rows + (cols // LANES) * (my_rows // BLOCK)
    outs = pl.pallas_call(
        functools.partial(values_kernel, n_sub),
        out_shape=[pltpu.VMEM((4 * rows, LANES), F32)]
        + [pltpu.VMEM((note_rows, LANES), F32)] * (n_sub - 1)
        + [
            pltpu.VMEM((rows_dev, cols), BF16),
            pltpu.VMEM((blocks, cols), I32),
            pltpu.VMEM((blocks, BLOCK), F32),
            pltpu.VMEM((2, cap), I32),
        ],
        in_specs=[hbm] * 5,
        out_specs=[vmem] * (n_sub + 4),
        scratch_shapes=[
            pltpu.VMEM((candidates // LANES, LANES), I32),
            pltpu.VMEM((ENDS, 2 * cap), BF16),
            pltpu.VMEM((cols, ENDS), BF16),
            pltpu.VMEM((SUBLANES, 2 * cap), F32),
            pltpu.SemaphoreType.DMA((4,)),
            pltpu.SemaphoreType.DMA((chunks,)),
        ],
        compiler_params=params,
        cost_estimate=pl.CostEstimate(
            flops=2 * rows_dev * cols * ENDS, bytes_accessed=rows_dev * cols * 2, transcendentals=0
        ),
        name="pair_values",
    )(*map(in_hbm, (dfactors, block_mask, base, table, slots)))
    share, notes = outs[0], outs[1:n_sub]
    factors[0], block_mask, base, slots = outs[n_sub:]

    notes = [lax.ppermute(note, "sub", ring) for note, ring in zip(notes, rings[1:])]
    share = functools.reduce(jnp.add, [share] + [note[: 4 * rows] for note in notes])

    width = chunk_of(cap, 256)
    hot = pltpu.VMEM((cap // width, n_sub * cols, width), BF16)
    columns = pltpu.VMEM((my_rows, cap), BF16)
    columns_cost = pl.CostEstimate(
        flops=2 * my_rows * cols * n_sub * cap,
        bytes_accessed=my_rows * (cols * n_sub + cap) * 2,
        transcendentals=0,
    )
    masked, first, handed_on = pl.pallas_call(
        functools.partial(first_kernel, n_sub),
        out_shape=[
            pltpu.VMEM((my_rows, n_sub * cols), BF16),
            columns,
            pltpu.VMEM(share.shape, F32),
        ],
        in_specs=[vmem] * (2 * n_sub + 2) + [smem],
        out_specs=[vmem] * 3,
        scratch_shapes=[hot],
        compiler_params=params,
        cost_estimate=columns_cost,
        name="first_columns",
    )(*map(in_vmem, (*factors, *notes, block_mask, slots, share)), pair_counts)
    shares = sum_over_mon(share, handed_on, lax.axis_size("mon"), n_sub)
    second = pl.pallas_call(
        functools.partial(second_kernel, n_sub),
        out_shape=columns,
        in_specs=[vmem] * 2 + [smem],
        out_specs=vmem,
        scratch_shapes=[hot],
        compiler_params=params,
        cost_estimate=columns_cost,
        name="second_columns",
    )(*map(in_vmem, (masked, slots)), pair_counts)
    return pl.pallas_call(
        functools.partial(flows_kernel, len(shares)),
        out_shape=jax.ShapeDtypeStruct((my_rows, cap), BF16),
        in_specs=[vmem] * (len(shares) + 3) + [smem],
        out_specs=hbm,
        scratch_shapes=[
            pltpu.VMEM((my_rows, cap), BF16),
            pltpu.SemaphoreType.DMA((my_rows // BLOCK,)),
        ],
        compiler_params=params,
        cost_estimate=pl.CostEstimate(
            flops=6 * my_rows * cap, bytes_accessed=my_rows * cap * 2, transcendentals=0
        ),
        name="post_flows",
    )(*map(in_vmem, (*shares, base, first, second)), pair_counts)


def solution(mesh):
    return jax.shard_map(
        on_device,
        mesh=mesh,
        in_specs=(
            P("mon", "sub"),
            P("mon", "sub"),
            P("mon"),
            P(),
            P(("grp", "pair"), None),
            P(("grp", "pair")),
        ),
        out_specs=P(("mon", "sub"), ("grp", "pair")),
        check_vma=False,
    )
```

```python
import functools

import jax
import jax.numpy as jnp
from jax import lax
from jax.experimental import pallas as pl
from jax.experimental.pallas import tpu as pltpu
from jax.sharding import PartitionSpec as P

BLOCK = 128
LANES = 128
SUBLANES = 8
ENDS = 256
VMEM_LIMIT = 16 * 1024 * 1024
F32 = jnp.float32
BF16 = jnp.bfloat16
I32 = jnp.int32


def chunk_of(total, want):
    size = min(total, want)
    while total % size:
        size -= BLOCK
    return size


def dense_rows(cap):
    return -(-cap // (LANES * SUBLANES)) * SUBLANES


def one_hot(hit):
    return jnp.where(hit, 1.0, 0.0).astype(BF16)


def iota(shape, axis):
    return lax.broadcasted_iota(I32, shape, axis)


def dense(line):
    cap = line.shape[1]
    rows = dense_rows(cap)
    pieces = [line[:, c : c + LANES] for c in range(0, cap, LANES)]
    if len(pieces) < rows:
        pieces.append(jnp.zeros((rows - len(pieces), LANES), line.dtype))
    return jnp.concatenate(pieces, axis=0)


def look_up(table, index):
    high, low = index >> 7, index & 127
    found = jnp.zeros(index.shape, table.dtype)
    for b in range(table.shape[0]):
        line = jnp.broadcast_to(table[b : b + 1], index.shape)
        value = jnp.take_along_axis(line, low, axis=1, mode="promise_in_bounds")
        found = jnp.where(high == b, value, found)
    return found


def values_kernel(
    n_sub, d_hbm, mask_hbm, base_hbm, rows_hbm, slots_hbm, *refs
):
    share_ref, *note_refs = refs[:n_sub]
    (
        d_ref, mask_ref, base_ref, slots_ref, rows_ref, perm_ref, hot_ref, cross_ref, sems, d_sems
    ) = refs[n_sub:]
    rows_dev, cols = d_ref.shape
    chunks = d_sems.shape[0]
    chunk = rows_dev // chunks
    cap = slots_ref.shape[1]
    lines = cap // LANES
    rows = dense_rows(cap)
    sub_index = lax.axis_index("sub")
    small = [
        pltpu.make_async_copy(src, dst, sems.at[i])
        for i, (src, dst) in enumerate(
            [(slots_hbm, slots_ref), (rows_hbm, rows_ref), (base_hbm, base_ref), (mask_hbm, mask_ref)]
        )
    ]
    large = [
        pltpu.make_async_copy(
            d_hbm.at[pl.ds(i * chunk, chunk)], d_ref.at[pl.ds(i * chunk, chunk)], d_sems.at[i]
        )
        for i in range(chunks)
    ]
    for copy in small + large:
        copy.start()

    small[0].wait()
    small[1].wait()
    first, second = dense(slots_ref[0:1, :]), dense(slots_ref[1:2, :])
    table = rows_ref[...]
    row = jnp.concatenate([look_up(table, first), look_up(table, second)], axis=0)
    row = row - lax.axis_index("mon") * rows_dev
    col = jnp.concatenate([second, first], axis=0) - sub_index * cols
    used = lax.rem(iota(row.shape, 0), rows) < lines
    here = used & (row >= 0) & (row < rows_dev) & (col >= 0) & (col < cols)

    flags = one_hot(here)
    height = flags.shape[0]
    above = jnp.dot(
        one_hot(iota((height, height), 1) < iota((height, height), 0)),
        flags,
        preferred_element_type=F32,
    ).astype(BF16)
    place = jnp.dot(
        jnp.concatenate([flags, above], axis=1),
        jnp.concatenate(
            [
                one_hot(iota((LANES, LANES), 0) <= iota((LANES, LANES), 1)),
                jnp.ones((LANES, LANES), BF16),
            ],
            axis=0,
        ),
        preferred_element_type=F32,
    ).astype(I32)
    place = jnp.where(here, place - 1, -1)
    digits = [(x >> shift) & 255 for x in (col, row) for shift in (0, 8)]
    order = [half * rows + b for half in range(2) for b in range(lines)]
    ends = jnp.concatenate(
        [jnp.concatenate([x[r : r + 1] for x in digits], axis=0) for r in order], axis=1
    )
    ends = ends.astype(F32).astype(BF16)

    def pick(start):
        for at, r in enumerate(order):
            perm_ref[:, at * LANES : (at + 1) * LANES] = one_hot(
                iota((ENDS, LANES), 0) + start == place[r : r + 1]
            )
        packed = lax.dot_general(
            ends, perm_ref[...], (((1,), (1,)), ((), ())), preferred_element_type=F32
        ).astype(I32)
        end_col = packed[0:1] + (packed[1:2] << 8)
        end_row = packed[2:3] + (packed[3:4] << 8)
        hot_ref[...] = one_hot(iota((cols, ENDS), 0) == end_col)
        keep = jnp.dot(
            mask_ref[...].astype(F32).astype(BF16), hot_ref[...], preferred_element_type=F32
        )
        keep = jnp.sum(
            jnp.where(iota(keep.shape, 0) == (end_row >> 7), keep, 0.0), axis=0, keepdims=True
        )
        total = jnp.zeros((SUBLANES, ENDS), F32)
        for i in range(chunks):
            values = jnp.dot(
                d_ref[i * chunk : (i + 1) * chunk, :], hot_ref[...], preferred_element_type=F32
            )
            picked = jnp.where(iota((chunk, ENDS), 0) + i * chunk == end_row, values, 0.0)
            total += jnp.sum(picked.reshape(chunk // SUBLANES, SUBLANES, ENDS), axis=0)
        value = jnp.sum(total, axis=0, keepdims=True) * keep
        return jnp.dot(
            jnp.broadcast_to(value, (SUBLANES, ENDS)).astype(BF16),
            perm_ref[...],
            preferred_element_type=F32,
        )

    for copy in small[2:] + large:
        copy.wait()
    cross_ref[...] = pick(0)
    flow = jnp.where(sub_index == 0, look_up(base_ref[...], row), 0.0)
    count = jnp.max(place) + 1

    @pl.when(count > ENDS)
    def _():
        def more(i, _):
            cross_ref[...] += pick(i * ENDS)
            return 0

        lax.fori_loop(1, pl.cdiv(count, ENDS), more, 0)

    for ref in (share_ref, *note_refs):
        for half in range(2):
            for b in range(rows):
                at = (half * lines + b) * LANES
                ref[half * rows + b : half * rows + b + 1, :] = (
                    cross_ref[0:1, at : at + LANES] if b < lines else jnp.zeros((1, LANES), F32)
                )
        ref[2 * rows : 4 * rows, :] = flow
    my_blocks = mask_ref.shape[0] // n_sub
    for s, ref in enumerate(note_refs, 1):
        block = pl.multiple_of(lax.rem(sub_index + s, n_sub) * my_blocks, my_blocks)
        for c in range(cols // LANES):
            at = 4 * rows + c * my_blocks
            ref[at : at + my_blocks, :] = mask_ref[
                pl.ds(block, my_blocks), c * LANES : (c + 1) * LANES
            ].astype(F32)


def pick_columns(count, slot, starts, cols, masked_ref, hot_ref, out_ref, prepare=lambda: None):
    parts, _, width = hot_ref.shape
    live_parts = jnp.minimum((count + width - 1) // width, parts)

    def pick(n_parts):
        prepare()
        for part in range(n_parts):
            lanes = slice(part * width, (part + 1) * width)
            for s, start in enumerate(starts):
                hot_ref[part, s * cols : (s + 1) * cols, :] = one_hot(
                    iota((cols, width), 0) == slot[:, lanes] - start
                )
            out_ref[:, lanes] = jnp.dot(
                masked_ref[...], hot_ref[part], preferred_element_type=F32
            ).astype(BF16)

    for n_parts in range(1, parts + 1):
        pl.when(live_parts == n_parts)(functools.partial(pick, n_parts))


def column_starts(n_sub, cols):
    return [lax.rem(lax.axis_index("sub") + n_sub - s, n_sub) * cols for s in range(n_sub)]


def first_kernel(n_sub, *refs):
    d_refs, refs = refs[:n_sub], refs[n_sub:]
    note_refs, refs = refs[: n_sub - 1], refs[n_sub - 1 :]
    mask_ref, slots_ref, count_ref, masked_ref, first_ref, hot_ref = refs
    my_rows, all_cols = masked_ref.shape
    cols = all_cols // n_sub
    my_blocks = my_rows // BLOCK
    share_rows = note_refs[0].shape[0] - (cols // LANES) * my_blocks if note_refs else 0
    sub_index = lax.axis_index("sub")
    my_start = pl.multiple_of(sub_index * my_rows, my_rows)
    my_block = pl.multiple_of(sub_index * my_blocks, my_blocks)
    def prepare():
        for s in range(n_sub):
            if s == 0:
                keep = mask_ref[pl.ds(my_block, my_blocks), :].astype(F32)
            else:
                keep = jnp.concatenate(
                    [
                        note_refs[s - 1][share_rows + c * my_blocks : share_rows + (c + 1) * my_blocks, :]
                        for c in range(cols // LANES)
                    ],
                    axis=1,
                )
            keep = keep.astype(BF16)
            for b in range(my_blocks):
                masked_ref[b * BLOCK : (b + 1) * BLOCK, s * cols : (s + 1) * cols] = (
                    d_refs[s][pl.ds(my_start + b * BLOCK, BLOCK), :] * keep[b : b + 1]
                )

    starts = column_starts(n_sub, cols)
    pick_columns(
        count_ref[0], slots_ref[0:1, :], starts, cols, masked_ref, hot_ref, first_ref, prepare
    )


def second_kernel(n_sub, masked_ref, slots_ref, count_ref, second_ref, hot_ref):
    cols = masked_ref.shape[1] // n_sub
    starts = column_starts(n_sub, cols)
    pick_columns(count_ref[0], slots_ref[1:2, :], starts, cols, masked_ref, hot_ref, second_ref)


def flows_kernel(n_shares, *refs):
    share_refs, refs = refs[:n_shares], refs[n_shares:]
    base_ref, first_ref, second_ref, count_ref, out_hbm, post_ref, out_sems = refs
    my_rows, cap = post_ref.shape
    my_blocks = my_rows // BLOCK
    rows = dense_rows(cap)
    total = share_refs[0][...]
    for ref in share_refs[1:]:
        total = total + ref[...]
    cross_first, cross_second, flow_first, flow_second = (
        total[i * rows : (i + 1) * rows] for i in range(4)
    )
    determinant = 1.0 - cross_first * cross_second
    shift_first = (flow_first + cross_first * flow_second) / determinant
    shift_second = (flow_second + cross_second * flow_first) / determinant
    lines = range(cap // LANES)
    weights = [
        [
            jnp.broadcast_to(shift[line : line + 1], (BLOCK, LANES)).astype(BF16)
            for line in lines
        ]
        for shift in (shift_first, shift_second)
    ]
    live = [iota((1, LANES), 1) + line * LANES < count_ref[0] for line in lines]
    my_block = pl.multiple_of(lax.axis_index("sub") * my_blocks, my_blocks)
    base = jnp.swapaxes(base_ref[pl.ds(my_block, my_blocks), :], 0, 1)
    out_copies = []
    for b in range(my_blocks):
        block = slice(b * BLOCK, (b + 1) * BLOCK)
        start = jnp.broadcast_to(base[:, b : b + 1], (BLOCK, LANES))
        for line in lines:
            lanes = slice(line * LANES, (line + 1) * LANES)
            change = (
                weights[0][line] * first_ref[block, lanes]
                + weights[1][line] * second_ref[block, lanes]
            )
            post_ref[block, lanes] = jnp.where(
                live[line], start + change.astype(F32), 0.0
            ).astype(BF16)
        out_copies.append(
            pltpu.make_async_copy(post_ref.at[block], out_hbm.at[block], out_sems.at[b])
        )
        out_copies[-1].start()
    for copy in out_copies:
        copy.wait()


def partners(n_mon):
    half = n_mon // 2
    if n_mon & (n_mon - 1):
        return [[(m + k) % n_mon for m in range(n_mon)] for k in range(1, n_mon)]
    across = [
        [m ^ (half + k) if m < half else m ^ (n_mon - 1 - k) for m in range(n_mon)]
        for k in range(half)
    ]
    return across + [[m ^ k for m in range(n_mon)] for k in range(half - 1, 0, -1)]


def from_other_mon(share, n_mon, n_sub):
    return [
        lax.ppermute(
            share,
            ("mon", "sub"),
            [
                (m * n_sub + s, to[m] * n_sub + n_sub - 1 - s)
                for m in range(n_mon)
                for s in range(n_sub)
            ],
        )
        for to in reversed(partners(n_mon))
    ]


def on_device(dfactors, block_mask, base_flow, branch_row, pair_slots, pair_counts):
    rows_dev, cols = dfactors.shape
    blocks = rows_dev // BLOCK
    candidates = branch_row.shape[0]
    cap = pair_slots.shape[0]
    rows = dense_rows(cap)
    n_sub = lax.axis_size("sub")
    my_rows = rows_dev // n_sub
    slots = pair_slots.T
    base = base_flow.reshape(blocks, BLOCK)
    table = branch_row.reshape(candidates // LANES, LANES)
    hbm = pl.BlockSpec(memory_space=pltpu.HBM)
    in_hbm = functools.partial(pltpu.with_memory_space_constraint, memory_space=pltpu.HBM)
    in_vmem = functools.partial(pltpu.with_memory_space_constraint, memory_space=pltpu.VMEM)
    vmem = pl.BlockSpec(memory_space=pltpu.VMEM)
    smem = pl.BlockSpec(memory_space=pltpu.SMEM)
    params = pltpu.CompilerParams(vmem_limit_bytes=VMEM_LIMIT)
    rings = [[(i, (i + s) % n_sub) for i in range(n_sub)] for s in range(n_sub)]

    factors = [dfactors] + [lax.ppermute(dfactors, "sub", ring) for ring in rings[1:]]

    chunks = rows_dev // chunk_of(rows_dev, 512)
    note_rows = 4 * rows + (cols // LANES) * (my_rows // BLOCK)
    outs = pl.pallas_call(
        functools.partial(values_kernel, n_sub),
        out_shape=[pltpu.VMEM((4 * rows, LANES), F32)]
        + [pltpu.VMEM((note_rows, LANES), F32)] * (n_sub - 1)
        + [
            pltpu.VMEM((rows_dev, cols), BF16),
            pltpu.VMEM((blocks, cols), I32),
            pltpu.VMEM((blocks, BLOCK), F32),
            pltpu.VMEM((2, cap), I32),
        ],
        in_specs=[hbm] * 5,
        out_specs=[vmem] * (n_sub + 4),
        scratch_shapes=[
            pltpu.VMEM((candidates // LANES, LANES), I32),
            pltpu.VMEM((ENDS, 2 * cap), BF16),
            pltpu.VMEM((cols, ENDS), BF16),
            pltpu.VMEM((SUBLANES, 2 * cap), F32),
            pltpu.SemaphoreType.DMA((4,)),
            pltpu.SemaphoreType.DMA((chunks,)),
        ],
        compiler_params=params,
        cost_estimate=pl.CostEstimate(
            flops=2 * rows_dev * cols * ENDS, bytes_accessed=rows_dev * cols * 2, transcendentals=0
        ),
        name="pair_values",
    )(*map(in_hbm, (dfactors, block_mask, base, table, slots)))
    share, notes = outs[0], outs[1:n_sub]
    factors[0], block_mask, base, slots = outs[n_sub:]

    notes = [lax.ppermute(note, "sub", ring) for note, ring in zip(notes, rings[1:])]
    share = functools.reduce(jnp.add, [share] + [note[: 4 * rows] for note in notes])
    shares = [share, *from_other_mon(share, lax.axis_size("mon"), n_sub)]

    width = chunk_of(cap, 256)
    hot = pltpu.VMEM((cap // width, n_sub * cols, width), BF16)
    columns = pltpu.VMEM((my_rows, cap), BF16)
    columns_cost = pl.CostEstimate(
        flops=2 * my_rows * cols * n_sub * cap,
        bytes_accessed=my_rows * (cols * n_sub + cap) * 2,
        transcendentals=0,
    )
    masked, first = pl.pallas_call(
        functools.partial(first_kernel, n_sub),
        out_shape=[pltpu.VMEM((my_rows, n_sub * cols), BF16), columns],
        in_specs=[vmem] * (2 * n_sub + 1) + [smem],
        out_specs=[vmem] * 2,
        scratch_shapes=[hot],
        compiler_params=params,
        cost_estimate=columns_cost,
        name="first_columns",
    )(*map(in_vmem, (*factors, *notes, block_mask, slots)), pair_counts)
    second = pl.pallas_call(
        functools.partial(second_kernel, n_sub),
        out_shape=columns,
        in_specs=[vmem] * 2 + [smem],
        out_specs=vmem,
        scratch_shapes=[hot],
        compiler_params=params,
        cost_estimate=columns_cost,
        name="second_columns",
    )(*map(in_vmem, (masked, slots)), pair_counts)
    return pl.pallas_call(
        functools.partial(flows_kernel, len(shares)),
        out_shape=jax.ShapeDtypeStruct((my_rows, cap), BF16),
        in_specs=[vmem] * (len(shares) + 3) + [smem],
        out_specs=hbm,
        scratch_shapes=[
            pltpu.VMEM((my_rows, cap), BF16),
            pltpu.SemaphoreType.DMA((my_rows // BLOCK,)),
        ],
        compiler_params=params,
        cost_estimate=pl.CostEstimate(
            flops=6 * my_rows * cap, bytes_accessed=my_rows * cap * 2, transcendentals=0
        ),
        name="post_flows",
    )(*map(in_vmem, (*shares, base, first, second)), pair_counts)


def solution(mesh):
    return jax.shard_map(
        on_device,
        mesh=mesh,
        in_specs=(
            P("mon", "sub"),
            P("mon", "sub"),
            P("mon"),
            P(),
            P(("grp", "pair"), None),
            P(("grp", "pair")),
        ),
        out_specs=P(("mon", "sub"), ("grp", "pair")),
        check_vma=False,
    )
```

```python
import functools

import jax
import jax.numpy as jnp
from jax import lax
from jax.experimental import pallas as pl
from jax.experimental.pallas import tpu as pltpu
from jax.sharding import PartitionSpec as P

BLOCK = 128
LANES = 128
SUBLANES = 8
ENDS = 256
VMEM_LIMIT = 16 * 1024 * 1024
F32 = jnp.float32
BF16 = jnp.bfloat16
I32 = jnp.int32


def chunk_of(total, want):
    size = min(total, want)
    while total % size:
        size -= BLOCK
    return size


def dense_rows(cap):
    return -(-cap // (LANES * SUBLANES)) * SUBLANES


def one_hot(hit):
    return jnp.where(hit, 1.0, 0.0).astype(BF16)


def iota(shape, axis):
    return lax.broadcasted_iota(I32, shape, axis)


def dense(line):
    cap = line.shape[1]
    rows = dense_rows(cap)
    pieces = [line[:, c : c + LANES] for c in range(0, cap, LANES)]
    if len(pieces) < rows:
        pieces.append(jnp.zeros((rows - len(pieces), LANES), line.dtype))
    return jnp.concatenate(pieces, axis=0)


def look_up(table, index):
    high, low = index >> 7, index & 127
    found = jnp.zeros(index.shape, table.dtype)
    for b in range(table.shape[0]):
        line = jnp.broadcast_to(table[b : b + 1], index.shape)
        value = jnp.take_along_axis(line, low, axis=1, mode="promise_in_bounds")
        found = jnp.where(high == b, value, found)
    return found


def values_kernel(
    n_sub, d_hbm, mask_hbm, base_hbm, rows_hbm, slots_hbm, *refs
):
    share_ref, *note_refs = refs[:n_sub]
    (
        d_ref, mask_ref, base_ref, slots_ref, rows_ref, perm_ref, hot_ref, cross_ref, sems, d_sems
    ) = refs[n_sub:]
    rows_dev, cols = d_ref.shape
    chunks = d_sems.shape[0]
    chunk = rows_dev // chunks
    cap = slots_ref.shape[1]
    lines = cap // LANES
    rows = dense_rows(cap)
    sub_index = lax.axis_index("sub")
    small = [
        pltpu.make_async_copy(src, dst, sems.at[i])
        for i, (src, dst) in enumerate(
            [(slots_hbm, slots_ref), (rows_hbm, rows_ref), (base_hbm, base_ref), (mask_hbm, mask_ref)]
        )
    ]
    large = [
        pltpu.make_async_copy(
            d_hbm.at[pl.ds(i * chunk, chunk)], d_ref.at[pl.ds(i * chunk, chunk)], d_sems.at[i]
        )
        for i in range(chunks)
    ]
    for copy in small + large:
        copy.start()

    small[0].wait()
    small[1].wait()
    first, second = dense(slots_ref[0:1, :]), dense(slots_ref[1:2, :])
    table = rows_ref[...]
    row = jnp.concatenate([look_up(table, first), look_up(table, second)], axis=0)
    row = row - lax.axis_index("mon") * rows_dev
    col = jnp.concatenate([second, first], axis=0) - sub_index * cols
    used = lax.rem(iota(row.shape, 0), rows) < lines
    here = used & (row >= 0) & (row < rows_dev) & (col >= 0) & (col < cols)

    flags = one_hot(here)
    height = flags.shape[0]
    above = jnp.dot(
        one_hot(iota((height, height), 1) < iota((height, height), 0)),
        flags,
        preferred_element_type=F32,
    ).astype(BF16)
    place = jnp.dot(
        jnp.concatenate([flags, above], axis=1),
        jnp.concatenate(
            [
                one_hot(iota((LANES, LANES), 0) <= iota((LANES, LANES), 1)),
                jnp.ones((LANES, LANES), BF16),
            ],
            axis=0,
        ),
        preferred_element_type=F32,
    ).astype(I32)
    place = jnp.where(here, place - 1, -1)
    digits = [(x >> shift) & 255 for x in (col, row) for shift in (0, 8)]
    order = [half * rows + b for half in range(2) for b in range(lines)]
    ends = jnp.concatenate(
        [jnp.concatenate([x[r : r + 1] for x in digits], axis=0) for r in order], axis=1
    )
    ends = ends.astype(F32).astype(BF16)

    def pick(start, copies=()):
        for at, r in enumerate(order):
            perm_ref[:, at * LANES : (at + 1) * LANES] = one_hot(
                iota((ENDS, LANES), 0) + start == place[r : r + 1]
            )
        packed = lax.dot_general(
            ends, perm_ref[...], (((1,), (1,)), ((), ())), preferred_element_type=F32
        ).astype(I32)
        end_col = packed[0:1] + (packed[1:2] << 8)
        end_row = packed[2:3] + (packed[3:4] << 8)
        hot_ref[...] = one_hot(iota((cols, ENDS), 0) == end_col)
        for copy in copies:
            copy.wait()
        keep = jnp.dot(
            mask_ref[...].astype(F32).astype(BF16), hot_ref[...], preferred_element_type=F32
        )
        keep = jnp.sum(
            jnp.where(iota(keep.shape, 0) == (end_row >> 7), keep, 0.0), axis=0, keepdims=True
        )
        total = jnp.zeros((SUBLANES, ENDS), F32)
        for i in range(chunks):
            values = jnp.dot(
                d_ref[i * chunk : (i + 1) * chunk, :], hot_ref[...], preferred_element_type=F32
            )
            picked = jnp.where(iota((chunk, ENDS), 0) + i * chunk == end_row, values, 0.0)
            total += jnp.sum(picked.reshape(chunk // SUBLANES, SUBLANES, ENDS), axis=0)
        value = jnp.sum(total, axis=0, keepdims=True) * keep
        return jnp.dot(
            jnp.broadcast_to(value, (SUBLANES, ENDS)).astype(BF16),
            perm_ref[...],
            preferred_element_type=F32,
        )

    cross_ref[...] = pick(0, small[2:] + large)
    flow = jnp.where(sub_index == 0, look_up(base_ref[...], row), 0.0)
    count = jnp.max(place) + 1

    @pl.when(count > ENDS)
    def _():
        def more(i, _):
            cross_ref[...] += pick(i * ENDS)
            return 0

        lax.fori_loop(1, pl.cdiv(count, ENDS), more, 0)

    for ref in (share_ref, *note_refs):
        for half in range(2):
            for b in range(rows):
                at = (half * lines + b) * LANES
                ref[half * rows + b : half * rows + b + 1, :] = (
                    cross_ref[0:1, at : at + LANES] if b < lines else jnp.zeros((1, LANES), F32)
                )
        ref[2 * rows : 4 * rows, :] = flow
    my_blocks = mask_ref.shape[0] // n_sub
    for s, ref in enumerate(note_refs, 1):
        block = pl.multiple_of(lax.rem(sub_index + s, n_sub) * my_blocks, my_blocks)
        for c in range(cols // LANES):
            at = 4 * rows + c * my_blocks
            ref[at : at + my_blocks, :] = mask_ref[
                pl.ds(block, my_blocks), c * LANES : (c + 1) * LANES
            ].astype(F32)


def pick_columns(parts, slot, starts, cols, masked_ref, hot_ref, out_ref):
    width = hot_ref.shape[2]
    for part in parts:
        lanes = slice(part * width, (part + 1) * width)
        for s, start in enumerate(starts):
            hot_ref[part, s * cols : (s + 1) * cols, :] = one_hot(
                iota((cols, width), 0) == slot[:, lanes] - start
            )
        out_ref[:, lanes] = jnp.dot(
            masked_ref[...], hot_ref[part], preferred_element_type=F32
        ).astype(BF16)


def live_parts(count, hot_ref):
    parts, _, width = hot_ref.shape
    return jnp.minimum((count + width - 1) // width, parts)


def is_early():
    return lax.axis_index("mon") < lax.axis_size("mon") // 4


def column_starts(n_sub, cols):
    return [lax.rem(lax.axis_index("sub") + n_sub - s, n_sub) * cols for s in range(n_sub)]


def mask_factors(n_sub, refs, masked_ref):
    d_refs, note_refs, mask_ref = refs[:n_sub], refs[n_sub:-1], refs[-1]
    my_rows, all_cols = masked_ref.shape
    cols = all_cols // n_sub
    my_blocks = my_rows // BLOCK
    sub_index = lax.axis_index("sub")
    my_start = pl.multiple_of(sub_index * my_rows, my_rows)
    my_block = pl.multiple_of(sub_index * my_blocks, my_blocks)
    for s in range(n_sub):
        if s == 0:
            keep = mask_ref[pl.ds(my_block, my_blocks), :].astype(F32)
        else:
            ref = note_refs[s - 1]
            ends = range(ref.shape[0] - (cols // LANES) * my_blocks, ref.shape[0], my_blocks)
            keep = jnp.concatenate([ref[at : at + my_blocks, :] for at in ends], axis=1)
        keep = keep.astype(BF16)
        for b in range(my_blocks):
            masked_ref[b * BLOCK : (b + 1) * BLOCK, s * cols : (s + 1) * cols] = (
                d_refs[s][pl.ds(my_start + b * BLOCK, BLOCK), :] * keep[b : b + 1]
            )


def early_kernel(n_sub, *refs):
    *factor_refs, slots_ref, share_ref, masked_ref, first_ref, shared_ref, hot_ref = refs
    shared_ref[...] = share_ref[...]
    cols = masked_ref.shape[1] // n_sub

    @pl.when(is_early())
    def _():
        mask_factors(n_sub, factor_refs, masked_ref)
        starts = column_starts(n_sub, cols)
        pick_columns([0], slots_ref[0:1, :], starts, cols, masked_ref, hot_ref, first_ref)


def first_kernel(n_sub, *refs):
    *factor_refs, slots_ref, count_ref, _, _, masked_ref, first_ref, hot_ref = refs
    cols = masked_ref.shape[1] // n_sub
    slot = slots_ref[0:1, :]
    starts = column_starts(n_sub, cols)
    live = live_parts(count_ref[0], hot_ref)
    for n_parts in range(1, hot_ref.shape[0] + 1):

        @pl.when((live == n_parts) & jnp.logical_not(is_early()))
        def _():
            mask_factors(n_sub, factor_refs, masked_ref)
            pick_columns(range(n_parts), slot, starts, cols, masked_ref, hot_ref, first_ref)

        @pl.when((live == n_parts) & is_early())
        def _():
            pick_columns(range(1, n_parts), slot, starts, cols, masked_ref, hot_ref, first_ref)


def second_kernel(n_sub, masked_ref, slots_ref, count_ref, second_ref, hot_ref):
    cols = masked_ref.shape[1] // n_sub
    slot = slots_ref[1:2, :]
    starts = column_starts(n_sub, cols)
    live = live_parts(count_ref[0], hot_ref)
    for n_parts in range(1, hot_ref.shape[0] + 1):

        @pl.when(live == n_parts)
        def _():
            pick_columns(range(n_parts), slot, starts, cols, masked_ref, hot_ref, second_ref)


def flows_kernel(n_shares, *refs):
    share_refs, refs = refs[:n_shares], refs[n_shares:]
    base_ref, first_ref, second_ref, count_ref, out_hbm, post_ref, out_sems = refs
    my_rows, cap = post_ref.shape
    my_blocks = my_rows // BLOCK
    rows = dense_rows(cap)
    total = share_refs[0][...]
    for ref in share_refs[1:]:
        total = total + ref[...]
    cross_first, cross_second, flow_first, flow_second = (
        total[i * rows : (i + 1) * rows] for i in range(4)
    )
    determinant = 1.0 - cross_first * cross_second
    shift_first = (flow_first + cross_first * flow_second) / determinant
    shift_second = (flow_second + cross_second * flow_first) / determinant
    lines = range(cap // LANES)
    weights = [
        [
            jnp.broadcast_to(shift[line : line + 1], (BLOCK, LANES)).astype(BF16)
            for line in lines
        ]
        for shift in (shift_first, shift_second)
    ]
    live = [iota((1, LANES), 1) + line * LANES < count_ref[0] for line in lines]
    my_block = pl.multiple_of(lax.axis_index("sub") * my_blocks, my_blocks)
    base = jnp.swapaxes(base_ref[pl.ds(my_block, my_blocks), :], 0, 1)
    out_copies = []
    for b in range(my_blocks):
        block = slice(b * BLOCK, (b + 1) * BLOCK)
        start = jnp.broadcast_to(base[:, b : b + 1], (BLOCK, LANES))
        for line in lines:
            lanes = slice(line * LANES, (line + 1) * LANES)
            change = (
                weights[0][line] * first_ref[block, lanes]
                + weights[1][line] * second_ref[block, lanes]
            )
            post_ref[block, lanes] = jnp.where(
                live[line], start + change.astype(F32), 0.0
            ).astype(BF16)
        out_copies.append(
            pltpu.make_async_copy(post_ref.at[block], out_hbm.at[block], out_sems.at[b])
        )
        out_copies[-1].start()
    for copy in out_copies:
        copy.wait()


def partners(n_mon):
    half = n_mon // 2
    if n_mon & (n_mon - 1):
        return [[(m + k) % n_mon for m in range(n_mon)] for k in range(1, n_mon)]
    across = [
        [m ^ (half + k) if m < half else m ^ (n_mon - 1 - k) for m in range(n_mon)]
        for k in range(half)
    ]
    return across + [[m ^ k for m in range(n_mon)] for k in range(half - 1, 0, -1)]


def from_other_mon(share, n_mon, n_sub):
    return [
        lax.ppermute(
            share,
            ("mon", "sub"),
            [
                (m * n_sub + s, to[m] * n_sub + n_sub - 1 - s)
                for m in range(n_mon)
                for s in range(n_sub)
            ],
        )
        for to in reversed(partners(n_mon))
    ]


def on_device(dfactors, block_mask, base_flow, branch_row, pair_slots, pair_counts):
    rows_dev, cols = dfactors.shape
    blocks = rows_dev // BLOCK
    candidates = branch_row.shape[0]
    cap = pair_slots.shape[0]
    rows = dense_rows(cap)
    n_sub = lax.axis_size("sub")
    my_rows = rows_dev // n_sub
    slots = pair_slots.T
    base = base_flow.reshape(blocks, BLOCK)
    table = branch_row.reshape(candidates // LANES, LANES)
    hbm = pl.BlockSpec(memory_space=pltpu.HBM)
    in_hbm = functools.partial(pltpu.with_memory_space_constraint, memory_space=pltpu.HBM)
    in_vmem = functools.partial(pltpu.with_memory_space_constraint, memory_space=pltpu.VMEM)
    vmem = pl.BlockSpec(memory_space=pltpu.VMEM)
    smem = pl.BlockSpec(memory_space=pltpu.SMEM)
    params = pltpu.CompilerParams(vmem_limit_bytes=VMEM_LIMIT)
    rings = [[(i, (i + s) % n_sub) for i in range(n_sub)] for s in range(n_sub)]

    factors = [dfactors] + [lax.ppermute(dfactors, "sub", ring) for ring in rings[1:]]

    chunks = rows_dev // chunk_of(rows_dev, 512)
    note_rows = 4 * rows + (cols // LANES) * (my_rows // BLOCK)
    outs = pl.pallas_call(
        functools.partial(values_kernel, n_sub),
        out_shape=[pltpu.VMEM((4 * rows, LANES), F32)]
        + [pltpu.VMEM((note_rows, LANES), F32)] * (n_sub - 1)
        + [
            pltpu.VMEM((rows_dev, cols), BF16),
            pltpu.VMEM((blocks, cols), I32),
            pltpu.VMEM((blocks, BLOCK), F32),
            pltpu.VMEM((2, cap), I32),
        ],
        in_specs=[hbm] * 5,
        out_specs=[vmem] * (n_sub + 4),
        scratch_shapes=[
            pltpu.VMEM((candidates // LANES, LANES), I32),
            pltpu.VMEM((ENDS, 2 * cap), BF16),
            pltpu.VMEM((cols, ENDS), BF16),
            pltpu.VMEM((SUBLANES, 2 * cap), F32),
            pltpu.SemaphoreType.DMA((4,)),
            pltpu.SemaphoreType.DMA((chunks,)),
        ],
        compiler_params=params,
        cost_estimate=pl.CostEstimate(
            flops=2 * rows_dev * cols * ENDS, bytes_accessed=rows_dev * cols * 2, transcendentals=0
        ),
        name="pair_values",
    )(*map(in_hbm, (dfactors, block_mask, base, table, slots)))
    share, notes = outs[0], outs[1:n_sub]
    factors[0], block_mask, base, slots = outs[n_sub:]

    notes = [lax.ppermute(note, "sub", ring) for note, ring in zip(notes, rings[1:])]
    share = functools.reduce(jnp.add, [share] + [note[: 4 * rows] for note in notes])
    width = chunk_of(cap, 256)
    hot = pltpu.VMEM((cap // width, n_sub * cols, width), BF16)
    columns = pltpu.VMEM((my_rows, cap), BF16)
    masked = pltpu.VMEM((my_rows, n_sub * cols), BF16)
    columns_cost = pl.CostEstimate(
        flops=2 * my_rows * cols * n_sub * cap,
        bytes_accessed=my_rows * (cols * n_sub + cap) * 2,
        transcendentals=0,
    )
    factors = [*factors, *notes, block_mask]
    masked, first, share = pl.pallas_call(
        functools.partial(early_kernel, n_sub),
        out_shape=[masked, columns, pltpu.VMEM(share.shape, F32)],
        in_specs=[vmem] * (len(factors) + 2),
        out_specs=[vmem] * 3,
        scratch_shapes=[hot],
        compiler_params=params,
        name="early_columns",
    )(*map(in_vmem, (*factors, slots, share)))
    shares = [share, *from_other_mon(share, lax.axis_size("mon"), n_sub)]

    masked, first = pl.pallas_call(
        functools.partial(first_kernel, n_sub),
        out_shape=[pltpu.VMEM(masked.shape, BF16), columns],
        in_specs=[vmem] * (len(factors) + 1) + [smem] + [vmem] * 2,
        out_specs=[vmem] * 2,
        input_output_aliases={len(factors) + 2: 0, len(factors) + 3: 1},
        scratch_shapes=[hot],
        compiler_params=params,
        cost_estimate=columns_cost,
        name="first_columns",
    )(*map(in_vmem, (*factors, slots)), pair_counts, *map(in_vmem, (masked, first)))
    second = pl.pallas_call(
        functools.partial(second_kernel, n_sub),
        out_shape=columns,
        in_specs=[vmem] * 2 + [smem],
        out_specs=vmem,
        scratch_shapes=[hot],
        compiler_params=params,
        cost_estimate=columns_cost,
        name="second_columns",
    )(*map(in_vmem, (masked, slots)), pair_counts)
    return pl.pallas_call(
        functools.partial(flows_kernel, len(shares)),
        out_shape=jax.ShapeDtypeStruct((my_rows, cap), BF16),
        in_specs=[vmem] * (len(shares) + 3) + [smem],
        out_specs=hbm,
        scratch_shapes=[
            pltpu.VMEM((my_rows, cap), BF16),
            pltpu.SemaphoreType.DMA((my_rows // BLOCK,)),
        ],
        compiler_params=params,
        cost_estimate=pl.CostEstimate(
            flops=6 * my_rows * cap, bytes_accessed=my_rows * cap * 2, transcendentals=0
        ),
        name="post_flows",
    )(*map(in_vmem, (*shares, base, first, second)), pair_counts)


def solution(mesh):
    return jax.shard_map(
        on_device,
        mesh=mesh,
        in_specs=(
            P("mon", "sub"),
            P("mon", "sub"),
            P("mon"),
            P(),
            P(("grp", "pair"), None),
            P(("grp", "pair")),
        ),
        out_specs=P(("mon", "sub"), ("grp", "pair")),
        check_vma=False,
    )
```

```python
import functools

import jax
import jax.numpy as jnp
from jax import lax
from jax.experimental import pallas as pl
from jax.experimental.pallas import tpu as pltpu
from jax.sharding import PartitionSpec as P

BLOCK = 128
LANES = 128
SUBLANES = 8
ENDS = 256
VMEM_LIMIT = 16 * 1024 * 1024
F32 = jnp.float32
BF16 = jnp.bfloat16
I32 = jnp.int32


def chunk_of(total, want):
    size = min(total, want)
    while total % size:
        size -= BLOCK
    return size


def dense_rows(cap):
    return -(-cap // (LANES * SUBLANES)) * SUBLANES


def one_hot(hit):
    return jnp.where(hit, 1.0, 0.0).astype(BF16)


def iota(shape, axis):
    return lax.broadcasted_iota(I32, shape, axis)


def dense(line):
    cap = line.shape[1]
    rows = dense_rows(cap)
    pieces = [line[:, c : c + LANES] for c in range(0, cap, LANES)]
    if len(pieces) < rows:
        pieces.append(jnp.zeros((rows - len(pieces), LANES), line.dtype))
    return jnp.concatenate(pieces, axis=0)


def look_up(table, index):
    high, low = index >> 7, index & 127
    found = jnp.zeros(index.shape, table.dtype)
    for b in range(table.shape[0]):
        line = jnp.broadcast_to(table[b : b + 1], index.shape)
        value = jnp.take_along_axis(line, low, axis=1, mode="promise_in_bounds")
        found = jnp.where(high == b, value, found)
    return found


def values_kernel(
    n_sub, d_hbm, mask_hbm, base_hbm, rows_hbm, slots_hbm, *refs
):
    share_ref, *note_refs = refs[:n_sub]
    (
        d_ref, mask_ref, base_ref, slots_ref, rows_ref, perm_ref, hot_ref, cross_ref, sems, d_sems
    ) = refs[n_sub:]
    rows_dev, cols = d_ref.shape
    chunks = d_sems.shape[0]
    chunk = rows_dev // chunks
    cap = slots_ref.shape[1]
    lines = cap // LANES
    rows = dense_rows(cap)
    sub_index = lax.axis_index("sub")
    small = [
        pltpu.make_async_copy(src, dst, sems.at[i])
        for i, (src, dst) in enumerate(
            [(slots_hbm, slots_ref), (rows_hbm, rows_ref), (base_hbm, base_ref), (mask_hbm, mask_ref)]
        )
    ]
    large = [
        pltpu.make_async_copy(
            d_hbm.at[pl.ds(i * chunk, chunk)], d_ref.at[pl.ds(i * chunk, chunk)], d_sems.at[i]
        )
        for i in range(chunks)
    ]
    for copy in small + large:
        copy.start()

    small[0].wait()
    small[1].wait()
    first, second = dense(slots_ref[0:1, :]), dense(slots_ref[1:2, :])
    table = rows_ref[...]
    row = jnp.concatenate([look_up(table, first), look_up(table, second)], axis=0)
    row = row - lax.axis_index("mon") * rows_dev
    col = jnp.concatenate([second, first], axis=0) - sub_index * cols
    used = lax.rem(iota(row.shape, 0), rows) < lines
    here = used & (row >= 0) & (row < rows_dev) & (col >= 0) & (col < cols)

    flags = one_hot(here)
    height = flags.shape[0]
    above = jnp.dot(
        one_hot(iota((height, height), 1) < iota((height, height), 0)),
        flags,
        preferred_element_type=F32,
    ).astype(BF16)
    place = jnp.dot(
        jnp.concatenate([flags, above], axis=1),
        jnp.concatenate(
            [
                one_hot(iota((LANES, LANES), 0) <= iota((LANES, LANES), 1)),
                jnp.ones((LANES, LANES), BF16),
            ],
            axis=0,
        ),
        preferred_element_type=F32,
    ).astype(I32)
    place = jnp.where(here, place - 1, -1)
    digits = [(x >> shift) & 255 for x in (col, row) for shift in (0, 8)]
    order = [half * rows + b for half in range(2) for b in range(lines)]
    ends = jnp.concatenate(
        [jnp.concatenate([x[r : r + 1] for x in digits], axis=0) for r in order], axis=1
    )
    ends = ends.astype(F32).astype(BF16)

    def pick(start, copies=()):
        for at, r in enumerate(order):
            perm_ref[:, at * LANES : (at + 1) * LANES] = one_hot(
                iota((ENDS, LANES), 0) + start == place[r : r + 1]
            )
        packed = lax.dot_general(
            ends, perm_ref[...], (((1,), (1,)), ((), ())), preferred_element_type=F32
        ).astype(I32)
        end_col = packed[0:1] + (packed[1:2] << 8)
        end_row = packed[2:3] + (packed[3:4] << 8)
        hot_ref[...] = one_hot(iota((cols, ENDS), 0) == end_col)
        for copy in copies[: 2 + (chunks + 1) // 2]:
            copy.wait()
        keep = jnp.dot(
            mask_ref[...].astype(F32).astype(BF16), hot_ref[...], preferred_element_type=F32
        )
        keep = jnp.sum(
            jnp.where(iota(keep.shape, 0) == (end_row >> 7), keep, 0.0), axis=0, keepdims=True
        )
        total = jnp.zeros((SUBLANES, ENDS), F32)
        for i in range(chunks):
            if i == (chunks + 1) // 2:
                for copy in copies[2 + i :]:
                    copy.wait()
            values = jnp.dot(
                d_ref[i * chunk : (i + 1) * chunk, :], hot_ref[...], preferred_element_type=F32
            )
            picked = jnp.where(iota((chunk, ENDS), 0) + i * chunk == end_row, values, 0.0)
            total += jnp.sum(picked.reshape(chunk // SUBLANES, SUBLANES, ENDS), axis=0)
        value = jnp.sum(total, axis=0, keepdims=True) * keep
        return jnp.dot(
            jnp.broadcast_to(value, (SUBLANES, ENDS)).astype(BF16),
            perm_ref[...],
            preferred_element_type=F32,
        )

    cross_ref[...] = pick(0, small[2:] + large)
    flow = jnp.where(sub_index == 0, look_up(base_ref[...], row), 0.0)
    count = jnp.max(place) + 1

    @pl.when(count > ENDS)
    def _():
        def more(i, _):
            cross_ref[...] += pick(i * ENDS)
            return 0

        lax.fori_loop(1, pl.cdiv(count, ENDS), more, 0)

    for ref in (share_ref, *note_refs):
        for half in range(2):
            for b in range(rows):
                at = (half * lines + b) * LANES
                ref[half * rows + b : half * rows + b + 1, :] = (
                    cross_ref[0:1, at : at + LANES] if b < lines else jnp.zeros((1, LANES), F32)
                )
        ref[2 * rows : 4 * rows, :] = flow
    my_blocks = mask_ref.shape[0] // n_sub
    for s, ref in enumerate(note_refs, 1):
        block = pl.multiple_of(lax.rem(sub_index + s, n_sub) * my_blocks, my_blocks)
        for c in range(cols // LANES):
            at = 4 * rows + c * my_blocks
            ref[at : at + my_blocks, :] = mask_ref[
                pl.ds(block, my_blocks), c * LANES : (c + 1) * LANES
            ].astype(F32)


def pick_columns(parts, slot, starts, cols, masked_ref, hot_ref, out_ref):
    width = hot_ref.shape[2]
    for part in parts:
        lanes = slice(part * width, (part + 1) * width)
        for s, start in enumerate(starts):
            hot_ref[part, s * cols : (s + 1) * cols, :] = one_hot(
                iota((cols, width), 0) == slot[:, lanes] - start
            )
        out_ref[:, lanes] = jnp.dot(
            masked_ref[...], hot_ref[part], preferred_element_type=F32
        ).astype(BF16)


def live_parts(count, hot_ref):
    parts, _, width = hot_ref.shape
    return jnp.minimum((count + width - 1) // width, parts)


def quarter():
    return lax.axis_index("mon") // jnp.maximum(lax.axis_size("mon") // 4, 1)


def column_starts(n_sub, cols):
    return [lax.rem(lax.axis_index("sub") + n_sub - s, n_sub) * cols for s in range(n_sub)]


def mask_factors(n_sub, refs, masked_ref):
    d_refs, note_refs, mask_ref = refs[:n_sub], refs[n_sub:-1], refs[-1]
    my_rows, all_cols = masked_ref.shape
    cols = all_cols // n_sub
    my_blocks = my_rows // BLOCK
    sub_index = lax.axis_index("sub")
    my_start = pl.multiple_of(sub_index * my_rows, my_rows)
    my_block = pl.multiple_of(sub_index * my_blocks, my_blocks)
    for s in range(n_sub):
        if s == 0:
            keep = mask_ref[pl.ds(my_block, my_blocks), :].astype(F32)
        else:
            ref = note_refs[s - 1]
            ends = range(ref.shape[0] - (cols // LANES) * my_blocks, ref.shape[0], my_blocks)
            keep = jnp.concatenate([ref[at : at + my_blocks, :] for at in ends], axis=1)
        keep = keep.astype(BF16)
        for b in range(my_blocks):
            masked_ref[b * BLOCK : (b + 1) * BLOCK, s * cols : (s + 1) * cols] = (
                d_refs[s][pl.ds(my_start + b * BLOCK, BLOCK), :] * keep[b : b + 1]
            )


def early_kernel(n_sub, *refs):
    (
        *factor_refs, slots_ref, share_ref, count_ref,
        masked_ref, first_ref, shared_ref, hot_ref,
    ) = refs
    shared_ref[...] = share_ref[...]
    cols = masked_ref.shape[1] // n_sub
    starts = column_starts(n_sub, cols)
    live = jnp.where(quarter() == 0, 1, live_parts(count_ref[0], hot_ref))
    for n_parts in range(1, hot_ref.shape[0] + 1):

        @pl.when((live == n_parts) & (quarter() < 2))
        def _():
            mask_factors(n_sub, factor_refs, masked_ref)
            pick_columns(
                range(n_parts), slots_ref[0:1, :], starts, cols, masked_ref, hot_ref, first_ref
            )


def first_kernel(n_sub, *refs):
    *factor_refs, slots_ref, count_ref, _, _, masked_ref, first_ref, hot_ref = refs
    cols = masked_ref.shape[1] // n_sub
    slot = slots_ref[0:1, :]
    starts = column_starts(n_sub, cols)
    live = live_parts(count_ref[0], hot_ref)
    for n_parts in range(1, hot_ref.shape[0] + 1):

        @pl.when((live == n_parts) & (quarter() >= 2))
        def _():
            mask_factors(n_sub, factor_refs, masked_ref)
            pick_columns(range(n_parts), slot, starts, cols, masked_ref, hot_ref, first_ref)

        @pl.when((live == n_parts) & (quarter() == 0))
        def _():
            pick_columns(range(1, n_parts), slot, starts, cols, masked_ref, hot_ref, first_ref)


def second_kernel(n_sub, masked_ref, slots_ref, count_ref, second_ref, hot_ref):
    cols = masked_ref.shape[1] // n_sub
    slot = slots_ref[1:2, :]
    starts = column_starts(n_sub, cols)
    live = live_parts(count_ref[0], hot_ref)
    for n_parts in range(1, hot_ref.shape[0] + 1):

        @pl.when(live == n_parts)
        def _():
            pick_columns(range(n_parts), slot, starts, cols, masked_ref, hot_ref, second_ref)


def flows_kernel(n_shares, *refs):
    share_refs, refs = refs[:n_shares], refs[n_shares:]
    base_ref, first_ref, second_ref, count_ref, out_hbm, post_ref, out_sems = refs
    my_rows, cap = post_ref.shape
    my_blocks = my_rows // BLOCK
    rows = dense_rows(cap)
    total = share_refs[0][...]
    for ref in share_refs[1:]:
        total = total + ref[...]
    cross_first, cross_second, flow_first, flow_second = (
        total[i * rows : (i + 1) * rows] for i in range(4)
    )
    determinant = 1.0 - cross_first * cross_second
    shift_first = (flow_first + cross_first * flow_second) / determinant
    shift_second = (flow_second + cross_second * flow_first) / determinant
    lines = range(cap // LANES)
    weights = [
        [
            jnp.broadcast_to(shift[line : line + 1], (BLOCK, LANES)).astype(BF16)
            for line in lines
        ]
        for shift in (shift_first, shift_second)
    ]
    live = [iota((1, LANES), 1) + line * LANES < count_ref[0] for line in lines]
    my_block = pl.multiple_of(lax.axis_index("sub") * my_blocks, my_blocks)
    base = jnp.swapaxes(base_ref[pl.ds(my_block, my_blocks), :], 0, 1)
    out_copies = []
    for b in range(my_blocks):
        block = slice(b * BLOCK, (b + 1) * BLOCK)
        start = jnp.broadcast_to(base[:, b : b + 1], (BLOCK, LANES))
        for line in lines:
            lanes = slice(line * LANES, (line + 1) * LANES)
            change = (
                weights[0][line] * first_ref[block, lanes]
                + weights[1][line] * second_ref[block, lanes]
            )
            post_ref[block, lanes] = jnp.where(
                live[line], start + change.astype(F32), 0.0
            ).astype(BF16)
        out_copies.append(
            pltpu.make_async_copy(post_ref.at[block], out_hbm.at[block], out_sems.at[b])
        )
        out_copies[-1].start()
    for copy in out_copies:
        copy.wait()


def partners(n_mon):
    half = n_mon // 2
    if n_mon & (n_mon - 1):
        return [[(m + k) % n_mon for m in range(n_mon)] for k in range(1, n_mon)]
    across = [
        [m ^ (half + k) if m < half else m ^ (n_mon - 1 - k) for m in range(n_mon)]
        for k in range(half)
    ]
    return across + [[m ^ k for m in range(n_mon)] for k in range(half - 1, 0, -1)]


def from_other_mon(share, n_mon, n_sub):
    return [
        lax.ppermute(
            share,
            ("mon", "sub"),
            [
                (m * n_sub + s, to[m] * n_sub + n_sub - 1 - s)
                for m in range(n_mon)
                for s in range(n_sub)
            ],
        )
        for to in reversed(partners(n_mon))
    ]


def on_device(dfactors, block_mask, base_flow, branch_row, pair_slots, pair_counts):
    rows_dev, cols = dfactors.shape
    blocks = rows_dev // BLOCK
    candidates = branch_row.shape[0]
    cap = pair_slots.shape[0]
    rows = dense_rows(cap)
    n_sub = lax.axis_size("sub")
    my_rows = rows_dev // n_sub
    slots = pair_slots.T
    base = base_flow.reshape(blocks, BLOCK)
    table = branch_row.reshape(candidates // LANES, LANES)
    hbm = pl.BlockSpec(memory_space=pltpu.HBM)
    in_hbm = functools.partial(pltpu.with_memory_space_constraint, memory_space=pltpu.HBM)
    in_vmem = functools.partial(pltpu.with_memory_space_constraint, memory_space=pltpu.VMEM)
    vmem = pl.BlockSpec(memory_space=pltpu.VMEM)
    smem = pl.BlockSpec(memory_space=pltpu.SMEM)
    params = pltpu.CompilerParams(vmem_limit_bytes=VMEM_LIMIT)
    rings = [[(i, (i + s) % n_sub) for i in range(n_sub)] for s in range(n_sub)]

    factors = [dfactors] + [lax.ppermute(dfactors, "sub", ring) for ring in rings[1:]]

    chunks = rows_dev // chunk_of(rows_dev, 512)
    note_rows = 4 * rows + (cols // LANES) * (my_rows // BLOCK)
    outs = pl.pallas_call(
        functools.partial(values_kernel, n_sub),
        out_shape=[pltpu.VMEM((4 * rows, LANES), F32)]
        + [pltpu.VMEM((note_rows, LANES), F32)] * (n_sub - 1)
        + [
            pltpu.VMEM((rows_dev, cols), BF16),
            pltpu.VMEM((blocks, cols), I32),
            pltpu.VMEM((blocks, BLOCK), F32),
            pltpu.VMEM((2, cap), I32),
        ],
        in_specs=[hbm] * 5,
        out_specs=[vmem] * (n_sub + 4),
        scratch_shapes=[
            pltpu.VMEM((candidates // LANES, LANES), I32),
            pltpu.VMEM((ENDS, 2 * cap), BF16),
            pltpu.VMEM((cols, ENDS), BF16),
            pltpu.VMEM((SUBLANES, 2 * cap), F32),
            pltpu.SemaphoreType.DMA((4,)),
            pltpu.SemaphoreType.DMA((chunks,)),
        ],
        compiler_params=params,
        cost_estimate=pl.CostEstimate(
            flops=2 * rows_dev * cols * ENDS, bytes_accessed=rows_dev * cols * 2, transcendentals=0
        ),
        name="pair_values",
    )(*map(in_hbm, (dfactors, block_mask, base, table, slots)))
    share, notes = outs[0], outs[1:n_sub]
    factors[0], block_mask, base, slots = outs[n_sub:]

    notes = [lax.ppermute(note, "sub", ring) for note, ring in zip(notes, rings[1:])]
    share = functools.reduce(jnp.add, [share] + [note[: 4 * rows] for note in notes])
    width = chunk_of(cap, 256)
    hot = pltpu.VMEM((cap // width, n_sub * cols, width), BF16)
    columns = pltpu.VMEM((my_rows, cap), BF16)
    masked = pltpu.VMEM((my_rows, n_sub * cols), BF16)
    columns_cost = pl.CostEstimate(
        flops=2 * my_rows * cols * n_sub * cap,
        bytes_accessed=my_rows * (cols * n_sub + cap) * 2,
        transcendentals=0,
    )
    factors = [*factors, *notes, block_mask]
    masked, first, share = pl.pallas_call(
        functools.partial(early_kernel, n_sub),
        out_shape=[masked, columns, pltpu.VMEM(share.shape, F32)],
        in_specs=[vmem] * (len(factors) + 2) + [smem],
        out_specs=[vmem] * 3,
        scratch_shapes=[hot],
        compiler_params=params,
        name="early_columns",
    )(*map(in_vmem, (*factors, slots, share)), pair_counts)
    shares = [share, *from_other_mon(share, lax.axis_size("mon"), n_sub)]

    masked, first = pl.pallas_call(
        functools.partial(first_kernel, n_sub),
        out_shape=[pltpu.VMEM(masked.shape, BF16), columns],
        in_specs=[vmem] * (len(factors) + 1) + [smem] + [vmem] * 2,
        out_specs=[vmem] * 2,
        input_output_aliases={len(factors) + 2: 0, len(factors) + 3: 1},
        scratch_shapes=[hot],
        compiler_params=params,
        cost_estimate=columns_cost,
        name="first_columns",
    )(*map(in_vmem, (*factors, slots)), pair_counts, *map(in_vmem, (masked, first)))
    second = pl.pallas_call(
        functools.partial(second_kernel, n_sub),
        out_shape=columns,
        in_specs=[vmem] * 2 + [smem],
        out_specs=vmem,
        scratch_shapes=[hot],
        compiler_params=params,
        cost_estimate=columns_cost,
        name="second_columns",
    )(*map(in_vmem, (masked, slots)), pair_counts)
    return pl.pallas_call(
        functools.partial(flows_kernel, len(shares)),
        out_shape=jax.ShapeDtypeStruct((my_rows, cap), BF16),
        in_specs=[vmem] * (len(shares) + 3) + [smem],
        out_specs=hbm,
        scratch_shapes=[
            pltpu.VMEM((my_rows, cap), BF16),
            pltpu.SemaphoreType.DMA((my_rows // BLOCK,)),
        ],
        compiler_params=params,
        cost_estimate=pl.CostEstimate(
            flops=6 * my_rows * cap, bytes_accessed=my_rows * cap * 2, transcendentals=0
        ),
        name="post_flows",
    )(*map(in_vmem, (*shares, base, first, second)), pair_counts)


def solution(mesh):
    return jax.shard_map(
        on_device,
        mesh=mesh,
        in_specs=(
            P("mon", "sub"),
            P("mon", "sub"),
            P("mon"),
            P(),
            P(("grp", "pair"), None),
            P(("grp", "pair")),
        ),
        out_specs=P(("mon", "sub"), ("grp", "pair")),
        check_vma=False,
    )
```

```python
import functools

import jax
import jax.numpy as jnp
from jax import lax
from jax.experimental import pallas as pl
from jax.experimental.pallas import tpu as pltpu
from jax.sharding import PartitionSpec as P

BLOCK = 128
LANES = 128
SUBLANES = 8
ENDS = 256
VMEM_LIMIT = 16 * 1024 * 1024
F32 = jnp.float32
BF16 = jnp.bfloat16
I32 = jnp.int32


def chunk_of(total, want):
    size = min(total, want)
    while total % size:
        size -= BLOCK
    return size


def dense_rows(cap):
    return -(-cap // (LANES * SUBLANES)) * SUBLANES


def one_hot(hit):
    return jnp.where(hit, 1.0, 0.0).astype(BF16)


def iota(shape, axis):
    return lax.broadcasted_iota(I32, shape, axis)


def dense(line):
    cap = line.shape[1]
    rows = dense_rows(cap)
    pieces = [line[:, c : c + LANES] for c in range(0, cap, LANES)]
    if len(pieces) < rows:
        pieces.append(jnp.zeros((rows - len(pieces), LANES), line.dtype))
    return jnp.concatenate(pieces, axis=0)


def look_up(table, index):
    high, low = index >> 7, index & 127
    found = jnp.zeros(index.shape, table.dtype)
    for b in range(table.shape[0]):
        line = jnp.broadcast_to(table[b : b + 1], index.shape)
        value = jnp.take_along_axis(line, low, axis=1, mode="promise_in_bounds")
        found = jnp.where(high == b, value, found)
    return found


def values_kernel(
    n_sub, d_hbm, mask_hbm, base_hbm, rows_hbm, slots_hbm, *refs
):
    share_ref, *note_refs = refs[:n_sub]
    (
        d_ref, mask_ref, base_ref, slots_ref, rows_ref, perm_ref, hot_ref, cross_ref, sems, d_sems
    ) = refs[n_sub:]
    rows_dev, cols = d_ref.shape
    chunks = d_sems.shape[0]
    chunk = rows_dev // chunks
    cap = slots_ref.shape[1]
    lines = cap // LANES
    rows = dense_rows(cap)
    sub_index = lax.axis_index("sub")
    small = [
        pltpu.make_async_copy(src, dst, sems.at[i])
        for i, (src, dst) in enumerate(
            [(slots_hbm, slots_ref), (rows_hbm, rows_ref), (base_hbm, base_ref), (mask_hbm, mask_ref)]
        )
    ]
    large = [
        pltpu.make_async_copy(
            d_hbm.at[pl.ds(i * chunk, chunk)], d_ref.at[pl.ds(i * chunk, chunk)], d_sems.at[i]
        )
        for i in range(chunks)
    ]
    for copy in small + large:
        copy.start()

    small[0].wait()
    small[1].wait()
    first, second = dense(slots_ref[0:1, :]), dense(slots_ref[1:2, :])
    table = rows_ref[...]
    row = jnp.concatenate([look_up(table, first), look_up(table, second)], axis=0)
    row = row - lax.axis_index("mon") * rows_dev
    col = jnp.concatenate([second, first], axis=0) - sub_index * cols
    used = lax.rem(iota(row.shape, 0), rows) < lines
    here = used & (row >= 0) & (row < rows_dev) & (col >= 0) & (col < cols)

    flags = one_hot(here)
    height = flags.shape[0]
    above = jnp.dot(
        one_hot(iota((height, height), 1) < iota((height, height), 0)),
        flags,
        preferred_element_type=F32,
    ).astype(BF16)
    place = jnp.dot(
        jnp.concatenate([flags, above], axis=1),
        jnp.concatenate(
            [
                one_hot(iota((LANES, LANES), 0) <= iota((LANES, LANES), 1)),
                jnp.ones((LANES, LANES), BF16),
            ],
            axis=0,
        ),
        preferred_element_type=F32,
    ).astype(I32)
    place = jnp.where(here, place - 1, -1)
    digits = [(x >> shift) & 255 for x in (col, row) for shift in (0, 8)]
    order = [half * rows + b for half in range(2) for b in range(lines)]
    ends = jnp.concatenate(
        [jnp.concatenate([x[r : r + 1] for x in digits], axis=0) for r in order], axis=1
    )
    ends = ends.astype(F32).astype(BF16)

    def pick(start, copies=()):
        for at, r in enumerate(order):
            perm_ref[:, at * LANES : (at + 1) * LANES] = one_hot(
                iota((ENDS, LANES), 0) + start == place[r : r + 1]
            )
        packed = lax.dot_general(
            ends, perm_ref[...], (((1,), (1,)), ((), ())), preferred_element_type=F32
        ).astype(I32)
        end_col = packed[0:1] + (packed[1:2] << 8)
        end_row = packed[2:3] + (packed[3:4] << 8)
        hot_ref[...] = one_hot(iota((cols, ENDS), 0) == end_col)
        for copy in copies:
            copy.wait()
        keep = jnp.dot(
            mask_ref[...].astype(F32).astype(BF16), hot_ref[...], preferred_element_type=F32
        )
        keep = jnp.sum(
            jnp.where(iota(keep.shape, 0) == (end_row >> 7), keep, 0.0), axis=0, keepdims=True
        )
        total = jnp.zeros((SUBLANES, ENDS), F32)
        for i in range(chunks):
            values = jnp.dot(
                d_ref[i * chunk : (i + 1) * chunk, :], hot_ref[...], preferred_element_type=F32
            )
            picked = jnp.where(iota((chunk, ENDS), 0) + i * chunk == end_row, values, 0.0)
            total += jnp.sum(picked.reshape(chunk // SUBLANES, SUBLANES, ENDS), axis=0)
        value = jnp.sum(total, axis=0, keepdims=True) * keep
        return jnp.dot(
            jnp.broadcast_to(value, (SUBLANES, ENDS)).astype(BF16),
            perm_ref[...],
            preferred_element_type=F32,
        )

    cross_ref[...] = pick(0, small[2:] + large)
    flow = jnp.where(sub_index == 0, look_up(base_ref[...], row), 0.0)
    count = jnp.max(place) + 1

    @pl.when(count > ENDS)
    def _():
        def more(i, _):
            cross_ref[...] += pick(i * ENDS)
            return 0

        lax.fori_loop(1, pl.cdiv(count, ENDS), more, 0)

    for ref in (share_ref, *note_refs):
        for half in range(2):
            for b in range(rows):
                at = (half * lines + b) * LANES
                ref[half * rows + b : half * rows + b + 1, :] = (
                    cross_ref[0:1, at : at + LANES] if b < lines else jnp.zeros((1, LANES), F32)
                )
        ref[2 * rows : 4 * rows, :] = flow
    my_blocks = mask_ref.shape[0] // n_sub
    for s, ref in enumerate(note_refs, 1):
        block = pl.multiple_of(lax.rem(sub_index + s, n_sub) * my_blocks, my_blocks)
        for c in range(cols // LANES):
            at = 4 * rows + c * my_blocks
            ref[at : at + my_blocks, :] = mask_ref[
                pl.ds(block, my_blocks), c * LANES : (c + 1) * LANES
            ].astype(F32)


def pick_columns(parts, slot, starts, cols, masked_ref, hot_ref, out_ref):
    width = hot_ref.shape[2]
    for part in parts:
        lanes = slice(part * width, (part + 1) * width)
        for s, start in enumerate(starts):
            hot_ref[part, s * cols : (s + 1) * cols, :] = one_hot(
                iota((cols, width), 0) == slot[:, lanes] - start
            )
        out_ref[:, lanes] = jnp.dot(
            masked_ref[...], hot_ref[part], preferred_element_type=F32
        ).astype(BF16)


def live_parts(count, hot_ref):
    parts, _, width = hot_ref.shape
    return jnp.minimum((count + width - 1) // width, parts)


def is_early():
    return lax.axis_index("mon") < lax.axis_size("mon") // 2


def column_starts(n_sub, cols):
    return [lax.rem(lax.axis_index("sub") + n_sub - s, n_sub) * cols for s in range(n_sub)]


def mask_factors(n_sub, refs, masked_ref):
    d_refs, note_refs, mask_ref = refs[:n_sub], refs[n_sub:-1], refs[-1]
    my_rows, all_cols = masked_ref.shape
    cols = all_cols // n_sub
    my_blocks = my_rows // BLOCK
    sub_index = lax.axis_index("sub")
    my_start = pl.multiple_of(sub_index * my_rows, my_rows)
    my_block = pl.multiple_of(sub_index * my_blocks, my_blocks)
    for s in range(n_sub):
        if s == 0:
            keep = mask_ref[pl.ds(my_block, my_blocks), :].astype(F32)
        else:
            ref = note_refs[s - 1]
            ends = range(ref.shape[0] - (cols // LANES) * my_blocks, ref.shape[0], my_blocks)
            keep = jnp.concatenate([ref[at : at + my_blocks, :] for at in ends], axis=1)
        keep = keep.astype(BF16)
        for b in range(my_blocks):
            masked_ref[b * BLOCK : (b + 1) * BLOCK, s * cols : (s + 1) * cols] = (
                d_refs[s][pl.ds(my_start + b * BLOCK, BLOCK), :] * keep[b : b + 1]
            )


def early_kernel(n_sub, *refs):
    *factor_refs, slots_ref, share_ref, masked_ref, first_ref, shared_ref, hot_ref = refs
    shared_ref[...] = share_ref[...]
    cols = masked_ref.shape[1] // n_sub

    @pl.when(is_early())
    def _():
        mask_factors(n_sub, factor_refs, masked_ref)
        starts = column_starts(n_sub, cols)
        pick_columns([0], slots_ref[0:1, :], starts, cols, masked_ref, hot_ref, first_ref)


def first_kernel(n_sub, *refs):
    *factor_refs, slots_ref, count_ref, _, _, masked_ref, first_ref, hot_ref = refs
    cols = masked_ref.shape[1] // n_sub
    slot = slots_ref[0:1, :]
    starts = column_starts(n_sub, cols)
    live = live_parts(count_ref[0], hot_ref)
    for n_parts in range(1, hot_ref.shape[0] + 1):

        @pl.when((live == n_parts) & jnp.logical_not(is_early()))
        def _():
            mask_factors(n_sub, factor_refs, masked_ref)
            pick_columns(range(n_parts), slot, starts, cols, masked_ref, hot_ref, first_ref)

        @pl.when((live == n_parts) & is_early())
        def _():
            pick_columns(range(1, n_parts), slot, starts, cols, masked_ref, hot_ref, first_ref)


def second_kernel(n_sub, masked_ref, slots_ref, count_ref, second_ref, hot_ref):
    cols = masked_ref.shape[1] // n_sub
    slot = slots_ref[1:2, :]
    starts = column_starts(n_sub, cols)
    live = live_parts(count_ref[0], hot_ref)
    for n_parts in range(1, hot_ref.shape[0] + 1):

        @pl.when(live == n_parts)
        def _():
            pick_columns(range(n_parts), slot, starts, cols, masked_ref, hot_ref, second_ref)


def flows_kernel(n_shares, *refs):
    share_refs, refs = refs[:n_shares], refs[n_shares:]
    base_ref, first_ref, second_ref, count_ref, out_hbm, post_ref, out_sems = refs
    my_rows, cap = post_ref.shape
    my_blocks = my_rows // BLOCK
    rows = dense_rows(cap)
    total = share_refs[0][...]
    for ref in share_refs[1:]:
        total = total + ref[...]
    cross_first, cross_second, flow_first, flow_second = (
        total[i * rows : (i + 1) * rows] for i in range(4)
    )
    determinant = 1.0 - cross_first * cross_second
    shift_first = (flow_first + cross_first * flow_second) / determinant
    shift_second = (flow_second + cross_second * flow_first) / determinant
    lines = range(cap // LANES)
    weights = [
        [
            jnp.broadcast_to(shift[line : line + 1], (BLOCK, LANES)).astype(BF16)
            for line in lines
        ]
        for shift in (shift_first, shift_second)
    ]
    live = [iota((1, LANES), 1) + line * LANES < count_ref[0] for line in lines]
    my_block = pl.multiple_of(lax.axis_index("sub") * my_blocks, my_blocks)
    base = jnp.swapaxes(base_ref[pl.ds(my_block, my_blocks), :], 0, 1)
    out_copies = []
    for b in range(my_blocks):
        block = slice(b * BLOCK, (b + 1) * BLOCK)
        start = jnp.broadcast_to(base[:, b : b + 1], (BLOCK, LANES))
        for line in lines:
            lanes = slice(line * LANES, (line + 1) * LANES)
            change = (
                weights[0][line] * first_ref[block, lanes]
                + weights[1][line] * second_ref[block, lanes]
            )
            post_ref[block, lanes] = jnp.where(
                live[line], start + change.astype(F32), 0.0
            ).astype(BF16)
        out_copies.append(
            pltpu.make_async_copy(post_ref.at[block], out_hbm.at[block], out_sems.at[b])
        )
        out_copies[-1].start()
    for copy in out_copies:
        copy.wait()


def partners(n_mon):
    half = n_mon // 2
    if n_mon & (n_mon - 1):
        return [[(m + k) % n_mon for m in range(n_mon)] for k in range(1, n_mon)]
    across = [
        [m ^ (half + k) if m < half else m ^ (n_mon - 1 - k) for m in range(n_mon)]
        for k in range(half)
    ]
    return across + [[m ^ k for m in range(n_mon)] for k in range(half - 1, 0, -1)]


def from_other_mon(share, n_mon, n_sub):
    return [
        lax.ppermute(
            share,
            ("mon", "sub"),
            [
                (m * n_sub + s, to[m] * n_sub + n_sub - 1 - s)
                for m in range(n_mon)
                for s in range(n_sub)
            ],
        )
        for to in reversed(partners(n_mon))
    ]


def on_device(dfactors, block_mask, base_flow, branch_row, pair_slots, pair_counts):
    rows_dev, cols = dfactors.shape
    blocks = rows_dev // BLOCK
    candidates = branch_row.shape[0]
    cap = pair_slots.shape[0]
    rows = dense_rows(cap)
    n_sub = lax.axis_size("sub")
    my_rows = rows_dev // n_sub
    slots = pair_slots.T
    base = base_flow.reshape(blocks, BLOCK)
    table = branch_row.reshape(candidates // LANES, LANES)
    hbm = pl.BlockSpec(memory_space=pltpu.HBM)
    in_hbm = functools.partial(pltpu.with_memory_space_constraint, memory_space=pltpu.HBM)
    in_vmem = functools.partial(pltpu.with_memory_space_constraint, memory_space=pltpu.VMEM)
    vmem = pl.BlockSpec(memory_space=pltpu.VMEM)
    smem = pl.BlockSpec(memory_space=pltpu.SMEM)
    params = pltpu.CompilerParams(vmem_limit_bytes=VMEM_LIMIT)
    rings = [[(i, (i + s) % n_sub) for i in range(n_sub)] for s in range(n_sub)]

    factors = [dfactors] + [lax.ppermute(dfactors, "sub", ring) for ring in rings[1:]]

    chunks = rows_dev // chunk_of(rows_dev, 512)
    note_rows = 4 * rows + (cols // LANES) * (my_rows // BLOCK)
    outs = pl.pallas_call(
        functools.partial(values_kernel, n_sub),
        out_shape=[pltpu.VMEM((4 * rows, LANES), F32)]
        + [pltpu.VMEM((note_rows, LANES), F32)] * (n_sub - 1)
        + [
            pltpu.VMEM((rows_dev, cols), BF16),
            pltpu.VMEM((blocks, cols), I32),
            pltpu.VMEM((blocks, BLOCK), F32),
            pltpu.VMEM((2, cap), I32),
        ],
        in_specs=[hbm] * 5,
        out_specs=[vmem] * (n_sub + 4),
        scratch_shapes=[
            pltpu.VMEM((candidates // LANES, LANES), I32),
            pltpu.VMEM((ENDS, 2 * cap), BF16),
            pltpu.VMEM((cols, ENDS), BF16),
            pltpu.VMEM((SUBLANES, 2 * cap), F32),
            pltpu.SemaphoreType.DMA((4,)),
            pltpu.SemaphoreType.DMA((chunks,)),
        ],
        compiler_params=params,
        cost_estimate=pl.CostEstimate(
            flops=2 * rows_dev * cols * ENDS, bytes_accessed=rows_dev * cols * 2, transcendentals=0
        ),
        name="pair_values",
    )(*map(in_hbm, (dfactors, block_mask, base, table, slots)))
    share, notes = outs[0], outs[1:n_sub]
    factors[0], block_mask, base, slots = outs[n_sub:]

    notes = [lax.ppermute(note, "sub", ring) for note, ring in zip(notes, rings[1:])]
    share = functools.reduce(jnp.add, [share] + [note[: 4 * rows] for note in notes])
    width = chunk_of(cap, 256)
    hot = pltpu.VMEM((cap // width, n_sub * cols, width), BF16)
    columns = pltpu.VMEM((my_rows, cap), BF16)
    masked = pltpu.VMEM((my_rows, n_sub * cols), BF16)
    columns_cost = pl.CostEstimate(
        flops=2 * my_rows * cols * n_sub * cap,
        bytes_accessed=my_rows * (cols * n_sub + cap) * 2,
        transcendentals=0,
    )
    factors = [*factors, *notes, block_mask]
    masked, first, share = pl.pallas_call(
        functools.partial(early_kernel, n_sub),
        out_shape=[masked, columns, pltpu.VMEM(share.shape, F32)],
        in_specs=[vmem] * (len(factors) + 2),
        out_specs=[vmem] * 3,
        scratch_shapes=[hot],
        compiler_params=params,
        name="early_columns",
    )(*map(in_vmem, (*factors, slots, share)))
    shares = [share, *from_other_mon(share, lax.axis_size("mon"), n_sub)]

    masked, first = pl.pallas_call(
        functools.partial(first_kernel, n_sub),
        out_shape=[pltpu.VMEM(masked.shape, BF16), columns],
        in_specs=[vmem] * (len(factors) + 1) + [smem] + [vmem] * 2,
        out_specs=[vmem] * 2,
        input_output_aliases={len(factors) + 2: 0, len(factors) + 3: 1},
        scratch_shapes=[hot],
        compiler_params=params,
        cost_estimate=columns_cost,
        name="first_columns",
    )(*map(in_vmem, (*factors, slots)), pair_counts, *map(in_vmem, (masked, first)))
    second = pl.pallas_call(
        functools.partial(second_kernel, n_sub),
        out_shape=columns,
        in_specs=[vmem] * 2 + [smem],
        out_specs=vmem,
        scratch_shapes=[hot],
        compiler_params=params,
        cost_estimate=columns_cost,
        name="second_columns",
    )(*map(in_vmem, (masked, slots)), pair_counts)
    return pl.pallas_call(
        functools.partial(flows_kernel, len(shares)),
        out_shape=jax.ShapeDtypeStruct((my_rows, cap), BF16),
        in_specs=[vmem] * (len(shares) + 3) + [smem],
        out_specs=hbm,
        scratch_shapes=[
            pltpu.VMEM((my_rows, cap), BF16),
            pltpu.SemaphoreType.DMA((my_rows // BLOCK,)),
        ],
        compiler_params=params,
        cost_estimate=pl.CostEstimate(
            flops=6 * my_rows * cap, bytes_accessed=my_rows * cap * 2, transcendentals=0
        ),
        name="post_flows",
    )(*map(in_vmem, (*shares, base, first, second)), pair_counts)


def solution(mesh):
    return jax.shard_map(
        on_device,
        mesh=mesh,
        in_specs=(
            P("mon", "sub"),
            P("mon", "sub"),
            P("mon"),
            P(),
            P(("grp", "pair"), None),
            P(("grp", "pair")),
        ),
        out_specs=P(("mon", "sub"), ("grp", "pair")),
        check_vma=False,
    )
```

```python
import functools

import jax
import jax.numpy as jnp
from jax import lax
from jax.experimental import pallas as pl
from jax.experimental.pallas import tpu as pltpu
from jax.sharding import PartitionSpec as P

BLOCK = 128
LANES = 128
SUBLANES = 8
ENDS = 256
VMEM_LIMIT = 16 * 1024 * 1024
F32 = jnp.float32
BF16 = jnp.bfloat16
I32 = jnp.int32


def chunk_of(total, want):
    size = min(total, want)
    while total % size:
        size -= BLOCK
    return size


def dense_rows(cap):
    return -(-cap // (LANES * SUBLANES)) * SUBLANES


def one_hot(hit):
    return jnp.where(hit, 1.0, 0.0).astype(BF16)


def iota(shape, axis):
    return lax.broadcasted_iota(I32, shape, axis)


def dense(line):
    cap = line.shape[1]
    rows = dense_rows(cap)
    pieces = [line[:, c : c + LANES] for c in range(0, cap, LANES)]
    if len(pieces) < rows:
        pieces.append(jnp.zeros((rows - len(pieces), LANES), line.dtype))
    return jnp.concatenate(pieces, axis=0)


def look_up(table, index):
    high, low = index >> 7, index & 127
    found = jnp.zeros(index.shape, table.dtype)
    for b in range(table.shape[0]):
        line = jnp.broadcast_to(table[b : b + 1], index.shape)
        value = jnp.take_along_axis(line, low, axis=1, mode="promise_in_bounds")
        found = jnp.where(high == b, value, found)
    return found


def values_kernel(
    n_sub, d_hbm, mask_hbm, base_hbm, rows_hbm, slots_hbm, *refs
):
    share_ref, *note_refs = refs[:n_sub]
    (
        d_ref, mask_ref, base_ref, slots_ref, rows_ref, perm_ref, hot_ref, cross_ref, sems, d_sems
    ) = refs[n_sub:]
    rows_dev, cols = d_ref.shape
    chunks = d_sems.shape[0]
    chunk = rows_dev // chunks
    cap = slots_ref.shape[1]
    lines = cap // LANES
    rows = dense_rows(cap)
    sub_index = lax.axis_index("sub")
    small = [
        pltpu.make_async_copy(src, dst, sems.at[i])
        for i, (src, dst) in enumerate(
            [(slots_hbm, slots_ref), (rows_hbm, rows_ref), (base_hbm, base_ref), (mask_hbm, mask_ref)]
        )
    ]
    large = [
        pltpu.make_async_copy(
            d_hbm.at[pl.ds(i * chunk, chunk)], d_ref.at[pl.ds(i * chunk, chunk)], d_sems.at[i]
        )
        for i in range(chunks)
    ]
    for copy in small + large:
        copy.start()

    small[0].wait()
    small[1].wait()
    first, second = dense(slots_ref[0:1, :]), dense(slots_ref[1:2, :])
    table = rows_ref[...]
    row = jnp.concatenate([look_up(table, first), look_up(table, second)], axis=0)
    row = row - lax.axis_index("mon") * rows_dev
    col = jnp.concatenate([second, first], axis=0) - sub_index * cols
    used = lax.rem(iota(row.shape, 0), rows) < lines
    here = used & (row >= 0) & (row < rows_dev) & (col >= 0) & (col < cols)

    flags = one_hot(here)
    height = flags.shape[0]
    above = jnp.dot(
        one_hot(iota((height, height), 1) < iota((height, height), 0)),
        flags,
        preferred_element_type=F32,
    ).astype(BF16)
    place = jnp.dot(
        jnp.concatenate([flags, above], axis=1),
        jnp.concatenate(
            [
                one_hot(iota((LANES, LANES), 0) <= iota((LANES, LANES), 1)),
                jnp.ones((LANES, LANES), BF16),
            ],
            axis=0,
        ),
        preferred_element_type=F32,
    ).astype(I32)
    place = jnp.where(here, place - 1, -1)
    digits = [(x >> shift) & 255 for x in (col, row) for shift in (0, 8)]
    order = [half * rows + b for half in range(2) for b in range(lines)]
    digits = jnp.concatenate(digits, axis=0).astype(F32)
    line = lax.rem(iota(digits.shape, 0), 2 * rows)
    ends = jnp.concatenate(
        [jnp.where(line == r, digits, 0.0).astype(BF16) for r in order], axis=1
    )

    def pick(start, copies=()):
        for at, r in enumerate(order):
            perm_ref[:, at * LANES : (at + 1) * LANES] = one_hot(
                iota((ENDS, LANES), 0) + start == place[r : r + 1]
            )
        packed = lax.dot_general(
            ends, perm_ref[...], (((1,), (1,)), ((), ())), preferred_element_type=F32
        )
        packed = [
            jnp.sum(packed[at : at + 2 * rows], axis=0, keepdims=True).astype(I32)
            for at in range(0, packed.shape[0], 2 * rows)
        ]
        end_col = packed[0] + (packed[1] << 8)
        end_row = packed[2] + (packed[3] << 8)
        hot_ref[...] = one_hot(iota((cols, ENDS), 0) == end_col)
        for copy in copies:
            copy.wait()
        keep = jnp.dot(
            mask_ref[...].astype(F32).astype(BF16), hot_ref[...], preferred_element_type=F32
        )
        keep = jnp.sum(
            jnp.where(iota(keep.shape, 0) == (end_row >> 7), keep, 0.0), axis=0, keepdims=True
        )
        total = jnp.zeros((SUBLANES, ENDS), F32)
        for i in range(chunks):
            values = jnp.dot(
                d_ref[i * chunk : (i + 1) * chunk, :], hot_ref[...], preferred_element_type=F32
            )
            picked = jnp.where(iota((chunk, ENDS), 0) + i * chunk == end_row, values, 0.0)
            total += jnp.sum(picked.reshape(chunk // SUBLANES, SUBLANES, ENDS), axis=0)
        value = jnp.sum(total, axis=0, keepdims=True) * keep
        return jnp.dot(
            jnp.broadcast_to(value, (SUBLANES, ENDS)).astype(BF16),
            perm_ref[...],
            preferred_element_type=F32,
        )

    def put(cross, flow):
        for ref in (share_ref, *note_refs):
            for half in range(2):
                for b in range(rows):
                    at = (half * lines + b) * LANES
                    ref[half * rows + b : half * rows + b + 1, :] = (
                        cross[0:1, at : at + LANES] if b < lines else jnp.zeros((1, LANES), F32)
                    )
            ref[2 * rows : 4 * rows, :] = flow

    cross = pick(0, small[2:] + large)
    flow = jnp.where(sub_index == 0, look_up(base_ref[...], row), 0.0)
    put(cross, flow)
    my_blocks = mask_ref.shape[0] // n_sub
    for s, ref in enumerate(note_refs, 1):
        block = pl.multiple_of(lax.rem(sub_index + s, n_sub) * my_blocks, my_blocks)
        for c in range(cols // LANES):
            at = 4 * rows + c * my_blocks
            ref[at : at + my_blocks, :] = mask_ref[
                pl.ds(block, my_blocks), c * LANES : (c + 1) * LANES
            ].astype(F32)
    count = jnp.max(place) + 1

    @pl.when(count > ENDS)
    def _():
        cross_ref[...] = cross

        def more(i, _):
            cross_ref[...] += pick(i * ENDS)
            return 0

        lax.fori_loop(1, pl.cdiv(count, ENDS), more, 0)
        put(cross_ref[...], flow)


def pick_columns(parts, slot, starts, cols, masked_ref, hot_ref, out_ref):
    width = hot_ref.shape[2]
    for part in parts:
        lanes = slice(part * width, (part + 1) * width)
        for s, start in enumerate(starts):
            hot_ref[part, s * cols : (s + 1) * cols, :] = one_hot(
                iota((cols, width), 0) == slot[:, lanes] - start
            )
        out_ref[:, lanes] = jnp.dot(
            masked_ref[...], hot_ref[part], preferred_element_type=F32
        ).astype(BF16)


def live_parts(count, hot_ref):
    parts, _, width = hot_ref.shape
    return jnp.minimum((count + width - 1) // width, parts)


def is_early():
    return lax.axis_index("mon") < lax.axis_size("mon") // 2


def column_starts(n_sub, cols):
    return [lax.rem(lax.axis_index("sub") + n_sub - s, n_sub) * cols for s in range(n_sub)]


def mask_factors(n_sub, refs, masked_ref):
    d_refs, note_refs, mask_ref = refs[:n_sub], refs[n_sub:-1], refs[-1]
    my_rows, all_cols = masked_ref.shape
    cols = all_cols // n_sub
    my_blocks = my_rows // BLOCK
    sub_index = lax.axis_index("sub")
    my_start = pl.multiple_of(sub_index * my_rows, my_rows)
    my_block = pl.multiple_of(sub_index * my_blocks, my_blocks)
    for s in range(n_sub):
        if s == 0:
            keep = mask_ref[pl.ds(my_block, my_blocks), :].astype(F32)
        else:
            ref = note_refs[s - 1]
            ends = range(ref.shape[0] - (cols // LANES) * my_blocks, ref.shape[0], my_blocks)
            keep = jnp.concatenate([ref[at : at + my_blocks, :] for at in ends], axis=1)
        keep = keep.astype(BF16)
        for b in range(my_blocks):
            masked_ref[b * BLOCK : (b + 1) * BLOCK, s * cols : (s + 1) * cols] = (
                d_refs[s][pl.ds(my_start + b * BLOCK, BLOCK), :] * keep[b : b + 1]
            )


def early_kernel(n_sub, *refs):
    *factor_refs, slots_ref, share_ref, masked_ref, first_ref, shared_ref, hot_ref = refs
    shared_ref[...] = share_ref[...]
    cols = masked_ref.shape[1] // n_sub

    @pl.when(is_early())
    def _():
        mask_factors(n_sub, factor_refs, masked_ref)
        starts = column_starts(n_sub, cols)
        pick_columns([0], slots_ref[0:1, :], starts, cols, masked_ref, hot_ref, first_ref)


def first_kernel(n_sub, *refs):
    *factor_refs, slots_ref, count_ref, _, _, masked_ref, first_ref, hot_ref = refs
    cols = masked_ref.shape[1] // n_sub
    slot = slots_ref[0:1, :]
    starts = column_starts(n_sub, cols)
    live = live_parts(count_ref[0], hot_ref)
    for n_parts in range(1, hot_ref.shape[0] + 1):

        @pl.when((live == n_parts) & jnp.logical_not(is_early()))
        def _():
            mask_factors(n_sub, factor_refs, masked_ref)
            pick_columns(range(n_parts), slot, starts, cols, masked_ref, hot_ref, first_ref)

        @pl.when((live == n_parts) & is_early())
        def _():
            pick_columns(range(1, n_parts), slot, starts, cols, masked_ref, hot_ref, first_ref)


def second_kernel(
    n_sub, masked_ref, slots_ref, count_ref, second_ref, out_hbm, hot_ref, zero_ref, sems
):
    cols = masked_ref.shape[1] // n_sub
    slot = slots_ref[1:2, :]
    starts = column_starts(n_sub, cols)
    live = live_parts(count_ref[0], hot_ref)
    parts, _, width = hot_ref.shape
    for n_parts in range(1, parts + 1):

        @pl.when(live == n_parts)
        def _():
            copies = [
                pltpu.make_async_copy(
                    zero_ref, out_hbm.at[:, part * width : (part + 1) * width], sems.at[part]
                )
                for part in range(n_parts, parts)
            ]
            if copies:
                zero_ref[...] = jnp.zeros_like(zero_ref)
            for copy in copies:
                copy.start()
            pick_columns(range(n_parts), slot, starts, cols, masked_ref, hot_ref, second_ref)
            for copy in copies:
                copy.wait()


def flows_kernel(n_shares, width, *refs):
    share_refs, refs = refs[:n_shares], refs[n_shares:]
    base_ref, first_ref, second_ref, count_ref, _, out_hbm, post_ref, out_sems = refs
    my_rows, cap = post_ref.shape
    my_blocks = my_rows // BLOCK
    rows = dense_rows(cap)
    total = share_refs[0][...]
    for ref in share_refs[1:]:
        total = total + ref[...]
    cross_first, cross_second, flow_first, flow_second = (
        total[i * rows : (i + 1) * rows] for i in range(4)
    )
    determinant = 1.0 - cross_first * cross_second
    shift_first = (flow_first + cross_first * flow_second) / determinant
    shift_second = (flow_second + cross_second * flow_first) / determinant
    my_block = pl.multiple_of(lax.axis_index("sub") * my_blocks, my_blocks)
    base = jnp.swapaxes(base_ref[pl.ds(my_block, my_blocks), :], 0, 1)

    def write(lines):
        live = [iota((1, LANES), 1) + line * LANES < count_ref[0] for line in lines]
        weights = [
            [
                jnp.broadcast_to(shift[line : line + 1], (BLOCK, LANES)).astype(BF16)
                for line in lines
            ]
            for shift in (shift_first, shift_second)
        ]
        wide = slice(0, len(lines) * LANES)
        out_copies = []
        for b in range(my_blocks):
            block = slice(b * BLOCK, (b + 1) * BLOCK)
            start = jnp.broadcast_to(base[:, b : b + 1], (BLOCK, LANES))
            for line in lines:
                lanes = slice(line * LANES, (line + 1) * LANES)
                change = (
                    weights[0][line] * first_ref[block, lanes]
                    + weights[1][line] * second_ref[block, lanes]
                )
                post_ref[block, lanes] = jnp.where(
                    live[line], start + change.astype(F32), 0.0
                ).astype(BF16)
            out_copies.append(
                pltpu.make_async_copy(
                    post_ref.at[block, wide], out_hbm.at[block, wide], out_sems.at[b]
                )
            )
            out_copies[-1].start()
        for copy in out_copies:
            copy.wait()

    parts = cap // width
    live_count = jnp.minimum((count_ref[0] + width - 1) // width, parts)
    for n_parts in range(1, parts + 1):
        pl.when(live_count == n_parts)(
            functools.partial(write, range(n_parts * width // LANES))
        )


def partners(n_mon):
    half = n_mon // 2
    if n_mon & (n_mon - 1):
        return [[(m + k) % n_mon for m in range(n_mon)] for k in range(1, n_mon)]
    across = [
        [m ^ (half + k) if m < half else m ^ (n_mon - 1 - k) for m in range(n_mon)]
        for k in range(half)
    ]
    return across + [[m ^ k for m in range(n_mon)] for k in range(half - 1, 0, -1)]


def from_other_mon(share, n_mon, n_sub):
    return [
        lax.ppermute(
            share,
            ("mon", "sub"),
            [
                (m * n_sub + s, to[m] * n_sub + n_sub - 1 - s)
                for m in range(n_mon)
                for s in range(n_sub)
            ],
        )
        for to in reversed(partners(n_mon))
    ]


def on_device(dfactors, block_mask, base_flow, branch_row, pair_slots, pair_counts):
    rows_dev, cols = dfactors.shape
    blocks = rows_dev // BLOCK
    candidates = branch_row.shape[0]
    cap = pair_slots.shape[0]
    rows = dense_rows(cap)
    n_sub = lax.axis_size("sub")
    my_rows = rows_dev // n_sub
    slots = pair_slots.T
    base = base_flow.reshape(blocks, BLOCK)
    table = branch_row.reshape(candidates // LANES, LANES)
    hbm = pl.BlockSpec(memory_space=pltpu.HBM)
    in_hbm = functools.partial(pltpu.with_memory_space_constraint, memory_space=pltpu.HBM)
    in_vmem = functools.partial(pltpu.with_memory_space_constraint, memory_space=pltpu.VMEM)
    vmem = pl.BlockSpec(memory_space=pltpu.VMEM)
    smem = pl.BlockSpec(memory_space=pltpu.SMEM)
    params = pltpu.CompilerParams(vmem_limit_bytes=VMEM_LIMIT)
    rings = [[(i, (i + s) % n_sub) for i in range(n_sub)] for s in range(n_sub)]

    factors = [dfactors] + [lax.ppermute(dfactors, "sub", ring) for ring in rings[1:]]

    chunks = rows_dev // chunk_of(rows_dev, 512)
    note_rows = 4 * rows + (cols // LANES) * (my_rows // BLOCK)
    outs = pl.pallas_call(
        functools.partial(values_kernel, n_sub),
        out_shape=[pltpu.VMEM((4 * rows, LANES), F32)]
        + [pltpu.VMEM((note_rows, LANES), F32)] * (n_sub - 1)
        + [
            pltpu.VMEM((rows_dev, cols), BF16),
            pltpu.VMEM((blocks, cols), I32),
            pltpu.VMEM((blocks, BLOCK), F32),
            pltpu.VMEM((2, cap), I32),
        ],
        in_specs=[hbm] * 5,
        out_specs=[vmem] * (n_sub + 4),
        scratch_shapes=[
            pltpu.VMEM((candidates // LANES, LANES), I32),
            pltpu.VMEM((ENDS, 2 * cap), BF16),
            pltpu.VMEM((cols, ENDS), BF16),
            pltpu.VMEM((SUBLANES, 2 * cap), F32),
            pltpu.SemaphoreType.DMA((4,)),
            pltpu.SemaphoreType.DMA((chunks,)),
        ],
        compiler_params=params,
        cost_estimate=pl.CostEstimate(
            flops=2 * rows_dev * cols * ENDS, bytes_accessed=rows_dev * cols * 2, transcendentals=0
        ),
        name="pair_values",
    )(*map(in_hbm, (dfactors, block_mask, base, table, slots)))
    share, notes = outs[0], outs[1:n_sub]
    factors[0], block_mask, base, slots = outs[n_sub:]

    notes = [lax.ppermute(note, "sub", ring) for note, ring in zip(notes, rings[1:])]
    share = functools.reduce(jnp.add, [share] + [note[: 4 * rows] for note in notes])
    width = chunk_of(cap, 256)
    hot = pltpu.VMEM((cap // width, n_sub * cols, width), BF16)
    columns = pltpu.VMEM((my_rows, cap), BF16)
    masked = pltpu.VMEM((my_rows, n_sub * cols), BF16)
    columns_cost = pl.CostEstimate(
        flops=2 * my_rows * cols * n_sub * cap,
        bytes_accessed=my_rows * (cols * n_sub + cap) * 2,
        transcendentals=0,
    )
    factors = [*factors, *notes, block_mask]
    masked, first, share = pl.pallas_call(
        functools.partial(early_kernel, n_sub),
        out_shape=[masked, columns, pltpu.VMEM(share.shape, F32)],
        in_specs=[vmem] * (len(factors) + 2),
        out_specs=[vmem] * 3,
        scratch_shapes=[hot],
        compiler_params=params,
        name="early_columns",
    )(*map(in_vmem, (*factors, slots, share)))
    shares = [share, *from_other_mon(share, lax.axis_size("mon"), n_sub)]

    masked, first = pl.pallas_call(
        functools.partial(first_kernel, n_sub),
        out_shape=[pltpu.VMEM(masked.shape, BF16), columns],
        in_specs=[vmem] * (len(factors) + 1) + [smem] + [vmem] * 2,
        out_specs=[vmem] * 2,
        input_output_aliases={len(factors) + 2: 0, len(factors) + 3: 1},
        scratch_shapes=[hot],
        compiler_params=params,
        cost_estimate=columns_cost,
        name="first_columns",
    )(*map(in_vmem, (*factors, slots)), pair_counts, *map(in_vmem, (masked, first)))
    second, out = pl.pallas_call(
        functools.partial(second_kernel, n_sub),
        out_shape=[columns, pltpu.HBM((my_rows, cap), BF16)],
        in_specs=[vmem] * 2 + [smem],
        out_specs=[vmem, hbm],
        scratch_shapes=[
            hot,
            pltpu.VMEM((my_rows, width), BF16),
            pltpu.SemaphoreType.DMA((cap // width,)),
        ],
        compiler_params=params,
        cost_estimate=columns_cost,
        name="second_columns",
    )(*map(in_vmem, (masked, slots)), pair_counts)
    return pl.pallas_call(
        functools.partial(flows_kernel, len(shares), width),
        out_shape=jax.ShapeDtypeStruct((my_rows, cap), BF16),
        in_specs=[vmem] * (len(shares) + 3) + [smem, hbm],
        out_specs=hbm,
        input_output_aliases={len(shares) + 4: 0},
        scratch_shapes=[
            pltpu.VMEM((my_rows, cap), BF16),
            pltpu.SemaphoreType.DMA((my_rows // BLOCK,)),
        ],
        compiler_params=params,
        cost_estimate=pl.CostEstimate(
            flops=6 * my_rows * cap, bytes_accessed=my_rows * cap * 2, transcendentals=0
        ),
        name="post_flows",
    )(*map(in_vmem, (*shares, base, first, second)), pair_counts, in_hbm(out))


def solution(mesh):
    return jax.shard_map(
        on_device,
        mesh=mesh,
        in_specs=(
            P("mon", "sub"),
            P("mon", "sub"),
            P("mon"),
            P(),
            P(("grp", "pair"), None),
            P(("grp", "pair")),
        ),
        out_specs=P(("mon", "sub"), ("grp", "pair")),
        check_vma=False,
    )
```

```python
import functools

import jax
import jax.numpy as jnp
from jax import lax
from jax.experimental import pallas as pl
from jax.experimental.pallas import tpu as pltpu
from jax.sharding import PartitionSpec as P

BLOCK = 128
LANES = 128
SUBLANES = 8
ENDS = 256
VMEM_LIMIT = 16 * 1024 * 1024
F32 = jnp.float32
BF16 = jnp.bfloat16
I32 = jnp.int32


def chunk_of(total, want):
    size = min(total, want)
    while total % size:
        size -= BLOCK
    return size


def dense_rows(cap):
    return -(-cap // (LANES * SUBLANES)) * SUBLANES


def one_hot(hit):
    return jnp.where(hit, 1.0, 0.0).astype(BF16)


def iota(shape, axis):
    return lax.broadcasted_iota(I32, shape, axis)


def dense(line):
    cap = line.shape[1]
    rows = dense_rows(cap)
    pieces = [line[:, c : c + LANES] for c in range(0, cap, LANES)]
    if len(pieces) < rows:
        pieces.append(jnp.zeros((rows - len(pieces), LANES), line.dtype))
    return jnp.concatenate(pieces, axis=0)


def look_up(table, index):
    high, low = index >> 7, index & 127
    found = jnp.zeros(index.shape, table.dtype)
    for b in range(table.shape[0]):
        line = jnp.broadcast_to(table[b : b + 1], index.shape)
        value = jnp.take_along_axis(line, low, axis=1, mode="promise_in_bounds")
        found = jnp.where(high == b, value, found)
    return found


def values_kernel(
    n_sub, d_hbm, mask_hbm, base_hbm, rows_hbm, slots_hbm, *refs
):
    share_ref, *note_refs = refs[:n_sub]
    (
        d_ref, mask_ref, base_ref, slots_ref, rows_ref, perm_ref, hot_ref, cross_ref, sems, d_sems
    ) = refs[n_sub:]
    rows_dev, cols = d_ref.shape
    chunks = d_sems.shape[0]
    chunk = rows_dev // chunks
    cap = slots_ref.shape[1]
    lines = cap // LANES
    rows = dense_rows(cap)
    sub_index = lax.axis_index("sub")
    small = [
        pltpu.make_async_copy(src, dst, sems.at[i])
        for i, (src, dst) in enumerate(
            [(slots_hbm, slots_ref), (rows_hbm, rows_ref), (base_hbm, base_ref), (mask_hbm, mask_ref)]
        )
    ]
    large = [
        pltpu.make_async_copy(
            d_hbm.at[pl.ds(i * chunk, chunk)], d_ref.at[pl.ds(i * chunk, chunk)], d_sems.at[i]
        )
        for i in range(chunks)
    ]
    for copy in small + large:
        copy.start()

    small[0].wait()
    small[1].wait()
    first, second = dense(slots_ref[0:1, :]), dense(slots_ref[1:2, :])
    table = rows_ref[...]
    row = jnp.concatenate([look_up(table, first), look_up(table, second)], axis=0)
    row = row - lax.axis_index("mon") * rows_dev
    col = jnp.concatenate([second, first], axis=0) - sub_index * cols
    used = lax.rem(iota(row.shape, 0), rows) < lines
    here = used & (row >= 0) & (row < rows_dev) & (col >= 0) & (col < cols)

    flags = one_hot(here)
    height = flags.shape[0]
    above = jnp.dot(
        one_hot(iota((height, height), 1) < iota((height, height), 0)),
        flags,
        preferred_element_type=F32,
    ).astype(BF16)
    place = jnp.dot(
        jnp.concatenate([flags, above], axis=1),
        jnp.concatenate(
            [
                one_hot(iota((LANES, LANES), 0) <= iota((LANES, LANES), 1)),
                jnp.ones((LANES, LANES), BF16),
            ],
            axis=0,
        ),
        preferred_element_type=F32,
    ).astype(I32)
    place = jnp.where(here, place - 1, -1)
    digits = [(x >> shift) & 255 for x in (col, row) for shift in (0, 8)]
    order = [half * rows + b for half in range(2) for b in range(lines)]
    ends = jnp.concatenate(
        [jnp.concatenate([x[r : r + 1] for x in digits], axis=0) for r in order], axis=1
    )
    ends = ends.astype(F32).astype(BF16)

    def pick(start, copies=()):
        for at, r in enumerate(order):
            perm_ref[:, at * LANES : (at + 1) * LANES] = one_hot(
                iota((ENDS, LANES), 0) + start == place[r : r + 1]
            )
        packed = lax.dot_general(
            ends, perm_ref[...], (((1,), (1,)), ((), ())), preferred_element_type=F32
        ).astype(I32)
        end_col = packed[0:1] + (packed[1:2] << 8)
        end_row = packed[2:3] + (packed[3:4] << 8)
        hot_ref[...] = one_hot(iota((cols, ENDS), 0) == end_col)
        for copy in copies:
            copy.wait()
        keep = jnp.dot(
            mask_ref[...].astype(F32).astype(BF16), hot_ref[...], preferred_element_type=F32
        )
        keep = jnp.sum(
            jnp.where(iota(keep.shape, 0) == (end_row >> 7), keep, 0.0), axis=0, keepdims=True
        )
        total = jnp.zeros((SUBLANES, ENDS), F32)
        for i in range(chunks):
            values = jnp.dot(
                d_ref[i * chunk : (i + 1) * chunk, :], hot_ref[...], preferred_element_type=F32
            )
            picked = jnp.where(iota((chunk, ENDS), 0) + i * chunk == end_row, values, 0.0)
            total += jnp.sum(picked.reshape(chunk // SUBLANES, SUBLANES, ENDS), axis=0)
        value = jnp.sum(total, axis=0, keepdims=True) * keep
        value = jnp.concatenate([value[:, q : q + LANES] for q in range(0, ENDS, LANES)], axis=0)
        return look_up(value, place - start)

    def put(cross, flow):
        for ref in (share_ref, *note_refs):
            ref[: 2 * rows, :] = cross
            ref[2 * rows : 4 * rows, :] = flow

    cross = pick(0, small[2:] + large)
    flow = jnp.where(sub_index == 0, look_up(base_ref[...], row), 0.0)
    put(cross, flow)
    my_blocks = mask_ref.shape[0] // n_sub
    for s, ref in enumerate(note_refs, 1):
        block = pl.multiple_of(lax.rem(sub_index + s, n_sub) * my_blocks, my_blocks)
        for c in range(cols // LANES):
            at = 4 * rows + c * my_blocks
            ref[at : at + my_blocks, :] = mask_ref[
                pl.ds(block, my_blocks), c * LANES : (c + 1) * LANES
            ].astype(F32)
    count = jnp.max(place) + 1

    @pl.when(count > ENDS)
    def _():
        cross_ref[...] = cross

        def more(i, _):
            cross_ref[...] += pick(i * ENDS)
            return 0

        lax.fori_loop(1, pl.cdiv(count, ENDS), more, 0)
        put(cross_ref[...], flow)


def pick_columns(parts, slot, starts, cols, masked_ref, hot_ref, out_ref):
    width = hot_ref.shape[2]
    for part in parts:
        lanes = slice(part * width, (part + 1) * width)
        for s, start in enumerate(starts):
            hot_ref[part, s * cols : (s + 1) * cols, :] = one_hot(
                iota((cols, width), 0) == slot[:, lanes] - start
            )
        out_ref[:, lanes] = jnp.dot(
            masked_ref[...], hot_ref[part], preferred_element_type=F32
        ).astype(BF16)


def live_parts(count, hot_ref):
    parts, _, width = hot_ref.shape
    return jnp.minimum((count + width - 1) // width, parts)


def is_early():
    return lax.axis_index("mon") < lax.axis_size("mon") // 2


def column_starts(n_sub, cols):
    return [lax.rem(lax.axis_index("sub") + n_sub - s, n_sub) * cols for s in range(n_sub)]


def mask_factors(n_sub, refs, masked_ref):
    d_refs, note_refs, mask_ref = refs[:n_sub], refs[n_sub:-1], refs[-1]
    my_rows, all_cols = masked_ref.shape
    cols = all_cols // n_sub
    my_blocks = my_rows // BLOCK
    sub_index = lax.axis_index("sub")
    my_start = pl.multiple_of(sub_index * my_rows, my_rows)
    my_block = pl.multiple_of(sub_index * my_blocks, my_blocks)
    for s in range(n_sub):
        if s == 0:
            keep = mask_ref[pl.ds(my_block, my_blocks), :].astype(F32)
        else:
            ref = note_refs[s - 1]
            ends = range(ref.shape[0] - (cols // LANES) * my_blocks, ref.shape[0], my_blocks)
            keep = jnp.concatenate([ref[at : at + my_blocks, :] for at in ends], axis=1)
        keep = keep.astype(BF16)
        for b in range(my_blocks):
            masked_ref[b * BLOCK : (b + 1) * BLOCK, s * cols : (s + 1) * cols] = (
                d_refs[s][pl.ds(my_start + b * BLOCK, BLOCK), :] * keep[b : b + 1]
            )


def early_kernel(n_sub, *refs):
    *factor_refs, slots_ref, share_ref, masked_ref, first_ref, shared_ref, hot_ref = refs
    shared_ref[...] = share_ref[...]
    cols = masked_ref.shape[1] // n_sub

    @pl.when(is_early())
    def _():
        mask_factors(n_sub, factor_refs, masked_ref)
        starts = column_starts(n_sub, cols)
        pick_columns([0], slots_ref[0:1, :], starts, cols, masked_ref, hot_ref, first_ref)


def first_kernel(n_sub, *refs):
    *factor_refs, slots_ref, count_ref, _, _, masked_ref, first_ref, hot_ref = refs
    cols = masked_ref.shape[1] // n_sub
    slot = slots_ref[0:1, :]
    starts = column_starts(n_sub, cols)
    live = live_parts(count_ref[0], hot_ref)
    for n_parts in range(1, hot_ref.shape[0] + 1):

        @pl.when((live == n_parts) & jnp.logical_not(is_early()))
        def _():
            mask_factors(n_sub, factor_refs, masked_ref)
            pick_columns(range(n_parts), slot, starts, cols, masked_ref, hot_ref, first_ref)

        @pl.when((live == n_parts) & is_early())
        def _():
            pick_columns(range(1, n_parts), slot, starts, cols, masked_ref, hot_ref, first_ref)


def second_kernel(
    n_sub, masked_ref, slots_ref, count_ref, second_ref, out_hbm, hot_ref, zero_ref, sems
):
    cols = masked_ref.shape[1] // n_sub
    slot = slots_ref[1:2, :]
    starts = column_starts(n_sub, cols)
    live = live_parts(count_ref[0], hot_ref)
    parts, _, width = hot_ref.shape
    for n_parts in range(1, parts + 1):

        @pl.when(live == n_parts)
        def _():
            copies = [
                pltpu.make_async_copy(
                    zero_ref, out_hbm.at[:, part * width : (part + 1) * width], sems.at[part]
                )
                for part in range(n_parts, parts)
            ]
            if copies:
                zero_ref[...] = jnp.zeros_like(zero_ref)
            for copy in copies:
                copy.start()
            pick_columns(range(n_parts), slot, starts, cols, masked_ref, hot_ref, second_ref)
            for copy in copies:
                copy.wait()


def flows_kernel(n_shares, width, *refs):
    share_refs, refs = refs[:n_shares], refs[n_shares:]
    base_ref, first_ref, second_ref, count_ref, _, out_hbm, post_ref, out_sems = refs
    my_rows, cap = post_ref.shape
    my_blocks = my_rows // BLOCK
    rows = dense_rows(cap)
    total = share_refs[0][...]
    for ref in share_refs[1:]:
        total = total + ref[...]
    cross_first, cross_second, flow_first, flow_second = (
        total[i * rows : (i + 1) * rows] for i in range(4)
    )
    determinant = 1.0 - cross_first * cross_second
    shift_first = (flow_first + cross_first * flow_second) / determinant
    shift_second = (flow_second + cross_second * flow_first) / determinant
    my_block = pl.multiple_of(lax.axis_index("sub") * my_blocks, my_blocks)
    base = jnp.swapaxes(base_ref[pl.ds(my_block, my_blocks), :], 0, 1)

    def write(lines):
        live = [iota((1, LANES), 1) + line * LANES < count_ref[0] for line in lines]
        weights = [
            [
                jnp.broadcast_to(shift[line : line + 1], (BLOCK, LANES)).astype(BF16)
                for line in lines
            ]
            for shift in (shift_first, shift_second)
        ]
        wide = slice(0, len(lines) * LANES)
        out_copies = []
        for b in range(my_blocks):
            block = slice(b * BLOCK, (b + 1) * BLOCK)
            start = jnp.broadcast_to(base[:, b : b + 1], (BLOCK, LANES))
            for line in lines:
                lanes = slice(line * LANES, (line + 1) * LANES)
                change = (
                    weights[0][line] * first_ref[block, lanes]
                    + weights[1][line] * second_ref[block, lanes]
                )
                post_ref[block, lanes] = jnp.where(
                    live[line], start + change.astype(F32), 0.0
                ).astype(BF16)
            out_copies.append(
                pltpu.make_async_copy(
                    post_ref.at[block, wide], out_hbm.at[block, wide], out_sems.at[b]
                )
            )
            out_copies[-1].start()
        for copy in out_copies:
            copy.wait()

    parts = cap // width
    live_count = jnp.minimum((count_ref[0] + width - 1) // width, parts)
    for n_parts in range(1, parts + 1):
        pl.when(live_count == n_parts)(
            functools.partial(write, range(n_parts * width // LANES))
        )


def partners(n_mon):
    half = n_mon // 2
    if n_mon & (n_mon - 1):
        return [[(m + k) % n_mon for m in range(n_mon)] for k in range(1, n_mon)]
    across = [
        [m ^ (half + k) if m < half else m ^ (n_mon - 1 - k) for m in range(n_mon)]
        for k in range(half)
    ]
    return across + [[m ^ k for m in range(n_mon)] for k in range(half - 1, 0, -1)]


def from_other_mon(share, n_mon, n_sub):
    return [
        lax.ppermute(
            share,
            ("mon", "sub"),
            [
                (m * n_sub + s, to[m] * n_sub + n_sub - 1 - s)
                for m in range(n_mon)
                for s in range(n_sub)
            ],
        )
        for to in reversed(partners(n_mon))
    ]


def on_device(dfactors, block_mask, base_flow, branch_row, pair_slots, pair_counts):
    rows_dev, cols = dfactors.shape
    blocks = rows_dev // BLOCK
    candidates = branch_row.shape[0]
    cap = pair_slots.shape[0]
    rows = dense_rows(cap)
    n_sub = lax.axis_size("sub")
    my_rows = rows_dev // n_sub
    slots = pair_slots.T
    base = base_flow.reshape(blocks, BLOCK)
    table = branch_row.reshape(candidates // LANES, LANES)
    hbm = pl.BlockSpec(memory_space=pltpu.HBM)
    in_hbm = functools.partial(pltpu.with_memory_space_constraint, memory_space=pltpu.HBM)
    in_vmem = functools.partial(pltpu.with_memory_space_constraint, memory_space=pltpu.VMEM)
    vmem = pl.BlockSpec(memory_space=pltpu.VMEM)
    smem = pl.BlockSpec(memory_space=pltpu.SMEM)
    params = pltpu.CompilerParams(vmem_limit_bytes=VMEM_LIMIT)
    rings = [[(i, (i + s) % n_sub) for i in range(n_sub)] for s in range(n_sub)]

    factors = [dfactors] + [lax.ppermute(dfactors, "sub", ring) for ring in rings[1:]]

    chunks = rows_dev // chunk_of(rows_dev, 512)
    note_rows = 4 * rows + (cols // LANES) * (my_rows // BLOCK)
    outs = pl.pallas_call(
        functools.partial(values_kernel, n_sub),
        out_shape=[pltpu.VMEM((4 * rows, LANES), F32)]
        + [pltpu.VMEM((note_rows, LANES), F32)] * (n_sub - 1)
        + [
            pltpu.VMEM((rows_dev, cols), BF16),
            pltpu.VMEM((blocks, cols), I32),
            pltpu.VMEM((blocks, BLOCK), F32),
            pltpu.VMEM((2, cap), I32),
        ],
        in_specs=[hbm] * 5,
        out_specs=[vmem] * (n_sub + 4),
        scratch_shapes=[
            pltpu.VMEM((candidates // LANES, LANES), I32),
            pltpu.VMEM((ENDS, 2 * cap), BF16),
            pltpu.VMEM((cols, ENDS), BF16),
            pltpu.VMEM((2 * rows, LANES), F32),
            pltpu.SemaphoreType.DMA((4,)),
            pltpu.SemaphoreType.DMA((chunks,)),
        ],
        compiler_params=params,
        cost_estimate=pl.CostEstimate(
            flops=2 * rows_dev * cols * ENDS, bytes_accessed=rows_dev * cols * 2, transcendentals=0
        ),
        name="pair_values",
    )(*map(in_hbm, (dfactors, block_mask, base, table, slots)))
    share, notes = outs[0], outs[1:n_sub]
    factors[0], block_mask, base, slots = outs[n_sub:]

    notes = [lax.ppermute(note, "sub", ring) for note, ring in zip(notes, rings[1:])]
    share = functools.reduce(jnp.add, [share] + [note[: 4 * rows] for note in notes])
    width = chunk_of(cap, 256)
    hot = pltpu.VMEM((cap // width, n_sub * cols, width), BF16)
    columns = pltpu.VMEM((my_rows, cap), BF16)
    masked = pltpu.VMEM((my_rows, n_sub * cols), BF16)
    columns_cost = pl.CostEstimate(
        flops=2 * my_rows * cols * n_sub * cap,
        bytes_accessed=my_rows * (cols * n_sub + cap) * 2,
        transcendentals=0,
    )
    factors = [*factors, *notes, block_mask]
    masked, first, share = pl.pallas_call(
        functools.partial(early_kernel, n_sub),
        out_shape=[masked, columns, pltpu.VMEM(share.shape, F32)],
        in_specs=[vmem] * (len(factors) + 2),
        out_specs=[vmem] * 3,
        scratch_shapes=[hot],
        compiler_params=params,
        name="early_columns",
    )(*map(in_vmem, (*factors, slots, share)))
    shares = [share, *from_other_mon(share, lax.axis_size("mon"), n_sub)]

    masked, first = pl.pallas_call(
        functools.partial(first_kernel, n_sub),
        out_shape=[pltpu.VMEM(masked.shape, BF16), columns],
        in_specs=[vmem] * (len(factors) + 1) + [smem] + [vmem] * 2,
        out_specs=[vmem] * 2,
        input_output_aliases={len(factors) + 2: 0, len(factors) + 3: 1},
        scratch_shapes=[hot],
        compiler_params=params,
        cost_estimate=columns_cost,
        name="first_columns",
    )(*map(in_vmem, (*factors, slots)), pair_counts, *map(in_vmem, (masked, first)))
    second, out = pl.pallas_call(
        functools.partial(second_kernel, n_sub),
        out_shape=[columns, pltpu.HBM((my_rows, cap), BF16)],
        in_specs=[vmem] * 2 + [smem],
        out_specs=[vmem, hbm],
        scratch_shapes=[
            hot,
            pltpu.VMEM((my_rows, width), BF16),
            pltpu.SemaphoreType.DMA((cap // width,)),
        ],
        compiler_params=params,
        cost_estimate=columns_cost,
        name="second_columns",
    )(*map(in_vmem, (masked, slots)), pair_counts)
    return pl.pallas_call(
        functools.partial(flows_kernel, len(shares), width),
        out_shape=jax.ShapeDtypeStruct((my_rows, cap), BF16),
        in_specs=[vmem] * (len(shares) + 3) + [smem, hbm],
        out_specs=hbm,
        input_output_aliases={len(shares) + 4: 0},
        scratch_shapes=[
            pltpu.VMEM((my_rows, cap), BF16),
            pltpu.SemaphoreType.DMA((my_rows // BLOCK,)),
        ],
        compiler_params=params,
        cost_estimate=pl.CostEstimate(
            flops=6 * my_rows * cap, bytes_accessed=my_rows * cap * 2, transcendentals=0
        ),
        name="post_flows",
    )(*map(in_vmem, (*shares, base, first, second)), pair_counts, in_hbm(out))


def solution(mesh):
    return jax.shard_map(
        on_device,
        mesh=mesh,
        in_specs=(
            P("mon", "sub"),
            P("mon", "sub"),
            P("mon"),
            P(),
            P(("grp", "pair"), None),
            P(("grp", "pair")),
        ),
        out_specs=P(("mon", "sub"), ("grp", "pair")),
        check_vma=False,
    )
```

```python
import functools

import jax
import jax.numpy as jnp
from jax import lax
from jax.experimental import pallas as pl
from jax.experimental.pallas import tpu as pltpu
from jax.sharding import PartitionSpec as P

BLOCK = 128
LANES = 128
SUBLANES = 8
ENDS = 256
VMEM_LIMIT = 16 * 1024 * 1024
F32 = jnp.float32
BF16 = jnp.bfloat16
I32 = jnp.int32


def chunk_of(total, want):
    size = min(total, want)
    while total % size:
        size -= BLOCK
    return size


def dense_rows(cap):
    return -(-cap // (LANES * SUBLANES)) * SUBLANES


def one_hot(hit):
    return jnp.where(hit, 1.0, 0.0).astype(BF16)


def iota(shape, axis):
    return lax.broadcasted_iota(I32, shape, axis)


def dense(line):
    cap = line.shape[1]
    rows = dense_rows(cap)
    pieces = [line[:, c : c + LANES] for c in range(0, cap, LANES)]
    if len(pieces) < rows:
        pieces.append(jnp.zeros((rows - len(pieces), LANES), line.dtype))
    return jnp.concatenate(pieces, axis=0)


def look_up(table, index):
    high, low = index >> 7, index & 127
    found = jnp.zeros(index.shape, table.dtype)
    for b in range(table.shape[0]):
        line = jnp.broadcast_to(table[b : b + 1], index.shape)
        value = jnp.take_along_axis(line, low, axis=1, mode="promise_in_bounds")
        found = jnp.where(high == b, value, found)
    return found


def values_kernel(
    n_sub, d_hbm, mask_hbm, base_hbm, rows_hbm, slots_hbm, *refs
):
    share_ref, *note_refs = refs[:n_sub]
    (
        d_ref, mask_ref, base_ref, slots_ref, rows_ref, perm_ref, hot_ref, cross_ref, sems, d_sems
    ) = refs[n_sub:]
    rows_dev, cols = d_ref.shape
    chunks = d_sems.shape[0]
    chunk = rows_dev // chunks
    cap = slots_ref.shape[1]
    lines = cap // LANES
    rows = dense_rows(cap)
    sub_index = lax.axis_index("sub")
    small = [
        pltpu.make_async_copy(src, dst, sems.at[i])
        for i, (src, dst) in enumerate(
            [(slots_hbm, slots_ref), (rows_hbm, rows_ref), (base_hbm, base_ref), (mask_hbm, mask_ref)]
        )
    ]
    large = [
        pltpu.make_async_copy(
            d_hbm.at[pl.ds(i * chunk, chunk)], d_ref.at[pl.ds(i * chunk, chunk)], d_sems.at[i]
        )
        for i in range(chunks)
    ]
    for copy in small + large:
        copy.start()

    small[0].wait()
    small[1].wait()
    first, second = dense(slots_ref[0:1, :]), dense(slots_ref[1:2, :])
    table = rows_ref[...]
    row = jnp.concatenate([look_up(table, first), look_up(table, second)], axis=0)
    row = row - lax.axis_index("mon") * rows_dev
    col = jnp.concatenate([second, first], axis=0) - sub_index * cols
    used = lax.rem(iota(row.shape, 0), rows) < lines
    here = used & (row >= 0) & (row < rows_dev) & (col >= 0) & (col < cols)

    flags = one_hot(here)
    height = flags.shape[0]
    above = jnp.dot(
        one_hot(iota((height, height), 1) < iota((height, height), 0)),
        flags,
        preferred_element_type=F32,
    ).astype(BF16)
    place = jnp.dot(
        jnp.concatenate([flags, above], axis=1),
        jnp.concatenate(
            [
                one_hot(iota((LANES, LANES), 0) <= iota((LANES, LANES), 1)),
                jnp.ones((LANES, LANES), BF16),
            ],
            axis=0,
        ),
        preferred_element_type=F32,
    ).astype(I32)
    place = jnp.where(here, place - 1, -1)
    digits = [(x >> shift) & 255 for x in (col, row) for shift in (0, 8)]
    order = [half * rows + b for half in range(2) for b in range(lines)]
    ends = jnp.concatenate(
        [jnp.concatenate([x[r : r + 1] for x in digits], axis=0) for r in order], axis=1
    )
    ends = ends.astype(F32).astype(BF16)

    def pick(start, copies=()):
        for at, r in enumerate(order):
            perm_ref[:, at * LANES : (at + 1) * LANES] = one_hot(
                iota((ENDS, LANES), 0) + start == place[r : r + 1]
            )
        packed = lax.dot_general(
            ends, perm_ref[...], (((1,), (1,)), ((), ())), preferred_element_type=F32
        ).astype(I32)
        end_col = packed[0:1] + (packed[1:2] << 8)
        end_row = packed[2:3] + (packed[3:4] << 8)
        hot_ref[...] = one_hot(iota((cols, ENDS), 0) == end_col)
        for copy in copies:
            copy.wait()
        keep = jnp.dot(
            mask_ref[...].astype(F32).astype(BF16), hot_ref[...], preferred_element_type=F32
        )
        keep = jnp.sum(
            jnp.where(iota(keep.shape, 0) == (end_row >> 7), keep, 0.0), axis=0, keepdims=True
        )
        total = jnp.zeros((SUBLANES, ENDS), F32)
        for i in range(chunks):
            values = jnp.dot(
                d_ref[i * chunk : (i + 1) * chunk, :], hot_ref[...], preferred_element_type=F32
            )
            picked = jnp.where(iota((chunk, ENDS), 0) + i * chunk == end_row, values, 0.0)
            total += jnp.sum(picked.reshape(chunk // SUBLANES, SUBLANES, ENDS), axis=0)
        value = jnp.sum(total, axis=0, keepdims=True) * keep
        value = jnp.concatenate([value[:, q : q + LANES] for q in range(0, ENDS, LANES)], axis=0)
        return look_up(value, place - start)

    def put(cross, flow):
        for ref in (share_ref, *note_refs):
            ref[: 2 * rows, :] = cross
            ref[2 * rows : 4 * rows, :] = flow

    cross = pick(0, small[2:] + large)
    flow = jnp.where(sub_index == 0, look_up(base_ref[...], row), 0.0)
    put(cross, flow)
    my_blocks = mask_ref.shape[0] // n_sub
    for s, ref in enumerate(note_refs, 1):
        block = pl.multiple_of(lax.rem(sub_index + s, n_sub) * my_blocks, my_blocks)
        for c in range(cols // LANES):
            at = 4 * rows + c * my_blocks
            ref[at : at + my_blocks, :] = mask_ref[
                pl.ds(block, my_blocks), c * LANES : (c + 1) * LANES
            ].astype(F32)
    count = jnp.max(place) + 1

    @pl.when(count > ENDS)
    def _():
        cross_ref[...] = cross

        def more(i, _):
            cross_ref[...] += pick(i * ENDS)
            return 0

        lax.fori_loop(1, pl.cdiv(count, ENDS), more, 0)
        put(cross_ref[...], flow)


def live_lines(count, cap):
    return jnp.clip((count + LANES - 1) // LANES, min(2, cap // LANES), cap // LANES)


def tiles(lines):
    first = [[(0, line), (0, line + 1)] for line in range(0, lines - 1, 2)]
    second = [[(1, line), (1, line + 1)] for line in range(0, lines - 1, 2)]
    if lines % 2:
        first.append([(0, lines - 1), (1, lines - 1)])
    return first, second


def pick_columns(some, slots_ref, n_sub, masked_ref, hot_ref, out_refs):
    cols = masked_ref.shape[1] // n_sub
    for at, tile in enumerate(some):
        slot = jnp.concatenate(
            [slots_ref[end : end + 1, line * LANES : (line + 1) * LANES] for end, line in tile],
            axis=1,
        )
        for s in range(n_sub):
            start = lax.rem(lax.axis_index("sub") + n_sub - s, n_sub) * cols
            hot_ref[at, s * cols : (s + 1) * cols, :] = one_hot(
                iota((cols, slot.shape[1]), 0) == slot - start
            )
        found = jnp.dot(masked_ref[...], hot_ref[at], preferred_element_type=F32).astype(BF16)
        if tile[0][0] == tile[1][0]:
            end, line = tile[0]
            out_refs[end][:, line * LANES : (line + 2) * LANES] = found
        else:
            for half, (end, line) in enumerate(tile):
                out_refs[end][:, line * LANES : (line + 1) * LANES] = found[
                    :, half * LANES : (half + 1) * LANES
                ]


def is_early():
    return lax.axis_index("mon") < lax.axis_size("mon") // 2


def mask_factors(n_sub, refs, masked_ref):
    d_refs, note_refs, mask_ref = refs[:n_sub], refs[n_sub:-1], refs[-1]
    my_rows, all_cols = masked_ref.shape
    cols = all_cols // n_sub
    my_blocks = my_rows // BLOCK
    sub_index = lax.axis_index("sub")
    my_start = pl.multiple_of(sub_index * my_rows, my_rows)
    my_block = pl.multiple_of(sub_index * my_blocks, my_blocks)
    for s in range(n_sub):
        if s == 0:
            keep = mask_ref[pl.ds(my_block, my_blocks), :].astype(F32)
        else:
            ref = note_refs[s - 1]
            ends = range(ref.shape[0] - (cols // LANES) * my_blocks, ref.shape[0], my_blocks)
            keep = jnp.concatenate([ref[at : at + my_blocks, :] for at in ends], axis=1)
        keep = keep.astype(BF16)
        for b in range(my_blocks):
            masked_ref[b * BLOCK : (b + 1) * BLOCK, s * cols : (s + 1) * cols] = (
                d_refs[s][pl.ds(my_start + b * BLOCK, BLOCK), :] * keep[b : b + 1]
            )


def early_kernel(n_sub, *refs):
    *factor_refs, slots_ref, share_ref, masked_ref, first_ref, shared_ref, hot_ref = refs
    shared_ref[...] = share_ref[...]

    @pl.when(is_early())
    def _():
        mask_factors(n_sub, factor_refs, masked_ref)
        some = tiles(first_ref.shape[1] // LANES)[0][:1]
        pick_columns(some, slots_ref, n_sub, masked_ref, hot_ref, [first_ref])


def first_kernel(n_sub, *refs):
    *factor_refs, slots_ref, count_ref, _, _, masked_ref, first_ref, second_ref, hot_ref = refs
    cap = first_ref.shape[1]
    live = live_lines(count_ref[0], cap)

    def late(some):
        mask_factors(n_sub, factor_refs, masked_ref)
        pick_columns(some, slots_ref, n_sub, masked_ref, hot_ref, [first_ref, second_ref])

    def early(some):
        pick_columns(some, slots_ref, n_sub, masked_ref, hot_ref, [first_ref, second_ref])

    for lines in range(min(2, cap // LANES), cap // LANES + 1):
        some = tiles(lines)[0]
        pl.when((live == lines) & jnp.logical_not(is_early()))(functools.partial(late, some))
        pl.when((live == lines) & is_early())(functools.partial(early, some[1:]))


def second_kernel(
    n_sub, masked_ref, slots_ref, count_ref, _, second_ref, out_hbm, hot_ref, zero_ref, sems
):
    my_rows, cap = second_ref.shape
    live = live_lines(count_ref[0], cap)

    def make(lines):
        dead = slice(lines * LANES, cap)
        copies = [
            pltpu.make_async_copy(
                zero_ref.at[:, dead], out_hbm.at[pl.ds(b * BLOCK, BLOCK), dead], sems.at[b]
            )
            for b in range(my_rows // BLOCK)
            if lines * LANES < cap
        ]
        if copies:
            zero_ref[...] = jnp.zeros_like(zero_ref)
        for copy in copies:
            copy.start()
        pick_columns(tiles(lines)[1], slots_ref, n_sub, masked_ref, hot_ref, [None, second_ref])
        for copy in copies:
            copy.wait()

    for lines in range(min(2, cap // LANES), cap // LANES + 1):
        pl.when(live == lines)(functools.partial(make, lines))


def flows_kernel(n_shares, *refs):
    share_refs, refs = refs[:n_shares], refs[n_shares:]
    base_ref, first_ref, second_ref, count_ref, _, out_hbm, post_ref, out_sems = refs
    my_rows, cap = post_ref.shape
    my_blocks = my_rows // BLOCK
    rows = dense_rows(cap)
    total = share_refs[0][...]
    for ref in share_refs[1:]:
        total = total + ref[...]
    cross_first, cross_second, flow_first, flow_second = (
        total[i * rows : (i + 1) * rows] for i in range(4)
    )
    determinant = 1.0 - cross_first * cross_second
    shift_first = (flow_first + cross_first * flow_second) / determinant
    shift_second = (flow_second + cross_second * flow_first) / determinant
    my_block = pl.multiple_of(lax.axis_index("sub") * my_blocks, my_blocks)
    base = jnp.swapaxes(base_ref[pl.ds(my_block, my_blocks), :], 0, 1)

    def write(lines):
        live = [iota((1, LANES), 1) + line * LANES < count_ref[0] for line in lines]
        weights = [
            [
                jnp.broadcast_to(shift[line : line + 1], (BLOCK, LANES)).astype(BF16)
                for line in lines
            ]
            for shift in (shift_first, shift_second)
        ]
        wide = slice(0, len(lines) * LANES)
        out_copies = []
        for b in range(my_blocks):
            block = slice(b * BLOCK, (b + 1) * BLOCK)
            start = jnp.broadcast_to(base[:, b : b + 1], (BLOCK, LANES))
            for line in lines:
                lanes = slice(line * LANES, (line + 1) * LANES)
                change = (
                    weights[0][line] * first_ref[block, lanes]
                    + weights[1][line] * second_ref[block, lanes]
                )
                post_ref[block, lanes] = jnp.where(
                    live[line], start + change.astype(F32), 0.0
                ).astype(BF16)
            out_copies.append(
                pltpu.make_async_copy(
                    post_ref.at[block, wide], out_hbm.at[block, wide], out_sems.at[b]
                )
            )
            out_copies[-1].start()
        for copy in out_copies:
            copy.wait()

    live_count = live_lines(count_ref[0], cap)
    for lines in range(min(2, cap // LANES), cap // LANES + 1):
        pl.when(live_count == lines)(functools.partial(write, range(lines)))


def partners(n_mon):
    half = n_mon // 2
    if n_mon & (n_mon - 1):
        return [[(m + k) % n_mon for m in range(n_mon)] for k in range(1, n_mon)]
    across = [
        [m ^ (half + k) if m < half else m ^ (n_mon - 1 - k) for m in range(n_mon)]
        for k in range(half)
    ]
    return across + [[m ^ k for m in range(n_mon)] for k in range(half - 1, 0, -1)]


def from_other_mon(share, n_mon, n_sub):
    return [
        lax.ppermute(
            share,
            ("mon", "sub"),
            [
                (m * n_sub + s, to[m] * n_sub + n_sub - 1 - s)
                for m in range(n_mon)
                for s in range(n_sub)
            ],
        )
        for to in reversed(partners(n_mon))
    ]


def on_device(dfactors, block_mask, base_flow, branch_row, pair_slots, pair_counts):
    rows_dev, cols = dfactors.shape
    blocks = rows_dev // BLOCK
    candidates = branch_row.shape[0]
    cap = pair_slots.shape[0]
    rows = dense_rows(cap)
    n_sub = lax.axis_size("sub")
    my_rows = rows_dev // n_sub
    slots = pair_slots.T
    base = base_flow.reshape(blocks, BLOCK)
    table = branch_row.reshape(candidates // LANES, LANES)
    hbm = pl.BlockSpec(memory_space=pltpu.HBM)
    in_hbm = functools.partial(pltpu.with_memory_space_constraint, memory_space=pltpu.HBM)
    in_vmem = functools.partial(pltpu.with_memory_space_constraint, memory_space=pltpu.VMEM)
    vmem = pl.BlockSpec(memory_space=pltpu.VMEM)
    smem = pl.BlockSpec(memory_space=pltpu.SMEM)
    params = pltpu.CompilerParams(vmem_limit_bytes=VMEM_LIMIT)
    rings = [[(i, (i + s) % n_sub) for i in range(n_sub)] for s in range(n_sub)]

    factors = [dfactors] + [lax.ppermute(dfactors, "sub", ring) for ring in rings[1:]]

    chunks = rows_dev // chunk_of(rows_dev, 512)
    note_rows = 4 * rows + (cols // LANES) * (my_rows // BLOCK)
    outs = pl.pallas_call(
        functools.partial(values_kernel, n_sub),
        out_shape=[pltpu.VMEM((4 * rows, LANES), F32)]
        + [pltpu.VMEM((note_rows, LANES), F32)] * (n_sub - 1)
        + [
            pltpu.VMEM((rows_dev, cols), BF16),
            pltpu.VMEM((blocks, cols), I32),
            pltpu.VMEM((blocks, BLOCK), F32),
            pltpu.VMEM((2, cap), I32),
        ],
        in_specs=[hbm] * 5,
        out_specs=[vmem] * (n_sub + 4),
        scratch_shapes=[
            pltpu.VMEM((candidates // LANES, LANES), I32),
            pltpu.VMEM((ENDS, 2 * cap), BF16),
            pltpu.VMEM((cols, ENDS), BF16),
            pltpu.VMEM((2 * rows, LANES), F32),
            pltpu.SemaphoreType.DMA((4,)),
            pltpu.SemaphoreType.DMA((chunks,)),
        ],
        compiler_params=params,
        cost_estimate=pl.CostEstimate(
            flops=2 * rows_dev * cols * ENDS, bytes_accessed=rows_dev * cols * 2, transcendentals=0
        ),
        name="pair_values",
    )(*map(in_hbm, (dfactors, block_mask, base, table, slots)))
    share, notes = outs[0], outs[1:n_sub]
    factors[0], block_mask, base, slots = outs[n_sub:]

    notes = [lax.ppermute(note, "sub", ring) for note, ring in zip(notes, rings[1:])]
    share = functools.reduce(jnp.add, [share] + [note[: 4 * rows] for note in notes])
    hot = pltpu.VMEM((-(-cap // (2 * LANES)), n_sub * cols, 2 * LANES), BF16)
    columns = pltpu.VMEM((my_rows, cap), BF16)
    masked = pltpu.VMEM((my_rows, n_sub * cols), BF16)
    columns_cost = pl.CostEstimate(
        flops=2 * my_rows * cols * n_sub * cap,
        bytes_accessed=my_rows * (cols * n_sub + cap) * 2,
        transcendentals=0,
    )
    factors = [*factors, *notes, block_mask]
    masked, first, share = pl.pallas_call(
        functools.partial(early_kernel, n_sub),
        out_shape=[masked, columns, pltpu.VMEM(share.shape, F32)],
        in_specs=[vmem] * (len(factors) + 2),
        out_specs=[vmem] * 3,
        scratch_shapes=[hot],
        compiler_params=params,
        name="early_columns",
    )(*map(in_vmem, (*factors, slots, share)))
    shares = [share, *from_other_mon(share, lax.axis_size("mon"), n_sub)]

    masked, first, second = pl.pallas_call(
        functools.partial(first_kernel, n_sub),
        out_shape=[pltpu.VMEM(masked.shape, BF16), columns, columns],
        in_specs=[vmem] * (len(factors) + 1) + [smem] + [vmem] * 2,
        out_specs=[vmem] * 3,
        input_output_aliases={len(factors) + 2: 0, len(factors) + 3: 1},
        scratch_shapes=[hot],
        compiler_params=params,
        cost_estimate=columns_cost,
        name="first_columns",
    )(*map(in_vmem, (*factors, slots)), pair_counts, *map(in_vmem, (masked, first)))
    second, out = pl.pallas_call(
        functools.partial(second_kernel, n_sub),
        out_shape=[columns, pltpu.HBM((my_rows, cap), BF16)],
        in_specs=[vmem] * 2 + [smem, vmem],
        out_specs=[vmem, hbm],
        input_output_aliases={3: 0},
        scratch_shapes=[
            hot,
            pltpu.VMEM((BLOCK, cap), BF16),
            pltpu.SemaphoreType.DMA((my_rows // BLOCK,)),
        ],
        compiler_params=params,
        cost_estimate=columns_cost,
        name="second_columns",
    )(*map(in_vmem, (masked, slots)), pair_counts, in_vmem(second))
    return pl.pallas_call(
        functools.partial(flows_kernel, len(shares)),
        out_shape=jax.ShapeDtypeStruct((my_rows, cap), BF16),
        in_specs=[vmem] * (len(shares) + 3) + [smem, hbm],
        out_specs=hbm,
        input_output_aliases={len(shares) + 4: 0},
        scratch_shapes=[
            pltpu.VMEM((my_rows, cap), BF16),
            pltpu.SemaphoreType.DMA((my_rows // BLOCK,)),
        ],
        compiler_params=params,
        cost_estimate=pl.CostEstimate(
            flops=6 * my_rows * cap, bytes_accessed=my_rows * cap * 2, transcendentals=0
        ),
        name="post_flows",
    )(*map(in_vmem, (*shares, base, first, second)), pair_counts, in_hbm(out))


def solution(mesh):
    return jax.shard_map(
        on_device,
        mesh=mesh,
        in_specs=(
            P("mon", "sub"),
            P("mon", "sub"),
            P("mon"),
            P(),
            P(("grp", "pair"), None),
            P(("grp", "pair")),
        ),
        out_specs=P(("mon", "sub"), ("grp", "pair")),
        check_vma=False,
    )
```

```python
import functools

import jax
import jax.numpy as jnp
from jax import lax
from jax.experimental import pallas as pl
from jax.experimental.pallas import tpu as pltpu
from jax.sharding import PartitionSpec as P

BLOCK = 128
LANES = 128
SUBLANES = 8
ENDS = 256
VMEM_LIMIT = 16 * 1024 * 1024
F32 = jnp.float32
BF16 = jnp.bfloat16
I32 = jnp.int32


def chunk_of(total, want):
    size = min(total, want)
    while total % size:
        size -= BLOCK
    return size


def dense_rows(cap):
    return -(-cap // (LANES * SUBLANES)) * SUBLANES


def one_hot(hit):
    return jnp.where(hit, 1.0, 0.0).astype(BF16)


def iota(shape, axis):
    return lax.broadcasted_iota(I32, shape, axis)


def dense(line):
    cap = line.shape[1]
    rows = dense_rows(cap)
    pieces = [line[:, c : c + LANES] for c in range(0, cap, LANES)]
    if len(pieces) < rows:
        pieces.append(jnp.zeros((rows - len(pieces), LANES), line.dtype))
    return jnp.concatenate(pieces, axis=0)


def look_up(table, index):
    high, low = index >> 7, index & 127
    found = jnp.zeros(index.shape, table.dtype)
    for b in range(table.shape[0]):
        line = jnp.broadcast_to(table[b : b + 1], index.shape)
        value = jnp.take_along_axis(line, low, axis=1, mode="promise_in_bounds")
        found = jnp.where(high == b, value, found)
    return found


def values_kernel(
    n_sub, d_hbm, mask_hbm, base_hbm, rows_hbm, slots_hbm, *refs
):
    share_ref, *note_refs = refs[:n_sub]
    (
        d_ref, mask_ref, base_ref, slots_ref, rows_ref, perm_ref, hot_ref, cross_ref, sems, d_sems
    ) = refs[n_sub:]
    rows_dev, cols = d_ref.shape
    chunks = d_sems.shape[0]
    chunk = rows_dev // chunks
    cap = slots_ref.shape[1]
    lines = cap // LANES
    rows = dense_rows(cap)
    sub_index = lax.axis_index("sub")
    small = [
        pltpu.make_async_copy(src, dst, sems.at[i])
        for i, (src, dst) in enumerate(
            [(slots_hbm, slots_ref), (rows_hbm, rows_ref), (base_hbm, base_ref), (mask_hbm, mask_ref)]
        )
    ]
    large = [
        pltpu.make_async_copy(
            d_hbm.at[pl.ds(i * chunk, chunk)], d_ref.at[pl.ds(i * chunk, chunk)], d_sems.at[i]
        )
        for i in range(chunks)
    ]
    for copy in small + large:
        copy.start()

    small[0].wait()
    small[1].wait()
    first, second = dense(slots_ref[0:1, :]), dense(slots_ref[1:2, :])
    table = rows_ref[...]
    row = jnp.concatenate([look_up(table, first), look_up(table, second)], axis=0)
    row = row - lax.axis_index("mon") * rows_dev
    col = jnp.concatenate([second, first], axis=0) - sub_index * cols
    used = lax.rem(iota(row.shape, 0), rows) < lines
    here = used & (row >= 0) & (row < rows_dev) & (col >= 0) & (col < cols)

    flags = one_hot(here)
    height = flags.shape[0]
    above = jnp.dot(
        one_hot(iota((height, height), 1) < iota((height, height), 0)),
        flags,
        preferred_element_type=F32,
    ).astype(BF16)
    place = jnp.dot(
        jnp.concatenate([flags, above], axis=1),
        jnp.concatenate(
            [
                one_hot(iota((LANES, LANES), 0) <= iota((LANES, LANES), 1)),
                jnp.ones((LANES, LANES), BF16),
            ],
            axis=0,
        ),
        preferred_element_type=F32,
    ).astype(I32)
    place = jnp.where(here, place - 1, -1)
    digits = [(x >> shift) & 255 for x in (col, row) for shift in (0, 8)]
    order = [half * rows + b for half in range(2) for b in range(lines)]
    ends = jnp.concatenate(
        [jnp.concatenate([x[r : r + 1] for x in digits], axis=0) for r in order], axis=1
    )
    ends = ends.astype(F32).astype(BF16)

    def pick(start, copies=()):
        for at, r in enumerate(order):
            perm_ref[:, at * LANES : (at + 1) * LANES] = one_hot(
                iota((ENDS, LANES), 0) + start == place[r : r + 1]
            )
        packed = lax.dot_general(
            ends, perm_ref[...], (((1,), (1,)), ((), ())), preferred_element_type=F32
        ).astype(I32)
        end_col = packed[0:1] + (packed[1:2] << 8)
        end_row = packed[2:3] + (packed[3:4] << 8)
        hot_ref[...] = one_hot(iota((cols, ENDS), 0) == end_col)
        for copy in copies:
            copy.wait()
        keep = jnp.dot(
            mask_ref[...].astype(F32).astype(BF16), hot_ref[...], preferred_element_type=F32
        )
        keep = jnp.sum(
            jnp.where(iota(keep.shape, 0) == (end_row >> 7), keep, 0.0), axis=0, keepdims=True
        )
        total = jnp.zeros((SUBLANES, ENDS), F32)
        for i in range(chunks):
            values = jnp.dot(
                d_ref[i * chunk : (i + 1) * chunk, :], hot_ref[...], preferred_element_type=F32
            )
            picked = jnp.where(iota((chunk, ENDS), 0) + i * chunk == end_row, values, 0.0)
            total += jnp.sum(picked.reshape(chunk // SUBLANES, SUBLANES, ENDS), axis=0)
        value = jnp.sum(total, axis=0, keepdims=True) * keep
        value = jnp.concatenate([value[:, q : q + LANES] for q in range(0, ENDS, LANES)], axis=0)
        return look_up(value, place - start)

    def put(cross, flow):
        for ref in (share_ref, *note_refs):
            ref[: 2 * rows, :] = cross
            ref[2 * rows : 4 * rows, :] = flow

    cross = pick(0, small[2:] + large)
    flow = jnp.where(sub_index == 0, look_up(base_ref[...], row), 0.0)
    put(cross, flow)
    my_blocks = mask_ref.shape[0] // n_sub
    for s, ref in enumerate(note_refs, 1):
        block = pl.multiple_of(lax.rem(sub_index + s, n_sub) * my_blocks, my_blocks)
        for c in range(cols // LANES):
            at = 4 * rows + c * my_blocks
            ref[at : at + my_blocks, :] = mask_ref[
                pl.ds(block, my_blocks), c * LANES : (c + 1) * LANES
            ].astype(F32)
    count = jnp.max(place) + 1

    @pl.when(count > ENDS)
    def _():
        cross_ref[...] = cross

        def more(i, _):
            cross_ref[...] += pick(i * ENDS)
            return 0

        lax.fori_loop(1, pl.cdiv(count, ENDS), more, 0)
        put(cross_ref[...], flow)


def column_picker(n_sub, slots_ref, end, masked_ref, hot_ref, out_ref):
    parts, _, width = hot_ref.shape
    cols = masked_ref.shape[1] // n_sub

    def build(part):
        if part == parts:
            return
        slot = slots_ref[end : end + 1, part * width : (part + 1) * width]
        for s in range(n_sub):
            start = lax.rem(lax.axis_index("sub") + n_sub - s, n_sub) * cols
            hot_ref[part, s * cols : (s + 1) * cols, :] = one_hot(
                iota((cols, width), 0) == slot - start
            )

    def multiply(part):
        out_ref[:, part * width : (part + 1) * width] = jnp.dot(
            masked_ref[...], hot_ref[part], preferred_element_type=F32
        ).astype(BF16)

    return build, multiply


def live_parts(count, hot_ref):
    parts, _, width = hot_ref.shape
    return jnp.minimum((count + width - 1) // width, parts)


def is_early():
    return lax.axis_index("mon") < lax.axis_size("mon") // 2


def mask_factors(n_sub, refs, masked_ref):
    d_refs, note_refs, mask_ref = refs[:n_sub], refs[n_sub:-1], refs[-1]
    my_rows, all_cols = masked_ref.shape
    cols = all_cols // n_sub
    my_blocks = my_rows // BLOCK
    sub_index = lax.axis_index("sub")
    my_start = pl.multiple_of(sub_index * my_rows, my_rows)
    my_block = pl.multiple_of(sub_index * my_blocks, my_blocks)
    for s in range(n_sub):
        if s == 0:
            keep = mask_ref[pl.ds(my_block, my_blocks), :].astype(F32)
        else:
            ref = note_refs[s - 1]
            ends = range(ref.shape[0] - (cols // LANES) * my_blocks, ref.shape[0], my_blocks)
            keep = jnp.concatenate([ref[at : at + my_blocks, :] for at in ends], axis=1)
        keep = keep.astype(BF16)
        for b in range(my_blocks):
            masked_ref[b * BLOCK : (b + 1) * BLOCK, s * cols : (s + 1) * cols] = (
                d_refs[s][pl.ds(my_start + b * BLOCK, BLOCK), :] * keep[b : b + 1]
            )


def early_kernel(n_sub, *refs):
    *factor_refs, slots_ref, share_ref, masked_ref, first_ref, shared_ref, hot_ref = refs
    shared_ref[...] = share_ref[...]
    build, multiply = column_picker(n_sub, slots_ref, 0, masked_ref, hot_ref, first_ref)

    @pl.when(is_early())
    def _():
        mask_factors(n_sub, factor_refs, masked_ref)
        build(0)
        multiply(0)


def first_kernel(n_sub, *refs):
    *factor_refs, slots_ref, count_ref, _, _, masked_ref, first_ref, hot_ref = refs
    build, multiply = column_picker(n_sub, slots_ref, 0, masked_ref, hot_ref, first_ref)
    live = live_parts(count_ref[0], hot_ref)

    @pl.when(jnp.logical_not(is_early()))
    def _():
        mask_factors(n_sub, factor_refs, masked_ref)
        build(0)
        multiply(0)
        build(1)

    @pl.when(is_early())
    def _():
        build(1)

    for part in range(1, hot_ref.shape[0]):

        @pl.when(part < live)
        def _():
            multiply(part)
            build(part + 1)


def second_kernel(n_sub, masked_ref, slots_ref, count_ref, second_ref, hot_ref):
    build, multiply = column_picker(n_sub, slots_ref, 1, masked_ref, hot_ref, second_ref)
    live = live_parts(count_ref[0], hot_ref)
    build(0)
    multiply(0)
    build(1)
    for part in range(1, hot_ref.shape[0]):

        @pl.when(part < live)
        def _():
            multiply(part)
            build(part + 1)


def flows_kernel(n_shares, *refs):
    share_refs, refs = refs[:n_shares], refs[n_shares:]
    base_ref, first_ref, second_ref, count_ref, out_hbm, post_ref, out_sems = refs
    my_rows, cap = post_ref.shape
    my_blocks = my_rows // BLOCK
    rows = dense_rows(cap)
    total = share_refs[0][...]
    for ref in share_refs[1:]:
        total = total + ref[...]
    cross_first, cross_second, flow_first, flow_second = (
        total[i * rows : (i + 1) * rows] for i in range(4)
    )
    determinant = 1.0 - cross_first * cross_second
    shift_first = (flow_first + cross_first * flow_second) / determinant
    shift_second = (flow_second + cross_second * flow_first) / determinant
    my_block = pl.multiple_of(lax.axis_index("sub") * my_blocks, my_blocks)
    base = jnp.swapaxes(base_ref[pl.ds(my_block, my_blocks), :], 0, 1)

    lines = range(cap // LANES)
    live = [iota((1, LANES), 1) + line * LANES < count_ref[0] for line in lines]
    weights = [
        [
            jnp.broadcast_to(shift[line : line + 1], (BLOCK, LANES)).astype(BF16)
            for line in lines
        ]
        for shift in (shift_first, shift_second)
    ]
    out_copies = []
    for b in range(my_blocks):
        block = slice(b * BLOCK, (b + 1) * BLOCK)
        start = jnp.broadcast_to(base[:, b : b + 1], (BLOCK, LANES))
        for line in lines:
            lanes = slice(line * LANES, (line + 1) * LANES)
            change = (
                weights[0][line] * first_ref[block, lanes]
                + weights[1][line] * second_ref[block, lanes]
            )
            post_ref[block, lanes] = jnp.where(
                live[line], start + change.astype(F32), 0.0
            ).astype(BF16)
        out_copies.append(
            pltpu.make_async_copy(post_ref.at[block], out_hbm.at[block], out_sems.at[b])
        )
        out_copies[-1].start()
    for copy in out_copies:
        copy.wait()


def partners(n_mon):
    half = n_mon // 2
    if n_mon & (n_mon - 1):
        return [[(m + k) % n_mon for m in range(n_mon)] for k in range(1, n_mon)]
    across = [
        [m ^ (half + k) if m < half else m ^ (n_mon - 1 - k) for m in range(n_mon)]
        for k in range(half)
    ]
    return across + [[m ^ k for m in range(n_mon)] for k in range(half - 1, 0, -1)]


def from_other_mon(share, n_mon, n_sub):
    return [
        lax.ppermute(
            share,
            ("mon", "sub"),
            [
                (m * n_sub + s, to[m] * n_sub + n_sub - 1 - s)
                for m in range(n_mon)
                for s in range(n_sub)
            ],
        )
        for to in reversed(partners(n_mon))
    ]


def on_device(dfactors, block_mask, base_flow, branch_row, pair_slots, pair_counts):
    rows_dev, cols = dfactors.shape
    blocks = rows_dev // BLOCK
    candidates = branch_row.shape[0]
    cap = pair_slots.shape[0]
    rows = dense_rows(cap)
    n_sub = lax.axis_size("sub")
    my_rows = rows_dev // n_sub
    slots = pair_slots.T
    base = base_flow.reshape(blocks, BLOCK)
    table = branch_row.reshape(candidates // LANES, LANES)
    hbm = pl.BlockSpec(memory_space=pltpu.HBM)
    in_hbm = functools.partial(pltpu.with_memory_space_constraint, memory_space=pltpu.HBM)
    in_vmem = functools.partial(pltpu.with_memory_space_constraint, memory_space=pltpu.VMEM)
    vmem = pl.BlockSpec(memory_space=pltpu.VMEM)
    smem = pl.BlockSpec(memory_space=pltpu.SMEM)
    params = pltpu.CompilerParams(vmem_limit_bytes=VMEM_LIMIT)
    rings = [[(i, (i + s) % n_sub) for i in range(n_sub)] for s in range(n_sub)]

    factors = [dfactors] + [lax.ppermute(dfactors, "sub", ring) for ring in rings[1:]]

    chunks = rows_dev // chunk_of(rows_dev, 512)
    note_rows = 4 * rows + (cols // LANES) * (my_rows // BLOCK)
    outs = pl.pallas_call(
        functools.partial(values_kernel, n_sub),
        out_shape=[pltpu.VMEM((4 * rows, LANES), F32)]
        + [pltpu.VMEM((note_rows, LANES), F32)] * (n_sub - 1)
        + [
            pltpu.VMEM((rows_dev, cols), BF16),
            pltpu.VMEM((blocks, cols), I32),
            pltpu.VMEM((blocks, BLOCK), F32),
            pltpu.VMEM((2, cap), I32),
        ],
        in_specs=[hbm] * 5,
        out_specs=[vmem] * (n_sub + 4),
        scratch_shapes=[
            pltpu.VMEM((candidates // LANES, LANES), I32),
            pltpu.VMEM((ENDS, 2 * cap), BF16),
            pltpu.VMEM((cols, ENDS), BF16),
            pltpu.VMEM((2 * rows, LANES), F32),
            pltpu.SemaphoreType.DMA((4,)),
            pltpu.SemaphoreType.DMA((chunks,)),
        ],
        compiler_params=params,
        cost_estimate=pl.CostEstimate(
            flops=2 * rows_dev * cols * ENDS, bytes_accessed=rows_dev * cols * 2, transcendentals=0
        ),
        name="pair_values",
    )(*map(in_hbm, (dfactors, block_mask, base, table, slots)))
    share, notes = outs[0], outs[1:n_sub]
    factors[0], block_mask, base, slots = outs[n_sub:]

    notes = [lax.ppermute(note, "sub", ring) for note, ring in zip(notes, rings[1:])]
    share = functools.reduce(jnp.add, [share] + [note[: 4 * rows] for note in notes])
    width = chunk_of(cap, 256)
    hot = pltpu.VMEM((cap // width, n_sub * cols, width), BF16)
    columns = pltpu.VMEM((my_rows, cap), BF16)
    masked = pltpu.VMEM((my_rows, n_sub * cols), BF16)
    columns_cost = pl.CostEstimate(
        flops=2 * my_rows * cols * n_sub * cap,
        bytes_accessed=my_rows * (cols * n_sub + cap) * 2,
        transcendentals=0,
    )
    factors = [*factors, *notes, block_mask]
    masked, first, share = pl.pallas_call(
        functools.partial(early_kernel, n_sub),
        out_shape=[masked, columns, pltpu.VMEM(share.shape, F32)],
        in_specs=[vmem] * (len(factors) + 2),
        out_specs=[vmem] * 3,
        scratch_shapes=[hot],
        compiler_params=params,
        name="early_columns",
    )(*map(in_vmem, (*factors, slots, share)))
    shares = [share, *from_other_mon(share, lax.axis_size("mon"), n_sub)]

    masked, first = pl.pallas_call(
        functools.partial(first_kernel, n_sub),
        out_shape=[pltpu.VMEM(masked.shape, BF16), columns],
        in_specs=[vmem] * (len(factors) + 1) + [smem] + [vmem] * 2,
        out_specs=[vmem] * 2,
        input_output_aliases={len(factors) + 2: 0, len(factors) + 3: 1},
        scratch_shapes=[hot],
        compiler_params=params,
        cost_estimate=columns_cost,
        name="first_columns",
    )(*map(in_vmem, (*factors, slots)), pair_counts, *map(in_vmem, (masked, first)))
    second = pl.pallas_call(
        functools.partial(second_kernel, n_sub),
        out_shape=columns,
        in_specs=[vmem] * 2 + [smem],
        out_specs=vmem,
        scratch_shapes=[hot],
        compiler_params=params,
        cost_estimate=columns_cost,
        name="second_columns",
    )(*map(in_vmem, (masked, slots)), pair_counts)
    return pl.pallas_call(
        functools.partial(flows_kernel, len(shares)),
        out_shape=jax.ShapeDtypeStruct((my_rows, cap), BF16),
        in_specs=[vmem] * (len(shares) + 3) + [smem],
        out_specs=hbm,
        scratch_shapes=[
            pltpu.VMEM((my_rows, cap), BF16),
            pltpu.SemaphoreType.DMA((my_rows // BLOCK,)),
        ],
        compiler_params=params,
        cost_estimate=pl.CostEstimate(
            flops=6 * my_rows * cap, bytes_accessed=my_rows * cap * 2, transcendentals=0
        ),
        name="post_flows",
    )(*map(in_vmem, (*shares, base, first, second)), pair_counts)


def solution(mesh):
    return jax.shard_map(
        on_device,
        mesh=mesh,
        in_specs=(
            P("mon", "sub"),
            P("mon", "sub"),
            P("mon"),
            P(),
            P(("grp", "pair"), None),
            P(("grp", "pair")),
        ),
        out_specs=P(("mon", "sub"), ("grp", "pair")),
        check_vma=False,
    )
```

```python
import functools

import jax
import jax.numpy as jnp
from jax import lax
from jax.experimental import pallas as pl
from jax.experimental.pallas import tpu as pltpu
from jax.sharding import PartitionSpec as P

BLOCK = 128
LANES = 128
SUBLANES = 8
ENDS = 256
VMEM_LIMIT = 16 * 1024 * 1024
F32 = jnp.float32
BF16 = jnp.bfloat16
I32 = jnp.int32


def chunk_of(total, want):
    size = min(total, want)
    while total % size:
        size -= BLOCK
    return size


def dense_rows(cap):
    return -(-cap // (LANES * SUBLANES)) * SUBLANES


def one_hot(hit):
    return jnp.where(hit, 1.0, 0.0).astype(BF16)


def iota(shape, axis):
    return lax.broadcasted_iota(I32, shape, axis)


def dense(line):
    cap = line.shape[1]
    rows = dense_rows(cap)
    pieces = [line[:, c : c + LANES] for c in range(0, cap, LANES)]
    if len(pieces) < rows:
        pieces.append(jnp.zeros((rows - len(pieces), LANES), line.dtype))
    return jnp.concatenate(pieces, axis=0)


def look_up(table, index):
    high, low = index >> 7, index & 127
    found = jnp.zeros(index.shape, table.dtype)
    for b in range(table.shape[0]):
        line = jnp.broadcast_to(table[b : b + 1], index.shape)
        value = jnp.take_along_axis(line, low, axis=1, mode="promise_in_bounds")
        found = jnp.where(high == b, value, found)
    return found


def values_kernel(
    n_sub, d_hbm, mask_hbm, base_hbm, rows_hbm, slots_hbm, *refs
):
    share_ref, *note_refs = refs[:n_sub]
    (
        d_ref, mask_ref, base_ref, slots_ref, rows_ref, perm_ref, hot_ref, cross_ref, sems, d_sems
    ) = refs[n_sub:]
    rows_dev, cols = d_ref.shape
    chunks = d_sems.shape[0]
    chunk = rows_dev // chunks
    cap = slots_ref.shape[1]
    lines = cap // LANES
    rows = dense_rows(cap)
    sub_index = lax.axis_index("sub")
    small = [
        pltpu.make_async_copy(src, dst, sems.at[i])
        for i, (src, dst) in enumerate(
            [(slots_hbm, slots_ref), (rows_hbm, rows_ref), (base_hbm, base_ref), (mask_hbm, mask_ref)]
        )
    ]
    large = [
        pltpu.make_async_copy(
            d_hbm.at[pl.ds(i * chunk, chunk)], d_ref.at[pl.ds(i * chunk, chunk)], d_sems.at[i]
        )
        for i in range(chunks)
    ]
    for copy in small + large:
        copy.start()

    small[0].wait()
    small[1].wait()
    first, second = dense(slots_ref[0:1, :]), dense(slots_ref[1:2, :])
    table = rows_ref[...]
    row = jnp.concatenate([look_up(table, first), look_up(table, second)], axis=0)
    row = row - lax.axis_index("mon") * rows_dev
    col = jnp.concatenate([second, first], axis=0) - sub_index * cols
    used = lax.rem(iota(row.shape, 0), rows) < lines
    here = used & (row >= 0) & (row < rows_dev) & (col >= 0) & (col < cols)

    flags = one_hot(here)
    height = flags.shape[0]
    above = jnp.dot(
        one_hot(iota((height, height), 1) < iota((height, height), 0)),
        flags,
        preferred_element_type=F32,
    ).astype(BF16)
    place = jnp.dot(
        jnp.concatenate([flags, above], axis=1),
        jnp.concatenate(
            [
                one_hot(iota((LANES, LANES), 0) <= iota((LANES, LANES), 1)),
                jnp.ones((LANES, LANES), BF16),
            ],
            axis=0,
        ),
        preferred_element_type=F32,
    ).astype(I32)
    place = jnp.where(here, place - 1, -1)
    digits = [(x >> shift) & 255 for x in (col, row) for shift in (0, 8)]
    order = [half * rows + b for half in range(2) for b in range(lines)]
    ends = jnp.concatenate(
        [jnp.concatenate([x[r : r + 1] for x in digits], axis=0) for r in order], axis=1
    )
    ends = ends.astype(F32).astype(BF16)

    def pick(start, copies=()):
        for at, r in enumerate(order):
            perm_ref[:, at * LANES : (at + 1) * LANES] = one_hot(
                iota((ENDS, LANES), 0) + start == place[r : r + 1]
            )
        packed = lax.dot_general(
            ends, perm_ref[...], (((1,), (1,)), ((), ())), preferred_element_type=F32
        ).astype(I32)
        end_col = packed[0:1] + (packed[1:2] << 8)
        end_row = packed[2:3] + (packed[3:4] << 8)
        hot_ref[...] = one_hot(iota((cols, ENDS), 0) == end_col)
        for copy in copies:
            copy.wait()
        keep = jnp.dot(
            mask_ref[...].astype(F32).astype(BF16), hot_ref[...], preferred_element_type=F32
        )
        keep = jnp.sum(
            jnp.where(iota(keep.shape, 0) == (end_row >> 7), keep, 0.0), axis=0, keepdims=True
        )
        total = jnp.zeros((SUBLANES, ENDS), F32)
        for i in range(chunks):
            values = jnp.dot(
                d_ref[i * chunk : (i + 1) * chunk, :], hot_ref[...], preferred_element_type=F32
            )
            picked = jnp.where(iota((chunk, ENDS), 0) + i * chunk == end_row, values, 0.0)
            total += jnp.sum(picked.reshape(chunk // SUBLANES, SUBLANES, ENDS), axis=0)
        value = jnp.sum(total, axis=0, keepdims=True) * keep
        value = jnp.concatenate([value[:, q : q + LANES] for q in range(0, ENDS, LANES)], axis=0)
        return look_up(value, place - start)

    def put(cross, flow):
        for ref in (share_ref, *note_refs):
            ref[: 2 * rows, :] = cross
            ref[2 * rows : 4 * rows, :] = flow

    cross = pick(0, small[2:] + large)
    flow = jnp.where(sub_index == 0, look_up(base_ref[...], row), 0.0)
    put(cross, flow)
    my_blocks = mask_ref.shape[0] // n_sub
    for s, ref in enumerate(note_refs, 1):
        block = pl.multiple_of(lax.rem(sub_index + s, n_sub) * my_blocks, my_blocks)
        for c in range(cols // LANES):
            at = 4 * rows + c * my_blocks
            ref[at : at + my_blocks, :] = mask_ref[
                pl.ds(block, my_blocks), c * LANES : (c + 1) * LANES
            ].astype(F32)
    count = jnp.max(place) + 1

    @pl.when(count > ENDS)
    def _():
        cross_ref[...] = cross

        def more(i, _):
            cross_ref[...] += pick(i * ENDS)
            return 0

        lax.fori_loop(1, pl.cdiv(count, ENDS), more, 0)
        put(cross_ref[...], flow)


def pick_columns(parts, slot, starts, cols, masked_ref, hot_ref, out_ref):
    width = hot_ref.shape[2]
    my_rows = masked_ref.shape[0]
    half = chunk_of(my_rows, my_rows // 2)
    for part in parts:
        lanes = slice(part * width, (part + 1) * width)
        for s, start in enumerate(starts):
            hot_ref[part, s * cols : (s + 1) * cols, :] = one_hot(
                iota((cols, width), 0) == slot[:, lanes] - start
            )
        for row in range(0, my_rows, half):
            out_ref[row : row + half, lanes] = jnp.dot(
                masked_ref[row : row + half, :], hot_ref[part], preferred_element_type=F32
            ).astype(BF16)


def live_parts(count, hot_ref):
    parts, _, width = hot_ref.shape
    return jnp.minimum((count + width - 1) // width, parts)


def is_early():
    return lax.axis_index("mon") < lax.axis_size("mon") // 2


def column_starts(n_sub, cols):
    return [lax.rem(lax.axis_index("sub") + n_sub - s, n_sub) * cols for s in range(n_sub)]


def mask_factors(n_sub, refs, masked_ref):
    d_refs, note_refs, mask_ref = refs[:n_sub], refs[n_sub:-1], refs[-1]
    my_rows, all_cols = masked_ref.shape
    cols = all_cols // n_sub
    my_blocks = my_rows // BLOCK
    sub_index = lax.axis_index("sub")
    my_start = pl.multiple_of(sub_index * my_rows, my_rows)
    my_block = pl.multiple_of(sub_index * my_blocks, my_blocks)
    for s in range(n_sub):
        if s == 0:
            keep = mask_ref[pl.ds(my_block, my_blocks), :].astype(F32)
        else:
            ref = note_refs[s - 1]
            ends = range(ref.shape[0] - (cols // LANES) * my_blocks, ref.shape[0], my_blocks)
            keep = jnp.concatenate([ref[at : at + my_blocks, :] for at in ends], axis=1)
        keep = keep.astype(BF16)
        for b in range(my_blocks):
            masked_ref[b * BLOCK : (b + 1) * BLOCK, s * cols : (s + 1) * cols] = (
                d_refs[s][pl.ds(my_start + b * BLOCK, BLOCK), :] * keep[b : b + 1]
            )


def early_kernel(n_sub, *refs):
    *factor_refs, slots_ref, share_ref, masked_ref, first_ref, shared_ref, hot_ref = refs
    shared_ref[...] = share_ref[...]
    cols = masked_ref.shape[1] // n_sub

    @pl.when(is_early())
    def _():
        mask_factors(n_sub, factor_refs, masked_ref)
        starts = column_starts(n_sub, cols)
        pick_columns([0], slots_ref[0:1, :], starts, cols, masked_ref, hot_ref, first_ref)


def first_kernel(n_sub, *refs):
    *factor_refs, slots_ref, count_ref, _, _, masked_ref, first_ref, hot_ref = refs
    cols = masked_ref.shape[1] // n_sub
    slot = slots_ref[0:1, :]
    starts = column_starts(n_sub, cols)
    live = live_parts(count_ref[0], hot_ref)
    for n_parts in range(1, hot_ref.shape[0] + 1):

        @pl.when((live == n_parts) & jnp.logical_not(is_early()))
        def _():
            mask_factors(n_sub, factor_refs, masked_ref)
            pick_columns(range(n_parts), slot, starts, cols, masked_ref, hot_ref, first_ref)

        @pl.when((live == n_parts) & is_early())
        def _():
            pick_columns(range(1, n_parts), slot, starts, cols, masked_ref, hot_ref, first_ref)


def second_kernel(
    n_sub, masked_ref, slots_ref, count_ref, second_ref, out_hbm, hot_ref, zero_ref, sems
):
    cols = masked_ref.shape[1] // n_sub
    slot = slots_ref[1:2, :]
    starts = column_starts(n_sub, cols)
    width = zero_ref.shape[1]
    parts = hot_ref.shape[1] // width
    live = jnp.minimum((count_ref[0] + width - 1) // width, parts)
    for n_parts in range(1, parts + 1):

        @pl.when(live == n_parts)
        def _():
            copies = [
                pltpu.make_async_copy(
                    zero_ref, out_hbm.at[:, part * width : (part + 1) * width], sems.at[part]
                )
                for part in range(n_parts, parts)
            ]
            if copies:
                zero_ref[...] = jnp.zeros_like(zero_ref)
            for copy in copies:
                copy.start()
            wide = slice(0, n_parts * width)
            for s, start in enumerate(starts):
                hot_ref[s * cols : (s + 1) * cols, wide] = one_hot(
                    iota((cols, n_parts * width), 0) == slot[:, wide] - start
                )
            second_ref[:, wide] = jnp.dot(
                masked_ref[...], hot_ref[:, wide], preferred_element_type=F32
            ).astype(BF16)
            for copy in copies:
                copy.wait()


def flows_kernel(n_shares, width, *refs):
    share_refs, refs = refs[:n_shares], refs[n_shares:]
    base_ref, first_ref, second_ref, count_ref, _, out_hbm, post_ref, out_sems = refs
    my_rows, cap = post_ref.shape
    my_blocks = my_rows // BLOCK
    rows = dense_rows(cap)
    total = share_refs[0][...]
    for ref in share_refs[1:]:
        total = total + ref[...]
    cross_first, cross_second, flow_first, flow_second = (
        total[i * rows : (i + 1) * rows] for i in range(4)
    )
    determinant = 1.0 - cross_first * cross_second
    shift_first = (flow_first + cross_first * flow_second) / determinant
    shift_second = (flow_second + cross_second * flow_first) / determinant
    my_block = pl.multiple_of(lax.axis_index("sub") * my_blocks, my_blocks)
    base = jnp.swapaxes(base_ref[pl.ds(my_block, my_blocks), :], 0, 1)

    def write(lines):
        live = [iota((1, LANES), 1) + line * LANES < count_ref[0] for line in lines]
        weights = [
            [
                jnp.broadcast_to(shift[line : line + 1], (BLOCK, LANES)).astype(BF16)
                for line in lines
            ]
            for shift in (shift_first, shift_second)
        ]
        wide = slice(0, len(lines) * LANES)
        out_copies = []
        for b in range(my_blocks):
            block = slice(b * BLOCK, (b + 1) * BLOCK)
            start = jnp.broadcast_to(base[:, b : b + 1], (BLOCK, LANES))
            for line in lines:
                lanes = slice(line * LANES, (line + 1) * LANES)
                change = (
                    weights[0][line] * first_ref[block, lanes]
                    + weights[1][line] * second_ref[block, lanes]
                )
                post_ref[block, lanes] = jnp.where(
                    live[line], start + change.astype(F32), 0.0
                ).astype(BF16)
            out_copies.append(
                pltpu.make_async_copy(
                    post_ref.at[block, wide], out_hbm.at[block, wide], out_sems.at[b]
                )
            )
            out_copies[-1].start()
        for copy in out_copies:
            copy.wait()

    parts = cap // width
    live_count = jnp.minimum((count_ref[0] + width - 1) // width, parts)
    for n_parts in range(1, parts + 1):
        pl.when(live_count == n_parts)(
            functools.partial(write, range(n_parts * width // LANES))
        )


def partners(n_mon):
    half = n_mon // 2
    if n_mon & (n_mon - 1):
        return [[(m + k) % n_mon for m in range(n_mon)] for k in range(1, n_mon)]
    across = [
        [m ^ (half + k) if m < half else m ^ (n_mon - 1 - k) for m in range(n_mon)]
        for k in range(half)
    ]
    return across + [[m ^ k for m in range(n_mon)] for k in range(half - 1, 0, -1)]


def from_other_mon(share, n_mon, n_sub):
    return [
        lax.ppermute(
            share,
            ("mon", "sub"),
            [
                (m * n_sub + s, to[m] * n_sub + n_sub - 1 - s)
                for m in range(n_mon)
                for s in range(n_sub)
            ],
        )
        for to in reversed(partners(n_mon))
    ]


def on_device(dfactors, block_mask, base_flow, branch_row, pair_slots, pair_counts):
    rows_dev, cols = dfactors.shape
    blocks = rows_dev // BLOCK
    candidates = branch_row.shape[0]
    cap = pair_slots.shape[0]
    rows = dense_rows(cap)
    n_sub = lax.axis_size("sub")
    my_rows = rows_dev // n_sub
    slots = pair_slots.T
    base = base_flow.reshape(blocks, BLOCK)
    table = branch_row.reshape(candidates // LANES, LANES)
    hbm = pl.BlockSpec(memory_space=pltpu.HBM)
    in_hbm = functools.partial(pltpu.with_memory_space_constraint, memory_space=pltpu.HBM)
    in_vmem = functools.partial(pltpu.with_memory_space_constraint, memory_space=pltpu.VMEM)
    vmem = pl.BlockSpec(memory_space=pltpu.VMEM)
    smem = pl.BlockSpec(memory_space=pltpu.SMEM)
    params = pltpu.CompilerParams(vmem_limit_bytes=VMEM_LIMIT)
    rings = [[(i, (i + s) % n_sub) for i in range(n_sub)] for s in range(n_sub)]

    factors = [dfactors] + [lax.ppermute(dfactors, "sub", ring) for ring in rings[1:]]

    chunks = rows_dev // chunk_of(rows_dev, 512)
    note_rows = 4 * rows + (cols // LANES) * (my_rows // BLOCK)
    outs = pl.pallas_call(
        functools.partial(values_kernel, n_sub),
        out_shape=[pltpu.VMEM((4 * rows, LANES), F32)]
        + [pltpu.VMEM((note_rows, LANES), F32)] * (n_sub - 1)
        + [
            pltpu.VMEM((rows_dev, cols), BF16),
            pltpu.VMEM((blocks, cols), I32),
            pltpu.VMEM((blocks, BLOCK), F32),
            pltpu.VMEM((2, cap), I32),
        ],
        in_specs=[hbm] * 5,
        out_specs=[vmem] * (n_sub + 4),
        scratch_shapes=[
            pltpu.VMEM((candidates // LANES, LANES), I32),
            pltpu.VMEM((ENDS, 2 * cap), BF16),
            pltpu.VMEM((cols, ENDS), BF16),
            pltpu.VMEM((2 * rows, LANES), F32),
            pltpu.SemaphoreType.DMA((4,)),
            pltpu.SemaphoreType.DMA((chunks,)),
        ],
        compiler_params=params,
        cost_estimate=pl.CostEstimate(
            flops=2 * rows_dev * cols * ENDS, bytes_accessed=rows_dev * cols * 2, transcendentals=0
        ),
        name="pair_values",
    )(*map(in_hbm, (dfactors, block_mask, base, table, slots)))
    share, notes = outs[0], outs[1:n_sub]
    factors[0], block_mask, base, slots = outs[n_sub:]

    notes = [lax.ppermute(note, "sub", ring) for note, ring in zip(notes, rings[1:])]
    share = functools.reduce(jnp.add, [share] + [note[: 4 * rows] for note in notes])
    width = chunk_of(cap, 256)
    hot = pltpu.VMEM((cap // width, n_sub * cols, width), BF16)
    columns = pltpu.VMEM((my_rows, cap), BF16)
    masked = pltpu.VMEM((my_rows, n_sub * cols), BF16)
    columns_cost = pl.CostEstimate(
        flops=2 * my_rows * cols * n_sub * cap,
        bytes_accessed=my_rows * (cols * n_sub + cap) * 2,
        transcendentals=0,
    )
    factors = [*factors, *notes, block_mask]
    masked, first, share = pl.pallas_call(
        functools.partial(early_kernel, n_sub),
        out_shape=[masked, columns, pltpu.VMEM(share.shape, F32)],
        in_specs=[vmem] * (len(factors) + 2),
        out_specs=[vmem] * 3,
        scratch_shapes=[hot],
        compiler_params=params,
        name="early_columns",
    )(*map(in_vmem, (*factors, slots, share)))
    shares = [share, *from_other_mon(share, lax.axis_size("mon"), n_sub)]

    masked, first = pl.pallas_call(
        functools.partial(first_kernel, n_sub),
        out_shape=[pltpu.VMEM(masked.shape, BF16), columns],
        in_specs=[vmem] * (len(factors) + 1) + [smem] + [vmem] * 2,
        out_specs=[vmem] * 2,
        input_output_aliases={len(factors) + 2: 0, len(factors) + 3: 1},
        scratch_shapes=[hot],
        compiler_params=params,
        cost_estimate=columns_cost,
        name="first_columns",
    )(*map(in_vmem, (*factors, slots)), pair_counts, *map(in_vmem, (masked, first)))
    second, out = pl.pallas_call(
        functools.partial(second_kernel, n_sub),
        out_shape=[columns, pltpu.HBM((my_rows, cap), BF16)],
        in_specs=[vmem] * 2 + [smem],
        out_specs=[vmem, hbm],
        scratch_shapes=[
            pltpu.VMEM((n_sub * cols, cap), BF16),
            pltpu.VMEM((my_rows, width), BF16),
            pltpu.SemaphoreType.DMA((cap // width,)),
        ],
        compiler_params=params,
        cost_estimate=columns_cost,
        name="second_columns",
    )(*map(in_vmem, (masked, slots)), pair_counts)
    return pl.pallas_call(
        functools.partial(flows_kernel, len(shares), width),
        out_shape=jax.ShapeDtypeStruct((my_rows, cap), BF16),
        in_specs=[vmem] * (len(shares) + 3) + [smem, hbm],
        out_specs=hbm,
        input_output_aliases={len(shares) + 4: 0},
        scratch_shapes=[
            pltpu.VMEM((my_rows, cap), BF16),
            pltpu.SemaphoreType.DMA((my_rows // BLOCK,)),
        ],
        compiler_params=params,
        cost_estimate=pl.CostEstimate(
            flops=6 * my_rows * cap, bytes_accessed=my_rows * cap * 2, transcendentals=0
        ),
        name="post_flows",
    )(*map(in_vmem, (*shares, base, first, second)), pair_counts, in_hbm(out))


def solution(mesh):
    return jax.shard_map(
        on_device,
        mesh=mesh,
        in_specs=(
            P("mon", "sub"),
            P("mon", "sub"),
            P("mon"),
            P(),
            P(("grp", "pair"), None),
            P(("grp", "pair")),
        ),
        out_specs=P(("mon", "sub"), ("grp", "pair")),
        check_vma=False,
    )
```

```python
import functools

import jax
import jax.numpy as jnp
from jax import lax
from jax.experimental import pallas as pl
from jax.experimental.pallas import tpu as pltpu
from jax.sharding import PartitionSpec as P

BLOCK = 128
LANES = 128
SUBLANES = 8
ENDS = 256
VMEM_LIMIT = 16 * 1024 * 1024
F32 = jnp.float32
BF16 = jnp.bfloat16
I32 = jnp.int32


def chunk_of(total, want):
    size = min(total, want)
    while total % size:
        size -= BLOCK
    return size


def dense_rows(cap):
    return -(-cap // (LANES * SUBLANES)) * SUBLANES


def one_hot(hit):
    return jnp.where(hit, 1.0, 0.0).astype(BF16)


def iota(shape, axis):
    return lax.broadcasted_iota(I32, shape, axis)


def dense(line):
    cap = line.shape[1]
    rows = dense_rows(cap)
    pieces = [line[:, c : c + LANES] for c in range(0, cap, LANES)]
    if len(pieces) < rows:
        pieces.append(jnp.zeros((rows - len(pieces), LANES), line.dtype))
    return jnp.concatenate(pieces, axis=0)


def look_up(table, index):
    high, low = index >> 7, index & 127
    found = jnp.zeros(index.shape, table.dtype)
    for b in range(table.shape[0]):
        line = jnp.broadcast_to(table[b : b + 1], index.shape)
        value = jnp.take_along_axis(line, low, axis=1, mode="promise_in_bounds")
        found = jnp.where(high == b, value, found)
    return found


def values_kernel(
    n_sub, d_hbm, mask_hbm, base_hbm, rows_hbm, slots_hbm, *refs
):
    share_ref, *note_refs = refs[:n_sub]
    (
        d_ref, mask_ref, base_ref, slots_ref, rows_ref, perm_ref, hot_ref, cross_ref, sems, d_sems
    ) = refs[n_sub:]
    rows_dev, cols = d_ref.shape
    chunks = d_sems.shape[0]
    chunk = rows_dev // chunks
    cap = slots_ref.shape[1]
    lines = cap // LANES
    rows = dense_rows(cap)
    sub_index = lax.axis_index("sub")
    small = [
        pltpu.make_async_copy(src, dst, sems.at[i])
        for i, (src, dst) in enumerate(
            [(slots_hbm, slots_ref), (rows_hbm, rows_ref), (base_hbm, base_ref), (mask_hbm, mask_ref)]
        )
    ]
    large = [
        pltpu.make_async_copy(
            d_hbm.at[pl.ds(i * chunk, chunk)], d_ref.at[pl.ds(i * chunk, chunk)], d_sems.at[i]
        )
        for i in range(chunks)
    ]
    for copy in small + large:
        copy.start()

    small[0].wait()
    small[1].wait()
    first, second = dense(slots_ref[0:1, :]), dense(slots_ref[1:2, :])
    table = rows_ref[...]
    row = jnp.concatenate([look_up(table, first), look_up(table, second)], axis=0)
    row = row - lax.axis_index("mon") * rows_dev
    col = jnp.concatenate([second, first], axis=0) - sub_index * cols
    used = lax.rem(iota(row.shape, 0), rows) < lines
    here = used & (row >= 0) & (row < rows_dev) & (col >= 0) & (col < cols)

    flags = one_hot(here)
    height = flags.shape[0]
    above = jnp.dot(
        one_hot(iota((height, height), 1) < iota((height, height), 0)),
        flags,
        preferred_element_type=F32,
    ).astype(BF16)
    place = jnp.dot(
        jnp.concatenate([flags, above], axis=1),
        jnp.concatenate(
            [
                one_hot(iota((LANES, LANES), 0) <= iota((LANES, LANES), 1)),
                jnp.ones((LANES, LANES), BF16),
            ],
            axis=0,
        ),
        preferred_element_type=F32,
    ).astype(I32)
    place = jnp.where(here, place - 1, -1)
    digits = [(x >> shift) & 255 for x in (col, row) for shift in (0, 8)]
    order = [half * rows + b for half in range(2) for b in range(lines)]
    ends = jnp.concatenate(
        [jnp.concatenate([x[r : r + 1] for x in digits], axis=0) for r in order], axis=1
    )
    ends = ends.astype(F32).astype(BF16)

    def pick(start, copies=()):
        for at, r in enumerate(order):
            perm_ref[:, at * LANES : (at + 1) * LANES] = one_hot(
                iota((ENDS, LANES), 0) + start == place[r : r + 1]
            )
        packed = lax.dot_general(
            ends, perm_ref[...], (((1,), (1,)), ((), ())), preferred_element_type=F32
        ).astype(I32)
        end_col = packed[0:1] + (packed[1:2] << 8)
        end_row = packed[2:3] + (packed[3:4] << 8)
        hot_ref[...] = one_hot(iota((cols, ENDS), 0) == end_col)
        for copy in copies:
            copy.wait()
        keep = jnp.dot(
            mask_ref[...].astype(F32).astype(BF16), hot_ref[...], preferred_element_type=F32
        )
        keep = jnp.sum(
            jnp.where(iota(keep.shape, 0) == (end_row >> 7), keep, 0.0), axis=0, keepdims=True
        )
        total = jnp.zeros((SUBLANES, ENDS), F32)
        for i in range(chunks):
            values = jnp.dot(
                d_ref[i * chunk : (i + 1) * chunk, :], hot_ref[...], preferred_element_type=F32
            )
            picked = jnp.where(iota((chunk, ENDS), 0) + i * chunk == end_row, values, 0.0)
            total += jnp.sum(picked.reshape(chunk // SUBLANES, SUBLANES, ENDS), axis=0)
        value = jnp.sum(total, axis=0, keepdims=True) * keep
        value = jnp.concatenate([value[:, q : q + LANES] for q in range(0, ENDS, LANES)], axis=0)
        return look_up(value, place - start)

    def put(cross, flow):
        for ref in (share_ref, *note_refs):
            ref[: 2 * rows, :] = cross
            ref[2 * rows : 4 * rows, :] = flow

    cross = pick(0, small[2:] + large)
    flow = jnp.where(sub_index == 0, look_up(base_ref[...], row), 0.0)
    put(cross, flow)
    my_blocks = mask_ref.shape[0] // n_sub
    for s, ref in enumerate(note_refs, 1):
        block = pl.multiple_of(lax.rem(sub_index + s, n_sub) * my_blocks, my_blocks)
        for c in range(cols // LANES):
            at = 4 * rows + c * my_blocks
            ref[at : at + my_blocks, :] = mask_ref[
                pl.ds(block, my_blocks), c * LANES : (c + 1) * LANES
            ].astype(F32)
    count = jnp.max(place) + 1

    @pl.when(count > ENDS)
    def _():
        cross_ref[...] = cross

        def more(i, _):
            cross_ref[...] += pick(i * ENDS)
            return 0

        lax.fori_loop(1, pl.cdiv(count, ENDS), more, 0)
        put(cross_ref[...], flow)


def place_ones(part, slot, starts, cols, hot_ref):
    width = hot_ref.shape[1]
    for s, start in enumerate(starts):
        hot_ref[s * cols : (s + 1) * cols, :] = one_hot(
            iota((cols, width), 0) == slot[:, part * width : (part + 1) * width] - start
        )


def pick_columns(parts, slot, starts, cols, masked_ref, hot_ref, out_ref):
    width = hot_ref.shape[2]
    for part in parts:
        place_ones(part, slot, starts, cols, hot_ref.at[part])
        out_ref[:, part * width : (part + 1) * width] = jnp.dot(
            masked_ref[...], hot_ref[part], preferred_element_type=F32
        ).astype(BF16)


def live_parts(count, hot_ref):
    parts, _, width = hot_ref.shape
    return jnp.minimum((count + width - 1) // width, parts)


def is_early():
    return lax.axis_index("mon") < lax.axis_size("mon") // 2


def column_starts(n_sub, cols):
    return [lax.rem(lax.axis_index("sub") + n_sub - s, n_sub) * cols for s in range(n_sub)]


def mask_factors(n_sub, refs, masked_ref):
    d_refs, note_refs, mask_ref = refs[:n_sub], refs[n_sub:-1], refs[-1]
    my_rows, all_cols = masked_ref.shape
    cols = all_cols // n_sub
    my_blocks = my_rows // BLOCK
    sub_index = lax.axis_index("sub")
    my_start = pl.multiple_of(sub_index * my_rows, my_rows)
    my_block = pl.multiple_of(sub_index * my_blocks, my_blocks)
    for s in range(n_sub):
        if s == 0:
            keep = mask_ref[pl.ds(my_block, my_blocks), :].astype(F32)
        else:
            ref = note_refs[s - 1]
            ends = range(ref.shape[0] - (cols // LANES) * my_blocks, ref.shape[0], my_blocks)
            keep = jnp.concatenate([ref[at : at + my_blocks, :] for at in ends], axis=1)
        keep = keep.astype(BF16)
        for b in range(my_blocks):
            masked_ref[b * BLOCK : (b + 1) * BLOCK, s * cols : (s + 1) * cols] = (
                d_refs[s][pl.ds(my_start + b * BLOCK, BLOCK), :] * keep[b : b + 1]
            )


def early_kernel(n_sub, *refs):
    *factor_refs, slots_ref, share_ref, masked_ref, first_ref, shared_ref, hot_ref = refs
    shared_ref[...] = share_ref[...]
    cols = masked_ref.shape[1] // n_sub

    @pl.when(is_early())
    def _():
        mask_factors(n_sub, factor_refs, masked_ref)
        starts = column_starts(n_sub, cols)
        pick_columns([0], slots_ref[0:1, :], starts, cols, masked_ref, hot_ref, first_ref)


def first_kernel(n_sub, *refs):
    *factor_refs, slots_ref, count_ref, _, _, masked_ref, first_ref, hot_ref = refs
    cols = masked_ref.shape[1] // n_sub
    slot = slots_ref[0:1, :]
    starts = column_starts(n_sub, cols)
    live = live_parts(count_ref[0], hot_ref)
    for n_parts in range(1, hot_ref.shape[0] + 1):

        @pl.when((live == n_parts) & jnp.logical_not(is_early()))
        def _():
            mask_factors(n_sub, factor_refs, masked_ref)
            pick_columns(range(n_parts), slot, starts, cols, masked_ref, hot_ref, first_ref)

        @pl.when((live == n_parts) & is_early())
        def _():
            pick_columns(range(1, n_parts), slot, starts, cols, masked_ref, hot_ref, first_ref)


def second_kernel(
    n_sub, masked_ref, slots_ref, count_ref, second_ref, last_ref, out_hbm, hot_ref, zero_ref, sems
):
    cols = masked_ref.shape[1] // n_sub
    slot = slots_ref[1:2, :]
    starts = column_starts(n_sub, cols)
    live = live_parts(count_ref[0], hot_ref)
    parts, _, width = hot_ref.shape
    for n_parts in range(1, parts + 1):

        @pl.when(live == n_parts)
        def _():
            copies = [
                pltpu.make_async_copy(
                    zero_ref, out_hbm.at[:, part * width : (part + 1) * width], sems.at[part]
                )
                for part in range(n_parts, parts)
            ]
            if copies:
                zero_ref[...] = jnp.zeros_like(zero_ref)
            for copy in copies:
                copy.start()
            if n_parts == parts:
                place_ones(parts - 1, slot, starts, cols, last_ref)
            some = range(min(n_parts, parts - 1))
            pick_columns(some, slot, starts, cols, masked_ref, hot_ref, second_ref)
            for copy in copies:
                copy.wait()


def flows_kernel(n_shares, width, *refs):
    share_refs, refs = refs[:n_shares], refs[n_shares:]
    (
        base_ref, first_ref, second_ref, masked_ref, last_ref, count_ref, _,
        out_hbm, post_ref, made_ref, out_sems,
    ) = refs
    my_rows, cap = post_ref.shape
    my_blocks = my_rows // BLOCK
    rows = dense_rows(cap)
    total = share_refs[0][...]
    for ref in share_refs[1:]:
        total = total + ref[...]
    cross_first, cross_second, flow_first, flow_second = (
        total[i * rows : (i + 1) * rows] for i in range(4)
    )
    determinant = 1.0 - cross_first * cross_second
    shift_first = (flow_first + cross_first * flow_second) / determinant
    shift_second = (flow_second + cross_second * flow_first) / determinant
    my_block = pl.multiple_of(lax.axis_index("sub") * my_blocks, my_blocks)
    base = jnp.swapaxes(base_ref[pl.ds(my_block, my_blocks), :], 0, 1)

    def write(lines):
        live = [iota((1, LANES), 1) + line * LANES < count_ref[0] for line in lines]
        weights = [
            [
                jnp.broadcast_to(shift[line : line + 1], (BLOCK, LANES)).astype(BF16)
                for line in lines
            ]
            for shift in (shift_first, shift_second)
        ]
        wide = slice(0, len(lines) * LANES)
        made_from = (cap - width) // LANES
        half = chunk_of(my_rows, my_rows // 2)
        out_copies = []
        for b in range(my_blocks):
            block = slice(b * BLOCK, (b + 1) * BLOCK)
            if lines[-1] >= made_from and b * BLOCK % half == 0:
                rows_now = slice(b * BLOCK, b * BLOCK + half)
                made_ref[rows_now, :] = jnp.dot(
                    masked_ref[rows_now, :], last_ref[...], preferred_element_type=F32
                ).astype(BF16)
            start = jnp.broadcast_to(base[:, b : b + 1], (BLOCK, LANES))
            for line in lines:
                lanes = slice(line * LANES, (line + 1) * LANES)
                if line < made_from:
                    second = second_ref[block, lanes]
                else:
                    at = (line - made_from) * LANES
                    second = made_ref[block, at : at + LANES]
                change = weights[0][line] * first_ref[block, lanes] + weights[1][line] * second
                post_ref[block, lanes] = jnp.where(
                    live[line], start + change.astype(F32), 0.0
                ).astype(BF16)
            out_copies.append(
                pltpu.make_async_copy(
                    post_ref.at[block, wide], out_hbm.at[block, wide], out_sems.at[b]
                )
            )
            out_copies[-1].start()
        for copy in out_copies:
            copy.wait()

    parts = cap // width
    live_count = jnp.minimum((count_ref[0] + width - 1) // width, parts)
    for n_parts in range(1, parts + 1):
        pl.when(live_count == n_parts)(
            functools.partial(write, range(n_parts * width // LANES))
        )


def partners(n_mon):
    half = n_mon // 2
    if n_mon & (n_mon - 1):
        return [[(m + k) % n_mon for m in range(n_mon)] for k in range(1, n_mon)]
    across = [
        [m ^ (half + k) if m < half else m ^ (n_mon - 1 - k) for m in range(n_mon)]
        for k in range(half)
    ]
    return across + [[m ^ k for m in range(n_mon)] for k in range(half - 1, 0, -1)]


def from_other_mon(share, n_mon, n_sub):
    return [
        lax.ppermute(
            share,
            ("mon", "sub"),
            [
                (m * n_sub + s, to[m] * n_sub + n_sub - 1 - s)
                for m in range(n_mon)
                for s in range(n_sub)
            ],
        )
        for to in reversed(partners(n_mon))
    ]


def on_device(dfactors, block_mask, base_flow, branch_row, pair_slots, pair_counts):
    rows_dev, cols = dfactors.shape
    blocks = rows_dev // BLOCK
    candidates = branch_row.shape[0]
    cap = pair_slots.shape[0]
    rows = dense_rows(cap)
    n_sub = lax.axis_size("sub")
    my_rows = rows_dev // n_sub
    slots = pair_slots.T
    base = base_flow.reshape(blocks, BLOCK)
    table = branch_row.reshape(candidates // LANES, LANES)
    hbm = pl.BlockSpec(memory_space=pltpu.HBM)
    in_hbm = functools.partial(pltpu.with_memory_space_constraint, memory_space=pltpu.HBM)
    in_vmem = functools.partial(pltpu.with_memory_space_constraint, memory_space=pltpu.VMEM)
    vmem = pl.BlockSpec(memory_space=pltpu.VMEM)
    smem = pl.BlockSpec(memory_space=pltpu.SMEM)
    params = pltpu.CompilerParams(vmem_limit_bytes=VMEM_LIMIT)
    rings = [[(i, (i + s) % n_sub) for i in range(n_sub)] for s in range(n_sub)]

    factors = [dfactors] + [lax.ppermute(dfactors, "sub", ring) for ring in rings[1:]]

    chunks = rows_dev // chunk_of(rows_dev, 512)
    note_rows = 4 * rows + (cols // LANES) * (my_rows // BLOCK)
    outs = pl.pallas_call(
        functools.partial(values_kernel, n_sub),
        out_shape=[pltpu.VMEM((4 * rows, LANES), F32)]
        + [pltpu.VMEM((note_rows, LANES), F32)] * (n_sub - 1)
        + [
            pltpu.VMEM((rows_dev, cols), BF16),
            pltpu.VMEM((blocks, cols), I32),
            pltpu.VMEM((blocks, BLOCK), F32),
            pltpu.VMEM((2, cap), I32),
        ],
        in_specs=[hbm] * 5,
        out_specs=[vmem] * (n_sub + 4),
        scratch_shapes=[
            pltpu.VMEM((candidates // LANES, LANES), I32),
            pltpu.VMEM((ENDS, 2 * cap), BF16),
            pltpu.VMEM((cols, ENDS), BF16),
            pltpu.VMEM((2 * rows, LANES), F32),
            pltpu.SemaphoreType.DMA((4,)),
            pltpu.SemaphoreType.DMA((chunks,)),
        ],
        compiler_params=params,
        cost_estimate=pl.CostEstimate(
            flops=2 * rows_dev * cols * ENDS, bytes_accessed=rows_dev * cols * 2, transcendentals=0
        ),
        name="pair_values",
    )(*map(in_hbm, (dfactors, block_mask, base, table, slots)))
    share, notes = outs[0], outs[1:n_sub]
    factors[0], block_mask, base, slots = outs[n_sub:]

    notes = [lax.ppermute(note, "sub", ring) for note, ring in zip(notes, rings[1:])]
    share = functools.reduce(jnp.add, [share] + [note[: 4 * rows] for note in notes])
    width = chunk_of(cap, 256)
    hot = pltpu.VMEM((cap // width, n_sub * cols, width), BF16)
    columns = pltpu.VMEM((my_rows, cap), BF16)
    masked = pltpu.VMEM((my_rows, n_sub * cols), BF16)
    columns_cost = pl.CostEstimate(
        flops=2 * my_rows * cols * n_sub * cap,
        bytes_accessed=my_rows * (cols * n_sub + cap) * 2,
        transcendentals=0,
    )
    factors = [*factors, *notes, block_mask]
    masked, first, share = pl.pallas_call(
        functools.partial(early_kernel, n_sub),
        out_shape=[masked, columns, pltpu.VMEM(share.shape, F32)],
        in_specs=[vmem] * (len(factors) + 2),
        out_specs=[vmem] * 3,
        scratch_shapes=[hot],
        compiler_params=params,
        name="early_columns",
    )(*map(in_vmem, (*factors, slots, share)))
    shares = [share, *from_other_mon(share, lax.axis_size("mon"), n_sub)]

    masked, first = pl.pallas_call(
        functools.partial(first_kernel, n_sub),
        out_shape=[pltpu.VMEM(masked.shape, BF16), columns],
        in_specs=[vmem] * (len(factors) + 1) + [smem] + [vmem] * 2,
        out_specs=[vmem] * 2,
        input_output_aliases={len(factors) + 2: 0, len(factors) + 3: 1},
        scratch_shapes=[hot],
        compiler_params=params,
        cost_estimate=columns_cost,
        name="first_columns",
    )(*map(in_vmem, (*factors, slots)), pair_counts, *map(in_vmem, (masked, first)))
    second, last, out = pl.pallas_call(
        functools.partial(second_kernel, n_sub),
        out_shape=[
            columns,
            pltpu.VMEM((n_sub * cols, width), BF16),
            pltpu.HBM((my_rows, cap), BF16),
        ],
        in_specs=[vmem] * 2 + [smem],
        out_specs=[vmem, vmem, hbm],
        scratch_shapes=[
            hot,
            pltpu.VMEM((my_rows, width), BF16),
            pltpu.SemaphoreType.DMA((cap // width,)),
        ],
        compiler_params=params,
        cost_estimate=columns_cost,
        name="second_columns",
    )(*map(in_vmem, (masked, slots)), pair_counts)
    return pl.pallas_call(
        functools.partial(flows_kernel, len(shares), width),
        out_shape=jax.ShapeDtypeStruct((my_rows, cap), BF16),
        in_specs=[vmem] * (len(shares) + 5) + [smem, hbm],
        out_specs=hbm,
        input_output_aliases={len(shares) + 6: 0},
        scratch_shapes=[
            pltpu.VMEM((my_rows, cap), BF16),
            pltpu.VMEM((my_rows, width), BF16),
            pltpu.SemaphoreType.DMA((my_rows // BLOCK,)),
        ],
        compiler_params=params,
        cost_estimate=pl.CostEstimate(
            flops=6 * my_rows * cap, bytes_accessed=my_rows * cap * 2, transcendentals=0
        ),
        name="post_flows",
    )(
        *map(in_vmem, (*shares, base, first, second, masked, last)), pair_counts, in_hbm(out)
    )


def solution(mesh):
    return jax.shard_map(
        on_device,
        mesh=mesh,
        in_specs=(
            P("mon", "sub"),
            P("mon", "sub"),
            P("mon"),
            P(),
            P(("grp", "pair"), None),
            P(("grp", "pair")),
        ),
        out_specs=P(("mon", "sub"), ("grp", "pair")),
        check_vma=False,
    )
```

```python
import functools

import jax
import jax.numpy as jnp
from jax import lax
from jax.experimental import pallas as pl
from jax.experimental.pallas import tpu as pltpu
from jax.sharding import PartitionSpec as P

BLOCK = 128
LANES = 128
SUBLANES = 8
ENDS = 256
VMEM_LIMIT = 16 * 1024 * 1024
F32 = jnp.float32
BF16 = jnp.bfloat16
I32 = jnp.int32


def chunk_of(total, want):
    size = min(total, want)
    while total % size:
        size -= BLOCK
    return size


def dense_rows(cap):
    return -(-cap // (LANES * SUBLANES)) * SUBLANES


def one_hot(hit):
    return jnp.where(hit, 1.0, 0.0).astype(BF16)


def iota(shape, axis):
    return lax.broadcasted_iota(I32, shape, axis)


def dense(line):
    cap = line.shape[1]
    rows = dense_rows(cap)
    pieces = [line[:, c : c + LANES] for c in range(0, cap, LANES)]
    if len(pieces) < rows:
        pieces.append(jnp.zeros((rows - len(pieces), LANES), line.dtype))
    return jnp.concatenate(pieces, axis=0)


def look_up(table, index):
    high, low = index >> 7, index & 127
    found = jnp.zeros(index.shape, table.dtype)
    for b in range(table.shape[0]):
        line = jnp.broadcast_to(table[b : b + 1], index.shape)
        value = jnp.take_along_axis(line, low, axis=1, mode="promise_in_bounds")
        found = jnp.where(high == b, value, found)
    return found


def values_kernel(
    n_sub, d_hbm, mask_hbm, base_hbm, rows_hbm, slots_hbm, *refs
):
    share_ref, *note_refs = refs[:n_sub]
    (
        d_ref, mask_ref, base_ref, slots_ref, rows_ref, perm_ref, hot_ref, cross_ref, sems, d_sems
    ) = refs[n_sub:]
    rows_dev, cols = d_ref.shape
    chunks = d_sems.shape[0]
    chunk = rows_dev // chunks
    cap = slots_ref.shape[1]
    lines = cap // LANES
    rows = dense_rows(cap)
    sub_index = lax.axis_index("sub")
    small = [
        pltpu.make_async_copy(src, dst, sems.at[i])
        for i, (src, dst) in enumerate(
            [(slots_hbm, slots_ref), (rows_hbm, rows_ref), (base_hbm, base_ref), (mask_hbm, mask_ref)]
        )
    ]
    large = [
        pltpu.make_async_copy(
            d_hbm.at[pl.ds(i * chunk, chunk)], d_ref.at[pl.ds(i * chunk, chunk)], d_sems.at[i]
        )
        for i in range(chunks)
    ]
    for copy in small + large:
        copy.start()

    small[0].wait()
    small[1].wait()
    first, second = dense(slots_ref[0:1, :]), dense(slots_ref[1:2, :])
    table = rows_ref[...]
    row = jnp.concatenate([look_up(table, first), look_up(table, second)], axis=0)
    row = row - lax.axis_index("mon") * rows_dev
    col = jnp.concatenate([second, first], axis=0) - sub_index * cols
    used = lax.rem(iota(row.shape, 0), rows) < lines
    here = used & (row >= 0) & (row < rows_dev) & (col >= 0) & (col < cols)

    flags = one_hot(here)
    height = flags.shape[0]
    above = jnp.dot(
        one_hot(iota((height, height), 1) < iota((height, height), 0)),
        flags,
        preferred_element_type=F32,
    ).astype(BF16)
    place = jnp.dot(
        jnp.concatenate([flags, above], axis=1),
        jnp.concatenate(
            [
                one_hot(iota((LANES, LANES), 0) <= iota((LANES, LANES), 1)),
                jnp.ones((LANES, LANES), BF16),
            ],
            axis=0,
        ),
        preferred_element_type=F32,
    ).astype(I32)
    place = jnp.where(here, place - 1, -1)
    digits = [(x >> shift) & 255 for x in (col, row) for shift in (0, 8)]
    order = [half * rows + b for half in range(2) for b in range(lines)]
    ends = jnp.concatenate(
        [jnp.concatenate([x[r : r + 1] for x in digits], axis=0) for r in order], axis=1
    )
    ends = ends.astype(F32).astype(BF16)

    def pick(start, copies=()):
        for at, r in enumerate(order):
            perm_ref[:, at * LANES : (at + 1) * LANES] = one_hot(
                iota((ENDS, LANES), 0) + start == place[r : r + 1]
            )
        packed = lax.dot_general(
            ends, perm_ref[...], (((1,), (1,)), ((), ())), preferred_element_type=F32
        ).astype(I32)
        end_col = packed[0:1] + (packed[1:2] << 8)
        end_row = packed[2:3] + (packed[3:4] << 8)
        hot_ref[...] = one_hot(iota((cols, ENDS), 0) == end_col)
        for copy in copies:
            copy.wait()
        keep = jnp.dot(
            mask_ref[...].astype(F32).astype(BF16), hot_ref[...], preferred_element_type=F32
        )
        keep = jnp.sum(
            jnp.where(iota(keep.shape, 0) == (end_row >> 7), keep, 0.0), axis=0, keepdims=True
        )
        total = jnp.zeros((SUBLANES, ENDS), F32)
        for i in range(chunks):
            values = jnp.dot(
                d_ref[i * chunk : (i + 1) * chunk, :], hot_ref[...], preferred_element_type=F32
            )
            picked = jnp.where(iota((chunk, ENDS), 0) + i * chunk == end_row, values, 0.0)
            total += jnp.sum(picked.reshape(chunk // SUBLANES, SUBLANES, ENDS), axis=0)
        value = jnp.sum(total, axis=0, keepdims=True) * keep
        value = jnp.concatenate([value[:, q : q + LANES] for q in range(0, ENDS, LANES)], axis=0)
        return look_up(value, place - start)

    def put(cross, flow):
        for ref in (share_ref, *note_refs):
            ref[: 2 * rows, :] = cross
            ref[2 * rows : 4 * rows, :] = flow

    cross = pick(0, small[2:] + large)
    flow = jnp.where(sub_index == 0, look_up(base_ref[...], row), 0.0)
    put(cross, flow)
    my_blocks = mask_ref.shape[0] // n_sub
    for s, ref in enumerate(note_refs, 1):
        block = pl.multiple_of(lax.rem(sub_index + s, n_sub) * my_blocks, my_blocks)
        for c in range(cols // LANES):
            at = 4 * rows + c * my_blocks
            ref[at : at + my_blocks, :] = mask_ref[
                pl.ds(block, my_blocks), c * LANES : (c + 1) * LANES
            ].astype(F32)
    count = jnp.max(place) + 1

    @pl.when(count > ENDS)
    def _():
        cross_ref[...] = cross

        def more(i, _):
            cross_ref[...] += pick(i * ENDS)
            return 0

        lax.fori_loop(1, pl.cdiv(count, ENDS), more, 0)
        put(cross_ref[...], flow)


def pick_columns(parts, slot, starts, cols, masked_ref, hot_ref, out_ref):
    width = hot_ref.shape[2]
    for part in parts:
        lanes = slice(part * width, (part + 1) * width)
        for s, start in enumerate(starts):
            hot_ref[part, s * cols : (s + 1) * cols, :] = one_hot(
                iota((cols, width), 0) == slot[:, lanes] - start
            )
        out_ref[:, lanes] = jnp.dot(
            masked_ref[...], hot_ref[part], preferred_element_type=F32
        ).astype(BF16)


def fewest(parts):
    return min(2, parts)


def live_parts(count, width, parts):
    return jnp.clip((count + width - 1) // width, fewest(parts), parts)


def is_early():
    return lax.axis_index("mon") < lax.axis_size("mon") // 2


def column_starts(n_sub, cols):
    return [lax.rem(lax.axis_index("sub") + n_sub - s, n_sub) * cols for s in range(n_sub)]


def mask_factors(n_sub, refs, masked_ref):
    d_refs, note_refs, mask_ref = refs[:n_sub], refs[n_sub:-1], refs[-1]
    my_rows, all_cols = masked_ref.shape
    cols = all_cols // n_sub
    my_blocks = my_rows // BLOCK
    sub_index = lax.axis_index("sub")
    my_start = pl.multiple_of(sub_index * my_rows, my_rows)
    my_block = pl.multiple_of(sub_index * my_blocks, my_blocks)
    for s in range(n_sub):
        if s == 0:
            keep = mask_ref[pl.ds(my_block, my_blocks), :].astype(F32)
        else:
            ref = note_refs[s - 1]
            ends = range(ref.shape[0] - (cols // LANES) * my_blocks, ref.shape[0], my_blocks)
            keep = jnp.concatenate([ref[at : at + my_blocks, :] for at in ends], axis=1)
        keep = keep.astype(BF16)
        for b in range(my_blocks):
            masked_ref[b * BLOCK : (b + 1) * BLOCK, s * cols : (s + 1) * cols] = (
                d_refs[s][pl.ds(my_start + b * BLOCK, BLOCK), :] * keep[b : b + 1]
            )


def early_kernel(n_sub, *refs):
    *factor_refs, slots_ref, share_ref, masked_ref, first_ref, shared_ref, hot_ref = refs
    shared_ref[...] = share_ref[...]
    cols = masked_ref.shape[1] // n_sub

    @pl.when(is_early())
    def _():
        mask_factors(n_sub, factor_refs, masked_ref)
        starts = column_starts(n_sub, cols)
        pick_columns([0], slots_ref[0:1, :], starts, cols, masked_ref, hot_ref, first_ref)


def first_kernel(n_sub, *refs):
    *factor_refs, slots_ref, count_ref, _, _, masked_ref, first_ref, hot_ref = refs
    cols = masked_ref.shape[1] // n_sub
    slot = slots_ref[0:1, :]
    starts = column_starts(n_sub, cols)
    parts, _, width = hot_ref.shape
    live = live_parts(count_ref[0], width, parts)
    for n_parts in range(fewest(parts), parts + 1):

        @pl.when((live == n_parts) & jnp.logical_not(is_early()))
        def _():
            mask_factors(n_sub, factor_refs, masked_ref)
            pick_columns(range(n_parts), slot, starts, cols, masked_ref, hot_ref, first_ref)

        @pl.when((live == n_parts) & is_early())
        def _():
            pick_columns(range(1, n_parts), slot, starts, cols, masked_ref, hot_ref, first_ref)


def second_kernel(
    n_sub, masked_ref, slots_ref, count_ref, second_ref, out_hbm, hot_ref, zero_ref, sems
):
    cols = masked_ref.shape[1] // n_sub
    slot = slots_ref[1:2, :]
    starts = column_starts(n_sub, cols)
    parts, _, width = hot_ref.shape
    live = live_parts(count_ref[0], width, parts)
    for n_parts in range(fewest(parts), parts + 1):

        @pl.when(live == n_parts)
        def _():
            copies = [
                pltpu.make_async_copy(
                    zero_ref, out_hbm.at[:, part * width : (part + 1) * width], sems.at[part]
                )
                for part in range(n_parts, parts)
            ]
            if copies:
                zero_ref[...] = jnp.zeros_like(zero_ref)
            for copy in copies:
                copy.start()
            pick_columns(range(n_parts), slot, starts, cols, masked_ref, hot_ref, second_ref)
            for copy in copies:
                copy.wait()


def flows_kernel(n_shares, width, *refs):
    share_refs, refs = refs[:n_shares], refs[n_shares:]
    base_ref, first_ref, second_ref, count_ref, _, out_hbm, post_ref, out_sems = refs
    my_rows, cap = post_ref.shape
    my_blocks = my_rows // BLOCK
    rows = dense_rows(cap)
    total = share_refs[0][...]
    for ref in share_refs[1:]:
        total = total + ref[...]
    cross_first, cross_second, flow_first, flow_second = (
        total[i * rows : (i + 1) * rows] for i in range(4)
    )
    determinant = 1.0 - cross_first * cross_second
    shift_first = (flow_first + cross_first * flow_second) / determinant
    shift_second = (flow_second + cross_second * flow_first) / determinant
    my_block = pl.multiple_of(lax.axis_index("sub") * my_blocks, my_blocks)
    base = jnp.swapaxes(base_ref[pl.ds(my_block, my_blocks), :], 0, 1)

    def write(lines):
        live = [iota((1, LANES), 1) + line * LANES < count_ref[0] for line in lines]
        weights = [
            [
                jnp.broadcast_to(shift[line : line + 1], (BLOCK, LANES)).astype(BF16)
                for line in lines
            ]
            for shift in (shift_first, shift_second)
        ]
        wide = slice(0, len(lines) * LANES)
        out_copies = []
        for b in range(my_blocks):
            block = slice(b * BLOCK, (b + 1) * BLOCK)
            start = jnp.broadcast_to(base[:, b : b + 1], (BLOCK, LANES))
            for line in lines:
                lanes = slice(line * LANES, (line + 1) * LANES)
                change = (
                    weights[0][line] * first_ref[block, lanes]
                    + weights[1][line] * second_ref[block, lanes]
                )
                post_ref[block, lanes] = jnp.where(
                    live[line], start + change.astype(F32), 0.0
                ).astype(BF16)
            out_copies.append(
                pltpu.make_async_copy(
                    post_ref.at[block, wide], out_hbm.at[block, wide], out_sems.at[b]
                )
            )
            out_copies[-1].start()
        for copy in out_copies:
            copy.wait()

    parts = cap // width
    live_count = live_parts(count_ref[0], width, parts)
    for n_parts in range(fewest(parts), parts + 1):
        pl.when(live_count == n_parts)(
            functools.partial(write, range(n_parts * width // LANES))
        )


def partners(n_mon):
    half = n_mon // 2
    if n_mon & (n_mon - 1):
        return [[(m + k) % n_mon for m in range(n_mon)] for k in range(1, n_mon)]
    across = [
        [m ^ (half + k) if m < half else m ^ (n_mon - 1 - k) for m in range(n_mon)]
        for k in range(half)
    ]
    return across + [[m ^ k for m in range(n_mon)] for k in range(half - 1, 0, -1)]


def from_other_mon(share, n_mon, n_sub):
    return [
        lax.ppermute(
            share,
            ("mon", "sub"),
            [
                (m * n_sub + s, to[m] * n_sub + n_sub - 1 - s)
                for m in range(n_mon)
                for s in range(n_sub)
            ],
        )
        for to in reversed(partners(n_mon))
    ]


def on_device(dfactors, block_mask, base_flow, branch_row, pair_slots, pair_counts):
    rows_dev, cols = dfactors.shape
    blocks = rows_dev // BLOCK
    candidates = branch_row.shape[0]
    cap = pair_slots.shape[0]
    rows = dense_rows(cap)
    n_sub = lax.axis_size("sub")
    my_rows = rows_dev // n_sub
    slots = pair_slots.T
    base = base_flow.reshape(blocks, BLOCK)
    table = branch_row.reshape(candidates // LANES, LANES)
    hbm = pl.BlockSpec(memory_space=pltpu.HBM)
    in_hbm = functools.partial(pltpu.with_memory_space_constraint, memory_space=pltpu.HBM)
    in_vmem = functools.partial(pltpu.with_memory_space_constraint, memory_space=pltpu.VMEM)
    vmem = pl.BlockSpec(memory_space=pltpu.VMEM)
    smem = pl.BlockSpec(memory_space=pltpu.SMEM)
    params = pltpu.CompilerParams(vmem_limit_bytes=VMEM_LIMIT)
    rings = [[(i, (i + s) % n_sub) for i in range(n_sub)] for s in range(n_sub)]

    factors = [dfactors] + [lax.ppermute(dfactors, "sub", ring) for ring in rings[1:]]

    chunks = rows_dev // chunk_of(rows_dev, 512)
    note_rows = 4 * rows + (cols // LANES) * (my_rows // BLOCK)
    outs = pl.pallas_call(
        functools.partial(values_kernel, n_sub),
        out_shape=[pltpu.VMEM((4 * rows, LANES), F32)]
        + [pltpu.VMEM((note_rows, LANES), F32)] * (n_sub - 1)
        + [
            pltpu.VMEM((rows_dev, cols), BF16),
            pltpu.VMEM((blocks, cols), I32),
            pltpu.VMEM((blocks, BLOCK), F32),
            pltpu.VMEM((2, cap), I32),
        ],
        in_specs=[hbm] * 5,
        out_specs=[vmem] * (n_sub + 4),
        scratch_shapes=[
            pltpu.VMEM((candidates // LANES, LANES), I32),
            pltpu.VMEM((ENDS, 2 * cap), BF16),
            pltpu.VMEM((cols, ENDS), BF16),
            pltpu.VMEM((2 * rows, LANES), F32),
            pltpu.SemaphoreType.DMA((4,)),
            pltpu.SemaphoreType.DMA((chunks,)),
        ],
        compiler_params=params,
        cost_estimate=pl.CostEstimate(
            flops=2 * rows_dev * cols * ENDS, bytes_accessed=rows_dev * cols * 2, transcendentals=0
        ),
        name="pair_values",
    )(*map(in_hbm, (dfactors, block_mask, base, table, slots)))
    share, notes = outs[0], outs[1:n_sub]
    factors[0], block_mask, base, slots = outs[n_sub:]

    notes = [lax.ppermute(note, "sub", ring) for note, ring in zip(notes, rings[1:])]
    share = functools.reduce(jnp.add, [share] + [note[: 4 * rows] for note in notes])
    width = chunk_of(cap, 256)
    hot = pltpu.VMEM((cap // width, n_sub * cols, width), BF16)
    columns = pltpu.VMEM((my_rows, cap), BF16)
    masked = pltpu.VMEM((my_rows, n_sub * cols), BF16)
    columns_cost = pl.CostEstimate(
        flops=2 * my_rows * cols * n_sub * cap,
        bytes_accessed=my_rows * (cols * n_sub + cap) * 2,
        transcendentals=0,
    )
    factors = [*factors, *notes, block_mask]
    masked, first, share = pl.pallas_call(
        functools.partial(early_kernel, n_sub),
        out_shape=[masked, columns, pltpu.VMEM(share.shape, F32)],
        in_specs=[vmem] * (len(factors) + 2),
        out_specs=[vmem] * 3,
        scratch_shapes=[hot],
        compiler_params=params,
        name="early_columns",
    )(*map(in_vmem, (*factors, slots, share)))
    shares = [share, *from_other_mon(share, lax.axis_size("mon"), n_sub)]

    masked, first = pl.pallas_call(
        functools.partial(first_kernel, n_sub),
        out_shape=[pltpu.VMEM(masked.shape, BF16), columns],
        in_specs=[vmem] * (len(factors) + 1) + [smem] + [vmem] * 2,
        out_specs=[vmem] * 2,
        input_output_aliases={len(factors) + 2: 0, len(factors) + 3: 1},
        scratch_shapes=[hot],
        compiler_params=params,
        cost_estimate=columns_cost,
        name="first_columns",
    )(*map(in_vmem, (*factors, slots)), pair_counts, *map(in_vmem, (masked, first)))
    second, out = pl.pallas_call(
        functools.partial(second_kernel, n_sub),
        out_shape=[columns, pltpu.HBM((my_rows, cap), BF16)],
        in_specs=[vmem] * 2 + [smem],
        out_specs=[vmem, hbm],
        scratch_shapes=[
            hot,
            pltpu.VMEM((my_rows, width), BF16),
            pltpu.SemaphoreType.DMA((cap // width,)),
        ],
        compiler_params=params,
        cost_estimate=columns_cost,
        name="second_columns",
    )(*map(in_vmem, (masked, slots)), pair_counts)
    return pl.pallas_call(
        functools.partial(flows_kernel, len(shares), width),
        out_shape=jax.ShapeDtypeStruct((my_rows, cap), BF16),
        in_specs=[vmem] * (len(shares) + 3) + [smem, hbm],
        out_specs=hbm,
        input_output_aliases={len(shares) + 4: 0},
        scratch_shapes=[
            pltpu.VMEM((my_rows, cap), BF16),
            pltpu.SemaphoreType.DMA((my_rows // BLOCK,)),
        ],
        compiler_params=params,
        cost_estimate=pl.CostEstimate(
            flops=6 * my_rows * cap, bytes_accessed=my_rows * cap * 2, transcendentals=0
        ),
        name="post_flows",
    )(*map(in_vmem, (*shares, base, first, second)), pair_counts, in_hbm(out))


def solution(mesh):
    return jax.shard_map(
        on_device,
        mesh=mesh,
        in_specs=(
            P("mon", "sub"),
            P("mon", "sub"),
            P("mon"),
            P(),
            P(("grp", "pair"), None),
            P(("grp", "pair")),
        ),
        out_specs=P(("mon", "sub"), ("grp", "pair")),
        check_vma=False,
    )
```

```python
import functools

import jax
import jax.numpy as jnp
from jax import lax
from jax.experimental import pallas as pl
from jax.experimental.pallas import tpu as pltpu
from jax.sharding import PartitionSpec as P

BLOCK = 128
LANES = 128
SUBLANES = 8
ENDS = 256
VMEM_LIMIT = 16 * 1024 * 1024
F32 = jnp.float32
BF16 = jnp.bfloat16
I32 = jnp.int32


def chunk_of(total, want):
    size = min(total, want)
    while total % size:
        size -= BLOCK
    return size


def dense_rows(cap):
    return -(-cap // (LANES * SUBLANES)) * SUBLANES


def one_hot(hit):
    return jnp.where(hit, 1.0, 0.0).astype(BF16)


def iota(shape, axis):
    return lax.broadcasted_iota(I32, shape, axis)


def dense(line):
    cap = line.shape[1]
    rows = dense_rows(cap)
    pieces = [line[:, c : c + LANES] for c in range(0, cap, LANES)]
    if len(pieces) < rows:
        pieces.append(jnp.zeros((rows - len(pieces), LANES), line.dtype))
    return jnp.concatenate(pieces, axis=0)


def look_up(table, index):
    high, low = index >> 7, index & 127
    found = jnp.zeros(index.shape, table.dtype)
    for b in range(table.shape[0]):
        line = jnp.broadcast_to(table[b : b + 1], index.shape)
        value = jnp.take_along_axis(line, low, axis=1, mode="promise_in_bounds")
        found = jnp.where(high == b, value, found)
    return found


def values_kernel(
    n_sub, d_hbm, mask_hbm, base_hbm, rows_hbm, slots_hbm, *refs
):
    share_ref, *note_refs = refs[:n_sub]
    (
        d_ref, mask_ref, base_ref, slots_ref, rows_ref, perm_ref, hot_ref, cross_ref, sems, d_sems
    ) = refs[n_sub:]
    rows_dev, cols = d_ref.shape
    chunks = d_sems.shape[0]
    chunk = rows_dev // chunks
    cap = slots_ref.shape[1]
    lines = cap // LANES
    rows = dense_rows(cap)
    sub_index = lax.axis_index("sub")
    small = [
        pltpu.make_async_copy(src, dst, sems.at[i])
        for i, (src, dst) in enumerate(
            [(slots_hbm, slots_ref), (rows_hbm, rows_ref), (base_hbm, base_ref), (mask_hbm, mask_ref)]
        )
    ]
    large = [
        pltpu.make_async_copy(
            d_hbm.at[pl.ds(i * chunk, chunk)], d_ref.at[pl.ds(i * chunk, chunk)], d_sems.at[i]
        )
        for i in range(chunks)
    ]
    for copy in small + large:
        copy.start()

    small[0].wait()
    small[1].wait()
    first, second = dense(slots_ref[0:1, :]), dense(slots_ref[1:2, :])
    table = rows_ref[...]
    row = jnp.concatenate([look_up(table, first), look_up(table, second)], axis=0)
    row = row - lax.axis_index("mon") * rows_dev
    col = jnp.concatenate([second, first], axis=0) - sub_index * cols
    used = lax.rem(iota(row.shape, 0), rows) < lines
    here = used & (row >= 0) & (row < rows_dev) & (col >= 0) & (col < cols)

    flags = one_hot(here)
    height = flags.shape[0]
    above = jnp.dot(
        one_hot(iota((height, height), 1) < iota((height, height), 0)),
        flags,
        preferred_element_type=F32,
    ).astype(BF16)
    place = jnp.dot(
        jnp.concatenate([flags, above], axis=1),
        jnp.concatenate(
            [
                one_hot(iota((LANES, LANES), 0) <= iota((LANES, LANES), 1)),
                jnp.ones((LANES, LANES), BF16),
            ],
            axis=0,
        ),
        preferred_element_type=F32,
    ).astype(I32)
    place = jnp.where(here, place - 1, -1)
    digits = [(x >> shift) & 255 for x in (col, row) for shift in (0, 8)]
    order = [half * rows + b for half in range(2) for b in range(lines)]
    ends = jnp.concatenate(
        [jnp.concatenate([x[r : r + 1] for x in digits], axis=0) for r in order], axis=1
    )
    ends = ends.astype(F32).astype(BF16)

    def pick(start, copies=()):
        for at, r in enumerate(order):
            perm_ref[:, at * LANES : (at + 1) * LANES] = one_hot(
                iota((ENDS, LANES), 0) + start == place[r : r + 1]
            )
        packed = lax.dot_general(
            ends, perm_ref[...], (((1,), (1,)), ((), ())), preferred_element_type=F32
        ).astype(I32)
        end_col = packed[0:1] + (packed[1:2] << 8)
        end_row = packed[2:3] + (packed[3:4] << 8)
        hot_ref[...] = one_hot(iota((cols, ENDS), 0) == end_col)
        for copy in copies[:2]:
            copy.wait()
        keep = jnp.dot(
            mask_ref[...].astype(F32).astype(BF16), hot_ref[...], preferred_element_type=F32
        )
        keep = jnp.sum(
            jnp.where(iota(keep.shape, 0) == (end_row >> 7), keep, 0.0), axis=0, keepdims=True
        )
        for copy in copies[2:]:
            copy.wait()
        total = jnp.zeros((SUBLANES, ENDS), F32)
        for i in range(chunks):
            values = jnp.dot(
                d_ref[i * chunk : (i + 1) * chunk, :], hot_ref[...], preferred_element_type=F32
            )
            picked = jnp.where(iota((chunk, ENDS), 0) + i * chunk == end_row, values, 0.0)
            total += jnp.sum(picked.reshape(chunk // SUBLANES, SUBLANES, ENDS), axis=0)
        value = jnp.sum(total, axis=0, keepdims=True) * keep
        value = jnp.concatenate([value[:, q : q + LANES] for q in range(0, ENDS, LANES)], axis=0)
        return look_up(value, place - start)

    def put(cross, flow):
        for ref in (share_ref, *note_refs):
            ref[: 2 * rows, :] = cross
            ref[2 * rows : 4 * rows, :] = flow

    cross = pick(0, small[2:] + large)
    flow = jnp.where(sub_index == 0, look_up(base_ref[...], row), 0.0)
    put(cross, flow)
    my_blocks = mask_ref.shape[0] // n_sub
    for s, ref in enumerate(note_refs, 1):
        block = pl.multiple_of(lax.rem(sub_index + s, n_sub) * my_blocks, my_blocks)
        for c in range(cols // LANES):
            at = 4 * rows + c * my_blocks
            ref[at : at + my_blocks, :] = mask_ref[
                pl.ds(block, my_blocks), c * LANES : (c + 1) * LANES
            ].astype(F32)
    count = jnp.max(place) + 1

    @pl.when(count > ENDS)
    def _():
        cross_ref[...] = cross

        def more(i, _):
            cross_ref[...] += pick(i * ENDS)
            return 0

        lax.fori_loop(1, pl.cdiv(count, ENDS), more, 0)
        put(cross_ref[...], flow)


def pick_columns(parts, slot, starts, cols, masked_ref, hot_ref, out_ref):
    width = hot_ref.shape[2]
    for part in parts:
        lanes = slice(part * width, (part + 1) * width)
        for s, start in enumerate(starts):
            hot_ref[part, s * cols : (s + 1) * cols, :] = one_hot(
                iota((cols, width), 0) == slot[:, lanes] - start
            )
        out_ref[:, lanes] = jnp.dot(
            masked_ref[...], hot_ref[part], preferred_element_type=F32
        ).astype(BF16)


def fewest(parts):
    return min(2, parts)


def live_parts(count, width, parts):
    return jnp.clip((count + width - 1) // width, fewest(parts), parts)


def is_early():
    return lax.axis_index("mon") < lax.axis_size("mon") // 2


def column_starts(n_sub, cols):
    return [lax.rem(lax.axis_index("sub") + n_sub - s, n_sub) * cols for s in range(n_sub)]


def mask_factors(n_sub, refs, masked_ref):
    d_refs, note_refs, mask_ref = refs[:n_sub], refs[n_sub:-1], refs[-1]
    my_rows, all_cols = masked_ref.shape
    cols = all_cols // n_sub
    my_blocks = my_rows // BLOCK
    sub_index = lax.axis_index("sub")
    my_start = pl.multiple_of(sub_index * my_rows, my_rows)
    my_block = pl.multiple_of(sub_index * my_blocks, my_blocks)
    for s in range(n_sub):
        if s == 0:
            keep = mask_ref[pl.ds(my_block, my_blocks), :].astype(F32)
        else:
            ref = note_refs[s - 1]
            ends = range(ref.shape[0] - (cols // LANES) * my_blocks, ref.shape[0], my_blocks)
            keep = jnp.concatenate([ref[at : at + my_blocks, :] for at in ends], axis=1)
        keep = keep.astype(BF16)
        for b in range(my_blocks):
            masked_ref[b * BLOCK : (b + 1) * BLOCK, s * cols : (s + 1) * cols] = (
                d_refs[s][pl.ds(my_start + b * BLOCK, BLOCK), :] * keep[b : b + 1]
            )


def early_kernel(n_sub, *refs):
    *factor_refs, slots_ref, share_ref, masked_ref, first_ref, shared_ref, hot_ref = refs
    shared_ref[...] = share_ref[...]
    cols = masked_ref.shape[1] // n_sub

    @pl.when(is_early())
    def _():
        mask_factors(n_sub, factor_refs, masked_ref)
        starts = column_starts(n_sub, cols)
        pick_columns([0], slots_ref[0:1, :], starts, cols, masked_ref, hot_ref, first_ref)


def first_kernel(n_sub, *refs):
    *factor_refs, slots_ref, count_ref, _, _, masked_ref, first_ref, hot_ref = refs
    cols = masked_ref.shape[1] // n_sub
    slot = slots_ref[0:1, :]
    starts = column_starts(n_sub, cols)
    parts, _, width = hot_ref.shape
    live = live_parts(count_ref[0], width, parts)
    for n_parts in range(fewest(parts), parts + 1):

        @pl.when((live == n_parts) & jnp.logical_not(is_early()))
        def _():
            mask_factors(n_sub, factor_refs, masked_ref)
            pick_columns(range(n_parts), slot, starts, cols, masked_ref, hot_ref, first_ref)

        @pl.when((live == n_parts) & is_early())
        def _():
            pick_columns(range(1, n_parts), slot, starts, cols, masked_ref, hot_ref, first_ref)


def second_kernel(
    n_sub, masked_ref, slots_ref, count_ref, second_ref, out_hbm, hot_ref, zero_ref, sems
):
    cols = masked_ref.shape[1] // n_sub
    slot = slots_ref[1:2, :]
    starts = column_starts(n_sub, cols)
    parts, _, width = hot_ref.shape
    live = live_parts(count_ref[0], width, parts)
    for n_parts in range(fewest(parts), parts + 1):

        @pl.when(live == n_parts)
        def _():
            copies = [
                pltpu.make_async_copy(
                    zero_ref, out_hbm.at[:, part * width : (part + 1) * width], sems.at[part]
                )
                for part in range(n_parts, parts)
            ]
            if copies:
                zero_ref[...] = jnp.zeros_like(zero_ref)
            for copy in copies:
                copy.start()
            pick_columns(range(n_parts), slot, starts, cols, masked_ref, hot_ref, second_ref)
            for copy in copies:
                copy.wait()


def flows_kernel(n_shares, width, *refs):
    share_refs, refs = refs[:n_shares], refs[n_shares:]
    base_ref, first_ref, second_ref, count_ref, _, out_hbm, post_ref, out_sems = refs
    my_rows, cap = post_ref.shape
    my_blocks = my_rows // BLOCK
    rows = dense_rows(cap)
    total = share_refs[0][...]
    for ref in share_refs[1:]:
        total = total + ref[...]
    cross_first, cross_second, flow_first, flow_second = (
        total[i * rows : (i + 1) * rows] for i in range(4)
    )
    determinant = 1.0 - cross_first * cross_second
    shift_first = (flow_first + cross_first * flow_second) / determinant
    shift_second = (flow_second + cross_second * flow_first) / determinant
    my_block = pl.multiple_of(lax.axis_index("sub") * my_blocks, my_blocks)
    base = jnp.swapaxes(base_ref[pl.ds(my_block, my_blocks), :], 0, 1)

    per = 2
    step = BLOCK // per

    def write(lines):
        live = [iota((1, LANES), 1) + line * LANES < count_ref[0] for line in lines]
        weights = [
            [
                jnp.broadcast_to(shift[line : line + 1], (step, LANES)).astype(BF16)
                for line in lines
            ]
            for shift in (shift_first, shift_second)
        ]
        wide = slice(0, len(lines) * LANES)
        out_copies = []
        for b in range(my_rows // step):
            block = slice(b * step, (b + 1) * step)
            part, at = b // per, b % per * step
            start = jnp.broadcast_to(base[at : at + step, part : part + 1], (step, LANES))
            for line in lines:
                lanes = slice(line * LANES, (line + 1) * LANES)
                change = (
                    weights[0][line] * first_ref[block, lanes]
                    + weights[1][line] * second_ref[block, lanes]
                )
                post_ref[block, lanes] = jnp.where(
                    live[line], start + change.astype(F32), 0.0
                ).astype(BF16)
            out_copies.append(
                pltpu.make_async_copy(
                    post_ref.at[block, wide], out_hbm.at[block, wide], out_sems.at[b]
                )
            )
            out_copies[-1].start()
        for copy in out_copies:
            copy.wait()

    parts = cap // width
    live_count = live_parts(count_ref[0], width, parts)
    for n_parts in range(fewest(parts), parts + 1):
        pl.when(live_count == n_parts)(
            functools.partial(write, range(n_parts * width // LANES))
        )


def partners(n_mon):
    half = n_mon // 2
    if n_mon & (n_mon - 1):
        return [[(m + k) % n_mon for m in range(n_mon)] for k in range(1, n_mon)]
    across = [
        [m ^ (half + k) if m < half else m ^ (n_mon - 1 - k) for m in range(n_mon)]
        for k in range(half)
    ]
    return across + [[m ^ k for m in range(n_mon)] for k in range(half - 1, 0, -1)]


def from_other_mon(share, n_mon, n_sub):
    return [
        lax.ppermute(
            share,
            ("mon", "sub"),
            [
                (m * n_sub + s, to[m] * n_sub + n_sub - 1 - s)
                for m in range(n_mon)
                for s in range(n_sub)
            ],
        )
        for to in reversed(partners(n_mon))
    ]


def on_device(dfactors, block_mask, base_flow, branch_row, pair_slots, pair_counts):
    rows_dev, cols = dfactors.shape
    blocks = rows_dev // BLOCK
    candidates = branch_row.shape[0]
    cap = pair_slots.shape[0]
    rows = dense_rows(cap)
    n_sub = lax.axis_size("sub")
    my_rows = rows_dev // n_sub
    slots = pair_slots.T
    base = base_flow.reshape(blocks, BLOCK)
    table = branch_row.reshape(candidates // LANES, LANES)
    hbm = pl.BlockSpec(memory_space=pltpu.HBM)
    in_hbm = functools.partial(pltpu.with_memory_space_constraint, memory_space=pltpu.HBM)
    in_vmem = functools.partial(pltpu.with_memory_space_constraint, memory_space=pltpu.VMEM)
    vmem = pl.BlockSpec(memory_space=pltpu.VMEM)
    smem = pl.BlockSpec(memory_space=pltpu.SMEM)
    params = pltpu.CompilerParams(vmem_limit_bytes=VMEM_LIMIT)
    rings = [[(i, (i + s) % n_sub) for i in range(n_sub)] for s in range(n_sub)]

    factors = [dfactors] + [lax.ppermute(dfactors, "sub", ring) for ring in rings[1:]]

    chunks = rows_dev // chunk_of(rows_dev, 512)
    note_rows = 4 * rows + (cols // LANES) * (my_rows // BLOCK)
    outs = pl.pallas_call(
        functools.partial(values_kernel, n_sub),
        out_shape=[pltpu.VMEM((4 * rows, LANES), F32)]
        + [pltpu.VMEM((note_rows, LANES), F32)] * (n_sub - 1)
        + [
            pltpu.VMEM((rows_dev, cols), BF16),
            pltpu.VMEM((blocks, cols), I32),
            pltpu.VMEM((blocks, BLOCK), F32),
            pltpu.VMEM((2, cap), I32),
        ],
        in_specs=[hbm] * 5,
        out_specs=[vmem] * (n_sub + 4),
        scratch_shapes=[
            pltpu.VMEM((candidates // LANES, LANES), I32),
            pltpu.VMEM((ENDS, 2 * cap), BF16),
            pltpu.VMEM((cols, ENDS), BF16),
            pltpu.VMEM((2 * rows, LANES), F32),
            pltpu.SemaphoreType.DMA((4,)),
            pltpu.SemaphoreType.DMA((chunks,)),
        ],
        compiler_params=params,
        cost_estimate=pl.CostEstimate(
            flops=2 * rows_dev * cols * ENDS, bytes_accessed=rows_dev * cols * 2, transcendentals=0
        ),
        name="pair_values",
    )(*map(in_hbm, (dfactors, block_mask, base, table, slots)))
    share, notes = outs[0], outs[1:n_sub]
    factors[0], block_mask, base, slots = outs[n_sub:]

    notes = [lax.ppermute(note, "sub", ring) for note, ring in zip(notes, rings[1:])]
    share = functools.reduce(jnp.add, [share] + [note[: 4 * rows] for note in notes])
    width = chunk_of(cap, 256)
    hot = pltpu.VMEM((cap // width, n_sub * cols, width), BF16)
    columns = pltpu.VMEM((my_rows, cap), BF16)
    masked = pltpu.VMEM((my_rows, n_sub * cols), BF16)
    columns_cost = pl.CostEstimate(
        flops=2 * my_rows * cols * n_sub * cap,
        bytes_accessed=my_rows * (cols * n_sub + cap) * 2,
        transcendentals=0,
    )
    factors = [*factors, *notes, block_mask]
    masked, first, share = pl.pallas_call(
        functools.partial(early_kernel, n_sub),
        out_shape=[masked, columns, pltpu.VMEM(share.shape, F32)],
        in_specs=[vmem] * (len(factors) + 2),
        out_specs=[vmem] * 3,
        scratch_shapes=[hot],
        compiler_params=params,
        name="early_columns",
    )(*map(in_vmem, (*factors, slots, share)))
    shares = [share, *from_other_mon(share, lax.axis_size("mon"), n_sub)]

    masked, first = pl.pallas_call(
        functools.partial(first_kernel, n_sub),
        out_shape=[pltpu.VMEM(masked.shape, BF16), columns],
        in_specs=[vmem] * (len(factors) + 1) + [smem] + [vmem] * 2,
        out_specs=[vmem] * 2,
        input_output_aliases={len(factors) + 2: 0, len(factors) + 3: 1},
        scratch_shapes=[hot],
        compiler_params=params,
        cost_estimate=columns_cost,
        name="first_columns",
    )(*map(in_vmem, (*factors, slots)), pair_counts, *map(in_vmem, (masked, first)))
    second, out = pl.pallas_call(
        functools.partial(second_kernel, n_sub),
        out_shape=[columns, pltpu.HBM((my_rows, cap), BF16)],
        in_specs=[vmem] * 2 + [smem],
        out_specs=[vmem, hbm],
        scratch_shapes=[
            hot,
            pltpu.VMEM((my_rows, width), BF16),
            pltpu.SemaphoreType.DMA((cap // width,)),
        ],
        compiler_params=params,
        cost_estimate=columns_cost,
        name="second_columns",
    )(*map(in_vmem, (masked, slots)), pair_counts)
    return pl.pallas_call(
        functools.partial(flows_kernel, len(shares), width),
        out_shape=jax.ShapeDtypeStruct((my_rows, cap), BF16),
        in_specs=[vmem] * (len(shares) + 3) + [smem, hbm],
        out_specs=hbm,
        input_output_aliases={len(shares) + 4: 0},
        scratch_shapes=[
            pltpu.VMEM((my_rows, cap), BF16),
            pltpu.SemaphoreType.DMA((2 * my_rows // BLOCK,)),
        ],
        compiler_params=params,
        cost_estimate=pl.CostEstimate(
            flops=6 * my_rows * cap, bytes_accessed=my_rows * cap * 2, transcendentals=0
        ),
        name="post_flows",
    )(*map(in_vmem, (*shares, base, first, second)), pair_counts, in_hbm(out))


def solution(mesh):
    return jax.shard_map(
        on_device,
        mesh=mesh,
        in_specs=(
            P("mon", "sub"),
            P("mon", "sub"),
            P("mon"),
            P(),
            P(("grp", "pair"), None),
            P(("grp", "pair")),
        ),
        out_specs=P(("mon", "sub"), ("grp", "pair")),
        check_vma=False,
    )
```

```python
import functools

import jax
import jax.numpy as jnp
from jax import lax
from jax.experimental import pallas as pl
from jax.experimental.pallas import tpu as pltpu
from jax.sharding import PartitionSpec as P

BLOCK = 128
LANES = 128
SUBLANES = 8
ENDS = 256
VMEM_LIMIT = 16 * 1024 * 1024
F32 = jnp.float32
BF16 = jnp.bfloat16
I32 = jnp.int32


def chunk_of(total, want):
    size = min(total, want)
    while total % size:
        size -= BLOCK
    return size


def dense_rows(cap):
    return -(-cap // (LANES * SUBLANES)) * SUBLANES


def one_hot(hit):
    return jnp.where(hit, 1.0, 0.0).astype(BF16)


def iota(shape, axis):
    return lax.broadcasted_iota(I32, shape, axis)


def dense(line):
    cap = line.shape[1]
    rows = dense_rows(cap)
    pieces = [line[:, c : c + LANES] for c in range(0, cap, LANES)]
    if len(pieces) < rows:
        pieces.append(jnp.zeros((rows - len(pieces), LANES), line.dtype))
    return jnp.concatenate(pieces, axis=0)


def look_up(table, index):
    high, low = index >> 7, index & 127
    found = jnp.zeros(index.shape, table.dtype)
    for b in range(table.shape[0]):
        line = jnp.broadcast_to(table[b : b + 1], index.shape)
        value = jnp.take_along_axis(line, low, axis=1, mode="promise_in_bounds")
        found = jnp.where(high == b, value, found)
    return found


def values_kernel(
    n_sub, d_hbm, mask_hbm, base_hbm, rows_hbm, slots_hbm, *refs
):
    share_ref, *note_refs = refs[:n_sub]
    (
        d_ref, mask_ref, base_ref, slots_ref, rows_ref, perm_ref, hot_ref, cross_ref, sems, d_sems
    ) = refs[n_sub:]
    rows_dev, cols = d_ref.shape
    chunks = d_sems.shape[0]
    chunk = rows_dev // chunks
    cap = slots_ref.shape[1]
    lines = cap // LANES
    rows = dense_rows(cap)
    sub_index = lax.axis_index("sub")
    small = [
        pltpu.make_async_copy(src, dst, sems.at[i])
        for i, (src, dst) in enumerate(
            [(slots_hbm, slots_ref), (rows_hbm, rows_ref), (base_hbm, base_ref), (mask_hbm, mask_ref)]
        )
    ]
    large = [
        pltpu.make_async_copy(
            d_hbm.at[pl.ds(i * chunk, chunk)], d_ref.at[pl.ds(i * chunk, chunk)], d_sems.at[i]
        )
        for i in range(chunks)
    ]
    for copy in small + large:
        copy.start()

    small[0].wait()
    small[1].wait()
    first, second = dense(slots_ref[0:1, :]), dense(slots_ref[1:2, :])
    table = rows_ref[...]
    row = jnp.concatenate([look_up(table, first), look_up(table, second)], axis=0)
    row = row - lax.axis_index("mon") * rows_dev
    col = jnp.concatenate([second, first], axis=0) - sub_index * cols
    used = lax.rem(iota(row.shape, 0), rows) < lines
    here = used & (row >= 0) & (row < rows_dev) & (col >= 0) & (col < cols)

    flags = one_hot(here)
    height = flags.shape[0]
    above = jnp.dot(
        one_hot(iota((height, height), 1) < iota((height, height), 0)),
        flags,
        preferred_element_type=F32,
    ).astype(BF16)
    place = jnp.dot(
        jnp.concatenate([flags, above], axis=1),
        jnp.concatenate(
            [
                one_hot(iota((LANES, LANES), 0) <= iota((LANES, LANES), 1)),
                jnp.ones((LANES, LANES), BF16),
            ],
            axis=0,
        ),
        preferred_element_type=F32,
    ).astype(I32)
    place = jnp.where(here, place - 1, -1)
    digits = [(x >> shift) & 255 for x in (col, row) for shift in (0, 8)]
    order = [half * rows + b for half in range(2) for b in range(lines)]
    ends = jnp.concatenate(
        [jnp.concatenate([x[r : r + 1] for x in digits], axis=0) for r in order], axis=1
    )
    ends = ends.astype(F32).astype(BF16)

    def pick(start, copies=()):
        for at, r in enumerate(order):
            perm_ref[:, at * LANES : (at + 1) * LANES] = one_hot(
                iota((ENDS, LANES), 0) + start == place[r : r + 1]
            )
        for copy in copies:
            copy.wait()
        packed = lax.dot_general(
            ends, perm_ref[...], (((1,), (1,)), ((), ())), preferred_element_type=F32
        ).astype(I32)
        end_col = packed[0:1] + (packed[1:2] << 8)
        end_row = packed[2:3] + (packed[3:4] << 8)
        hot_ref[...] = one_hot(iota((cols, ENDS), 0) == end_col)
        keep = jnp.dot(
            mask_ref[...].astype(F32).astype(BF16), hot_ref[...], preferred_element_type=F32
        )
        keep = jnp.sum(
            jnp.where(iota(keep.shape, 0) == (end_row >> 7), keep, 0.0), axis=0, keepdims=True
        )
        total = jnp.zeros((SUBLANES, ENDS), F32)
        for i in range(chunks):
            values = jnp.dot(
                d_ref[i * chunk : (i + 1) * chunk, :], hot_ref[...], preferred_element_type=F32
            )
            picked = jnp.where(iota((chunk, ENDS), 0) + i * chunk == end_row, values, 0.0)
            total += jnp.sum(picked.reshape(chunk // SUBLANES, SUBLANES, ENDS), axis=0)
        value = jnp.sum(total, axis=0, keepdims=True) * keep
        value = jnp.concatenate([value[:, q : q + LANES] for q in range(0, ENDS, LANES)], axis=0)
        return look_up(value, place - start)

    def put(cross, flow):
        for ref in (share_ref, *note_refs):
            ref[: 2 * rows, :] = cross
            ref[2 * rows : 4 * rows, :] = flow

    cross = pick(0, small[2:] + large)
    flow = jnp.where(sub_index == 0, look_up(base_ref[...], row), 0.0)
    put(cross, flow)
    my_blocks = mask_ref.shape[0] // n_sub
    for s, ref in enumerate(note_refs, 1):
        block = pl.multiple_of(lax.rem(sub_index + s, n_sub) * my_blocks, my_blocks)
        for c in range(cols // LANES):
            at = 4 * rows + c * my_blocks
            ref[at : at + my_blocks, :] = mask_ref[
                pl.ds(block, my_blocks), c * LANES : (c + 1) * LANES
            ].astype(F32)
    count = jnp.max(place) + 1

    @pl.when(count > ENDS)
    def _():
        cross_ref[...] = cross

        def more(i, _):
            cross_ref[...] += pick(i * ENDS)
            return 0

        lax.fori_loop(1, pl.cdiv(count, ENDS), more, 0)
        put(cross_ref[...], flow)


def pick_columns(parts, slot, starts, cols, masked_ref, hot_ref, out_ref):
    width = hot_ref.shape[2]
    for part in parts:
        lanes = slice(part * width, (part + 1) * width)
        for s, start in enumerate(starts):
            hot_ref[part, s * cols : (s + 1) * cols, :] = one_hot(
                iota((cols, width), 0) == slot[:, lanes] - start
            )
        out_ref[:, lanes] = jnp.dot(
            masked_ref[...], hot_ref[part], preferred_element_type=F32
        ).astype(BF16)


def fewest(parts):
    return min(2, parts)


def live_parts(count, width, parts):
    return jnp.clip((count + width - 1) // width, fewest(parts), parts)


def is_early():
    return lax.axis_index("mon") < lax.axis_size("mon") // 2


def column_starts(n_sub, cols):
    return [lax.rem(lax.axis_index("sub") + n_sub - s, n_sub) * cols for s in range(n_sub)]


def mask_factors(n_sub, refs, masked_ref):
    d_refs, note_refs, mask_ref = refs[:n_sub], refs[n_sub:-1], refs[-1]
    my_rows, all_cols = masked_ref.shape
    cols = all_cols // n_sub
    my_blocks = my_rows // BLOCK
    sub_index = lax.axis_index("sub")
    my_start = pl.multiple_of(sub_index * my_rows, my_rows)
    my_block = pl.multiple_of(sub_index * my_blocks, my_blocks)
    for s in range(n_sub):
        if s == 0:
            keep = mask_ref[pl.ds(my_block, my_blocks), :].astype(F32)
        else:
            ref = note_refs[s - 1]
            ends = range(ref.shape[0] - (cols // LANES) * my_blocks, ref.shape[0], my_blocks)
            keep = jnp.concatenate([ref[at : at + my_blocks, :] for at in ends], axis=1)
        keep = keep.astype(BF16)
        for b in range(my_blocks):
            masked_ref[b * BLOCK : (b + 1) * BLOCK, s * cols : (s + 1) * cols] = (
                d_refs[s][pl.ds(my_start + b * BLOCK, BLOCK), :] * keep[b : b + 1]
            )


def early_kernel(n_sub, *refs):
    *factor_refs, slots_ref, share_ref, masked_ref, first_ref, shared_ref, hot_ref = refs
    shared_ref[...] = share_ref[...]
    cols = masked_ref.shape[1] // n_sub

    @pl.when(is_early())
    def _():
        mask_factors(n_sub, factor_refs, masked_ref)
        starts = column_starts(n_sub, cols)
        pick_columns([0], slots_ref[0:1, :], starts, cols, masked_ref, hot_ref, first_ref)


def first_kernel(n_sub, *refs):
    *factor_refs, slots_ref, count_ref, _, _, masked_ref, first_ref, hot_ref = refs
    cols = masked_ref.shape[1] // n_sub
    slot = slots_ref[0:1, :]
    starts = column_starts(n_sub, cols)
    parts, _, width = hot_ref.shape
    live = live_parts(count_ref[0], width, parts)
    for n_parts in range(fewest(parts), parts + 1):

        @pl.when((live == n_parts) & jnp.logical_not(is_early()))
        def _():
            mask_factors(n_sub, factor_refs, masked_ref)
            pick_columns(range(n_parts), slot, starts, cols, masked_ref, hot_ref, first_ref)

        @pl.when((live == n_parts) & is_early())
        def _():
            pick_columns(range(1, n_parts), slot, starts, cols, masked_ref, hot_ref, first_ref)


def second_kernel(
    n_sub, masked_ref, slots_ref, count_ref, second_ref, out_hbm, hot_ref, zero_ref, sems
):
    cols = masked_ref.shape[1] // n_sub
    slot = slots_ref[1:2, :]
    starts = column_starts(n_sub, cols)
    parts, _, width = hot_ref.shape
    live = live_parts(count_ref[0], width, parts)
    for n_parts in range(fewest(parts), parts + 1):

        @pl.when(live == n_parts)
        def _():
            copies = [
                pltpu.make_async_copy(
                    zero_ref, out_hbm.at[:, part * width : (part + 1) * width], sems.at[part]
                )
                for part in range(n_parts, parts)
            ]
            if copies:
                zero_ref[...] = jnp.zeros_like(zero_ref)
            for copy in copies:
                copy.start()
            pick_columns(range(n_parts), slot, starts, cols, masked_ref, hot_ref, second_ref)
            for copy in copies:
                copy.wait()


def flows_kernel(n_shares, width, *refs):
    share_refs, refs = refs[:n_shares], refs[n_shares:]
    base_ref, first_ref, second_ref, count_ref, _, out_hbm, post_ref, out_sems = refs
    my_rows, cap = post_ref.shape
    my_blocks = my_rows // BLOCK
    rows = dense_rows(cap)
    total = share_refs[0][...]
    for ref in share_refs[1:]:
        total = total + ref[...]
    cross_first, cross_second, flow_first, flow_second = (
        total[i * rows : (i + 1) * rows] for i in range(4)
    )
    determinant = 1.0 - cross_first * cross_second
    shift_first = (flow_first + cross_first * flow_second) / determinant
    shift_second = (flow_second + cross_second * flow_first) / determinant
    my_block = pl.multiple_of(lax.axis_index("sub") * my_blocks, my_blocks)
    base = jnp.swapaxes(base_ref[pl.ds(my_block, my_blocks), :], 0, 1)

    per = 1 if my_blocks % 2 else 2

    def write(lines):
        live = [iota((1, LANES), 1) + line * LANES < count_ref[0] for line in lines]
        weights = [
            [
                jnp.broadcast_to(shift[line : line + 1], (BLOCK, LANES)).astype(BF16)
                for line in lines
            ]
            for shift in (shift_first, shift_second)
        ]
        wide = slice(0, len(lines) * LANES)
        out_copies = []
        for b in range(my_blocks):
            block = slice(b * BLOCK, (b + 1) * BLOCK)
            start = jnp.broadcast_to(base[:, b : b + 1], (BLOCK, LANES))
            for line in lines:
                lanes = slice(line * LANES, (line + 1) * LANES)
                change = (
                    weights[0][line] * first_ref[block, lanes]
                    + weights[1][line] * second_ref[block, lanes]
                )
                post_ref[block, lanes] = jnp.where(
                    live[line], start + change.astype(F32), 0.0
                ).astype(BF16)
            if (b + 1) % per == 0:
                done = slice((b + 1 - per) * BLOCK, (b + 1) * BLOCK)
                out_copies.append(
                    pltpu.make_async_copy(
                        post_ref.at[done, wide], out_hbm.at[done, wide], out_sems.at[b]
                    )
                )
                out_copies[-1].start()
        for copy in out_copies:
            copy.wait()

    parts = cap // width
    live_count = live_parts(count_ref[0], width, parts)
    for n_parts in range(fewest(parts), parts + 1):
        pl.when(live_count == n_parts)(
            functools.partial(write, range(n_parts * width // LANES))
        )


def partners(n_mon):
    half = n_mon // 2
    if n_mon & (n_mon - 1):
        return [[(m + k) % n_mon for m in range(n_mon)] for k in range(1, n_mon)]
    across = [
        [m ^ (half + k) if m < half else m ^ (n_mon - 1 - k) for m in range(n_mon)]
        for k in range(half)
    ]
    return across + [[m ^ k for m in range(n_mon)] for k in range(half - 1, 0, -1)]


def from_other_mon(share, n_mon, n_sub):
    return [
        lax.ppermute(
            share,
            ("mon", "sub"),
            [
                (m * n_sub + s, to[m] * n_sub + n_sub - 1 - s)
                for m in range(n_mon)
                for s in range(n_sub)
            ],
        )
        for to in reversed(partners(n_mon))
    ]


def on_device(dfactors, block_mask, base_flow, branch_row, pair_slots, pair_counts):
    rows_dev, cols = dfactors.shape
    blocks = rows_dev // BLOCK
    candidates = branch_row.shape[0]
    cap = pair_slots.shape[0]
    rows = dense_rows(cap)
    n_sub = lax.axis_size("sub")
    my_rows = rows_dev // n_sub
    slots = pair_slots.T
    base = base_flow.reshape(blocks, BLOCK)
    table = branch_row.reshape(candidates // LANES, LANES)
    hbm = pl.BlockSpec(memory_space=pltpu.HBM)
    in_hbm = functools.partial(pltpu.with_memory_space_constraint, memory_space=pltpu.HBM)
    in_vmem = functools.partial(pltpu.with_memory_space_constraint, memory_space=pltpu.VMEM)
    vmem = pl.BlockSpec(memory_space=pltpu.VMEM)
    smem = pl.BlockSpec(memory_space=pltpu.SMEM)
    params = pltpu.CompilerParams(vmem_limit_bytes=VMEM_LIMIT)
    rings = [[(i, (i + s) % n_sub) for i in range(n_sub)] for s in range(n_sub)]

    factors = [dfactors] + [lax.ppermute(dfactors, "sub", ring) for ring in rings[1:]]

    chunks = rows_dev // chunk_of(rows_dev, 512)
    note_rows = 4 * rows + (cols // LANES) * (my_rows // BLOCK)
    outs = pl.pallas_call(
        functools.partial(values_kernel, n_sub),
        out_shape=[pltpu.VMEM((4 * rows, LANES), F32)]
        + [pltpu.VMEM((note_rows, LANES), F32)] * (n_sub - 1)
        + [
            pltpu.VMEM((rows_dev, cols), BF16),
            pltpu.VMEM((blocks, cols), I32),
            pltpu.VMEM((blocks, BLOCK), F32),
            pltpu.VMEM((2, cap), I32),
        ],
        in_specs=[hbm] * 5,
        out_specs=[vmem] * (n_sub + 4),
        scratch_shapes=[
            pltpu.VMEM((candidates // LANES, LANES), I32),
            pltpu.VMEM((ENDS, 2 * cap), BF16),
            pltpu.VMEM((cols, ENDS), BF16),
            pltpu.VMEM((2 * rows, LANES), F32),
            pltpu.SemaphoreType.DMA((4,)),
            pltpu.SemaphoreType.DMA((chunks,)),
        ],
        compiler_params=params,
        cost_estimate=pl.CostEstimate(
            flops=2 * rows_dev * cols * ENDS, bytes_accessed=rows_dev * cols * 2, transcendentals=0
        ),
        name="pair_values",
    )(*map(in_hbm, (dfactors, block_mask, base, table, slots)))
    share, notes = outs[0], outs[1:n_sub]
    factors[0], block_mask, base, slots = outs[n_sub:]

    notes = [lax.ppermute(note, "sub", ring) for note, ring in zip(notes, rings[1:])]
    share = functools.reduce(jnp.add, [share] + [note[: 4 * rows] for note in notes])
    width = chunk_of(cap, 256)
    hot = pltpu.VMEM((cap // width, n_sub * cols, width), BF16)
    columns = pltpu.VMEM((my_rows, cap), BF16)
    masked = pltpu.VMEM((my_rows, n_sub * cols), BF16)
    columns_cost = pl.CostEstimate(
        flops=2 * my_rows * cols * n_sub * cap,
        bytes_accessed=my_rows * (cols * n_sub + cap) * 2,
        transcendentals=0,
    )
    factors = [*factors, *notes, block_mask]
    masked, first, share = pl.pallas_call(
        functools.partial(early_kernel, n_sub),
        out_shape=[masked, columns, pltpu.VMEM(share.shape, F32)],
        in_specs=[vmem] * (len(factors) + 2),
        out_specs=[vmem] * 3,
        scratch_shapes=[hot],
        compiler_params=params,
        name="early_columns",
    )(*map(in_vmem, (*factors, slots, share)))
    shares = [share, *from_other_mon(share, lax.axis_size("mon"), n_sub)]

    masked, first = pl.pallas_call(
        functools.partial(first_kernel, n_sub),
        out_shape=[pltpu.VMEM(masked.shape, BF16), columns],
        in_specs=[vmem] * (len(factors) + 1) + [smem] + [vmem] * 2,
        out_specs=[vmem] * 2,
        input_output_aliases={len(factors) + 2: 0, len(factors) + 3: 1},
        scratch_shapes=[hot],
        compiler_params=params,
        cost_estimate=columns_cost,
        name="first_columns",
    )(*map(in_vmem, (*factors, slots)), pair_counts, *map(in_vmem, (masked, first)))
    second, out = pl.pallas_call(
        functools.partial(second_kernel, n_sub),
        out_shape=[columns, pltpu.HBM((my_rows, cap), BF16)],
        in_specs=[vmem] * 2 + [smem],
        out_specs=[vmem, hbm],
        scratch_shapes=[
            hot,
            pltpu.VMEM((my_rows, width), BF16),
            pltpu.SemaphoreType.DMA((cap // width,)),
        ],
        compiler_params=params,
        cost_estimate=columns_cost,
        name="second_columns",
    )(*map(in_vmem, (masked, slots)), pair_counts)
    return pl.pallas_call(
        functools.partial(flows_kernel, len(shares), width),
        out_shape=jax.ShapeDtypeStruct((my_rows, cap), BF16),
        in_specs=[vmem] * (len(shares) + 3) + [smem, hbm],
        out_specs=hbm,
        input_output_aliases={len(shares) + 4: 0},
        scratch_shapes=[
            pltpu.VMEM((my_rows, cap), BF16),
            pltpu.SemaphoreType.DMA((my_rows // BLOCK,)),
        ],
        compiler_params=params,
        cost_estimate=pl.CostEstimate(
            flops=6 * my_rows * cap, bytes_accessed=my_rows * cap * 2, transcendentals=0
        ),
        name="post_flows",
    )(*map(in_vmem, (*shares, base, first, second)), pair_counts, in_hbm(out))


def solution(mesh):
    return jax.shard_map(
        on_device,
        mesh=mesh,
        in_specs=(
            P("mon", "sub"),
            P("mon", "sub"),
            P("mon"),
            P(),
            P(("grp", "pair"), None),
            P(("grp", "pair")),
        ),
        out_specs=P(("mon", "sub"), ("grp", "pair")),
        check_vma=False,
    )
```

```python
import functools

import jax
import jax.numpy as jnp
from jax import lax
from jax.experimental import pallas as pl
from jax.experimental.pallas import tpu as pltpu
from jax.sharding import PartitionSpec as P

BLOCK = 128
LANES = 128
SUBLANES = 8
ENDS = 256
VMEM_LIMIT = 16 * 1024 * 1024
F32 = jnp.float32
BF16 = jnp.bfloat16
I32 = jnp.int32


def chunk_of(total, want):
    size = min(total, want)
    while total % size:
        size -= BLOCK
    return size


def dense_rows(cap):
    return -(-cap // (LANES * SUBLANES)) * SUBLANES


def one_hot(hit):
    return jnp.where(hit, 1.0, 0.0).astype(BF16)


def iota(shape, axis):
    return lax.broadcasted_iota(I32, shape, axis)


def dense(line):
    cap = line.shape[1]
    rows = dense_rows(cap)
    pieces = [line[:, c : c + LANES] for c in range(0, cap, LANES)]
    if len(pieces) < rows:
        pieces.append(jnp.zeros((rows - len(pieces), LANES), line.dtype))
    return jnp.concatenate(pieces, axis=0)


def look_up(table, index):
    high, low = index >> 7, index & 127
    found = jnp.zeros(index.shape, table.dtype)
    for b in range(table.shape[0]):
        line = jnp.broadcast_to(table[b : b + 1], index.shape)
        value = jnp.take_along_axis(line, low, axis=1, mode="promise_in_bounds")
        found = jnp.where(high == b, value, found)
    return found


def values_kernel(
    n_sub, d_hbm, mask_hbm, base_hbm, rows_hbm, slots_hbm, *refs
):
    share_ref, *note_refs = refs[:n_sub]
    (
        d_ref, mask_ref, base_ref, slots_ref, rows_ref, perm_ref, hot_ref, cross_ref, sems, d_sems
    ) = refs[n_sub:]
    rows_dev, cols = d_ref.shape
    chunks = d_sems.shape[0]
    chunk = rows_dev // chunks
    cap = slots_ref.shape[1]
    lines = cap // LANES
    rows = dense_rows(cap)
    sub_index = lax.axis_index("sub")
    small = [
        pltpu.make_async_copy(src, dst, sems.at[i])
        for i, (src, dst) in enumerate(
            [(slots_hbm, slots_ref), (rows_hbm, rows_ref), (base_hbm, base_ref), (mask_hbm, mask_ref)]
        )
    ]
    large = [
        pltpu.make_async_copy(
            d_hbm.at[pl.ds(i * chunk, chunk)], d_ref.at[pl.ds(i * chunk, chunk)], d_sems.at[i]
        )
        for i in range(chunks)
    ]
    for copy in small[:2] + large + small[2:]:
        copy.start()

    small[0].wait()
    small[1].wait()
    first, second = dense(slots_ref[0:1, :]), dense(slots_ref[1:2, :])
    table = rows_ref[...]
    row = jnp.concatenate([look_up(table, first), look_up(table, second)], axis=0)
    row = row - lax.axis_index("mon") * rows_dev
    col = jnp.concatenate([second, first], axis=0) - sub_index * cols
    used = lax.rem(iota(row.shape, 0), rows) < lines
    here = used & (row >= 0) & (row < rows_dev) & (col >= 0) & (col < cols)

    flags = one_hot(here)
    height = flags.shape[0]
    above = jnp.dot(
        one_hot(iota((height, height), 1) < iota((height, height), 0)),
        flags,
        preferred_element_type=F32,
    ).astype(BF16)
    place = jnp.dot(
        jnp.concatenate([flags, above], axis=1),
        jnp.concatenate(
            [
                one_hot(iota((LANES, LANES), 0) <= iota((LANES, LANES), 1)),
                jnp.ones((LANES, LANES), BF16),
            ],
            axis=0,
        ),
        preferred_element_type=F32,
    ).astype(I32)
    place = jnp.where(here, place - 1, -1)
    digits = [(x >> shift) & 255 for x in (col, row) for shift in (0, 8)]
    order = [half * rows + b for half in range(2) for b in range(lines)]
    ends = jnp.concatenate(
        [jnp.concatenate([x[r : r + 1] for x in digits], axis=0) for r in order], axis=1
    )
    ends = ends.astype(F32).astype(BF16)

    def pick(start, copies=()):
        for at, r in enumerate(order):
            perm_ref[:, at * LANES : (at + 1) * LANES] = one_hot(
                iota((ENDS, LANES), 0) + start == place[r : r + 1]
            )
        packed = lax.dot_general(
            ends, perm_ref[...], (((1,), (1,)), ((), ())), preferred_element_type=F32
        ).astype(I32)
        end_col = packed[0:1] + (packed[1:2] << 8)
        end_row = packed[2:3] + (packed[3:4] << 8)
        hot_ref[...] = one_hot(iota((cols, ENDS), 0) == end_col)
        for copy in copies:
            copy.wait()
        keep = jnp.dot(
            mask_ref[...].astype(F32).astype(BF16), hot_ref[...], preferred_element_type=F32
        )
        keep = jnp.sum(
            jnp.where(iota(keep.shape, 0) == (end_row >> 7), keep, 0.0), axis=0, keepdims=True
        )
        total = jnp.zeros((SUBLANES, ENDS), F32)
        for i in range(chunks):
            values = jnp.dot(
                d_ref[i * chunk : (i + 1) * chunk, :], hot_ref[...], preferred_element_type=F32
            )
            picked = jnp.where(iota((chunk, ENDS), 0) + i * chunk == end_row, values, 0.0)
            total += jnp.sum(picked.reshape(chunk // SUBLANES, SUBLANES, ENDS), axis=0)
        value = jnp.sum(total, axis=0, keepdims=True) * keep
        value = jnp.concatenate([value[:, q : q + LANES] for q in range(0, ENDS, LANES)], axis=0)
        return look_up(value, place - start)

    def put(cross, flow):
        for ref in (share_ref, *note_refs):
            ref[: 2 * rows, :] = cross
            ref[2 * rows : 4 * rows, :] = flow

    cross = pick(0, small[2:] + large)
    flow = jnp.where(sub_index == 0, look_up(base_ref[...], row), 0.0)
    put(cross, flow)
    my_blocks = mask_ref.shape[0] // n_sub
    for s, ref in enumerate(note_refs, 1):
        block = pl.multiple_of(lax.rem(sub_index + s, n_sub) * my_blocks, my_blocks)
        for c in range(cols // LANES):
            at = 4 * rows + c * my_blocks
            ref[at : at + my_blocks, :] = mask_ref[
                pl.ds(block, my_blocks), c * LANES : (c + 1) * LANES
            ].astype(F32)
    count = jnp.max(place) + 1

    @pl.when(count > ENDS)
    def _():
        cross_ref[...] = cross

        def more(i, _):
            cross_ref[...] += pick(i * ENDS)
            return 0

        lax.fori_loop(1, pl.cdiv(count, ENDS), more, 0)
        put(cross_ref[...], flow)


def pick_columns(parts, slot, starts, cols, masked_ref, hot_ref, out_ref):
    width = hot_ref.shape[2]
    for part in parts:
        lanes = slice(part * width, (part + 1) * width)
        for s, start in enumerate(starts):
            hot_ref[part, s * cols : (s + 1) * cols, :] = one_hot(
                iota((cols, width), 0) == slot[:, lanes] - start
            )
        out_ref[:, lanes] = jnp.dot(
            masked_ref[...], hot_ref[part], preferred_element_type=F32
        ).astype(BF16)


def fewest(parts):
    return min(2, parts)


def zero_rows(rows):
    return rows // BLOCK // 2 * BLOCK


def live_parts(count, width, parts):
    return jnp.clip((count + width - 1) // width, fewest(parts), parts)


def is_early():
    return lax.axis_index("mon") < lax.axis_size("mon") // 2


def column_starts(n_sub, cols):
    return [lax.rem(lax.axis_index("sub") + n_sub - s, n_sub) * cols for s in range(n_sub)]


def mask_factors(n_sub, refs, masked_ref):
    d_refs, note_refs, mask_ref = refs[:n_sub], refs[n_sub:-1], refs[-1]
    my_rows, all_cols = masked_ref.shape
    cols = all_cols // n_sub
    my_blocks = my_rows // BLOCK
    sub_index = lax.axis_index("sub")
    my_start = pl.multiple_of(sub_index * my_rows, my_rows)
    my_block = pl.multiple_of(sub_index * my_blocks, my_blocks)
    for s in range(n_sub):
        if s == 0:
            keep = mask_ref[pl.ds(my_block, my_blocks), :].astype(F32)
        else:
            ref = note_refs[s - 1]
            ends = range(ref.shape[0] - (cols // LANES) * my_blocks, ref.shape[0], my_blocks)
            keep = jnp.concatenate([ref[at : at + my_blocks, :] for at in ends], axis=1)
        keep = keep.astype(BF16)
        for b in range(my_blocks):
            masked_ref[b * BLOCK : (b + 1) * BLOCK, s * cols : (s + 1) * cols] = (
                d_refs[s][pl.ds(my_start + b * BLOCK, BLOCK), :] * keep[b : b + 1]
            )


def early_kernel(n_sub, *refs):
    *factor_refs, slots_ref, share_ref, masked_ref, first_ref, shared_ref, hot_ref = refs
    shared_ref[...] = share_ref[...]
    cols = masked_ref.shape[1] // n_sub

    @pl.when(is_early())
    def _():
        mask_factors(n_sub, factor_refs, masked_ref)
        starts = column_starts(n_sub, cols)
        pick_columns([0], slots_ref[0:1, :], starts, cols, masked_ref, hot_ref, first_ref)


def first_kernel(n_sub, *refs):
    *factor_refs, slots_ref, count_ref, _, _, masked_ref, first_ref, hot_ref = refs
    cols = masked_ref.shape[1] // n_sub
    slot = slots_ref[0:1, :]
    starts = column_starts(n_sub, cols)
    parts, _, width = hot_ref.shape
    live = live_parts(count_ref[0], width, parts)
    for n_parts in range(fewest(parts), parts + 1):

        @pl.when((live == n_parts) & jnp.logical_not(is_early()))
        def _():
            mask_factors(n_sub, factor_refs, masked_ref)
            pick_columns(range(n_parts), slot, starts, cols, masked_ref, hot_ref, first_ref)

        @pl.when((live == n_parts) & is_early())
        def _():
            pick_columns(range(1, n_parts), slot, starts, cols, masked_ref, hot_ref, first_ref)


def second_kernel(
    n_sub, masked_ref, slots_ref, count_ref, second_ref, out_hbm, hot_ref, zero_ref, sems
):
    cols = masked_ref.shape[1] // n_sub
    slot = slots_ref[1:2, :]
    starts = column_starts(n_sub, cols)
    parts, _, width = hot_ref.shape
    zero_start = masked_ref.shape[0] - zero_ref.shape[0]
    live = live_parts(count_ref[0], width, parts)
    for n_parts in range(fewest(parts), parts + 1):

        @pl.when(live == n_parts)
        def _():
            copies = [
                pltpu.make_async_copy(
                    zero_ref,
                    out_hbm.at[
                        pl.ds(zero_start, zero_ref.shape[0]), part * width : (part + 1) * width
                    ],
                    sems.at[part],
                )
                for part in range(n_parts, parts)
            ]
            if copies:
                zero_ref[...] = jnp.zeros_like(zero_ref)
            for copy in copies:
                copy.start()
            pick_columns(range(n_parts), slot, starts, cols, masked_ref, hot_ref, second_ref)
            for copy in copies:
                copy.wait()


def flows_kernel(n_shares, width, *refs):
    share_refs, refs = refs[:n_shares], refs[n_shares:]
    base_ref, first_ref, second_ref, count_ref, _, out_hbm, post_ref, out_sems = refs
    my_rows, cap = post_ref.shape
    my_blocks = my_rows // BLOCK
    rows = dense_rows(cap)
    total = share_refs[0][...]
    for ref in share_refs[1:]:
        total = total + ref[...]
    cross_first, cross_second, flow_first, flow_second = (
        total[i * rows : (i + 1) * rows] for i in range(4)
    )
    determinant = 1.0 - cross_first * cross_second
    shift_first = (flow_first + cross_first * flow_second) / determinant
    shift_second = (flow_second + cross_second * flow_first) / determinant
    my_block = pl.multiple_of(lax.axis_index("sub") * my_blocks, my_blocks)
    base = jnp.swapaxes(base_ref[pl.ds(my_block, my_blocks), :], 0, 1)

    def write(lines):
        live = [iota((1, LANES), 1) + line * LANES < count_ref[0] for line in lines]
        weights = [
            [
                jnp.broadcast_to(shift[line : line + 1], (BLOCK, LANES)).astype(BF16)
                for line in lines
            ]
            for shift in (shift_first, shift_second)
        ]
        out_copies = []
        for b in range(my_blocks):
            block = slice(b * BLOCK, (b + 1) * BLOCK)
            wide = slice(0, len(lines) * LANES)
            if b * BLOCK < my_rows - zero_rows(my_rows) and wide.stop < cap:
                post_ref[block, wide.stop :] = jnp.zeros((BLOCK, cap - wide.stop), BF16)
                wide = slice(0, cap)
            start = jnp.broadcast_to(base[:, b : b + 1], (BLOCK, LANES))
            for line in lines:
                lanes = slice(line * LANES, (line + 1) * LANES)
                change = (
                    weights[0][line] * first_ref[block, lanes]
                    + weights[1][line] * second_ref[block, lanes]
                )
                post_ref[block, lanes] = jnp.where(
                    live[line], start + change.astype(F32), 0.0
                ).astype(BF16)
            out_copies.append(
                pltpu.make_async_copy(
                    post_ref.at[block, wide], out_hbm.at[block, wide], out_sems.at[b]
                )
            )
            out_copies[-1].start()
        for copy in out_copies:
            copy.wait()

    parts = cap // width
    live_count = live_parts(count_ref[0], width, parts)
    for n_parts in range(fewest(parts), parts + 1):
        pl.when(live_count == n_parts)(
            functools.partial(write, range(n_parts * width // LANES))
        )


def partners(n_mon):
    half = n_mon // 2
    if n_mon & (n_mon - 1):
        return [[(m + k) % n_mon for m in range(n_mon)] for k in range(1, n_mon)]
    across = [
        [m ^ (half + k) if m < half else m ^ (n_mon - 1 - k) for m in range(n_mon)]
        for k in range(half)
    ]
    return across + [[m ^ k for m in range(n_mon)] for k in range(half - 1, 0, -1)]


def from_other_mon(share, n_mon, n_sub):
    return [
        lax.ppermute(
            share,
            ("mon", "sub"),
            [
                (m * n_sub + s, to[m] * n_sub + n_sub - 1 - s)
                for m in range(n_mon)
                for s in range(n_sub)
            ],
        )
        for to in reversed(partners(n_mon))
    ]


def on_device(dfactors, block_mask, base_flow, branch_row, pair_slots, pair_counts):
    rows_dev, cols = dfactors.shape
    blocks = rows_dev // BLOCK
    candidates = branch_row.shape[0]
    cap = pair_slots.shape[0]
    rows = dense_rows(cap)
    n_sub = lax.axis_size("sub")
    my_rows = rows_dev // n_sub
    slots = pair_slots.T
    base = base_flow.reshape(blocks, BLOCK)
    table = branch_row.reshape(candidates // LANES, LANES)
    hbm = pl.BlockSpec(memory_space=pltpu.HBM)
    in_hbm = functools.partial(pltpu.with_memory_space_constraint, memory_space=pltpu.HBM)
    in_vmem = functools.partial(pltpu.with_memory_space_constraint, memory_space=pltpu.VMEM)
    vmem = pl.BlockSpec(memory_space=pltpu.VMEM)
    smem = pl.BlockSpec(memory_space=pltpu.SMEM)
    params = pltpu.CompilerParams(vmem_limit_bytes=VMEM_LIMIT)
    rings = [[(i, (i + s) % n_sub) for i in range(n_sub)] for s in range(n_sub)]

    factors = [dfactors] + [lax.ppermute(dfactors, "sub", ring) for ring in rings[1:]]

    chunks = rows_dev // chunk_of(rows_dev, 512)
    note_rows = 4 * rows + (cols // LANES) * (my_rows // BLOCK)
    outs = pl.pallas_call(
        functools.partial(values_kernel, n_sub),
        out_shape=[pltpu.VMEM((4 * rows, LANES), F32)]
        + [pltpu.VMEM((note_rows, LANES), F32)] * (n_sub - 1)
        + [
            pltpu.VMEM((rows_dev, cols), BF16),
            pltpu.VMEM((blocks, cols), I32),
            pltpu.VMEM((blocks, BLOCK), F32),
            pltpu.VMEM((2, cap), I32),
        ],
        in_specs=[hbm] * 5,
        out_specs=[vmem] * (n_sub + 4),
        scratch_shapes=[
            pltpu.VMEM((candidates // LANES, LANES), I32),
            pltpu.VMEM((ENDS, 2 * cap), BF16),
            pltpu.VMEM((cols, ENDS), BF16),
            pltpu.VMEM((2 * rows, LANES), F32),
            pltpu.SemaphoreType.DMA((4,)),
            pltpu.SemaphoreType.DMA((chunks,)),
        ],
        compiler_params=params,
        cost_estimate=pl.CostEstimate(
            flops=2 * rows_dev * cols * ENDS, bytes_accessed=rows_dev * cols * 2, transcendentals=0
        ),
        name="pair_values",
    )(*map(in_hbm, (dfactors, block_mask, base, table, slots)))
    share, notes = outs[0], outs[1:n_sub]
    factors[0], block_mask, base, slots = outs[n_sub:]

    notes = [lax.ppermute(note, "sub", ring) for note, ring in zip(notes, rings[1:])]
    share = functools.reduce(jnp.add, [share] + [note[: 4 * rows] for note in notes])
    width = chunk_of(cap, 256)
    hot = pltpu.VMEM((cap // width, n_sub * cols, width), BF16)
    columns = pltpu.VMEM((my_rows, cap), BF16)
    masked = pltpu.VMEM((my_rows, n_sub * cols), BF16)
    columns_cost = pl.CostEstimate(
        flops=2 * my_rows * cols * n_sub * cap,
        bytes_accessed=my_rows * (cols * n_sub + cap) * 2,
        transcendentals=0,
    )
    factors = [*factors, *notes, block_mask]
    masked, first, share = pl.pallas_call(
        functools.partial(early_kernel, n_sub),
        out_shape=[masked, columns, pltpu.VMEM(share.shape, F32)],
        in_specs=[vmem] * (len(factors) + 2),
        out_specs=[vmem] * 3,
        scratch_shapes=[hot],
        compiler_params=params,
        name="early_columns",
    )(*map(in_vmem, (*factors, slots, share)))
    shares = [share, *from_other_mon(share, lax.axis_size("mon"), n_sub)]

    masked, first = pl.pallas_call(
        functools.partial(first_kernel, n_sub),
        out_shape=[pltpu.VMEM(masked.shape, BF16), columns],
        in_specs=[vmem] * (len(factors) + 1) + [smem] + [vmem] * 2,
        out_specs=[vmem] * 2,
        input_output_aliases={len(factors) + 2: 0, len(factors) + 3: 1},
        scratch_shapes=[hot],
        compiler_params=params,
        cost_estimate=columns_cost,
        name="first_columns",
    )(*map(in_vmem, (*factors, slots)), pair_counts, *map(in_vmem, (masked, first)))
    second, out = pl.pallas_call(
        functools.partial(second_kernel, n_sub),
        out_shape=[columns, pltpu.HBM((my_rows, cap), BF16)],
        in_specs=[vmem] * 2 + [smem],
        out_specs=[vmem, hbm],
        scratch_shapes=[
            hot,
            pltpu.VMEM((zero_rows(my_rows), width), BF16),
            pltpu.SemaphoreType.DMA((cap // width,)),
        ],
        compiler_params=params,
        cost_estimate=columns_cost,
        name="second_columns",
    )(*map(in_vmem, (masked, slots)), pair_counts)
    return pl.pallas_call(
        functools.partial(flows_kernel, len(shares), width),
        out_shape=jax.ShapeDtypeStruct((my_rows, cap), BF16),
        in_specs=[vmem] * (len(shares) + 3) + [smem, hbm],
        out_specs=hbm,
        input_output_aliases={len(shares) + 4: 0},
        scratch_shapes=[
            pltpu.VMEM((my_rows, cap), BF16),
            pltpu.SemaphoreType.DMA((my_rows // BLOCK,)),
        ],
        compiler_params=params,
        cost_estimate=pl.CostEstimate(
            flops=6 * my_rows * cap, bytes_accessed=my_rows * cap * 2, transcendentals=0
        ),
        name="post_flows",
    )(*map(in_vmem, (*shares, base, first, second)), pair_counts, in_hbm(out))


def solution(mesh):
    return jax.shard_map(
        on_device,
        mesh=mesh,
        in_specs=(
            P("mon", "sub"),
            P("mon", "sub"),
            P("mon"),
            P(),
            P(("grp", "pair"), None),
            P(("grp", "pair")),
        ),
        out_specs=P(("mon", "sub"), ("grp", "pair")),
        check_vma=False,
    )
```

```python
import functools

import jax
import jax.numpy as jnp
from jax import lax
from jax.experimental import pallas as pl
from jax.experimental.pallas import tpu as pltpu
from jax.sharding import PartitionSpec as P

BLOCK = 128
LANES = 128
SUBLANES = 8
ENDS = 256
VMEM_LIMIT = 16 * 1024 * 1024
F32 = jnp.float32
BF16 = jnp.bfloat16
I32 = jnp.int32


def chunk_of(total, want):
    size = min(total, want)
    while total % size:
        size -= BLOCK
    return size


def dense_rows(cap):
    return -(-cap // (LANES * SUBLANES)) * SUBLANES


def one_hot(hit):
    return jnp.where(hit, 1.0, 0.0).astype(BF16)


def iota(shape, axis):
    return lax.broadcasted_iota(I32, shape, axis)


def dense(line):
    cap = line.shape[1]
    rows = dense_rows(cap)
    pieces = [line[:, c : c + LANES] for c in range(0, cap, LANES)]
    if len(pieces) < rows:
        pieces.append(jnp.zeros((rows - len(pieces), LANES), line.dtype))
    return jnp.concatenate(pieces, axis=0)


def look_up(table, index):
    high, low = index >> 7, index & 127
    found = jnp.zeros(index.shape, table.dtype)
    for b in range(table.shape[0]):
        line = jnp.broadcast_to(table[b : b + 1], index.shape)
        value = jnp.take_along_axis(line, low, axis=1, mode="promise_in_bounds")
        found = jnp.where(high == b, value, found)
    return found


def values_kernel(
    n_sub, d_hbm, mask_hbm, base_hbm, rows_hbm, slots_hbm, *refs
):
    share_ref, *note_refs = refs[:n_sub]
    (
        d_ref, mask_ref, base_ref, slots_ref, rows_ref, perm_ref, hot_ref, cross_ref, sems, d_sems
    ) = refs[n_sub:]
    rows_dev, cols = d_ref.shape
    pieces = d_sems.shape[0]
    piece = rows_dev // pieces
    chunk = chunk_of(rows_dev, 512)
    chunks = rows_dev // chunk
    cap = slots_ref.shape[1]
    lines = cap // LANES
    rows = dense_rows(cap)
    sub_index = lax.axis_index("sub")
    small = [
        pltpu.make_async_copy(src, dst, sems.at[i])
        for i, (src, dst) in enumerate(
            [(slots_hbm, slots_ref), (rows_hbm, rows_ref), (base_hbm, base_ref), (mask_hbm, mask_ref)]
        )
    ]
    large = [
        pltpu.make_async_copy(
            d_hbm.at[pl.ds(i * piece, piece)], d_ref.at[pl.ds(i * piece, piece)], d_sems.at[i]
        )
        for i in range(pieces)
    ]
    for copy in small[:2] + large + small[2:]:
        copy.start()

    small[0].wait()
    small[1].wait()
    first, second = dense(slots_ref[0:1, :]), dense(slots_ref[1:2, :])
    table = rows_ref[...]
    row = jnp.concatenate([look_up(table, first), look_up(table, second)], axis=0)
    row = row - lax.axis_index("mon") * rows_dev
    col = jnp.concatenate([second, first], axis=0) - sub_index * cols
    used = lax.rem(iota(row.shape, 0), rows) < lines
    here = used & (row >= 0) & (row < rows_dev) & (col >= 0) & (col < cols)

    flags = one_hot(here)
    height = flags.shape[0]
    above = jnp.dot(
        one_hot(iota((height, height), 1) < iota((height, height), 0)),
        flags,
        preferred_element_type=F32,
    ).astype(BF16)
    place = jnp.dot(
        jnp.concatenate([flags, above], axis=1),
        jnp.concatenate(
            [
                one_hot(iota((LANES, LANES), 0) <= iota((LANES, LANES), 1)),
                jnp.ones((LANES, LANES), BF16),
            ],
            axis=0,
        ),
        preferred_element_type=F32,
    ).astype(I32)
    place = jnp.where(here, place - 1, -1)
    digits = [(x >> shift) & 255 for x in (col, row) for shift in (0, 8)]
    order = [half * rows + b for half in range(2) for b in range(lines)]
    ends = jnp.concatenate(
        [jnp.concatenate([x[r : r + 1] for x in digits], axis=0) for r in order], axis=1
    )
    ends = ends.astype(F32).astype(BF16)

    def pick(start, copies=()):
        for at, r in enumerate(order):
            perm_ref[:, at * LANES : (at + 1) * LANES] = one_hot(
                iota((ENDS, LANES), 0) + start == place[r : r + 1]
            )
        packed = lax.dot_general(
            ends, perm_ref[...], (((1,), (1,)), ((), ())), preferred_element_type=F32
        ).astype(I32)
        end_col = packed[0:1] + (packed[1:2] << 8)
        end_row = packed[2:3] + (packed[3:4] << 8)
        hot_ref[...] = one_hot(iota((cols, ENDS), 0) == end_col)
        for copy in copies:
            copy.wait()
        keep = jnp.dot(
            mask_ref[...].astype(F32).astype(BF16), hot_ref[...], preferred_element_type=F32
        )
        keep = jnp.sum(
            jnp.where(iota(keep.shape, 0) == (end_row >> 7), keep, 0.0), axis=0, keepdims=True
        )
        total = jnp.zeros((SUBLANES, ENDS), F32)
        for i in range(chunks):
            values = jnp.dot(
                d_ref[i * chunk : (i + 1) * chunk, :], hot_ref[...], preferred_element_type=F32
            )
            picked = jnp.where(iota((chunk, ENDS), 0) + i * chunk == end_row, values, 0.0)
            total += jnp.sum(picked.reshape(chunk // SUBLANES, SUBLANES, ENDS), axis=0)
        value = jnp.sum(total, axis=0, keepdims=True) * keep
        value = jnp.concatenate([value[:, q : q + LANES] for q in range(0, ENDS, LANES)], axis=0)
        return look_up(value, place - start)

    def put(cross, flow):
        for ref in (share_ref, *note_refs):
            ref[: 2 * rows, :] = cross
            ref[2 * rows : 4 * rows, :] = flow

    cross = pick(0, small[2:] + large)
    flow = jnp.where(sub_index == 0, look_up(base_ref[...], row), 0.0)
    put(cross, flow)
    my_blocks = mask_ref.shape[0] // n_sub
    for s, ref in enumerate(note_refs, 1):
        block = pl.multiple_of(lax.rem(sub_index + s, n_sub) * my_blocks, my_blocks)
        for c in range(cols // LANES):
            at = 4 * rows + c * my_blocks
            ref[at : at + my_blocks, :] = mask_ref[
                pl.ds(block, my_blocks), c * LANES : (c + 1) * LANES
            ].astype(F32)
    count = jnp.max(place) + 1

    @pl.when(count > ENDS)
    def _():
        cross_ref[...] = cross

        def more(i, _):
            cross_ref[...] += pick(i * ENDS)
            return 0

        lax.fori_loop(1, pl.cdiv(count, ENDS), more, 0)
        put(cross_ref[...], flow)


def pick_columns(parts, slot, starts, cols, masked_ref, hot_ref, out_ref):
    width = hot_ref.shape[2]
    for part in parts:
        lanes = slice(part * width, (part + 1) * width)
        for s, start in enumerate(starts):
            hot_ref[part, s * cols : (s + 1) * cols, :] = one_hot(
                iota((cols, width), 0) == slot[:, lanes] - start
            )
        out_ref[:, lanes] = jnp.dot(
            masked_ref[...], hot_ref[part], preferred_element_type=F32
        ).astype(BF16)


def fewest(parts):
    return min(2, parts)


def zero_rows(rows):
    return rows // BLOCK // 2 * BLOCK


def live_parts(count, width, parts):
    return jnp.clip((count + width - 1) // width, fewest(parts), parts)


def is_early():
    return lax.axis_index("mon") < lax.axis_size("mon") // 2


def column_starts(n_sub, cols):
    return [lax.rem(lax.axis_index("sub") + n_sub - s, n_sub) * cols for s in range(n_sub)]


def mask_factors(n_sub, refs, masked_ref):
    d_refs, note_refs, mask_ref = refs[:n_sub], refs[n_sub:-1], refs[-1]
    my_rows, all_cols = masked_ref.shape
    cols = all_cols // n_sub
    my_blocks = my_rows // BLOCK
    sub_index = lax.axis_index("sub")
    my_start = pl.multiple_of(sub_index * my_rows, my_rows)
    my_block = pl.multiple_of(sub_index * my_blocks, my_blocks)
    for s in range(n_sub):
        if s == 0:
            keep = mask_ref[pl.ds(my_block, my_blocks), :].astype(F32)
        else:
            ref = note_refs[s - 1]
            ends = range(ref.shape[0] - (cols // LANES) * my_blocks, ref.shape[0], my_blocks)
            keep = jnp.concatenate([ref[at : at + my_blocks, :] for at in ends], axis=1)
        keep = keep.astype(BF16)
        for b in range(my_blocks):
            masked_ref[b * BLOCK : (b + 1) * BLOCK, s * cols : (s + 1) * cols] = (
                d_refs[s][pl.ds(my_start + b * BLOCK, BLOCK), :] * keep[b : b + 1]
            )


def early_kernel(n_sub, *refs):
    *factor_refs, slots_ref, share_ref, masked_ref, first_ref, shared_ref, hot_ref = refs
    shared_ref[...] = share_ref[...]
    cols = masked_ref.shape[1] // n_sub

    @pl.when(is_early())
    def _():
        mask_factors(n_sub, factor_refs, masked_ref)
        starts = column_starts(n_sub, cols)
        pick_columns([0], slots_ref[0:1, :], starts, cols, masked_ref, hot_ref, first_ref)


def first_kernel(n_sub, *refs):
    *factor_refs, slots_ref, count_ref, _, _, masked_ref, first_ref, hot_ref = refs
    cols = masked_ref.shape[1] // n_sub
    slot = slots_ref[0:1, :]
    starts = column_starts(n_sub, cols)
    parts, _, width = hot_ref.shape
    live = live_parts(count_ref[0], width, parts)
    for n_parts in range(fewest(parts), parts + 1):

        @pl.when((live == n_parts) & jnp.logical_not(is_early()))
        def _():
            mask_factors(n_sub, factor_refs, masked_ref)
            pick_columns(range(n_parts), slot, starts, cols, masked_ref, hot_ref, first_ref)

        @pl.when((live == n_parts) & is_early())
        def _():
            pick_columns(range(1, n_parts), slot, starts, cols, masked_ref, hot_ref, first_ref)


def second_kernel(
    n_sub, masked_ref, slots_ref, count_ref, second_ref, out_hbm, hot_ref, zero_ref, sems
):
    cols = masked_ref.shape[1] // n_sub
    slot = slots_ref[1:2, :]
    starts = column_starts(n_sub, cols)
    parts, _, width = hot_ref.shape
    zero_start = masked_ref.shape[0] - zero_ref.shape[0]
    live = live_parts(count_ref[0], width, parts)
    for n_parts in range(fewest(parts), parts + 1):

        @pl.when(live == n_parts)
        def _():
            copies = [
                pltpu.make_async_copy(
                    zero_ref,
                    out_hbm.at[
                        pl.ds(zero_start, zero_ref.shape[0]), part * width : (part + 1) * width
                    ],
                    sems.at[part],
                )
                for part in range(n_parts, parts)
            ]
            if copies:
                zero_ref[...] = jnp.zeros_like(zero_ref)
            for copy in copies:
                copy.start()
            pick_columns(range(n_parts), slot, starts, cols, masked_ref, hot_ref, second_ref)
            for copy in copies:
                copy.wait()


def flows_kernel(n_shares, width, *refs):
    share_refs, refs = refs[:n_shares], refs[n_shares:]
    base_ref, first_ref, second_ref, count_ref, _, out_hbm, post_ref, out_sems = refs
    my_rows, cap = post_ref.shape
    my_blocks = my_rows // BLOCK
    rows = dense_rows(cap)
    total = share_refs[0][...]
    for ref in share_refs[1:]:
        total = total + ref[...]
    cross_first, cross_second, flow_first, flow_second = (
        total[i * rows : (i + 1) * rows] for i in range(4)
    )
    determinant = 1.0 - cross_first * cross_second
    shift_first = (flow_first + cross_first * flow_second) / determinant
    shift_second = (flow_second + cross_second * flow_first) / determinant
    my_block = pl.multiple_of(lax.axis_index("sub") * my_blocks, my_blocks)
    base = jnp.swapaxes(base_ref[pl.ds(my_block, my_blocks), :], 0, 1)

    def write(lines):
        live = [iota((1, LANES), 1) + line * LANES < count_ref[0] for line in lines]
        weights = [
            [
                jnp.broadcast_to(shift[line : line + 1], (BLOCK, LANES)).astype(BF16)
                for line in lines
            ]
            for shift in (shift_first, shift_second)
        ]
        out_copies = []
        for b in range(my_blocks):
            block = slice(b * BLOCK, (b + 1) * BLOCK)
            wide = slice(0, len(lines) * LANES)
            if b * BLOCK < my_rows - zero_rows(my_rows) and wide.stop < cap:
                post_ref[block, wide.stop :] = jnp.zeros((BLOCK, cap - wide.stop), BF16)
                wide = slice(0, cap)
            start = jnp.broadcast_to(base[:, b : b + 1], (BLOCK, LANES))
            for line in lines:
                lanes = slice(line * LANES, (line + 1) * LANES)
                change = (
                    weights[0][line] * first_ref[block, lanes]
                    + weights[1][line] * second_ref[block, lanes]
                )
                post_ref[block, lanes] = jnp.where(
                    live[line], start + change.astype(F32), 0.0
                ).astype(BF16)
            out_copies.append(
                pltpu.make_async_copy(
                    post_ref.at[block, wide], out_hbm.at[block, wide], out_sems.at[b]
                )
            )
            out_copies[-1].start()
        for copy in out_copies:
            copy.wait()

    parts = cap // width
    live_count = live_parts(count_ref[0], width, parts)
    for n_parts in range(fewest(parts), parts + 1):
        pl.when(live_count == n_parts)(
            functools.partial(write, range(n_parts * width // LANES))
        )


def partners(n_mon):
    half = n_mon // 2
    if n_mon & (n_mon - 1):
        return [[(m + k) % n_mon for m in range(n_mon)] for k in range(1, n_mon)]
    across = [
        [m ^ (half + k) if m < half else m ^ (n_mon - 1 - k) for m in range(n_mon)]
        for k in range(half)
    ]
    return across + [[m ^ k for m in range(n_mon)] for k in range(half - 1, 0, -1)]


def from_other_mon(share, n_mon, n_sub):
    return [
        lax.ppermute(
            share,
            ("mon", "sub"),
            [
                (m * n_sub + s, to[m] * n_sub + n_sub - 1 - s)
                for m in range(n_mon)
                for s in range(n_sub)
            ],
        )
        for to in reversed(partners(n_mon))
    ]


def on_device(dfactors, block_mask, base_flow, branch_row, pair_slots, pair_counts):
    rows_dev, cols = dfactors.shape
    blocks = rows_dev // BLOCK
    candidates = branch_row.shape[0]
    cap = pair_slots.shape[0]
    rows = dense_rows(cap)
    n_sub = lax.axis_size("sub")
    my_rows = rows_dev // n_sub
    slots = pair_slots.T
    base = base_flow.reshape(blocks, BLOCK)
    table = branch_row.reshape(candidates // LANES, LANES)
    hbm = pl.BlockSpec(memory_space=pltpu.HBM)
    in_hbm = functools.partial(pltpu.with_memory_space_constraint, memory_space=pltpu.HBM)
    in_vmem = functools.partial(pltpu.with_memory_space_constraint, memory_space=pltpu.VMEM)
    vmem = pl.BlockSpec(memory_space=pltpu.VMEM)
    smem = pl.BlockSpec(memory_space=pltpu.SMEM)
    params = pltpu.CompilerParams(vmem_limit_bytes=VMEM_LIMIT)
    rings = [[(i, (i + s) % n_sub) for i in range(n_sub)] for s in range(n_sub)]

    factors = [dfactors] + [lax.ppermute(dfactors, "sub", ring) for ring in rings[1:]]

    pieces = rows_dev // chunk_of(rows_dev, 256)
    note_rows = 4 * rows + (cols // LANES) * (my_rows // BLOCK)
    outs = pl.pallas_call(
        functools.partial(values_kernel, n_sub),
        out_shape=[pltpu.VMEM((4 * rows, LANES), F32)]
        + [pltpu.VMEM((note_rows, LANES), F32)] * (n_sub - 1)
        + [
            pltpu.VMEM((rows_dev, cols), BF16),
            pltpu.VMEM((blocks, cols), I32),
            pltpu.VMEM((blocks, BLOCK), F32),
            pltpu.VMEM((2, cap), I32),
        ],
        in_specs=[hbm] * 5,
        out_specs=[vmem] * (n_sub + 4),
        scratch_shapes=[
            pltpu.VMEM((candidates // LANES, LANES), I32),
            pltpu.VMEM((ENDS, 2 * cap), BF16),
            pltpu.VMEM((cols, ENDS), BF16),
            pltpu.VMEM((2 * rows, LANES), F32),
            pltpu.SemaphoreType.DMA((4,)),
            pltpu.SemaphoreType.DMA((pieces,)),
        ],
        compiler_params=params,
        cost_estimate=pl.CostEstimate(
            flops=2 * rows_dev * cols * ENDS, bytes_accessed=rows_dev * cols * 2, transcendentals=0
        ),
        name="pair_values",
    )(*map(in_hbm, (dfactors, block_mask, base, table, slots)))
    share, notes = outs[0], outs[1:n_sub]
    factors[0], block_mask, base, slots = outs[n_sub:]

    notes = [lax.ppermute(note, "sub", ring) for note, ring in zip(notes, rings[1:])]
    share = functools.reduce(jnp.add, [share] + [note[: 4 * rows] for note in notes])
    width = chunk_of(cap, 256)
    hot = pltpu.VMEM((cap // width, n_sub * cols, width), BF16)
    columns = pltpu.VMEM((my_rows, cap), BF16)
    masked = pltpu.VMEM((my_rows, n_sub * cols), BF16)
    columns_cost = pl.CostEstimate(
        flops=2 * my_rows * cols * n_sub * cap,
        bytes_accessed=my_rows * (cols * n_sub + cap) * 2,
        transcendentals=0,
    )
    factors = [*factors, *notes, block_mask]
    masked, first, share = pl.pallas_call(
        functools.partial(early_kernel, n_sub),
        out_shape=[masked, columns, pltpu.VMEM(share.shape, F32)],
        in_specs=[vmem] * (len(factors) + 2),
        out_specs=[vmem] * 3,
        scratch_shapes=[hot],
        compiler_params=params,
        name="early_columns",
    )(*map(in_vmem, (*factors, slots, share)))
    shares = [share, *from_other_mon(share, lax.axis_size("mon"), n_sub)]

    masked, first = pl.pallas_call(
        functools.partial(first_kernel, n_sub),
        out_shape=[pltpu.VMEM(masked.shape, BF16), columns],
        in_specs=[vmem] * (len(factors) + 1) + [smem] + [vmem] * 2,
        out_specs=[vmem] * 2,
        input_output_aliases={len(factors) + 2: 0, len(factors) + 3: 1},
        scratch_shapes=[hot],
        compiler_params=params,
        cost_estimate=columns_cost,
        name="first_columns",
    )(*map(in_vmem, (*factors, slots)), pair_counts, *map(in_vmem, (masked, first)))
    second, out = pl.pallas_call(
        functools.partial(second_kernel, n_sub),
        out_shape=[columns, pltpu.HBM((my_rows, cap), BF16)],
        in_specs=[vmem] * 2 + [smem],
        out_specs=[vmem, hbm],
        scratch_shapes=[
            hot,
            pltpu.VMEM((zero_rows(my_rows), width), BF16),
            pltpu.SemaphoreType.DMA((cap // width,)),
        ],
        compiler_params=params,
        cost_estimate=columns_cost,
        name="second_columns",
    )(*map(in_vmem, (masked, slots)), pair_counts)
    return pl.pallas_call(
        functools.partial(flows_kernel, len(shares), width),
        out_shape=jax.ShapeDtypeStruct((my_rows, cap), BF16),
        in_specs=[vmem] * (len(shares) + 3) + [smem, hbm],
        out_specs=hbm,
        input_output_aliases={len(shares) + 4: 0},
        scratch_shapes=[
            pltpu.VMEM((my_rows, cap), BF16),
            pltpu.SemaphoreType.DMA((my_rows // BLOCK,)),
        ],
        compiler_params=params,
        cost_estimate=pl.CostEstimate(
            flops=6 * my_rows * cap, bytes_accessed=my_rows * cap * 2, transcendentals=0
        ),
        name="post_flows",
    )(*map(in_vmem, (*shares, base, first, second)), pair_counts, in_hbm(out))


def solution(mesh):
    return jax.shard_map(
        on_device,
        mesh=mesh,
        in_specs=(
            P("mon", "sub"),
            P("mon", "sub"),
            P("mon"),
            P(),
            P(("grp", "pair"), None),
            P(("grp", "pair")),
        ),
        out_specs=P(("mon", "sub"), ("grp", "pair")),
        check_vma=False,
    )
```

```python
import functools

import jax
import jax.numpy as jnp
from jax import lax
from jax.experimental import pallas as pl
from jax.experimental.pallas import tpu as pltpu
from jax.sharding import PartitionSpec as P

BLOCK = 128
LANES = 128
SUBLANES = 8
ENDS = 256
VMEM_LIMIT = 16 * 1024 * 1024
F32 = jnp.float32
BF16 = jnp.bfloat16
I32 = jnp.int32


def chunk_of(total, want):
    size = min(total, want)
    while total % size:
        size -= BLOCK
    return size


def dense_rows(cap):
    return -(-cap // (LANES * SUBLANES)) * SUBLANES


def one_hot(hit):
    return jnp.where(hit, 1.0, 0.0).astype(BF16)


def iota(shape, axis):
    return lax.broadcasted_iota(I32, shape, axis)


def dense(line):
    cap = line.shape[1]
    rows = dense_rows(cap)
    pieces = [line[:, c : c + LANES] for c in range(0, cap, LANES)]
    if len(pieces) < rows:
        pieces.append(jnp.zeros((rows - len(pieces), LANES), line.dtype))
    return jnp.concatenate(pieces, axis=0)


def look_up(table, index):
    high, low = index >> 7, index & 127
    found = jnp.zeros(index.shape, table.dtype)
    for b in range(table.shape[0]):
        line = jnp.broadcast_to(table[b : b + 1], index.shape)
        value = jnp.take_along_axis(line, low, axis=1, mode="promise_in_bounds")
        found = jnp.where(high == b, value, found)
    return found


def values_kernel(
    n_sub, d_hbm, mask_hbm, base_hbm, rows_hbm, slots_hbm, *refs
):
    share_ref, *note_refs = refs[:n_sub]
    (
        d_ref, mask_ref, base_ref, slots_ref, rows_ref, perm_ref, hot_ref, cross_ref, sems, d_sems
    ) = refs[n_sub:]
    rows_dev, cols = d_ref.shape
    pieces = d_sems.shape[0]
    piece = rows_dev // pieces
    chunk = chunk_of(rows_dev, 512)
    chunks = rows_dev // chunk
    cap = slots_ref.shape[1]
    lines = cap // LANES
    rows = dense_rows(cap)
    sub_index = lax.axis_index("sub")
    small = [
        pltpu.make_async_copy(src, dst, sems.at[i])
        for i, (src, dst) in enumerate(
            [(slots_hbm, slots_ref), (rows_hbm, rows_ref), (base_hbm, base_ref), (mask_hbm, mask_ref)]
        )
    ]
    large = [
        pltpu.make_async_copy(
            d_hbm.at[pl.ds(i * piece, piece)], d_ref.at[pl.ds(i * piece, piece)], d_sems.at[i]
        )
        for i in range(pieces)
    ]
    for copy in small[:2] + large + small[2:]:
        copy.start()

    small[0].wait()
    small[1].wait()
    first, second = dense(slots_ref[0:1, :]), dense(slots_ref[1:2, :])
    table = rows_ref[...]
    row = jnp.concatenate([look_up(table, first), look_up(table, second)], axis=0)
    row = row - lax.axis_index("mon") * rows_dev
    col = jnp.concatenate([second, first], axis=0) - sub_index * cols
    used = lax.rem(iota(row.shape, 0), rows) < lines
    here = used & (row >= 0) & (row < rows_dev) & (col >= 0) & (col < cols)

    flags = one_hot(here)
    height = flags.shape[0]
    above = jnp.dot(
        one_hot(iota((height, height), 1) < iota((height, height), 0)),
        flags,
        preferred_element_type=F32,
    ).astype(BF16)
    place = jnp.dot(
        jnp.concatenate([flags, above], axis=1),
        jnp.concatenate(
            [
                one_hot(iota((LANES, LANES), 0) <= iota((LANES, LANES), 1)),
                jnp.ones((LANES, LANES), BF16),
            ],
            axis=0,
        ),
        preferred_element_type=F32,
    ).astype(I32)
    place = jnp.where(here, place - 1, -1)
    digits = [(x >> shift) & 255 for x in (col, row) for shift in (0, 8)]
    order = [half * rows + b for half in range(2) for b in range(lines)]
    ends = jnp.concatenate(
        [jnp.concatenate([x[r : r + 1] for x in digits], axis=0) for r in order], axis=1
    )
    ends = ends.astype(F32).astype(BF16)

    def pick(start, copies=()):
        for at, r in enumerate(order):
            perm_ref[:, at * LANES : (at + 1) * LANES] = one_hot(
                iota((ENDS, LANES), 0) + start == place[r : r + 1]
            )
        packed = lax.dot_general(
            ends, perm_ref[...], (((1,), (1,)), ((), ())), preferred_element_type=F32
        ).astype(I32)
        end_col = packed[0:1] + (packed[1:2] << 8)
        end_row = packed[2:3] + (packed[3:4] << 8)
        hot_ref[...] = one_hot(iota((cols, ENDS), 0) == end_col)
        for copy in copies:
            copy.wait()
        keep = jnp.dot(
            mask_ref[...].astype(F32).astype(BF16), hot_ref[...], preferred_element_type=F32
        )
        keep = jnp.sum(
            jnp.where(iota(keep.shape, 0) == (end_row >> 7), keep, 0.0), axis=0, keepdims=True
        )
        total = jnp.zeros((SUBLANES, ENDS), F32)
        for i in range(chunks):
            values = jnp.dot(
                d_ref[i * chunk : (i + 1) * chunk, :], hot_ref[...], preferred_element_type=F32
            )
            picked = jnp.where(iota((chunk, ENDS), 0) + i * chunk == end_row, values, 0.0)
            total += jnp.sum(picked.reshape(chunk // SUBLANES, SUBLANES, ENDS), axis=0)
        value = jnp.sum(total, axis=0, keepdims=True) * keep
        value = jnp.concatenate([value[:, q : q + LANES] for q in range(0, ENDS, LANES)], axis=0)
        return look_up(value, place - start)

    def put(cross, flow):
        for ref in (share_ref, *note_refs):
            ref[: 2 * rows, :] = cross
            ref[2 * rows : 4 * rows, :] = flow

    cross = pick(0, small[2:] + large)
    flow = jnp.where(sub_index == 0, look_up(base_ref[...], row), 0.0)
    put(cross, flow)
    my_blocks = mask_ref.shape[0] // n_sub
    for s, ref in enumerate(note_refs, 1):
        block = pl.multiple_of(lax.rem(sub_index + s, n_sub) * my_blocks, my_blocks)
        for c in range(cols // LANES):
            at = 4 * rows + c * my_blocks
            ref[at : at + my_blocks, :] = mask_ref[
                pl.ds(block, my_blocks), c * LANES : (c + 1) * LANES
            ].astype(F32)
    count = jnp.max(place) + 1

    @pl.when(count > ENDS)
    def _():
        cross_ref[...] = cross

        def more(i, _):
            cross_ref[...] += pick(i * ENDS)
            return 0

        lax.fori_loop(1, pl.cdiv(count, ENDS), more, 0)
        put(cross_ref[...], flow)


def pick_columns(parts, slot, starts, cols, masked_ref, hot_ref, out_ref):
    width = hot_ref.shape[2]
    for part in parts:
        lanes = slice(part * width, (part + 1) * width)
        for s, start in enumerate(starts):
            hot_ref[part, s * cols : (s + 1) * cols, :] = one_hot(
                iota((cols, width), 0) == slot[:, lanes] - start
            )
        out_ref[:, lanes] = jnp.dot(
            masked_ref[...], hot_ref[part], preferred_element_type=F32
        ).astype(BF16)


def fewest(parts):
    return min(2, parts)


def zero_rows(rows):
    return rows // BLOCK // 2 * BLOCK


def live_parts(count, width, parts):
    return jnp.clip((count + width - 1) // width, fewest(parts), parts)


def is_early():
    return lax.axis_index("mon") < lax.axis_size("mon") // 2


def column_starts(n_sub, cols):
    return [lax.rem(lax.axis_index("sub") + n_sub - s, n_sub) * cols for s in range(n_sub)]


def mask_factors(n_sub, refs, masked_ref):
    d_refs, note_refs, mask_ref = refs[:n_sub], refs[n_sub:-1], refs[-1]
    my_rows, all_cols = masked_ref.shape
    cols = all_cols // n_sub
    my_blocks = my_rows // BLOCK
    sub_index = lax.axis_index("sub")
    my_start = pl.multiple_of(sub_index * my_rows, my_rows)
    my_block = pl.multiple_of(sub_index * my_blocks, my_blocks)
    for s in range(n_sub):
        if s == 0:
            keep = mask_ref[pl.ds(my_block, my_blocks), :].astype(F32)
        else:
            ref = note_refs[s - 1]
            ends = range(ref.shape[0] - (cols // LANES) * my_blocks, ref.shape[0], my_blocks)
            keep = jnp.concatenate([ref[at : at + my_blocks, :] for at in ends], axis=1)
        keep = keep.astype(BF16)
        for b in range(my_blocks):
            masked_ref[b * BLOCK : (b + 1) * BLOCK, s * cols : (s + 1) * cols] = (
                d_refs[s][pl.ds(my_start + b * BLOCK, BLOCK), :] * keep[b : b + 1]
            )


def early_kernel(n_sub, *refs):
    *factor_refs, slots_ref, share_ref, masked_ref, first_ref, shared_ref, hot_ref = refs
    shared_ref[...] = share_ref[...]
    cols = masked_ref.shape[1] // n_sub

    @pl.when(is_early())
    def _():
        mask_factors(n_sub, factor_refs, masked_ref)
        starts = column_starts(n_sub, cols)
        pick_columns([0], slots_ref[0:1, :], starts, cols, masked_ref, hot_ref, first_ref)


def first_kernel(n_sub, *refs):
    *factor_refs, slots_ref, count_ref, _, _, masked_ref, first_ref, hot_ref = refs
    cols = masked_ref.shape[1] // n_sub
    slot = slots_ref[0:1, :]
    starts = column_starts(n_sub, cols)
    parts, _, width = hot_ref.shape
    live = live_parts(count_ref[0], width, parts)
    for n_parts in range(fewest(parts), parts + 1):

        @pl.when((live == n_parts) & jnp.logical_not(is_early()))
        def _():
            mask_factors(n_sub, factor_refs, masked_ref)
            pick_columns(range(n_parts), slot, starts, cols, masked_ref, hot_ref, first_ref)

        @pl.when((live == n_parts) & is_early())
        def _():
            pick_columns(range(1, n_parts), slot, starts, cols, masked_ref, hot_ref, first_ref)


def second_kernel(
    n_sub, masked_ref, slots_ref, count_ref, second_ref, out_hbm, hot_ref, zero_ref, sems
):
    cols = masked_ref.shape[1] // n_sub
    slot = slots_ref[1:2, :]
    starts = column_starts(n_sub, cols)
    parts, _, width = hot_ref.shape
    zero_start = masked_ref.shape[0] - zero_ref.shape[0]
    live = live_parts(count_ref[0], width, parts)
    for n_parts in range(fewest(parts), parts + 1):

        @pl.when(live == n_parts)
        def _():
            copies = [
                pltpu.make_async_copy(
                    zero_ref,
                    out_hbm.at[
                        pl.ds(zero_start, zero_ref.shape[0]), part * width : (part + 1) * width
                    ],
                    sems.at[part],
                )
                for part in range(n_parts, parts)
            ]
            if copies:
                zero_ref[...] = jnp.zeros_like(zero_ref)
            for copy in copies:
                copy.start()
            pick_columns(range(n_parts), slot, starts, cols, masked_ref, hot_ref, second_ref)
            for copy in copies:
                copy.wait()


def flows_kernel(n_shares, width, *refs):
    share_refs, refs = refs[:n_shares], refs[n_shares:]
    base_ref, first_ref, second_ref, count_ref, _, out_hbm, post_ref, out_sems = refs
    my_rows, cap = post_ref.shape
    my_blocks = my_rows // BLOCK
    rows = dense_rows(cap)
    total = share_refs[0][...]
    for ref in share_refs[1:]:
        total = total + ref[...]
    cross_first, cross_second, flow_first, flow_second = (
        total[i * rows : (i + 1) * rows] for i in range(4)
    )
    determinant = 1.0 - cross_first * cross_second
    shift_first = (flow_first + cross_first * flow_second) / determinant
    shift_second = (flow_second + cross_second * flow_first) / determinant
    my_block = pl.multiple_of(lax.axis_index("sub") * my_blocks, my_blocks)
    base = jnp.swapaxes(base_ref[pl.ds(my_block, my_blocks), :], 0, 1)

    def write(lines):
        live = [iota((1, LANES), 1) + line * LANES < count_ref[0] for line in lines]
        weights = [
            [
                jnp.broadcast_to(shift[line : line + 1], (BLOCK, LANES)).astype(BF16)
                for line in lines
            ]
            for shift in (shift_first, shift_second)
        ]
        out_copies = []
        for b in range(my_blocks):
            block = slice(b * BLOCK, (b + 1) * BLOCK)
            wide = slice(0, len(lines) * LANES)
            if b * BLOCK < my_rows - zero_rows(my_rows) and wide.stop < cap:
                post_ref[block, wide.stop :] = jnp.zeros((BLOCK, cap - wide.stop), BF16)
                wide = slice(0, cap)
            start = jnp.broadcast_to(base[:, b : b + 1], (BLOCK, LANES))
            for line in lines:
                lanes = slice(line * LANES, (line + 1) * LANES)
                change = (
                    weights[0][line] * first_ref[block, lanes]
                    + weights[1][line] * second_ref[block, lanes]
                )
                post_ref[block, lanes] = jnp.where(
                    live[line], start + change.astype(F32), 0.0
                ).astype(BF16)
            out_copies.append(
                pltpu.make_async_copy(
                    post_ref.at[block, wide], out_hbm.at[block, wide], out_sems.at[b]
                )
            )
            out_copies[-1].start()
        for copy in out_copies:
            copy.wait()

    parts = cap // width
    live_count = live_parts(count_ref[0], width, parts)
    for n_parts in range(fewest(parts), parts + 1):
        pl.when(live_count == n_parts)(
            functools.partial(write, range(n_parts * width // LANES))
        )


def partners(n_mon):
    half = n_mon // 2
    if n_mon & (n_mon - 1):
        return [[(m + k) % n_mon for m in range(n_mon)] for k in range(1, n_mon)]
    across = [
        [m ^ (half + k) if m < half else m ^ (n_mon - 1 - k) for m in range(n_mon)]
        for k in range(half)
    ]
    return across + [[m ^ k for m in range(n_mon)] for k in range(half - 1, 0, -1)]


def from_other_mon(share, n_mon, n_sub):
    return [
        lax.ppermute(
            share,
            ("mon", "sub"),
            [
                (m * n_sub + s, to[m] * n_sub + n_sub - 1 - s)
                for m in range(n_mon)
                for s in range(n_sub)
            ],
        )
        for to in reversed(partners(n_mon))
    ]


def on_device(dfactors, block_mask, base_flow, branch_row, pair_slots, pair_counts):
    rows_dev, cols = dfactors.shape
    blocks = rows_dev // BLOCK
    candidates = branch_row.shape[0]
    cap = pair_slots.shape[0]
    rows = dense_rows(cap)
    n_sub = lax.axis_size("sub")
    my_rows = rows_dev // n_sub
    slots = pair_slots.T
    base = base_flow.reshape(blocks, BLOCK)
    table = branch_row.reshape(candidates // LANES, LANES)
    hbm = pl.BlockSpec(memory_space=pltpu.HBM)
    in_hbm = functools.partial(pltpu.with_memory_space_constraint, memory_space=pltpu.HBM)
    in_vmem = functools.partial(pltpu.with_memory_space_constraint, memory_space=pltpu.VMEM)
    vmem = pl.BlockSpec(memory_space=pltpu.VMEM)
    smem = pl.BlockSpec(memory_space=pltpu.SMEM)
    params = pltpu.CompilerParams(vmem_limit_bytes=VMEM_LIMIT)
    rings = [[(i, (i + s) % n_sub) for i in range(n_sub)] for s in range(n_sub)]

    factors = [dfactors] + [lax.ppermute(dfactors, "sub", ring) for ring in rings[1:]]

    pieces = rows_dev // chunk_of(rows_dev, rows_dev)
    note_rows = 4 * rows + (cols // LANES) * (my_rows // BLOCK)
    outs = pl.pallas_call(
        functools.partial(values_kernel, n_sub),
        out_shape=[pltpu.VMEM((4 * rows, LANES), F32)]
        + [pltpu.VMEM((note_rows, LANES), F32)] * (n_sub - 1)
        + [
            pltpu.VMEM((rows_dev, cols), BF16),
            pltpu.VMEM((blocks, cols), I32),
            pltpu.VMEM((blocks, BLOCK), F32),
            pltpu.VMEM((2, cap), I32),
        ],
        in_specs=[hbm] * 5,
        out_specs=[vmem] * (n_sub + 4),
        scratch_shapes=[
            pltpu.VMEM((candidates // LANES, LANES), I32),
            pltpu.VMEM((ENDS, 2 * cap), BF16),
            pltpu.VMEM((cols, ENDS), BF16),
            pltpu.VMEM((2 * rows, LANES), F32),
            pltpu.SemaphoreType.DMA((4,)),
            pltpu.SemaphoreType.DMA((pieces,)),
        ],
        compiler_params=params,
        cost_estimate=pl.CostEstimate(
            flops=2 * rows_dev * cols * ENDS, bytes_accessed=rows_dev * cols * 2, transcendentals=0
        ),
        name="pair_values",
    )(*map(in_hbm, (dfactors, block_mask, base, table, slots)))
    share, notes = outs[0], outs[1:n_sub]
    factors[0], block_mask, base, slots = outs[n_sub:]

    notes = [lax.ppermute(note, "sub", ring) for note, ring in zip(notes, rings[1:])]
    share = functools.reduce(jnp.add, [share] + [note[: 4 * rows] for note in notes])
    width = chunk_of(cap, 256)
    hot = pltpu.VMEM((cap // width, n_sub * cols, width), BF16)
    columns = pltpu.VMEM((my_rows, cap), BF16)
    masked = pltpu.VMEM((my_rows, n_sub * cols), BF16)
    columns_cost = pl.CostEstimate(
        flops=2 * my_rows * cols * n_sub * cap,
        bytes_accessed=my_rows * (cols * n_sub + cap) * 2,
        transcendentals=0,
    )
    factors = [*factors, *notes, block_mask]
    masked, first, share = pl.pallas_call(
        functools.partial(early_kernel, n_sub),
        out_shape=[masked, columns, pltpu.VMEM(share.shape, F32)],
        in_specs=[vmem] * (len(factors) + 2),
        out_specs=[vmem] * 3,
        scratch_shapes=[hot],
        compiler_params=params,
        name="early_columns",
    )(*map(in_vmem, (*factors, slots, share)))
    shares = [share, *from_other_mon(share, lax.axis_size("mon"), n_sub)]

    masked, first = pl.pallas_call(
        functools.partial(first_kernel, n_sub),
        out_shape=[pltpu.VMEM(masked.shape, BF16), columns],
        in_specs=[vmem] * (len(factors) + 1) + [smem] + [vmem] * 2,
        out_specs=[vmem] * 2,
        input_output_aliases={len(factors) + 2: 0, len(factors) + 3: 1},
        scratch_shapes=[hot],
        compiler_params=params,
        cost_estimate=columns_cost,
        name="first_columns",
    )(*map(in_vmem, (*factors, slots)), pair_counts, *map(in_vmem, (masked, first)))
    second, out = pl.pallas_call(
        functools.partial(second_kernel, n_sub),
        out_shape=[columns, pltpu.HBM((my_rows, cap), BF16)],
        in_specs=[vmem] * 2 + [smem],
        out_specs=[vmem, hbm],
        scratch_shapes=[
            hot,
            pltpu.VMEM((zero_rows(my_rows), width), BF16),
            pltpu.SemaphoreType.DMA((cap // width,)),
        ],
        compiler_params=params,
        cost_estimate=columns_cost,
        name="second_columns",
    )(*map(in_vmem, (masked, slots)), pair_counts)
    return pl.pallas_call(
        functools.partial(flows_kernel, len(shares), width),
        out_shape=jax.ShapeDtypeStruct((my_rows, cap), BF16),
        in_specs=[vmem] * (len(shares) + 3) + [smem, hbm],
        out_specs=hbm,
        input_output_aliases={len(shares) + 4: 0},
        scratch_shapes=[
            pltpu.VMEM((my_rows, cap), BF16),
            pltpu.SemaphoreType.DMA((my_rows // BLOCK,)),
        ],
        compiler_params=params,
        cost_estimate=pl.CostEstimate(
            flops=6 * my_rows * cap, bytes_accessed=my_rows * cap * 2, transcendentals=0
        ),
        name="post_flows",
    )(*map(in_vmem, (*shares, base, first, second)), pair_counts, in_hbm(out))


def solution(mesh):
    return jax.shard_map(
        on_device,
        mesh=mesh,
        in_specs=(
            P("mon", "sub"),
            P("mon", "sub"),
            P("mon"),
            P(),
            P(("grp", "pair"), None),
            P(("grp", "pair")),
        ),
        out_specs=P(("mon", "sub"), ("grp", "pair")),
        check_vma=False,
    )
```
